32 devices in a mesh: lat: 8 (over y, x, core), lon: 4 (over z).
Axes of the slice: x: 2, y: 2, z: 4, core: 2. Of those that a mesh axis runs over, the one named last changes fastest.
Arguments:
- spectral: bfloat16 [6, 32, 640, 1280], P(None, 'lon', 'lat'), may hold values from -6 to 6
- legendre: bfloat16 [640, 1280, 128], P('lat'), may hold values from -0.15625 to 0.15625
- wave_ids: int32 [640], replicated, may hold values from 0 to 639, each once
- points: int32 [128], P('lat'), may hold values from 512 to 1024
- tracers: bfloat16 [16, 32, 128, 1024], P(None, None, 'lat', 'lon'), may hold values from -6 to 6
- react_base: float32 [16, 16], replicated, may hold values from -0.75 to 0.75
- react_temp: float32 [16, 16], replicated, may hold values from -0.75 to 0.75
- active_ids: int32 [4], replicated, may hold values from 0 to 15, as said below
Outputs:
- tracers_new: bfloat16 [16, 32, 128, 1024], P(None, None, 'lat', 'lon')
- active: float32 [4, 32, 128, 1024], P(None, 'lon', 'lat')
The draws below stay inside these ranges and needn't reach their ends.
Inputs may be any that keep to these rules, and one draw needn't show every extreme that they name: `active_ids`: distinct tracer indices. `wave_ids`: each slot a different wavenumber.
All inputs are finite; a program needn't handle non-finite values.
Results may differ from the reference program's by a relative error of at most 0.0042.
Values may be sent and summed in bfloat16 or wider, within the bound.
No kernel may reach another device: no remote copies, remote signals or barrier semaphores. Data moves between devices by JAX's collectives and lax.ppermute only.
A program may use at most 256 MiB of HBM per device.

```python
import jax
import jax.numpy as jnp
from jax import lax

NSPEC = 1280
MW = 640
TRACERS = 16
ACTIVE = 4
NLAT = 128
LEV = 32
NLON = 1024


def draw_active_ids(key, part):
    return jax.random.permutation(key, TRACERS)[:ACTIVE].astype(jnp.int32)


def place_ends(result, stream_key, low, high):
    place = [jax.random.randint(jax.random.fold_in(stream_key, axis), (), 0, length) for axis, length in enumerate(result.shape)]
    main_axis = result.shape.index(max(result.shape))
    next_to = place[:main_axis] + [(place[main_axis] + 1) % result.shape[main_axis]] + place[main_axis + 1:]
    return result.at[tuple(place)].set(low).at[tuple(next_to)].set(high)


def steps_of(stream_key, shape, pieces, least, top_value):
    def one(axis_at, shards_of):
        heights = jax.random.uniform(jax.random.fold_in(jax.random.fold_in(stream_key, 6), axis_at), (shards_of,), jnp.float32, least / len(pieces), top_value / len(pieces))
        return jnp.repeat(jnp.exp(heights), shape[axis_at] // shards_of).reshape((-1,) + (1,) * (len(shape) - axis_at - 1))

    factor_of = one(*pieces[0])
    for cut in pieces[1:]:
        factor_of = factor_of * one(*cut)
    return factor_of


def normal_values(rng, extent, spread, reach, cuts=(), dtype=jnp.bfloat16):
    entries = spread * jax.random.normal(rng, extent, jnp.float32)
    if cuts:
        entries = entries * steps_of(rng, extent, cuts, -0.22, 0.18)
    return jnp.clip(entries, -reach, reach).astype(dtype)


def setup_inputs(seed: int = 0) -> dict:
    key_list = jax.random.split(jax.random.key(seed), 9)
    spectral = normal_values(key_list[0], (6, LEV, MW, NSPEC), 1.0, 6.0, ((1, 4), (2, 8)))
    legendre = normal_values(key_list[1], (MW, NSPEC, NLAT), NSPEC ** -0.5, 0.15625, ((0, 8),))
    wave_ids = jax.random.permutation(key_list[2], MW).astype(jnp.int32)
    points = place_ends(jax.random.randint(key_list[3], (NLAT,), NLON // 2, NLON + 1), jax.random.fold_in(key_list[3], 1), NLON // 2, NLON).astype(jnp.int32)
    tracers = normal_values(key_list[4], (TRACERS, LEV, NLAT, NLON), 1.0, 6.0, ((2, 8), (3, 4)))
    react_base = normal_values(key_list[5], (TRACERS, TRACERS), 64 ** -0.5, 0.75, (), jnp.float32)
    react_temp = normal_values(key_list[6], (TRACERS, TRACERS), 64 ** -0.5, 0.75, (), jnp.float32)
    active_ids = draw_active_ids(jax.random.fold_in(key_list[8], 71), 0)
    return dict(spectral=spectral, legendre=legendre, wave_ids=wave_ids, points=points, tracers=tracers, react_base=react_base, react_temp=react_temp, active_ids=active_ids)


def reference(spectral, legendre, wave_ids, points, tracers, react_base, react_temp, active_ids):
    high = lax.Precision.HIGHEST
    fourier = jnp.einsum('rlmn,mnj->rlmj', spectral.astype(jnp.float32), legendre.astype(jnp.float32), precision=high)
    fourier = lax.optimization_barrier(fourier.astype(jnp.bfloat16)).astype(jnp.float32)
    parted = fourier.reshape(3, 2, LEV, MW, NLAT)
    by_row = jnp.moveaxis(parted, 4, 0)
    columns = jnp.arange(NLON).astype(jnp.int32)

    def one_row(item):
        coeffs, count = item
        product = columns[:, None] * wave_ids[None, :].astype(jnp.int32) % count
        angle = 2.0 * jnp.pi * product.astype(jnp.float32) / count.astype(jnp.float32)
        cosine = lax.optimization_barrier(jnp.cos(angle).astype(jnp.bfloat16)).astype(jnp.float32)
        sine = lax.optimization_barrier(jnp.sin(angle).astype(jnp.bfloat16)).astype(jnp.float32)
        first = jnp.einsum('flm,im->fli', coeffs[:, 0], cosine, precision=high)
        second = jnp.einsum('flm,im->fli', coeffs[:, 1], sine, precision=high)
        return first - second
    rows = lax.map(one_row, (by_row, points))
    grid = jnp.transpose(rows, (1, 2, 0, 3)) / jnp.sqrt(jnp.float32(MW))
    wind_u, wind_v, temper = (grid[0], grid[1], grid[2])
    state = tracers.astype(jnp.float32)
    padded = jnp.pad(state, ((0, 0), (0, 0), (1, 1), (1, 1)))
    east = padded[:, :, 1:-1, 2:]
    west = padded[:, :, 1:-1, :-2]
    north = padded[:, :, 2:, 1:-1]
    south = padded[:, :, :-2, 1:-1]
    moved = state - 0.1 * wind_u * (east - west) - 0.1 * wind_v * (north - south) + 0.05 * (east + west + north + south - 4.0 * state)
    base_term = jnp.einsum('st,tlji->slji', react_base, moved, precision=high)
    temp_term = jnp.einsum('st,tlji->slji', react_temp, moved, precision=high)
    mask = (columns[None, :] < points[:, None]).astype(jnp.float32)
    reacted = (moved + base_term + temper * temp_term) * mask
    active = jnp.take(reacted, active_ids, axis=0)
    return (reacted.astype(jnp.bfloat16), active)
```

```python
import functools

import jax
import jax.numpy as jnp
import numpy as np
from jax import lax
from jax.experimental import pallas as pl
from jax.experimental.pallas import tpu as pltpu
from jax.sharding import PartitionSpec as P

F32 = jnp.float32
BF16 = jnp.bfloat16
LANES = 128
LOW = 16
VMEM = 56 * 1024 * 1024

COS = (
    0.9999999890590228,
    -19.739204499454026,
    64.93911745990036,
    -85.45013953095037,
    60.16763095136588,
    -25.96759924965491,
    6.528658162567069,
)
SIN = (
    6.283185302511503,
    -41.34170040531769,
    81.60513138580204,
    -76.7030153539128,
    42.02592698618416,
    -14.899846668691637,
    3.238137510515757,
)


def dot(a, b, dims):
    return lax.dot_general(a, b, (dims, ((), ())), preferred_element_type=F32)


def unit_circle(step, rows, waves, count):
    index = lax.broadcasted_iota(jnp.int32, (rows, waves.shape[1]), 0) * step
    product = index.astype(F32) * waves
    inverse = 1.0 / count
    turns = (product - jnp.floor(product * inverse) * count) * inverse
    y = turns - jnp.floor(turns + 0.5)
    z = y * y
    cosine = jnp.full_like(z, COS[-1])
    sine = jnp.full_like(z, SIN[-1])
    for c, s in zip(COS[-2::-1], SIN[-2::-1]):
        cosine = cosine * z + c
        sine = sine * z + s
    return cosine, sine * y


def table_kernel(points, waves_ref, table_ref, twiddle_ref):
    count = jnp.full(waves_ref.shape, points[pl.program_id(0)], jnp.int32).astype(F32)
    waves = waves_ref[...]
    size = waves.shape[1]
    cos_low, sin_low = unit_circle(1, LOW, waves, count)
    cos_high, sin_high = unit_circle(LOW, LANES // LOW, waves, count)
    for a in range(LANES // LOW):
        ch, sh = cos_high[a : a + 1], sin_high[a : a + 1]
        rows = slice(a * LOW, (a + 1) * LOW)
        table_ref[0, rows, :size] = (ch * cos_low - sh * sin_low).astype(BF16)
        table_ref[0, rows, size:] = (-sh * cos_low - ch * sin_low).astype(BF16)
    turns = twiddle_ref.shape[2]
    cos_turn, sin_turn = unit_circle(LANES, turns, waves, count)
    twiddle_ref[0, 0] = cos_turn
    twiddle_ref[0, 1] = sin_turn


def tables(points, wave_ids, turns):
    rows, waves = points.shape[0], wave_ids.shape[0]
    return pl.pallas_call(
        table_kernel,
        grid_spec=pltpu.PrefetchScalarGridSpec(
            num_scalar_prefetch=1,
            grid=(rows,),
            in_specs=[pl.BlockSpec((1, waves), lambda j, p: (0, 0))],
            out_specs=[
                pl.BlockSpec((1, LANES, 2 * waves), lambda j, p: (j, 0, 0)),
                pl.BlockSpec((1, 2, turns, waves), lambda j, p: (j, 0, 0, 0)),
            ],
        ),
        out_shape=[
            jax.ShapeDtypeStruct((rows, LANES, 2 * waves), BF16),
            jax.ShapeDtypeStruct((rows, 2, turns, waves), F32),
        ],
        compiler_params=pltpu.CompilerParams(vmem_limit_bytes=VMEM),
        name="tables",
    )(points, wave_ids.astype(F32)[None, :])


def place(pieces, width):
    out = [None] * (width // LANES)
    lane = lax.broadcasted_iota(jnp.int32, (pieces[0][0].shape[0], LANES), 1)
    for value, start, count, here in pieces:
        shift = (here - start) % LANES
        for a in range(start // LANES, (start + count - 1) // LANES + 1):
            part = value[:, a * LANES : (a + 1) * LANES]
            if shift:
                part = pltpu.roll(part, shift, 1)
            first = max(start, a * LANES) - start + here
            last = min(start + count, (a + 1) * LANES) - start + here
            for v in range(first // LANES, (last - 1) // LANES + 1):
                low, high = max(first - v * LANES, 0), min(last - v * LANES, LANES)
                if out[v] is None:
                    out[v] = part
                else:
                    out[v] = jnp.where((lane >= low) & (lane < high), part, out[v])
    return out


def synth_kernel(recv_ref, table_ref, twiddle_ref, out_ref, coef, grid):
    sources, levels, rows, _ = recv_ref.shape
    fields, waves = coef.shape[0] // 2, coef.shape[1] * LANES
    share = waves // sources
    turns = twiddle_ref.shape[2]
    j = pl.program_id(0)

    @pl.when(j == 0)
    def _():
        def level(l, carry):
            values = [recv_ref[s, l].astype(F32) for s in range(sources)]
            for r in range(2 * fields):
                windows = [
                    (values[s], r * share, share, s * share) for s in range(sources)
                ]
                for v, part in enumerate(place(windows, waves)):
                    coef[r, v, pl.ds(l * rows, rows), :] = part
            return carry

        lax.fori_loop(0, levels, level, 0)

    def own_row(r):
        parts = [coef[r, v, pl.ds(j, levels, stride=rows), :] for v in range(waves // LANES)]
        return jnp.concatenate(parts, axis=1)

    values = [own_row(r) for r in range(2 * fields)]
    real, imag = [], []
    for t in range(turns):
        c, s = twiddle_ref[0, 0, t : t + 1], twiddle_ref[0, 1, t : t + 1]
        for f in range(fields):
            re, im = values[2 * f], values[2 * f + 1]
            real.append(re * c - im * s)
            imag.append(re * s + im * c)
    real = jnp.concatenate(real, axis=0).astype(BF16)
    imag = jnp.concatenate(imag, axis=0).astype(BF16)
    nt = ((1,), (1,))
    values = dot(real, table_ref[0, :, :waves], nt) + dot(imag, table_ref[0, :, waves:], nt)
    grid[pl.ds(j, turns * fields * levels, stride=rows), :] = values

    @pl.when(j == rows - 1)
    def _():
        dests = out_ref.shape[0]
        each = turns // dests
        size = levels * rows
        for t in range(turns):
            lanes = slice((t % each) * LANES, (t % each + 1) * LANES)
            for f in range(fields):
                block = grid[(t * fields + f) * size : (t * fields + f + 1) * size, :]
                out_ref[t // each, f, :, :, lanes] = block.reshape(levels, rows, LANES).astype(BF16)


def synthesis(recv, table, twiddle, dests, tile):
    sources, levels, rows, lanes = recv.shape
    turns, waves = twiddle.shape[2:]
    fields = 3
    return pl.pallas_call(
        synth_kernel,
        grid=(rows,),
        in_specs=[
            pl.BlockSpec(recv.shape, lambda j: (0, 0, 0, 0)),
            pl.BlockSpec((1, LANES, 2 * waves), lambda j: (j, 0, 0)),
            pl.BlockSpec((1, 2, turns, waves), lambda j: (j, 0, 0, 0)),
        ],
        out_specs=pl.BlockSpec((dests, fields, levels, rows, tile), lambda j: (0, 0, 0, 0, 0)),
        out_shape=jax.ShapeDtypeStruct((dests, fields, levels, rows, tile), BF16),
        scratch_shapes=[
            pltpu.VMEM((2 * fields, waves // LANES, levels * rows, LANES), F32),
            pltpu.VMEM((turns * fields * levels * rows, LANES), F32),
        ],
        compiler_params=pltpu.CompilerParams(vmem_limit_bytes=VMEM),
        name="synthesis",
    )(recv, table, twiddle)


def edge_kernel(state_ref, pick_ref, first_ref, last_ref, west_ref, east_ref):
    tracers, levels, rows, tile = state_ref.shape
    ends = lax.broadcasted_iota(jnp.int32, (2 * levels, tile), 1)
    row = lax.broadcasted_iota(jnp.int32, (2 * levels, tile), 0)
    columns = jnp.zeros((2 * levels, tracers * rows), F32)
    for l in range(levels):
        x = state_ref[:, l].reshape(tracers * rows, tile)
        picked = dot(pick_ref[...], x, ((1,), (0,)))
        first_ref[l] = picked[:tracers].astype(BF16)
        last_ref[l] = picked[tracers:].astype(BF16)
        mark = ((row == l) & (ends == 0)) | ((row == levels + l) & (ends == tile - 1))
        columns = columns + dot(jnp.where(mark, 1.0, 0.0).astype(BF16), x, ((1,), (1,)))
    west_ref[...] = columns[:levels].astype(BF16)
    east_ref[...] = columns[levels:].astype(BF16)


def edges(state):
    tracers, levels, rows, tile = state.shape
    block = 16
    pick = np.zeros((2 * tracers, tracers * rows), np.float32)
    for t in range(tracers):
        pick[t, t * rows] = 1
        pick[tracers + t, t * rows + rows - 1] = 1
    rowed = jax.ShapeDtypeStruct((levels, tracers, tile), BF16)
    columned = jax.ShapeDtypeStruct((levels, tracers * rows), BF16)
    row_spec = pl.BlockSpec((block, tracers, tile), lambda i: (i, 0, 0))
    col_spec = pl.BlockSpec((block, tracers * rows), lambda i: (i, 0))
    return pl.pallas_call(
        edge_kernel,
        grid=(levels // block,),
        in_specs=[
            pl.BlockSpec((tracers, block, rows, tile), lambda i: (0, i, 0, 0)),
            pl.BlockSpec(pick.shape, lambda i: (0, 0)),
        ],
        out_specs=[row_spec, row_spec, col_spec, col_spec],
        out_shape=[rowed, rowed, columned, columned],
        compiler_params=pltpu.CompilerParams(vmem_limit_bytes=VMEM),
        name="edges",
    )(state, jnp.asarray(pick, BF16))


def chem_kernel(
    ids, state_ref, south_ref, north_ref, west_ref, east_ref, grid_ref, mask_ref, react_ref,
    along_ref, across_ref, new_ref, active_ref, react, scale,
):
    tracers, levels, rows, tile = state_ref.shape
    cells = tracers * rows

    @pl.when(pl.program_id(0) == 0)
    def _():
        value = react_ref[...]
        high = value.astype(BF16)
        react[:, :cells] = high
        react[:, cells : 2 * cells] = (value - high.astype(F32)).astype(BF16)
        react[:, 2 * cells :] = high

    outside = jnp.concatenate([west_ref[...], east_ref[...]], axis=0).astype(F32)
    outside = outside.T.astype(BF16)
    row = lax.broadcasted_iota(jnp.int32, (2 * levels, 2 * tile), 0)
    lane = lax.broadcasted_iota(jnp.int32, (2 * levels, 2 * tile), 1)
    mask = mask_ref[...]
    nn = ((1,), (0,))
    for l in range(levels):
        x = state_ref[:, l].reshape(cells, tile)
        west = (row == l) & ((lane == 0) | (lane == tile))
        east = (row == levels + l) & ((lane == tile - 1) | (lane == 2 * tile - 1))
        mark = jnp.where(east, 1.0, jnp.where(west, jnp.where(lane == 0, -1.0, 1.0), 0.0))
        lon = dot(x, along_ref[...], nn) + dot(outside, mark.astype(BF16), nn)
        stacked = jnp.concatenate([x, south_ref[l], north_ref[l]], axis=0)
        lat = dot(across_ref[...], stacked, nn)

        def three(v):
            return v.reshape(tracers, rows, tile)

        wind_u = grid_ref[0, 0, l].astype(F32) * (scale * 0.1)
        wind_v = grid_ref[0, 1, l].astype(F32) * (scale * 0.1)
        temper = grid_ref[0, 2, l].astype(F32) * scale
        moved = (
            three(x.astype(F32))
            - wind_u * three(lon[:, :tile])
            - wind_v * three(lat[:cells])
            + 0.05 * three(lon[:, tile:] + lat[cells:])
        )
        flat = moved.reshape(cells, tile)
        high = flat.astype(BF16)
        low = (flat - high.astype(F32)).astype(BF16)
        terms = dot(react[...], jnp.concatenate([high, high, low], axis=0), nn)
        reacted = (moved + three(terms[:cells]) + temper * three(terms[cells:])) * mask
        new_ref[:, l] = reacted.astype(BF16)
        for a in range(active_ref.shape[1]):
            active_ref[0, a, l] = new_ref[ids[a], l]


def chemistry(state, halos, grid, mask, react, active_ids, waves):
    tracers, levels, rows, tile = state.shape
    sources, fields, own = grid.shape[:3]
    south, north, west, east = halos
    actives = active_ids.shape[0]
    cells = tracers * rows
    block = own
    eye, one = np.eye(tracers), np.eye(tile)
    along = np.concatenate(
        [np.eye(tile, k=-1) - np.eye(tile, k=1), np.eye(tile, k=-1) + np.eye(tile, k=1) - 4 * one], 1
    )
    down, up = np.eye(rows, k=-1), np.eye(rows, k=1)
    at_first, at_last = np.eye(rows)[:, :1], np.eye(rows)[:, -1:]
    across = np.block(
        [
            [np.kron(eye, up - down), np.kron(eye, -at_first), np.kron(eye, at_last)],
            [np.kron(eye, up + down), np.kron(eye, at_first), np.kron(eye, at_last)],
        ]
    )
    kernel = functools.partial(chem_kernel)
    body = lambda *refs: kernel(*refs, 1.0 / float(np.sqrt(np.float32(waves))))
    whole = lambda shape: pl.BlockSpec(shape, lambda i, ids: (0,) * len(shape))
    return pl.pallas_call(
        body,
        grid_spec=pltpu.PrefetchScalarGridSpec(
            num_scalar_prefetch=1,
            grid=(levels // block,),
            in_specs=[
                pl.BlockSpec((tracers, block, rows, tile), lambda i, ids: (0, i, 0, 0)),
                pl.BlockSpec((block, tracers, tile), lambda i, ids: (i, 0, 0)),
                pl.BlockSpec((block, tracers, tile), lambda i, ids: (i, 0, 0)),
                pl.BlockSpec((block, cells), lambda i, ids: (i, 0)),
                pl.BlockSpec((block, cells), lambda i, ids: (i, 0)),
                pl.BlockSpec((1, fields, own, rows, tile), lambda i, ids: (i, 0, 0, 0, 0)),
                whole((rows, tile)),
                whole((2 * cells, cells)),
                whole(along.shape),
                whole(across.shape),
            ],
            out_specs=[
                pl.BlockSpec((tracers, block, rows, tile), lambda i, ids: (0, i, 0, 0)),
                pl.BlockSpec((1, actives, own, rows, tile), lambda i, ids: (i, 0, 0, 0, 0)),
            ],
            scratch_shapes=[pltpu.VMEM((2 * cells, 3 * cells), BF16)],
        ),
        out_shape=[
            jax.ShapeDtypeStruct(state.shape, BF16),
            jax.ShapeDtypeStruct((sources, actives, own, rows, tile), BF16),
        ],
        compiler_params=pltpu.CompilerParams(vmem_limit_bytes=VMEM),
        name="chemistry",
    )(
        active_ids, state, south, north, west, east, grid, mask, react,
        jnp.asarray(along, BF16), jnp.asarray(across, BF16),
    )


def spread_kernel(recv_ref, out_ref):
    tile = recv_ref.shape[4]
    for s in range(recv_ref.shape[0]):
        out_ref[0, :, :, s * tile : (s + 1) * tile] = recv_ref[s, 0].astype(F32)


def spread(recv):
    sources, actives, own, rows, tile = recv.shape
    return pl.pallas_call(
        spread_kernel,
        grid=(actives,),
        in_specs=[pl.BlockSpec((sources, 1, own, rows, tile), lambda a: (0, a, 0, 0, 0))],
        out_specs=pl.BlockSpec((1, own, rows, sources * tile), lambda a: (a, 0, 0, 0)),
        out_shape=jax.ShapeDtypeStruct((actives, own, rows, sources * tile), F32),
        compiler_params=pltpu.CompilerParams(vmem_limit_bytes=VMEM),
        name="spread",
    )(recv)


def to_next(value, axis):
    size = lax.axis_size(axis)
    return lax.ppermute(value, axis, [(i, i + 1) for i in range(size - 1)])


def to_previous(value, axis):
    size = lax.axis_size(axis)
    return lax.ppermute(value, axis, [(i + 1, i) for i in range(size - 1)])


def body(spectral, legendre, wave_ids, points, tracers, react_base, react_temp, active_ids):
    bands, tiles = lax.axis_size("lat"), lax.axis_size("lon")
    count, levels, rows, tile = tracers.shape
    own, share = spectral.shape[1:3]
    waves = wave_ids.shape[0]

    fourier = lax.dot_general(
        spectral, legendre, (((3,), (1,)), ((2,), (0,))), preferred_element_type=F32
    ).astype(BF16)
    fourier = fourier.reshape(share, 6, own, bands, rows)
    sent = jnp.transpose(fourier, (3, 2, 4, 1, 0)).reshape(bands, own, rows, 6 * share)
    sent = jnp.pad(sent, ((0, 0), (0, 0), (0, 0), (0, -(6 * share) % LANES)))
    recv = lax.all_to_all(sent, "lat", split_axis=0, concat_axis=0, tiled=True)

    first, last, west, east = edges(tracers)
    halos = (
        to_next(last, "lat"),
        to_previous(first, "lat"),
        to_next(east, "lon"),
        to_previous(west, "lon"),
    )
    table, twiddle = tables(points, wave_ids, tiles * tile // LANES)

    grid = synthesis(recv, table, twiddle, tiles, tile)
    grid = lax.all_to_all(grid, "lon", split_axis=0, concat_axis=0, tiled=True)

    columns = lax.axis_index("lon") * tile + jnp.arange(tile)
    mask = (columns[None, :] < points[:, None]).astype(F32)
    react = jnp.concatenate([react_base, react_temp], axis=0)
    eye = jnp.eye(rows, dtype=F32)
    react = (react[:, None, :, None] * eye[None, :, None, :]).reshape(2 * count * rows, count * rows)
    new, active = chemistry(tracers, halos, grid, mask, react, active_ids, waves)
    active = lax.all_to_all(active, "lon", split_axis=0, concat_axis=0, tiled=True)
    return new, spread(active)


def solution(mesh):
    return jax.shard_map(
        body,
        mesh=mesh,
        in_specs=(
            P(None, "lon", "lat", None),
            P("lat", None, None),
            P(),
            P("lat"),
            P(None, None, "lat", "lon"),
            P(),
            P(),
            P(),
        ),
        out_specs=(P(None, None, "lat", "lon"), P(None, "lon", "lat", None)),
        check_vma=False,
    )
```

```python
import functools

import jax
import jax.numpy as jnp
import numpy as np
from jax import lax
from jax.experimental import pallas as pl
from jax.experimental.pallas import tpu as pltpu
from jax.sharding import PartitionSpec as P

F32 = jnp.float32
BF16 = jnp.bfloat16
LANES = 128
LOW = 16
STEP = 4
PARTS = 2
VMEM = 56 * 1024 * 1024

COS = (
    0.9999999890590228,
    -19.739204499454026,
    64.93911745990036,
    -85.45013953095037,
    60.16763095136588,
    -25.96759924965491,
    6.528658162567069,
)
SIN = (
    6.283185302511503,
    -41.34170040531769,
    81.60513138580204,
    -76.7030153539128,
    42.02592698618416,
    -14.899846668691637,
    3.238137510515757,
)


def dot(a, b, dims):
    return lax.dot_general(a, b, (dims, ((), ())), preferred_element_type=F32)


def cost(flops, moved):
    return pl.CostEstimate(flops=int(flops), bytes_accessed=int(moved), transcendentals=0)


def unit_circle(step, rows, waves, count):
    index = lax.broadcasted_iota(jnp.int32, (rows, waves.shape[1]), 0) * step
    product = index.astype(F32) * waves
    inverse = 1.0 / count
    turns = (product - jnp.floor(product * inverse) * count) * inverse
    y = turns - jnp.floor(turns + 0.5)
    z = y * y
    cosine = jnp.full_like(z, COS[-1])
    sine = jnp.full_like(z, SIN[-1])
    for c, s in zip(COS[-2::-1], SIN[-2::-1]):
        cosine = cosine * z + c
        sine = sine * z + s
    return cosine, sine * y


def table_kernel(points, waves_ref, table_ref, twiddle_ref):
    size, turns = waves_ref.shape[1], twiddle_ref.shape[2]
    waves = waves_ref[...]
    for k in range(table_ref.shape[0]):
        row = pl.program_id(0) * table_ref.shape[0] + k
        count = jnp.full(waves.shape, points[row], jnp.int32).astype(F32)
        cos_low, sin_low = unit_circle(1, LOW, waves, count)
        cos_high, sin_high = unit_circle(LOW, LANES // LOW, waves, count)
        cosine, sine = [], []
        for a in range(LANES // LOW):
            ch, sh = cos_high[a : a + 1], sin_high[a : a + 1]
            cosine.append(ch * cos_low - sh * sin_low)
            sine.append(-sh * cos_low - ch * sin_low)
        table_ref[k, :size, :] = jnp.concatenate(cosine, axis=0).T.astype(BF16)
        table_ref[k, size:, :] = jnp.concatenate(sine, axis=0).T.astype(BF16)
        cos_turn, sin_turn = unit_circle(LANES, turns, waves, count)
        twiddle_ref[k, 0] = cos_turn
        twiddle_ref[k, 1] = sin_turn


def tables(points, wave_ids, turns):
    rows, waves = points.shape[0], wave_ids.shape[0]
    each = STEP if rows % STEP == 0 else 1
    return pl.pallas_call(
        table_kernel,
        grid_spec=pltpu.PrefetchScalarGridSpec(
            num_scalar_prefetch=1,
            grid=(rows // each,),
            in_specs=[pl.BlockSpec((1, waves), lambda j, p: (0, 0))],
            out_specs=[
                pl.BlockSpec((each, 2 * waves, LANES), lambda j, p: (j, 0, 0)),
                pl.BlockSpec((each, 2, turns, waves), lambda j, p: (j, 0, 0, 0)),
            ],
        ),
        out_shape=[
            jax.ShapeDtypeStruct((rows, 2 * waves, LANES), BF16),
            jax.ShapeDtypeStruct((rows, 2, turns, waves), F32),
        ],
        compiler_params=pltpu.CompilerParams(vmem_limit_bytes=VMEM),
        cost_estimate=cost(rows * waves * LANES * 8, rows * waves * LANES * 4),
        name="tables",
    )(points, wave_ids.astype(F32)[None, :])


def place(pieces, width):
    out = [None] * (width // LANES)
    lane = lax.broadcasted_iota(jnp.int32, (pieces[0][0].shape[0], LANES), 1)
    for value, start, count, here in pieces:
        shift = (here - start) % LANES
        for a in range(start // LANES, (start + count - 1) // LANES + 1):
            part = value[:, a * LANES : (a + 1) * LANES]
            if shift:
                part = pltpu.roll(part, shift, 1)
            first = max(start, a * LANES) - start + here
            last = min(start + count, (a + 1) * LANES) - start + here
            for v in range(first // LANES, (last - 1) // LANES + 1):
                low, high = max(first - v * LANES, 0), min(last - v * LANES, LANES)
                if out[v] is None:
                    out[v] = part
                else:
                    out[v] = jnp.where((lane >= low) & (lane < high), part, out[v])
    return out


def synth_kernel(recv_ref, table_ref, twiddle_ref, *refs):
    *out_refs, coef, grid = refs
    sources, levels, rows, _ = recv_ref.shape
    fields, waves = coef.shape[0] // 2, coef.shape[1] * LANES
    share = waves // sources
    each, _, turns = twiddle_ref.shape[:3]
    step = pl.program_id(0)

    @pl.when(step == 0)
    def _():
        def level(l, carry):
            values = [recv_ref[s, l].astype(F32) for s in range(sources)]
            for r in range(2 * fields):
                windows = [
                    (values[s], r * share, share, s * share) for s in range(sources)
                ]
                for v, part in enumerate(place(windows, waves)):
                    coef[r, v, pl.ds(l * rows, rows), :] = part
            return carry

        lax.fori_loop(0, levels, level, 0)

    for k in range(each):
        j = step * each + k

        def own_row(r):
            parts = [coef[r, v, pl.ds(j, levels, stride=rows), :] for v in range(waves // LANES)]
            return jnp.concatenate(parts, axis=1)

        values = [own_row(r) for r in range(2 * fields)]
        real, imag = [], []
        for t in range(turns):
            c, s = twiddle_ref[k, 0, t : t + 1], twiddle_ref[k, 1, t : t + 1]
            for f in range(fields):
                re, im = values[2 * f], values[2 * f + 1]
                real.append(re * c - im * s)
                imag.append(re * s + im * c)
        both = [jnp.concatenate(part, axis=0).astype(BF16) for part in (real, imag)]
        result = dot(jnp.concatenate(both, axis=1), table_ref[k], ((1,), (0,)))
        grid[pl.ds(j, turns * fields * levels, stride=rows), :] = result

    @pl.when(step == pl.num_programs(0) - 1)
    def _():
        dests = out_refs[0].shape[0]
        tiles = turns // dests
        size = levels * rows
        some = levels // len(out_refs)
        for t in range(turns):
            lanes = slice((t % tiles) * LANES, (t % tiles + 1) * LANES)
            for f in range(fields):
                block = grid[(t * fields + f) * size : (t * fields + f + 1) * size, :]
                block = block.reshape(levels, rows, LANES).astype(BF16)
                for p, out_ref in enumerate(out_refs):
                    out_ref[t // tiles, f, :, :, lanes] = block[p * some : (p + 1) * some]


def synthesis(recv, table, twiddle, dests, tile, parts):
    sources, levels, rows, lanes = recv.shape
    turns, waves = twiddle.shape[2:]
    fields = 3
    each = STEP if rows % STEP == 0 else 1
    shape = (dests, fields, levels // parts, rows, tile)
    return pl.pallas_call(
        synth_kernel,
        grid=(rows // each,),
        in_specs=[
            pl.BlockSpec(recv.shape, lambda j: (0, 0, 0, 0)),
            pl.BlockSpec((each, 2 * waves, LANES), lambda j: (j, 0, 0)),
            pl.BlockSpec((each, 2, turns, waves), lambda j: (j, 0, 0, 0)),
        ],
        out_specs=[pl.BlockSpec(shape, lambda j: (0, 0, 0, 0, 0))] * parts,
        out_shape=[jax.ShapeDtypeStruct(shape, BF16)] * parts,
        scratch_shapes=[
            pltpu.VMEM((2 * fields, waves // LANES, levels * rows, LANES), F32),
            pltpu.VMEM((turns * fields * levels * rows, LANES), F32),
        ],
        compiler_params=pltpu.CompilerParams(vmem_limit_bytes=VMEM),
        cost_estimate=cost(4 * rows * waves * fields * levels * turns * LANES, 4 * rows * waves * LANES),
        name="synthesis",
    )(recv, table, twiddle)


def edge_kernel(
    state_ref, pick_ref, base_ref, temp_ref, first_ref, last_ref, west_ref, east_ref, react_ref
):
    tracers, levels, rows, tile = state_ref.shape
    cells = tracers * rows

    @pl.when(pl.program_id(0) == 0)
    def _():
        rates = jnp.concatenate([base_ref[...], temp_ref[...]], axis=0)
        high = rates.astype(BF16)
        low = (rates - high.astype(F32)).astype(BF16)

        def iota(shape, axis):
            return lax.broadcasted_iota(jnp.int32, shape, axis)

        shape = (2 * cells, 2 * tracers)
        down = jnp.where(iota(shape, 0) // rows == iota(shape, 1), 1.0, 0.0).astype(BF16)
        shape = (tracers, cells)
        over = jnp.where(iota(shape, 0) == iota(shape, 1) // rows, 1.0, 0.0).astype(BF16)
        shape = (2 * cells, cells)
        same = iota(shape, 0) % rows == iota(shape, 1) % rows
        for k, part in enumerate((high, low)):
            wide = dot(dot(down, part, ((1,), (0,))).astype(BF16), over, ((1,), (0,)))
            react_ref[:, k * cells : (k + 1) * cells] = jnp.where(same, wide, 0.0).astype(BF16)

    ends = lax.broadcasted_iota(jnp.int32, (2 * levels, tile), 1)
    row = lax.broadcasted_iota(jnp.int32, (2 * levels, tile), 0)
    columns = jnp.zeros((2 * levels, tracers * rows), F32)
    for l in range(levels):
        x = state_ref[:, l].reshape(tracers * rows, tile)
        picked = dot(pick_ref[...], x, ((1,), (0,)))
        first_ref[l] = picked[:tracers].astype(BF16)
        last_ref[l] = picked[tracers:].astype(BF16)
        mark = ((row == l) & (ends == 0)) | ((row == levels + l) & (ends == tile - 1))
        columns = columns + dot(jnp.where(mark, 1.0, 0.0).astype(BF16), x, ((1,), (1,)))
    west_ref[...] = columns[:levels].astype(BF16)
    east_ref[...] = columns[levels:].astype(BF16)


def edges(state, react_base, react_temp):
    tracers, levels, rows, tile = state.shape
    block = 16
    pick = np.zeros((2 * tracers, tracers * rows), np.float32)
    for t in range(tracers):
        pick[t, t * rows] = 1
        pick[tracers + t, t * rows + rows - 1] = 1
    rowed = jax.ShapeDtypeStruct((levels, tracers, tile), BF16)
    columned = jax.ShapeDtypeStruct((levels, tracers * rows), BF16)
    row_spec = pl.BlockSpec((block, tracers, tile), lambda i: (i, 0, 0))
    col_spec = pl.BlockSpec((block, tracers * rows), lambda i: (i, 0))
    wide = (2 * tracers * rows, 2 * tracers * rows)
    return pl.pallas_call(
        edge_kernel,
        grid=(levels // block,),
        in_specs=[
            pl.BlockSpec((tracers, block, rows, tile), lambda i: (0, i, 0, 0)),
            pl.BlockSpec(pick.shape, lambda i: (0, 0)),
            pl.BlockSpec(react_base.shape, lambda i: (0, 0)),
            pl.BlockSpec(react_temp.shape, lambda i: (0, 0)),
        ],
        out_specs=[row_spec, row_spec, col_spec, col_spec, pl.BlockSpec(wide, lambda i: (0, 0))],
        out_shape=[rowed, rowed, columned, columned, jax.ShapeDtypeStruct(wide, BF16)],
        cost_estimate=cost(4 * state.size * 32, 2 * state.size),
        compiler_params=pltpu.CompilerParams(vmem_limit_bytes=VMEM),
        name="edges",
    )(state, jnp.asarray(pick, BF16), react_base, react_temp)


def chem_kernel(scale, part, parts, ids, *refs):
    (state_ref, south_ref, north_ref, west_ref, east_ref, grid_ref, mask_ref, react_ref) = refs[:8]
    along_ref, across_ref = refs[8:10]
    new_ref, active_ref, south, north = refs[-4:]
    tracers, levels, rows, tile = state_ref.shape
    cells = tracers * rows
    half, side = rows // 2, tile // 2
    first = (pl.program_id(0) * parts + part) * levels

    def column(ref):
        value = ref[...].astype(F32)
        pad = jnp.zeros((LANES - value.shape[0], cells), F32)
        return pltpu.roll(jnp.concatenate([value, pad], axis=0).T, lax.rem(LANES - first, LANES), 1)

    west, east = column(west_ref), column(east_ref)
    row = lax.broadcasted_iota(jnp.int32, (rows, tile), 0)
    lane = lax.broadcasted_iota(jnp.int32, (rows, tile), 1)
    mask = mask_ref[...]
    nn = ((1,), (0,))

    def three(v):
        return v.reshape(tracers, rows, tile)

    for l in range(levels):
        x = state_ref[:, l].reshape(cells, tile)
        lon = dot(x, along_ref[...], nn)
        lat = dot(across_ref[...], x, nn)
        wind_u = grid_ref[0, 0, l].astype(F32) * (scale * 0.1)
        wind_v = grid_ref[0, 1, l].astype(F32) * (scale * 0.1)
        temper = grid_ref[0, 2, l].astype(F32) * scale
        moved = (
            three(x.astype(F32))
            - wind_u * three(lon[:, :tile])
            - wind_v * three(lat[:cells])
            + 0.05 * three(lon[:, tile:] + lat[cells:])
        )
        south[...] = south_ref[l].astype(F32)
        north[...] = north_ref[l].astype(F32)
        in_row = jnp.where(row == 0, 0.05 + wind_v, jnp.where(row == rows - 1, 0.05 - wind_v, 0.0))
        in_col = jnp.where(lane == 0, 0.05 + wind_u, jnp.where(lane == tile - 1, 0.05 - wind_u, 0.0))
        outer = []
        for t in range(tracers):
            up = [jnp.broadcast_to(ref[t : t + 1], (half, tile)) for ref in (south, north)]
            cell = slice(t * rows, (t + 1) * rows)
            across = [
                jnp.broadcast_to(col[cell, l : l + 1], (rows, side)) for col in (west, east)
            ]
            outer.append(
                in_row * jnp.concatenate(up, axis=0) + in_col * jnp.concatenate(across, axis=1)
            )
        moved = moved + jnp.stack(outer, axis=0)
        high = moved.reshape(cells, tile).astype(BF16)
        terms = dot(react_ref[...], jnp.concatenate([high, high], axis=0), nn)
        reacted = (moved + three(terms[:cells]) + temper * three(terms[cells:])) * mask
        new_ref[:, l] = reacted.astype(BF16)
        for a in range(active_ref.shape[1]):
            active_ref[0, a, l] = new_ref[ids[a], l]


def chemistry(state, halos, grid, mask, react, active_ids, waves, part, parts, before):
    tracers, levels, rows, tile = state.shape
    sources, fields, some = grid.shape[:3]
    south, north, west, east = halos
    actives = active_ids.shape[0]
    cells = tracers * rows
    eye, one = np.eye(tracers), np.eye(tile)
    along = np.concatenate(
        [np.eye(tile, k=-1) - np.eye(tile, k=1), np.eye(tile, k=-1) + np.eye(tile, k=1) - 4 * one], 1
    )
    down, up = np.eye(rows, k=-1), np.eye(rows, k=1)
    across = np.concatenate([np.kron(eye, up - down), np.kron(eye, up + down)], 0)
    scale = 1.0 / float(np.sqrt(np.float32(waves)))

    def whole(shape):
        return pl.BlockSpec(shape, lambda i, ids: (0,) * len(shape))

    def leveled(*shape):
        return pl.BlockSpec((some,) + shape, lambda i, ids: (i * parts + part, 0, 0))

    state_spec = pl.BlockSpec((tracers, some, rows, tile), lambda i, ids: (0, i * parts + part, 0, 0))
    operands = [
        state, south, north, west, east, grid, mask, react,
        jnp.asarray(along, BF16), jnp.asarray(across, BF16),
    ]
    in_specs = [
        state_spec,
        leveled(tracers, tile),
        leveled(tracers, tile),
        whole(west.shape),
        whole(east.shape),
        pl.BlockSpec((1, fields, some, rows, tile), lambda i, ids: (i, 0, 0, 0, 0)),
        whole(mask.shape),
        whole(react.shape),
        whole(along.shape),
        whole(across.shape),
    ]
    aliases = {}
    if before is not None:
        aliases = {1 + len(operands): 0}
        operands.append(before)
        in_specs.append(pl.BlockSpec(memory_space=pl.ANY))
    return pl.pallas_call(
        functools.partial(chem_kernel, scale, part, parts),
        grid_spec=pltpu.PrefetchScalarGridSpec(
            num_scalar_prefetch=1,
            grid=(sources,),
            in_specs=in_specs,
            out_specs=[
                state_spec,
                pl.BlockSpec((1, actives, some, rows, tile), lambda i, ids: (i, 0, 0, 0, 0)),
            ],
            scratch_shapes=[pltpu.VMEM((tracers, tile), F32)] * 2,
        ),
        out_shape=[
            jax.ShapeDtypeStruct(state.shape, BF16),
            jax.ShapeDtypeStruct((sources, actives, some, rows, tile), BF16),
        ],
        input_output_aliases=aliases,
        compiler_params=pltpu.CompilerParams(vmem_limit_bytes=VMEM),
        cost_estimate=cost(state.size // parts * 2 * 2048, state.size // parts * 4),
        name="chemistry",
    )(active_ids, *operands)


def spread_kernel(recv_ref, *refs):
    out_ref = refs[-1]
    tile = recv_ref.shape[4]
    for s in range(recv_ref.shape[0]):
        out_ref[:, :, :, s * tile : (s + 1) * tile] = recv_ref[s].astype(F32)


def spread(recv, part, parts, before):
    sources, actives, some, rows, tile = recv.shape
    each = 2 if actives % 2 == 0 else 1
    operands = [recv]
    in_specs = [pl.BlockSpec((sources, each, some, rows, tile), lambda a: (0, a, 0, 0, 0))]
    aliases = {}
    if before is not None:
        operands.append(before)
        in_specs.append(pl.BlockSpec(memory_space=pl.ANY))
        aliases = {1: 0}
    return pl.pallas_call(
        spread_kernel,
        grid=(actives // each,),
        in_specs=in_specs,
        out_specs=pl.BlockSpec((each, some, rows, sources * tile), lambda a: (a, part, 0, 0)),
        out_shape=jax.ShapeDtypeStruct((actives, some * parts, rows, sources * tile), F32),
        input_output_aliases=aliases,
        compiler_params=pltpu.CompilerParams(vmem_limit_bytes=VMEM),
        cost_estimate=cost(recv.size, recv.size * 6),
        name="spread",
    )(*operands)


def to_next(value, axis):
    size = lax.axis_size(axis)
    return lax.ppermute(value, axis, [(i, i + 1) for i in range(size - 1)])


def to_previous(value, axis):
    size = lax.axis_size(axis)
    return lax.ppermute(value, axis, [(i + 1, i) for i in range(size - 1)])


def body(spectral, legendre, wave_ids, points, tracers, react_base, react_temp, active_ids):
    bands, tiles = lax.axis_size("lat"), lax.axis_size("lon")
    count, levels, rows, tile = tracers.shape
    own, share = spectral.shape[1:3]
    waves = wave_ids.shape[0]

    fourier = lax.dot_general(
        spectral, legendre, (((3,), (1,)), ((2,), (0,))), preferred_element_type=F32
    ).astype(BF16)
    fourier = fourier.reshape(share, 6, own, bands, rows)
    sent = jnp.transpose(fourier, (3, 2, 4, 1, 0)).reshape(bands, own, rows, 6 * share)
    sent = jnp.pad(sent, ((0, 0), (0, 0), (0, 0), (0, -(6 * share) % LANES)))
    recv = lax.all_to_all(sent, "lat", split_axis=0, concat_axis=0, tiled=True)

    first, last, west, east, react = edges(tracers, react_base, react_temp)
    halos = (
        to_next(last, "lat"),
        to_previous(first, "lat"),
        to_next(east, "lon"),
        to_previous(west, "lon"),
    )
    table, twiddle = tables(points, wave_ids, tiles * tile // LANES)
    columns = lax.axis_index("lon") * tile + jnp.arange(tile)
    mask = (columns[None, :] < points[:, None]).astype(F32)
    recv, table, twiddle, halos, mask = lax.optimization_barrier(
        (recv, table, twiddle, halos, mask)
    )

    parts = PARTS if own % PARTS == 0 else 1
    grids = synthesis(recv, table, twiddle, tiles, tile, parts)
    grids = [lax.all_to_all(g, "lon", split_axis=0, concat_axis=0, tiled=True) for g in grids]
    new, sent = None, []
    for p, grid in enumerate(grids):
        new, active = chemistry(
            tracers, halos, grid, mask, react, active_ids, waves, p, parts, new
        )
        sent.append(lax.all_to_all(active, "lon", split_axis=0, concat_axis=0, tiled=True))
    spreaded = None
    for p, active in enumerate(sent):
        spreaded = spread(active, p, parts, spreaded)
    return new, spreaded


def solution(mesh):
    return jax.shard_map(
        body,
        mesh=mesh,
        in_specs=(
            P(None, "lon", "lat", None),
            P("lat", None, None),
            P(),
            P("lat"),
            P(None, None, "lat", "lon"),
            P(),
            P(),
            P(),
        ),
        out_specs=(P(None, None, "lat", "lon"), P(None, "lon", "lat", None)),
        check_vma=False,
    )
```

```python
import functools

import jax
import jax.numpy as jnp
import numpy as np
from jax import lax
from jax.experimental import pallas as pl
from jax.experimental.pallas import tpu as pltpu
from jax.sharding import PartitionSpec as P

F32 = jnp.float32
BF16 = jnp.bfloat16
LANES = 128
LOW = 16
STEP = 4
VMEM = 56 * 1024 * 1024

COS = (
    0.9999999890590228,
    -19.739204499454026,
    64.93911745990036,
    -85.45013953095037,
    60.16763095136588,
    -25.96759924965491,
    6.528658162567069,
)
SIN = (
    6.283185302511503,
    -41.34170040531769,
    81.60513138580204,
    -76.7030153539128,
    42.02592698618416,
    -14.899846668691637,
    3.238137510515757,
)


def dot(a, b, dims):
    return lax.dot_general(a, b, (dims, ((), ())), preferred_element_type=F32)


def cost(flops, moved):
    return pl.CostEstimate(flops=int(flops), bytes_accessed=int(moved), transcendentals=0)


def unit_circle(step, rows, waves, count):
    index = lax.broadcasted_iota(jnp.int32, (rows, waves.shape[1]), 0) * step
    product = index.astype(F32) * waves
    inverse = 1.0 / count
    turns = (product - jnp.floor(product * inverse) * count) * inverse
    y = turns - jnp.floor(turns + 0.5)
    z = y * y
    cosine = jnp.full_like(z, COS[-1])
    sine = jnp.full_like(z, SIN[-1])
    for c, s in zip(COS[-2::-1], SIN[-2::-1]):
        cosine = cosine * z + c
        sine = sine * z + s
    return cosine, sine * y


def table_kernel(points, waves_ref, table_ref, twiddle_ref):
    size, turns = waves_ref.shape[1], twiddle_ref.shape[2]
    waves = waves_ref[...]
    for k in range(table_ref.shape[0]):
        row = pl.program_id(0) * table_ref.shape[0] + k
        count = jnp.full(waves.shape, points[row], jnp.int32).astype(F32)
        cos_low, sin_low = unit_circle(1, LOW, waves, count)
        cos_high, sin_high = unit_circle(LOW, LANES // LOW, waves, count)
        cosine, sine = [], []
        for a in range(LANES // LOW):
            ch, sh = cos_high[a : a + 1], sin_high[a : a + 1]
            cosine.append(ch * cos_low - sh * sin_low)
            sine.append(-sh * cos_low - ch * sin_low)
        table_ref[k, :size, :] = jnp.concatenate(cosine, axis=0).T.astype(BF16)
        table_ref[k, size:, :] = jnp.concatenate(sine, axis=0).T.astype(BF16)
        cos_turn, sin_turn = unit_circle(LANES, turns, waves, count)
        twiddle_ref[k, 0] = cos_turn
        twiddle_ref[k, 1] = sin_turn


def tables(points, wave_ids, turns):
    rows, waves = points.shape[0], wave_ids.shape[0]
    each = STEP if rows % STEP == 0 else 1
    return pl.pallas_call(
        table_kernel,
        grid_spec=pltpu.PrefetchScalarGridSpec(
            num_scalar_prefetch=1,
            grid=(rows // each,),
            in_specs=[pl.BlockSpec((1, waves), lambda j, p: (0, 0))],
            out_specs=[
                pl.BlockSpec((each, 2 * waves, LANES), lambda j, p: (j, 0, 0)),
                pl.BlockSpec((each, 2, turns, waves), lambda j, p: (j, 0, 0, 0)),
            ],
        ),
        out_shape=[
            jax.ShapeDtypeStruct((rows, 2 * waves, LANES), BF16),
            jax.ShapeDtypeStruct((rows, 2, turns, waves), F32),
        ],
        compiler_params=pltpu.CompilerParams(vmem_limit_bytes=VMEM),
        cost_estimate=cost(rows * waves * LANES * 8, rows * waves * LANES * 4),
        name="tables",
    )(points, wave_ids.astype(F32)[None, :])


def place(pieces, width):
    out = [None] * (width // LANES)
    lane = lax.broadcasted_iota(jnp.int32, (pieces[0][0].shape[0], LANES), 1)
    for value, start, count, here in pieces:
        shift = (here - start) % LANES
        for a in range(start // LANES, (start + count - 1) // LANES + 1):
            part = value[:, a * LANES : (a + 1) * LANES]
            if shift:
                part = pltpu.roll(part, shift, 1)
            first = max(start, a * LANES) - start + here
            last = min(start + count, (a + 1) * LANES) - start + here
            for v in range(first // LANES, (last - 1) // LANES + 1):
                low, high = max(first - v * LANES, 0), min(last - v * LANES, LANES)
                if out[v] is None:
                    out[v] = part
                else:
                    out[v] = jnp.where((lane >= low) & (lane < high), part, out[v])
    return out


def synth_kernel(me, recv_ref, table_ref, twiddle_ref, *refs):
    *out_refs, coef, grid = refs
    sources, levels, rows, _ = recv_ref.shape
    fields, waves = coef.shape[0] // 2, coef.shape[1] * LANES
    share = waves // sources
    each, _, turns = twiddle_ref.shape[:3]
    step = pl.program_id(0)

    @pl.when(step == 0)
    def _():
        def level(l, carry):
            values = [recv_ref[s, l].astype(F32) for s in range(sources)]
            for r in range(2 * fields):
                windows = [
                    (values[s], r * share, share, s * share) for s in range(sources)
                ]
                for v, part in enumerate(place(windows, waves)):
                    coef[r, v, pl.ds(l * rows, rows), :] = part
            return carry

        lax.fori_loop(0, levels, level, 0)

    for k in range(each):
        j = step * each + k

        def own_row(r):
            parts = [coef[r, v, pl.ds(j, levels, stride=rows), :] for v in range(waves // LANES)]
            return jnp.concatenate(parts, axis=1)

        values = [own_row(r) for r in range(2 * fields)]
        real, imag = [], []
        for t in range(turns):
            c, s = twiddle_ref[k, 0, t : t + 1], twiddle_ref[k, 1, t : t + 1]
            for f in range(fields):
                re, im = values[2 * f], values[2 * f + 1]
                real.append(re * c - im * s)
                imag.append(re * s + im * c)
        both = [jnp.concatenate(part, axis=0).astype(BF16) for part in (real, imag)]
        result = dot(jnp.concatenate(both, axis=1), table_ref[k], ((1,), (0,)))
        grid[pl.ds(j, turns * fields * levels, stride=rows), :] = result

    @pl.when(step == pl.num_programs(0) - 1)
    def _():
        tiles = turns // len(out_refs)
        size = levels * rows
        for k, out_ref in enumerate(out_refs):
            for t in range(tiles):
                for f in range(fields):
                    start = (((me[0] ^ k) * tiles + t) * fields + f) * size
                    block = grid[pl.ds(pl.multiple_of(start, size), size), :]
                    block = block.reshape(levels, rows, LANES).astype(BF16)
                    out_ref[f, :, :, t * LANES : (t + 1) * LANES] = block


def synthesis(recv, table, twiddle, me, dests, tile):
    sources, levels, rows, lanes = recv.shape
    turns, waves = twiddle.shape[2:]
    fields = 3
    each = STEP if rows % STEP == 0 else 1
    shape = (fields, levels, rows, tile)
    return pl.pallas_call(
        synth_kernel,
        grid_spec=pltpu.PrefetchScalarGridSpec(
            num_scalar_prefetch=1,
            grid=(rows // each,),
            in_specs=[
                pl.BlockSpec(recv.shape, lambda j, me: (0, 0, 0, 0)),
                pl.BlockSpec((each, 2 * waves, LANES), lambda j, me: (j, 0, 0)),
                pl.BlockSpec((each, 2, turns, waves), lambda j, me: (j, 0, 0, 0)),
            ],
            out_specs=[pl.BlockSpec(shape, lambda j, me: (0, 0, 0, 0))] * dests,
            scratch_shapes=[
                pltpu.VMEM((2 * fields, waves // LANES, levels * rows, LANES), F32),
                pltpu.VMEM((turns * fields * levels * rows, LANES), F32),
            ],
        ),
        out_shape=[jax.ShapeDtypeStruct(shape, BF16)] * dests,
        compiler_params=pltpu.CompilerParams(vmem_limit_bytes=VMEM),
        cost_estimate=cost(4 * rows * waves * fields * levels * turns * LANES, 4 * rows * waves * LANES),
        name="synthesis",
    )(me, recv, table, twiddle)


def edge_kernel(
    odd, state_ref, base_ref, temp_ref, row_a_ref, row_b_ref, col_a_ref, col_b_ref, react_ref
):
    tracers, levels, rows, tile = state_ref.shape
    cells = tracers * rows

    @pl.when(pl.program_id(0) == 0)
    def _():
        rates = jnp.concatenate([base_ref[...], temp_ref[...]], axis=0)
        high = rates.astype(BF16)
        low = (rates - high.astype(F32)).astype(BF16)

        def iota(shape, axis):
            return lax.broadcasted_iota(jnp.int32, shape, axis)

        shape = (2 * cells, 2 * tracers)
        down = jnp.where(iota(shape, 0) // rows == iota(shape, 1), 1.0, 0.0).astype(BF16)
        shape = (tracers, cells)
        over = jnp.where(iota(shape, 0) == iota(shape, 1) // rows, 1.0, 0.0).astype(BF16)
        shape = (2 * cells, cells)
        same = iota(shape, 0) % rows == iota(shape, 1) % rows
        for k, part in enumerate((high, low)):
            wide = dot(dot(down, part, ((1,), (0,))).astype(BF16), over, ((1,), (0,)))
            react_ref[:, k * cells : (k + 1) * cells] = jnp.where(same, wide, 0.0).astype(BF16)

    def iota(shape, axis):
        return lax.broadcasted_iota(jnp.int32, shape, axis)

    far, near = (1 - odd[0]) * (rows - 1), odd[0] * (rows - 1)
    shape = (2 * tracers, cells)
    end = jnp.where(iota(shape, 0) < tracers, far, near)
    pick = iota(shape, 1) == (iota(shape, 0) % tracers) * rows + end
    pick = jnp.where(pick, 1.0, 0.0).astype(BF16)
    shape = (2 * levels, tile)
    far, near = (1 - odd[1]) * (tile - 1), odd[1] * (tile - 1)
    is_end = iota(shape, 1) == jnp.where(iota(shape, 0) < levels, far, near)
    row = iota(shape, 0) % levels
    columns = jnp.zeros((2 * levels, cells), F32)
    for l in range(levels):
        x = state_ref[:, l].reshape(cells, tile)
        picked = dot(pick, x, ((1,), (0,)))
        row_a_ref[l] = picked[:tracers].astype(BF16)
        row_b_ref[l] = picked[tracers:].astype(BF16)
        mark = jnp.where(is_end & (row == l), 1.0, 0.0).astype(BF16)
        columns = columns + dot(mark, x, ((1,), (1,)))
    col_a_ref[...] = columns[:levels].astype(BF16)
    col_b_ref[...] = columns[levels:].astype(BF16)


def edges(state, react_base, react_temp, odd):
    tracers, levels, rows, tile = state.shape
    block = 16
    cells = tracers * rows
    rowed = jax.ShapeDtypeStruct((levels, tracers, tile), BF16)
    columned = jax.ShapeDtypeStruct((levels, cells), BF16)
    row_spec = pl.BlockSpec((block, tracers, tile), lambda i, odd: (i, 0, 0))
    col_spec = pl.BlockSpec((block, cells), lambda i, odd: (i, 0))
    wide = (2 * cells, 2 * cells)
    return pl.pallas_call(
        edge_kernel,
        grid_spec=pltpu.PrefetchScalarGridSpec(
            num_scalar_prefetch=1,
            grid=(levels // block,),
            in_specs=[
                pl.BlockSpec((tracers, block, rows, tile), lambda i, odd: (0, i, 0, 0)),
                pl.BlockSpec(react_base.shape, lambda i, odd: (0, 0)),
                pl.BlockSpec(react_temp.shape, lambda i, odd: (0, 0)),
            ],
            out_specs=[
                row_spec, row_spec, col_spec, col_spec, pl.BlockSpec(wide, lambda i, odd: (0, 0)),
            ],
        ),
        out_shape=[rowed, rowed, columned, columned, jax.ShapeDtypeStruct(wide, BF16)],
        compiler_params=pltpu.CompilerParams(vmem_limit_bytes=VMEM),
        cost_estimate=cost(4 * state.size * 32, 2 * state.size),
        name="edges",
    )(odd, state, react_base, react_temp)


def chem_kernel(scale, info, *refs):
    state_ref, row_a_ref, row_b_ref, col_a_ref, col_b_ref, grid_ref, mask_ref, react_ref = refs[:8]
    along_ref, across_ref = refs[8:10]
    new_ref, active_ref, south, north = refs[-4:]
    tracers, levels, rows, tile = state_ref.shape
    cells = tracers * rows
    half, side = rows // 2, tile // 2
    group, odd_band, odd_tile = info[0], info[1] == 1, info[2] == 1
    first = (group * pl.num_programs(0) + pl.program_id(0)) * levels

    def column(value):
        pad = jnp.zeros((LANES - value.shape[0], cells), F32)
        turn = lax.rem(LANES - first, LANES)
        return pltpu.roll(jnp.concatenate([value, pad], axis=0).T, turn, 1)

    a, b = col_a_ref[...].astype(F32), col_b_ref[...].astype(F32)
    west, east = column(jnp.where(odd_tile, a, b)), column(jnp.where(odd_tile, b, a))
    row = lax.broadcasted_iota(jnp.int32, (rows, tile), 0)
    lane = lax.broadcasted_iota(jnp.int32, (rows, tile), 1)
    mask = mask_ref[...]
    nn = ((1,), (0,))

    def three(v):
        return v.reshape(tracers, rows, tile)

    for l in range(levels):
        x = state_ref[:, l].reshape(cells, tile)
        lon = dot(x, along_ref[...], nn)
        lat = dot(across_ref[...], x, nn)
        wind_u = grid_ref[0, l].astype(F32) * (scale * 0.1)
        wind_v = grid_ref[1, l].astype(F32) * (scale * 0.1)
        temper = grid_ref[2, l].astype(F32) * scale
        moved = (
            three(x.astype(F32))
            - wind_u * three(lon[:, :tile])
            - wind_v * three(lat[:cells])
            + 0.05 * three(lon[:, tile:] + lat[cells:])
        )
        a, b = row_a_ref[l].astype(F32), row_b_ref[l].astype(F32)
        south[l] = jnp.where(odd_band, a, b)
        north[l] = jnp.where(odd_band, b, a)
        in_row = jnp.where(row == 0, 0.05 + wind_v, jnp.where(row == rows - 1, 0.05 - wind_v, 0.0))
        in_col = jnp.where(lane == 0, 0.05 + wind_u, jnp.where(lane == tile - 1, 0.05 - wind_u, 0.0))
        outer = []
        for t in range(tracers):
            up = [jnp.broadcast_to(ref[l, t : t + 1], (half, tile)) for ref in (south, north)]
            cell = slice(t * rows, (t + 1) * rows)
            across = [
                jnp.broadcast_to(col[cell, l : l + 1], (rows, side)) for col in (west, east)
            ]
            outer.append(
                in_row * jnp.concatenate(up, axis=0) + in_col * jnp.concatenate(across, axis=1)
            )
        moved = moved + jnp.stack(outer, axis=0)
        high = moved.reshape(cells, tile).astype(BF16)
        terms = dot(react_ref[...], jnp.concatenate([high, high], axis=0), nn)
        reacted = (moved + three(terms[:cells]) + temper * three(terms[cells:])) * mask
        new_ref[:, l] = reacted.astype(BF16)
    for a in range(active_ref.shape[0]):
        active_ref[a] = new_ref[info[3 + a]]


def chemistry(state, halos, grid, mask, react, info, actives, waves, before):
    tracers, levels, rows, tile = state.shape
    fields, own = grid.shape[:2]
    some = 4 if own % 4 == 0 else own
    steps = own // some
    cells = tracers * rows
    eye, one = np.eye(tracers), np.eye(tile)
    along = np.concatenate(
        [np.eye(tile, k=-1) - np.eye(tile, k=1), np.eye(tile, k=-1) + np.eye(tile, k=1) - 4 * one], 1
    )
    down, up = np.eye(rows, k=-1), np.eye(rows, k=1)
    across = np.concatenate([np.kron(eye, up - down), np.kron(eye, up + down)], 0)
    scale = 1.0 / float(np.sqrt(np.float32(waves)))

    def whole(shape):
        return pl.BlockSpec(shape, lambda i, info: (0,) * len(shape))

    row_spec = pl.BlockSpec((some, tracers, tile), lambda i, info: (info[0] * steps + i, 0, 0))
    state_spec = pl.BlockSpec(
        (tracers, some, rows, tile), lambda i, info: (0, info[0] * steps + i, 0, 0)
    )
    operands = [
        state, *halos, grid, mask, react, jnp.asarray(along, BF16), jnp.asarray(across, BF16),
    ]
    in_specs = [
        state_spec,
        row_spec,
        row_spec,
        whole(halos[2].shape),
        whole(halos[3].shape),
        pl.BlockSpec((fields, some, rows, tile), lambda i, info: (0, i, 0, 0)),
        whole(mask.shape),
        whole(react.shape),
        whole(along.shape),
        whole(across.shape),
    ]
    aliases = {}
    if before is not None:
        aliases = {1 + len(operands): 0}
        operands.append(before)
        in_specs.append(pl.BlockSpec(memory_space=pl.ANY))
    return pl.pallas_call(
        functools.partial(chem_kernel, scale),
        grid_spec=pltpu.PrefetchScalarGridSpec(
            num_scalar_prefetch=1,
            grid=(steps,),
            in_specs=in_specs,
            out_specs=[
                state_spec,
                pl.BlockSpec((actives, some, rows, tile), lambda i, info: (0, i, 0, 0)),
            ],
            scratch_shapes=[pltpu.VMEM((some, tracers, tile), F32)] * 2,
        ),
        out_shape=[
            jax.ShapeDtypeStruct(state.shape, BF16),
            jax.ShapeDtypeStruct((actives, own, rows, tile), BF16),
        ],
        input_output_aliases=aliases,
        compiler_params=pltpu.CompilerParams(vmem_limit_bytes=VMEM),
        cost_estimate=cost(own * cells * tile * 2 * 2048, own * cells * tile * 4),
        name="chemistry",
    )(info, *operands)


def spread_kernel(info, recv_ref, *refs):
    refs[-1][...] = recv_ref[...].astype(F32)


def spread(recv, info, sources, before):
    actives, own, rows, tile = recv.shape
    each = 2 if actives % 2 == 0 else 1
    operands = [recv]
    in_specs = [pl.BlockSpec((each, own, rows, tile), lambda a, info: (a, 0, 0, 0))]
    aliases = {}
    if before is not None:
        operands.append(before)
        in_specs.append(pl.BlockSpec(memory_space=pl.ANY))
        aliases = {2: 0}
    return pl.pallas_call(
        spread_kernel,
        grid_spec=pltpu.PrefetchScalarGridSpec(
            num_scalar_prefetch=1,
            grid=(actives // each,),
            in_specs=in_specs,
            out_specs=pl.BlockSpec((each, own, rows, tile), lambda a, info: (a, 0, 0, info[0])),
        ),
        out_shape=jax.ShapeDtypeStruct((actives, own, rows, sources * tile), F32),
        input_output_aliases=aliases,
        compiler_params=pltpu.CompilerParams(vmem_limit_bytes=VMEM),
        cost_estimate=cost(recv.size, recv.size * 6),
        name="spread",
    )(info, *operands)


def legendre_kernel(spectral_ref, legendre_ref, out_ref, rows_of, sums):
    parts, own, block, size = spectral_ref.shape
    bands, _, rows, pitch = out_ref.shape
    share = block * pl.num_programs(0)
    step = pl.program_id(0)
    lines = parts * own

    @pl.when(step == 0)
    def _():
        for h in range(sums.shape[0]):
            for l in range(own):
                tail = slice(l * pitch + parts * share, (l + 1) * pitch)
                sums[h, tail, :] = jnp.zeros((pitch - parts * share, LANES), F32)

    for v in range(size // LANES):
        part = spectral_ref[:, :, :, v * LANES : (v + 1) * LANES].astype(F32)
        rows_of[v] = part.reshape(lines * block, LANES)
    for m in range(block):
        x = [rows_of[v, pl.ds(m, lines, stride=block), :] for v in range(size // LANES)]
        x = jnp.concatenate(x, axis=1).astype(BF16)
        result = dot(x, legendre_ref[m], ((1,), (0,)))
        for r in range(parts):
            at = r * share + step * block + m
            for h in range(sums.shape[0]):
                piece = result[r * own : (r + 1) * own, h * LANES : (h + 1) * LANES]
                sums[h, pl.ds(at, own, stride=pitch), :] = piece

    @pl.when(step == pl.num_programs(0) - 1)
    def _():
        some = LANES // rows
        for l in range(own):
            for h in range(sums.shape[0]):
                turned = sums[h, l * pitch : (l + 1) * pitch, :].T.astype(BF16)
                out_ref[h * some : (h + 1) * some, l] = turned.reshape(some, rows, pitch)


def legendre_sums(spectral, legendre, bands):
    parts, own, share, size = spectral.shape
    rows = legendre.shape[2] // bands
    pitch = -(-parts * share // LANES) * LANES
    block = 16 if share % 16 == 0 else 8
    shape = (bands, own, rows, pitch)
    return pl.pallas_call(
        legendre_kernel,
        grid=(share // block,),
        in_specs=[
            pl.BlockSpec((parts, own, block, size), lambda i: (0, 0, i, 0)),
            pl.BlockSpec((block,) + legendre.shape[1:], lambda i: (i, 0, 0)),
        ],
        out_specs=pl.BlockSpec(shape, lambda i: (0, 0, 0, 0)),
        out_shape=jax.ShapeDtypeStruct(shape, BF16),
        scratch_shapes=[
            pltpu.VMEM((size // LANES, parts * own * block, LANES), F32),
            pltpu.VMEM((legendre.shape[2] // LANES, own * pitch, LANES), F32),
        ],
        compiler_params=pltpu.CompilerParams(vmem_limit_bytes=VMEM),
        cost_estimate=cost(2 * parts * own * legendre.size, 2 * (spectral.size + legendre.size)),
        name="legendre",
    )(spectral, legendre)


def exchange(value, axis, pairs):
    return lax.ppermute(value, axis, [p for a, b in pairs for p in ((a, b), (b, a))])


def neighbours(axis, first):
    size = lax.axis_size(axis)
    return [(i, i + 1) for i in range(first, size - 1, 2)]


def partners(axis, k):
    return [(i, i ^ k) for i in range(lax.axis_size(axis)) if i < i ^ k]


def body(spectral, legendre, wave_ids, points, tracers, react_base, react_temp, active_ids):
    bands, tiles = lax.axis_size("lat"), lax.axis_size("lon")
    tile = tracers.shape[3]
    waves = wave_ids.shape[0]
    band, me = lax.axis_index("lat"), lax.axis_index("lon")

    sent = legendre_sums(spectral, legendre, bands)
    recv = lax.all_to_all(sent, "lat", split_axis=0, concat_axis=0, tiled=True)

    table, twiddle = tables(points, wave_ids, tiles * tile // LANES)
    odd = jnp.stack([band % 2, me % 2]).astype(jnp.int32)
    row_a, row_b, col_a, col_b, react = edges(tracers, react_base, react_temp, odd)
    columns = me * tile + jnp.arange(tile)
    mask = (columns[None, :] < points[:, None]).astype(F32)
    infos = [
        jnp.concatenate([jnp.stack([me ^ k, odd[0], odd[1]]), active_ids]).astype(jnp.int32)
        for k in range(tiles)
    ]
    recv, table, twiddle, row_a, row_b, col_a, col_b, react, mask, infos = lax.optimization_barrier(
        (recv, table, twiddle, row_a, row_b, col_a, col_b, react, mask, infos)
    )

    grids = synthesis(recv, table, twiddle, infos[0][:1], tiles, tile)
    row_a, row_b, col_a, col_b, grids = lax.optimization_barrier((row_a, row_b, col_a, col_b, grids))
    order = list(range(2, tiles)) + [1]
    grids = {0: grids[0]} | {k: exchange(grids[k], "lon", partners("lon", k)) for k in order}
    halos = (
        exchange(row_a, "lat", neighbours("lat", 0)),
        exchange(row_b, "lat", neighbours("lat", 1)),
        exchange(col_a, "lon", neighbours("lon", 0)),
        exchange(col_b, "lon", neighbours("lon", 1)),
    )
    new, active = None, {}
    for k in [0] + order:
        new, active[k] = chemistry(
            tracers, halos, grids[k], mask, react, infos[k], active_ids.shape[0], waves, new
        )
        if k:
            active[k] = exchange(active[k], "lon", partners("lon", k))
    spreaded = None
    for k in [0] + order:
        spreaded = spread(active[k], infos[k], tiles, spreaded)
    return new, spreaded


def solution(mesh):
    return jax.shard_map(
        body,
        mesh=mesh,
        in_specs=(
            P(None, "lon", "lat", None),
            P("lat", None, None),
            P(),
            P("lat"),
            P(None, None, "lat", "lon"),
            P(),
            P(),
            P(),
        ),
        out_specs=(P(None, None, "lat", "lon"), P(None, "lon", "lat", None)),
        check_vma=False,
    )
```

```python
import functools

import jax
import jax.numpy as jnp
import numpy as np
from jax import lax
from jax.experimental import pallas as pl
from jax.experimental.pallas import tpu as pltpu
from jax.sharding import PartitionSpec as P

F32 = jnp.float32
BF16 = jnp.bfloat16
LANES = 128
LOW = 16
STEP = 4
MIB = 1024 * 1024

COS = (
    0.9999999890590228,
    -19.739204499454026,
    64.93911745990036,
    -85.45013953095037,
    60.16763095136588,
    -25.96759924965491,
    6.528658162567069,
)
SIN = (
    6.283185302511503,
    -41.34170040531769,
    81.60513138580204,
    -76.7030153539128,
    42.02592698618416,
    -14.899846668691637,
    3.238137510515757,
)


def dot(a, b, dims):
    return lax.dot_general(a, b, (dims, ((), ())), preferred_element_type=F32)


BAND, ME, IDS = 0, 1, 2


def cost(flops, moved):
    return pl.CostEstimate(flops=int(flops), bytes_accessed=int(moved), transcendentals=0)


def unit_circle(step, rows, waves, count):
    index = lax.broadcasted_iota(jnp.int32, (rows, waves.shape[1]), 0) * step
    product = index.astype(F32) * waves
    inverse = 1.0 / count
    turns = (product - jnp.floor(product * inverse) * count) * inverse
    y = turns - jnp.floor(turns + 0.5)
    z = y * y
    cosine = jnp.full_like(z, COS[-1])
    sine = jnp.full_like(z, SIN[-1])
    for c, s in zip(COS[-2::-1], SIN[-2::-1]):
        cosine = cosine * z + c
        sine = sine * z + s
    return cosine, sine * y


def table_kernel(first, info, waves_ref, table_ref, twiddle_ref):
    size, turns = waves_ref.shape[1], twiddle_ref.shape[2]
    waves = waves_ref[...].astype(F32)
    for k in range(table_ref.shape[0]):
        row = pl.program_id(0) * table_ref.shape[0] + k
        count = jnp.full(waves.shape, info[first + row], jnp.int32).astype(F32)
        cos_low, sin_low = unit_circle(1, LOW, waves, count)
        cos_high, sin_high = unit_circle(LOW, LANES // LOW, waves, count)
        cosine, sine = [], []
        for a in range(LANES // LOW):
            ch, sh = cos_high[a : a + 1], sin_high[a : a + 1]
            cosine.append(ch * cos_low - sh * sin_low)
            sine.append(-sh * cos_low - ch * sin_low)
        table_ref[k, :size, :] = jnp.concatenate(cosine, axis=0).T.astype(BF16)
        table_ref[k, size:, :] = jnp.concatenate(sine, axis=0).T.astype(BF16)
        cos_turn, sin_turn = unit_circle(LANES, turns, waves, count)
        twiddle_ref[k, 0] = cos_turn
        twiddle_ref[k, 1] = sin_turn


def tables(info, wave_ids, rows, turns):
    waves = wave_ids.shape[0]
    each = STEP if rows % STEP == 0 else 1
    return pl.pallas_call(
        functools.partial(table_kernel, info.shape[0] - rows),
        grid_spec=pltpu.PrefetchScalarGridSpec(
            num_scalar_prefetch=1,
            grid=(rows // each,),
            in_specs=[pl.BlockSpec((1, waves), lambda j, p: (0, 0))],
            out_specs=[
                pl.BlockSpec((each, 2 * waves, LANES), lambda j, p: (j, 0, 0)),
                pl.BlockSpec((each, 2, turns, waves), lambda j, p: (j, 0, 0, 0)),
            ],
        ),
        out_shape=[
            jax.ShapeDtypeStruct((rows, 2 * waves, LANES), BF16),
            jax.ShapeDtypeStruct((rows, 2, turns, waves), F32),
        ],
        compiler_params=pltpu.CompilerParams(vmem_limit_bytes=20 * MIB),
        cost_estimate=cost(rows * waves * LANES * 8, rows * waves * LANES * 4),
        name="tables",
    )(info, wave_ids[None, :])


def place(pieces, width):
    out = [None] * (width // LANES)
    lane = lax.broadcasted_iota(jnp.int32, (pieces[0][0].shape[0], LANES), 1)
    for value, start, count, here in pieces:
        shift = (here - start) % LANES
        for a in range(start // LANES, (start + count - 1) // LANES + 1):
            part = value[:, a * LANES : (a + 1) * LANES]
            if shift:
                part = pltpu.roll(part, shift, 1)
            first = max(start, a * LANES) - start + here
            last = min(start + count, (a + 1) * LANES) - start + here
            for v in range(first // LANES, (last - 1) // LANES + 1):
                low, high = max(first - v * LANES, 0), min(last - v * LANES, LANES)
                if out[v] is None:
                    out[v] = part
                else:
                    out[v] = jnp.where((lane >= low) & (lane < high), part, out[v])
    return out


def synth_kernel(info, recv_ref, table_ref, twiddle_ref, *refs):
    *out_refs, coef, grid = refs
    sources, levels, rows, _ = recv_ref.shape
    fields, waves = coef.shape[0] // 2, coef.shape[1] * LANES
    share = waves // sources
    each, _, turns = twiddle_ref.shape[:3]
    pitch = rows + 1
    step = pl.program_id(0)

    @pl.when(step == 0)
    def _():
        def level(l, carry):
            values = [recv_ref[s, l].astype(F32) for s in range(sources)]
            for r in range(2 * fields):
                windows = [
                    (values[s], r * share, share, s * share) for s in range(sources)
                ]
                for v, part in enumerate(place(windows, waves)):
                    coef[r, v, pl.ds(l * pitch, rows), :] = part
            return carry

        lax.fori_loop(0, levels, level, 0)

    for k in range(each):
        j = step * each + k

        def own_row(r):
            parts = [coef[r, v, pl.ds(j, levels, stride=pitch), :] for v in range(waves // LANES)]
            return jnp.concatenate(parts, axis=1)

        values = [own_row(r) for r in range(2 * fields)]
        real, imag = [], []
        for t in range(turns):
            c, s = twiddle_ref[k, 0, t : t + 1], twiddle_ref[k, 1, t : t + 1]
            for f in range(fields):
                re, im = values[2 * f], values[2 * f + 1]
                real.append(re * c - im * s)
                imag.append(re * s + im * c)
        both = [jnp.concatenate(part, axis=0).astype(BF16) for part in (real, imag)]
        result = dot(jnp.concatenate(both, axis=1), table_ref[k], ((1,), (0,)))
        grid[pl.ds(j, turns * fields * levels, stride=pitch), :] = result

    @pl.when(step == pl.num_programs(0) - 1)
    def _():
        tiles = turns // len(out_refs)
        for k, out_ref in enumerate(out_refs):
            for t in range(tiles):
                for f in range(fields):
                    start = (((info[ME] ^ k) * tiles + t) * fields + f) * levels
                    for l in range(levels):
                        block = grid[pl.ds((start + l) * pitch, rows), :].astype(BF16)
                        out_ref[f, l, :, t * LANES : (t + 1) * LANES] = block


def synthesis(recv, table, twiddle, info, dests, tile):
    sources, levels, rows, lanes = recv.shape
    turns, waves = twiddle.shape[2:]
    fields = 3
    each = STEP if rows % STEP == 0 else 1
    shape = (fields, levels, rows, tile)
    return pl.pallas_call(
        synth_kernel,
        grid_spec=pltpu.PrefetchScalarGridSpec(
            num_scalar_prefetch=1,
            grid=(rows // each,),
            in_specs=[
                pl.BlockSpec(recv.shape, lambda j, info: (0, 0, 0, 0)),
                pl.BlockSpec((each, 2 * waves, LANES), lambda j, info: (j, 0, 0)),
                pl.BlockSpec((each, 2, turns, waves), lambda j, info: (j, 0, 0, 0)),
            ],
            out_specs=[pl.BlockSpec(shape, lambda j, info: (0, 0, 0, 0))] * dests,
            scratch_shapes=[
                pltpu.VMEM((2 * fields, waves // LANES, levels * (rows + 1), LANES), F32),
                pltpu.VMEM((turns * fields * levels * (rows + 1), LANES), F32),
            ],
        ),
        out_shape=[jax.ShapeDtypeStruct(shape, BF16)] * dests,
        compiler_params=pltpu.CompilerParams(vmem_limit_bytes=24 * MIB),
        cost_estimate=cost(4 * rows * waves * fields * levels * turns * LANES, 4 * rows * waves * LANES),
        name="synthesis",
    )(info, recv, table, twiddle)


def edge_kernel(
    info, state_ref, base_ref, temp_ref, row_a_ref, row_b_ref, col_a_ref, col_b_ref, react_ref
):
    tracers, levels, rows, tile = state_ref.shape
    cells = tracers * rows

    @pl.when(pl.program_id(0) == 0)
    def _():
        rates = jnp.concatenate([base_ref[...], temp_ref[...]], axis=0)
        high = rates.astype(BF16)
        low = (rates - high.astype(F32)).astype(BF16)

        def iota(shape, axis):
            return lax.broadcasted_iota(jnp.int32, shape, axis)

        shape = (2 * cells, 2 * tracers)
        down = jnp.where(iota(shape, 0) // rows == iota(shape, 1), 1.0, 0.0).astype(BF16)
        shape = (tracers, cells)
        over = jnp.where(iota(shape, 0) == iota(shape, 1) // rows, 1.0, 0.0).astype(BF16)
        shape = (2 * cells, cells)
        same = iota(shape, 0) % rows == iota(shape, 1) % rows
        for k, part in enumerate((high, low)):
            wide = dot(dot(down, part, ((1,), (0,))).astype(BF16), over, ((1,), (0,)))
            react_ref[:, k * cells : (k + 1) * cells] = jnp.where(same, wide, 0.0).astype(BF16)

    def iota(shape, axis):
        return lax.broadcasted_iota(jnp.int32, shape, axis)

    odd = info[BAND] % 2, info[ME] % 2
    far, near = (1 - odd[0]) * (rows - 1), odd[0] * (rows - 1)
    shape = (2 * tracers, cells)
    end = jnp.where(iota(shape, 0) < tracers, far, near)
    pick = iota(shape, 1) == (iota(shape, 0) % tracers) * rows + end
    pick = jnp.where(pick, 1.0, 0.0).astype(BF16)
    shape = (2 * levels, tile)
    far, near = (1 - odd[1]) * (tile - 1), odd[1] * (tile - 1)
    is_end = iota(shape, 1) == jnp.where(iota(shape, 0) < levels, far, near)
    row = iota(shape, 0) % levels
    columns = jnp.zeros((2 * levels, cells), F32)
    for l in range(levels):
        x = state_ref[:, l].reshape(cells, tile)
        picked = dot(pick, x, ((1,), (0,)))
        row_a_ref[l] = picked[:tracers].astype(BF16)
        row_b_ref[l] = picked[tracers:].astype(BF16)
        mark = jnp.where(is_end & (row == l), 1.0, 0.0).astype(BF16)
        columns = columns + dot(mark, x, ((1,), (1,)))
    col_a_ref[...] = columns[:levels].astype(BF16)
    col_b_ref[...] = columns[levels:].astype(BF16)


def edges(state, react_base, react_temp, info):
    tracers, levels, rows, tile = state.shape
    block = 16
    cells = tracers * rows
    rowed = jax.ShapeDtypeStruct((levels, tracers, tile), BF16)
    columned = jax.ShapeDtypeStruct((levels, cells), BF16)
    row_spec = pl.BlockSpec((block, tracers, tile), lambda i, info: (i, 0, 0))
    col_spec = pl.BlockSpec((block, cells), lambda i, info: (i, 0))
    wide = (2 * cells, 2 * cells)
    return pl.pallas_call(
        edge_kernel,
        grid_spec=pltpu.PrefetchScalarGridSpec(
            num_scalar_prefetch=1,
            grid=(levels // block,),
            in_specs=[
                pl.BlockSpec((tracers, block, rows, tile), lambda i, info: (0, i, 0, 0)),
                pl.BlockSpec(react_base.shape, lambda i, info: (0, 0)),
                pl.BlockSpec(react_temp.shape, lambda i, info: (0, 0)),
            ],
            out_specs=[
                row_spec, row_spec, col_spec, col_spec, pl.BlockSpec(wide, lambda i, info: (0, 0)),
            ],
        ),
        out_shape=[rowed, rowed, columned, columned, jax.ShapeDtypeStruct(wide, BF16)],
        compiler_params=pltpu.CompilerParams(vmem_limit_bytes=16 * MIB),
        cost_estimate=cost(4 * state.size * 32, 2 * state.size),
        name="edges",
    )(info, state, react_base, react_temp)


def chem_kernel(scale, k, info, *refs):
    state_ref, row_a_ref, row_b_ref, col_a_ref, col_b_ref, grid_ref, react_ref = refs[:7]
    along_ref, across_ref = refs[7:9]
    new_ref, active_ref, south, north = refs[-4:]
    tracers, levels, rows, tile = state_ref.shape
    cells = tracers * rows
    half, side = rows // 2, tile // 2
    odd_band, odd_tile = info[BAND] % 2 == 1, info[ME] % 2 == 1
    first = ((info[ME] ^ k) * pl.num_programs(0) + pl.program_id(0)) * levels

    def column(value):
        pad = jnp.zeros((LANES - value.shape[0], cells), F32)
        turn = lax.rem(LANES - first, LANES)
        return pltpu.roll(jnp.concatenate([value, pad], axis=0).T, turn, 1)

    a, b = col_a_ref[...].astype(F32), col_b_ref[...].astype(F32)
    west, east = column(jnp.where(odd_tile, a, b)), column(jnp.where(odd_tile, b, a))
    row = lax.broadcasted_iota(jnp.int32, (rows, tile), 0)
    lane = lax.broadcasted_iota(jnp.int32, (rows, tile), 1)
    ids, points = IDS, IDS + active_ref.shape[0]
    count = jnp.full((rows, tile), info[points], jnp.int32)
    for j in range(1, rows):
        count = jnp.where(row == j, info[points + j], count)
    mask = jnp.where(info[ME] * tile + lane < count, 1.0, 0.0)
    nn = ((1,), (0,))

    def three(v):
        return v.reshape(tracers, rows, tile)

    for l in range(levels):
        x = state_ref[:, l].reshape(cells, tile)
        lon = dot(x, along_ref[...], nn)
        lat = dot(across_ref[...], x, nn)
        wind_u = grid_ref[0, l].astype(F32) * (scale * 0.1)
        wind_v = grid_ref[1, l].astype(F32) * (scale * 0.1)
        temper = grid_ref[2, l].astype(F32) * scale
        moved = (
            three(x.astype(F32))
            - wind_u * three(lon[:, :tile])
            - wind_v * three(lat[:cells])
            + 0.05 * three(lon[:, tile:] + lat[cells:])
        )
        a, b = row_a_ref[l].astype(F32), row_b_ref[l].astype(F32)
        south[l] = jnp.where(odd_band, a, b)
        north[l] = jnp.where(odd_band, b, a)
        in_row = jnp.where(row == 0, 0.05 + wind_v, jnp.where(row == rows - 1, 0.05 - wind_v, 0.0))
        in_col = jnp.where(lane == 0, 0.05 + wind_u, jnp.where(lane == tile - 1, 0.05 - wind_u, 0.0))
        outer = []
        for t in range(tracers):
            up = [jnp.broadcast_to(ref[l, t : t + 1], (half, tile)) for ref in (south, north)]
            cell = slice(t * rows, (t + 1) * rows)
            across = [
                jnp.broadcast_to(col[cell, l : l + 1], (rows, side)) for col in (west, east)
            ]
            outer.append(
                in_row * jnp.concatenate(up, axis=0) + in_col * jnp.concatenate(across, axis=1)
            )
        moved = moved + jnp.stack(outer, axis=0)
        high = moved.reshape(cells, tile).astype(BF16)
        terms = dot(react_ref[...], jnp.concatenate([high, high], axis=0), nn)
        reacted = (moved + three(terms[:cells]) + temper * three(terms[cells:])) * mask
        new_ref[:, l] = reacted.astype(BF16)
    for a in range(active_ref.shape[0]):
        active_ref[a] = new_ref[info[ids + a]]


def chemistry(state, halos, grid, react, info, k, actives, waves, before):
    tracers, levels, rows, tile = state.shape
    fields, own = grid.shape[:2]
    some = 4 if own % 4 == 0 else own
    steps = own // some
    cells = tracers * rows
    eye, one = np.eye(tracers), np.eye(tile)
    along = np.concatenate(
        [np.eye(tile, k=-1) - np.eye(tile, k=1), np.eye(tile, k=-1) + np.eye(tile, k=1) - 4 * one], 1
    )
    down, up = np.eye(rows, k=-1), np.eye(rows, k=1)
    across = np.concatenate([np.kron(eye, up - down), np.kron(eye, up + down)], 0)
    scale = 1.0 / float(np.sqrt(np.float32(waves)))

    def whole(shape):
        return pl.BlockSpec(shape, lambda i, info: (0,) * len(shape))

    row_spec = pl.BlockSpec((some, tracers, tile), lambda i, info: ((info[ME] ^ k) * steps + i, 0, 0))
    state_spec = pl.BlockSpec(
        (tracers, some, rows, tile), lambda i, info: (0, (info[ME] ^ k) * steps + i, 0, 0)
    )
    operands = [
        state, *halos, grid, react, jnp.asarray(along, BF16), jnp.asarray(across, BF16),
    ]
    in_specs = [
        state_spec,
        row_spec,
        row_spec,
        whole(halos[2].shape),
        whole(halos[3].shape),
        pl.BlockSpec((fields, some, rows, tile), lambda i, info: (0, i, 0, 0)),
        whole(react.shape),
        whole(along.shape),
        whole(across.shape),
    ]
    aliases = {}
    if before is not None:
        aliases = {1 + len(operands): 0}
        operands.append(before)
        in_specs.append(pl.BlockSpec(memory_space=pl.ANY))
    return pl.pallas_call(
        functools.partial(chem_kernel, scale, k),
        grid_spec=pltpu.PrefetchScalarGridSpec(
            num_scalar_prefetch=1,
            grid=(steps,),
            in_specs=in_specs,
            out_specs=[
                state_spec,
                pl.BlockSpec((actives, some, rows, tile), lambda i, info: (0, i, 0, 0)),
            ],
            scratch_shapes=[pltpu.VMEM((some, tracers, tile), F32)] * 2,
        ),
        out_shape=[
            jax.ShapeDtypeStruct(state.shape, BF16),
            jax.ShapeDtypeStruct((actives, own, rows, tile), BF16),
        ],
        input_output_aliases=aliases,
        compiler_params=pltpu.CompilerParams(vmem_limit_bytes=16 * MIB),
        cost_estimate=cost(own * cells * tile, own * tile),
        name="chemistry",
    )(info, *operands)


def spread_kernel(info, recv_ref, *refs):
    refs[-1][...] = recv_ref[...].astype(F32)


def spread(recv, info, k, sources, before):
    actives, own, rows, tile = recv.shape
    each = 2 if actives % 2 == 0 else 1
    operands = [recv]
    in_specs = [pl.BlockSpec((each, own, rows, tile), lambda a, info: (a, 0, 0, 0))]
    aliases = {}
    if before is not None:
        operands.append(before)
        in_specs.append(pl.BlockSpec(memory_space=pl.ANY))
        aliases = {2: 0}
    return pl.pallas_call(
        spread_kernel,
        grid_spec=pltpu.PrefetchScalarGridSpec(
            num_scalar_prefetch=1,
            grid=(actives // each,),
            in_specs=in_specs,
            out_specs=pl.BlockSpec((each, own, rows, tile), lambda a, info: (a, 0, 0, info[ME] ^ k)),
        ),
        out_shape=jax.ShapeDtypeStruct((actives, own, rows, sources * tile), F32),
        input_output_aliases=aliases,
        compiler_params=pltpu.CompilerParams(vmem_limit_bytes=8 * MIB),
        cost_estimate=cost(recv.size, recv.shape[0]),
        name="spread",
    )(info, *operands)


def legendre_kernel(spectral_ref, legendre_ref, out_ref, rows_of, sums):
    parts, own, block, size = spectral_ref.shape
    bands, _, rows, pitch = out_ref.shape
    share = block * pl.num_programs(0)
    step = pl.program_id(0)
    lines = parts * own
    apart, stretch = block + 1, pitch + 1

    @pl.when(step == 0)
    def _():
        for h in range(sums.shape[0]):
            for l in range(own):
                tail = pl.ds(l * stretch + parts * share, pitch - parts * share)
                sums[h, tail, :] = jnp.zeros((pitch - parts * share, LANES), F32)

    for v in range(size // LANES):
        part = spectral_ref[:, :, :, v * LANES : (v + 1) * LANES].astype(F32)
        part = part.reshape(lines, block, LANES)
        for i in range(lines):
            rows_of[v, pl.ds(i * apart, block), :] = part[i]
    for m in range(block):
        x = [rows_of[v, pl.ds(m, lines, stride=apart), :] for v in range(size // LANES)]
        x = jnp.concatenate(x, axis=1).astype(BF16)
        result = dot(x, legendre_ref[m], ((1,), (0,)))
        for r in range(parts):
            at = r * share + step * block + m
            for h in range(sums.shape[0]):
                piece = result[r * own : (r + 1) * own, h * LANES : (h + 1) * LANES]
                sums[h, pl.ds(at, own, stride=stretch), :] = piece

    @pl.when(step == pl.num_programs(0) - 1)
    def _():
        some = LANES // rows
        for l in range(own):
            for h in range(sums.shape[0]):
                turned = sums[h, pl.ds(l * stretch, pitch), :].T.astype(BF16)
                out_ref[h * some : (h + 1) * some, l] = turned.reshape(some, rows, pitch)


def legendre_sums(spectral, legendre, bands):
    parts, own, share, size = spectral.shape
    rows = legendre.shape[2] // bands
    pitch = -(-parts * share // LANES) * LANES
    block = 16 if share % 16 == 0 else 8
    shape = (bands, own, rows, pitch)
    return pl.pallas_call(
        legendre_kernel,
        grid=(share // block,),
        in_specs=[
            pl.BlockSpec((parts, own, block, size), lambda i: (0, 0, i, 0)),
            pl.BlockSpec((block,) + legendre.shape[1:], lambda i: (i, 0, 0)),
        ],
        out_specs=pl.BlockSpec(shape, lambda i: (0, 0, 0, 0)),
        out_shape=jax.ShapeDtypeStruct(shape, BF16),
        scratch_shapes=[
            pltpu.VMEM((size // LANES, parts * own * (block + 1), LANES), F32),
            pltpu.VMEM((legendre.shape[2] // LANES, own * (pitch + 1), LANES), F32),
        ],
        compiler_params=pltpu.CompilerParams(vmem_limit_bytes=56 * MIB),
        cost_estimate=cost(2 * parts * own * legendre.size, 2 * (spectral.size + legendre.size)),
        name="legendre",
    )(spectral, legendre)


def exchange(value, axis, pairs):
    return lax.ppermute(value, axis, [p for a, b in pairs for p in ((a, b), (b, a))])


def neighbours(axis, first):
    size = lax.axis_size(axis)
    return [(i, i + 1) for i in range(first, size - 1, 2)]


def partners(axis, k):
    return [(i, i ^ k) for i in range(lax.axis_size(axis)) if i < i ^ k]


def body(spectral, legendre, wave_ids, points, tracers, react_base, react_temp, active_ids):
    bands, tiles = lax.axis_size("lat"), lax.axis_size("lon")
    tile = tracers.shape[3]
    waves = wave_ids.shape[0]
    band, me = lax.axis_index("lat"), lax.axis_index("lon")

    sent = legendre_sums(spectral, legendre, bands)
    recv = lax.all_to_all(sent, "lat", split_axis=0, concat_axis=0, tiled=True)

    rows = points.shape[0]
    info = jnp.concatenate([jnp.stack([band, me]), active_ids, points]).astype(jnp.int32)
    table, twiddle = tables(info, wave_ids, rows, tiles * tile // LANES)
    *ends, react = edges(tracers, react_base, react_temp, info)
    recv, table, twiddle, ends, react = lax.optimization_barrier((recv, table, twiddle, ends, react))

    grids = synthesis(recv, table, twiddle, info, tiles, tile)
    ends, grids = lax.optimization_barrier((ends, grids))
    middle = list(range(tiles // 2, tiles))
    soon, late = middle[: tiles // 4], middle[tiles // 4 :]
    inner = list(range(tiles // 2 - 1, 0, -1))

    def send(value, k):
        return exchange(value, "lon", partners("lon", k))

    moved = {0: grids[0]} | {k: send(grids[k], k) for k in soon + inner}
    halos = (
        exchange(ends[0], "lat", neighbours("lat", 0)),
        exchange(ends[1], "lat", neighbours("lat", 1)),
        exchange(ends[2], "lon", neighbours("lon", 0)),
        exchange(ends[3], "lon", neighbours("lon", 1)),
    )
    new, active = None, {}
    for k in [0] + soon + late + inner:
        new, active[k] = chemistry(
            tracers, halos, moved[k], react, info, k, active_ids.shape[0], waves, new
        )
        if k:
            active[k] = send(active[k], k)
        else:
            held, active[0] = lax.optimization_barrier(([grids[i] for i in late], active[0]))
            moved |= {i: send(value, i) for i, value in zip(late, held)}
    spreaded = None
    for k in [0] + soon + inner + late:
        spreaded = spread(active[k], info, k, tiles, spreaded)
    return new, spreaded


def solution(mesh):
    return jax.shard_map(
        body,
        mesh=mesh,
        in_specs=(
            P(None, "lon", "lat", None),
            P("lat", None, None),
            P(),
            P("lat"),
            P(None, None, "lat", "lon"),
            P(),
            P(),
            P(),
        ),
        out_specs=(P(None, None, "lat", "lon"), P(None, "lon", "lat", None)),
        check_vma=False,
    )
```

```python
import functools

import jax
import jax.numpy as jnp
import numpy as np
from jax import lax
from jax.experimental import pallas as pl
from jax.experimental.pallas import tpu as pltpu
from jax.sharding import PartitionSpec as P

F32 = jnp.float32
BF16 = jnp.bfloat16
LANES = 128
LOW = 16
STEP = 4
MIB = 1024 * 1024

COS = (
    0.9999999890590228,
    -19.739204499454026,
    64.93911745990036,
    -85.45013953095037,
    60.16763095136588,
    -25.96759924965491,
    6.528658162567069,
)
SIN = (
    6.283185302511503,
    -41.34170040531769,
    81.60513138580204,
    -76.7030153539128,
    42.02592698618416,
    -14.899846668691637,
    3.238137510515757,
)


def dot(a, b, dims):
    return lax.dot_general(a, b, (dims, ((), ())), preferred_element_type=F32)


BAND, ME, IDS = 0, 1, 2


def cost(flops, moved):
    return pl.CostEstimate(flops=int(flops), bytes_accessed=int(moved), transcendentals=0)


def unit_circle(step, rows, waves, count):
    index = lax.broadcasted_iota(jnp.int32, (rows, waves.shape[1]), 0) * step
    product = index.astype(F32) * waves
    inverse = 1.0 / count
    turns = (product - jnp.floor(product * inverse) * count) * inverse
    y = turns - jnp.floor(turns + 0.5)
    z = y * y
    cosine = jnp.full_like(z, COS[-1])
    sine = jnp.full_like(z, SIN[-1])
    for c, s in zip(COS[-2::-1], SIN[-2::-1]):
        cosine = cosine * z + c
        sine = sine * z + s
    return cosine, sine * y


def table_kernel(first, info, waves_ref, table_ref, twiddle_ref):
    size, turns = waves_ref.shape[1], twiddle_ref.shape[2]
    waves = waves_ref[...].astype(F32)
    for k in range(table_ref.shape[0]):
        row = pl.program_id(0) * table_ref.shape[0] + k
        count = jnp.full(waves.shape, info[first + row], jnp.int32).astype(F32)
        cos_low, sin_low = unit_circle(1, LOW, waves, count)
        cos_high, sin_high = unit_circle(LOW, LANES // LOW, waves, count)
        cosine, sine = [], []
        for a in range(LANES // LOW):
            ch, sh = cos_high[a : a + 1], sin_high[a : a + 1]
            cosine.append(ch * cos_low - sh * sin_low)
            sine.append(-sh * cos_low - ch * sin_low)
        table_ref[k, :size, :] = jnp.concatenate(cosine, axis=0).T.astype(BF16)
        table_ref[k, size:, :] = jnp.concatenate(sine, axis=0).T.astype(BF16)
        cos_turn, sin_turn = unit_circle(LANES, turns, waves, count)
        twiddle_ref[k, 0] = cos_turn
        twiddle_ref[k, 1] = sin_turn


def tables(info, wave_ids, rows, turns):
    waves = wave_ids.shape[0]
    each = STEP if rows % STEP == 0 else 1
    return pl.pallas_call(
        functools.partial(table_kernel, info.shape[0] - rows),
        grid_spec=pltpu.PrefetchScalarGridSpec(
            num_scalar_prefetch=1,
            grid=(rows // each,),
            in_specs=[pl.BlockSpec((1, waves), lambda j, p: (0, 0))],
            out_specs=[
                pl.BlockSpec((each, 2 * waves, LANES), lambda j, p: (j, 0, 0)),
                pl.BlockSpec((each, 2, turns, waves), lambda j, p: (j, 0, 0, 0)),
            ],
        ),
        out_shape=[
            jax.ShapeDtypeStruct((rows, 2 * waves, LANES), BF16),
            jax.ShapeDtypeStruct((rows, 2, turns, waves), F32),
        ],
        compiler_params=pltpu.CompilerParams(vmem_limit_bytes=20 * MIB),
        cost_estimate=cost(rows * waves * LANES * 8, rows * waves * LANES * 4),
        name="tables",
    )(info, wave_ids[None, :])


def place(pieces, width):
    out = [None] * (width // LANES)
    lane = lax.broadcasted_iota(jnp.int32, (pieces[0][0].shape[0], LANES), 1)
    for value, start, count, here in pieces:
        shift = (here - start) % LANES
        for a in range(start // LANES, (start + count - 1) // LANES + 1):
            part = value[:, a * LANES : (a + 1) * LANES]
            if shift:
                part = pltpu.roll(part, shift, 1)
            first = max(start, a * LANES) - start + here
            last = min(start + count, (a + 1) * LANES) - start + here
            for v in range(first // LANES, (last - 1) // LANES + 1):
                low, high = max(first - v * LANES, 0), min(last - v * LANES, LANES)
                if out[v] is None:
                    out[v] = part
                else:
                    out[v] = jnp.where((lane >= low) & (lane < high), part, out[v])
    return out


def synth_kernel(info, recv_ref, table_ref, twiddle_ref, *refs):
    *out_refs, coef, grid = refs
    sources, levels, rows, _ = recv_ref.shape
    fields, waves = coef.shape[0] // 2, coef.shape[1] * LANES
    share = waves // sources
    each, _, turns = twiddle_ref.shape[:3]
    pitch = rows + 1
    step = pl.program_id(0)

    @pl.when(step == 0)
    def _():
        def level(l, carry):
            values = [recv_ref[s, l].astype(F32) for s in range(sources)]
            for r in range(2 * fields):
                windows = [
                    (values[s], r * share, share, s * share) for s in range(sources)
                ]
                for v, part in enumerate(place(windows, waves)):
                    coef[r, v, pl.ds(l * pitch, rows), :] = part
            return carry

        lax.fori_loop(0, levels, level, 0)

    for k in range(each):
        j = step * each + k

        def own_row(r):
            parts = [coef[r, v, pl.ds(j, levels, stride=pitch), :] for v in range(waves // LANES)]
            return jnp.concatenate(parts, axis=1)

        values = [own_row(r) for r in range(2 * fields)]
        real, imag = [], []
        for t in range(turns):
            c, s = twiddle_ref[k, 0, t : t + 1], twiddle_ref[k, 1, t : t + 1]
            for f in range(fields):
                re, im = values[2 * f], values[2 * f + 1]
                real.append(re * c - im * s)
                imag.append(re * s + im * c)
        both = [jnp.concatenate(part, axis=0).astype(BF16) for part in (real, imag)]
        result = dot(jnp.concatenate(both, axis=1), table_ref[k], ((1,), (0,)))
        grid[pl.ds(j, turns * fields * levels, stride=pitch), :] = result

    @pl.when(step == pl.num_programs(0) - 1)
    def _():
        tiles = turns // len(out_refs)
        for k, out_ref in enumerate(out_refs):
            for t in range(tiles):
                for f in range(fields):
                    start = (((info[ME] ^ k) * tiles + t) * fields + f) * levels
                    for l in range(levels):
                        block = grid[pl.ds((start + l) * pitch, rows), :].astype(BF16)
                        out_ref[f, l, :, t * LANES : (t + 1) * LANES] = block


def synthesis(recv, table, twiddle, info, dests, tile):
    sources, levels, rows, lanes = recv.shape
    turns, waves = twiddle.shape[2:]
    fields = 3
    each = STEP if rows % STEP == 0 else 1
    shape = (fields, levels, rows, tile)
    return pl.pallas_call(
        synth_kernel,
        grid_spec=pltpu.PrefetchScalarGridSpec(
            num_scalar_prefetch=1,
            grid=(rows // each,),
            in_specs=[
                pl.BlockSpec(recv.shape, lambda j, info: (0, 0, 0, 0)),
                pl.BlockSpec((each, 2 * waves, LANES), lambda j, info: (j, 0, 0)),
                pl.BlockSpec((each, 2, turns, waves), lambda j, info: (j, 0, 0, 0)),
            ],
            out_specs=[pl.BlockSpec(shape, lambda j, info: (0, 0, 0, 0))] * dests,
            scratch_shapes=[
                pltpu.VMEM((2 * fields, waves // LANES, levels * (rows + 1), LANES), F32),
                pltpu.VMEM((turns * fields * levels * (rows + 1), LANES), F32),
            ],
        ),
        out_shape=[jax.ShapeDtypeStruct(shape, BF16)] * dests,
        compiler_params=pltpu.CompilerParams(vmem_limit_bytes=24 * MIB),
        cost_estimate=cost(4 * rows * waves * fields * levels * turns * LANES, 4 * rows * waves * LANES),
        name="synthesis",
    )(info, recv, table, twiddle)


def edge_kernel(
    info, state_ref, base_ref, temp_ref, row_a_ref, row_b_ref, col_a_ref, col_b_ref, react_ref
):
    tracers, levels, rows, tile = state_ref.shape
    cells = tracers * rows

    @pl.when(pl.program_id(0) == 0)
    def _():
        rates = jnp.concatenate([base_ref[...], temp_ref[...]], axis=0)
        high = rates.astype(BF16)
        low = (rates - high.astype(F32)).astype(BF16)

        def iota(shape, axis):
            return lax.broadcasted_iota(jnp.int32, shape, axis)

        shape = (2 * cells, 2 * tracers)
        down = jnp.where(iota(shape, 0) // rows == iota(shape, 1), 1.0, 0.0).astype(BF16)
        shape = (tracers, cells)
        over = jnp.where(iota(shape, 0) == iota(shape, 1) // rows, 1.0, 0.0).astype(BF16)
        shape = (2 * cells, cells)
        same = iota(shape, 0) % rows == iota(shape, 1) % rows
        for k, part in enumerate((high, low)):
            wide = dot(dot(down, part, ((1,), (0,))).astype(BF16), over, ((1,), (0,)))
            react_ref[:, k * cells : (k + 1) * cells] = jnp.where(same, wide, 0.0).astype(BF16)

    def iota(shape, axis):
        return lax.broadcasted_iota(jnp.int32, shape, axis)

    odd = info[BAND] % 2, info[ME] % 2
    far, near = (1 - odd[0]) * (rows - 1), odd[0] * (rows - 1)
    shape = (2 * tracers, cells)
    end = jnp.where(iota(shape, 0) < tracers, far, near)
    pick = iota(shape, 1) == (iota(shape, 0) % tracers) * rows + end
    pick = jnp.where(pick, 1.0, 0.0).astype(BF16)
    shape = (2 * levels, tile)
    far, near = (1 - odd[1]) * (tile - 1), odd[1] * (tile - 1)
    is_end = iota(shape, 1) == jnp.where(iota(shape, 0) < levels, far, near)
    row = iota(shape, 0) % levels
    columns = jnp.zeros((2 * levels, cells), F32)
    for l in range(levels):
        x = state_ref[:, l].reshape(cells, tile)
        picked = dot(pick, x, ((1,), (0,)))
        row_a_ref[l] = picked[:tracers].astype(BF16)
        row_b_ref[l] = picked[tracers:].astype(BF16)
        mark = jnp.where(is_end & (row == l), 1.0, 0.0).astype(BF16)
        columns = columns + dot(mark, x, ((1,), (1,)))
    col_a_ref[...] = columns[:levels].astype(BF16)
    col_b_ref[...] = columns[levels:].astype(BF16)


def edges(state, react_base, react_temp, info):
    tracers, levels, rows, tile = state.shape
    block = 16
    cells = tracers * rows
    rowed = jax.ShapeDtypeStruct((levels, tracers, tile), BF16)
    columned = jax.ShapeDtypeStruct((levels, cells), BF16)
    row_spec = pl.BlockSpec((block, tracers, tile), lambda i, info: (i, 0, 0))
    col_spec = pl.BlockSpec((block, cells), lambda i, info: (i, 0))
    wide = (2 * cells, 2 * cells)
    return pl.pallas_call(
        edge_kernel,
        grid_spec=pltpu.PrefetchScalarGridSpec(
            num_scalar_prefetch=1,
            grid=(levels // block,),
            in_specs=[
                pl.BlockSpec((tracers, block, rows, tile), lambda i, info: (0, i, 0, 0)),
                pl.BlockSpec(react_base.shape, lambda i, info: (0, 0)),
                pl.BlockSpec(react_temp.shape, lambda i, info: (0, 0)),
            ],
            out_specs=[
                row_spec, row_spec, col_spec, col_spec, pl.BlockSpec(wide, lambda i, info: (0, 0)),
            ],
        ),
        out_shape=[rowed, rowed, columned, columned, jax.ShapeDtypeStruct(wide, BF16)],
        compiler_params=pltpu.CompilerParams(vmem_limit_bytes=52 * MIB),
        cost_estimate=cost(4 * state.size * 32, 2 * state.size),
        name="edges",
    )(info, state, react_base, react_temp)


def chem_kernel(scale, k, info, *refs):
    state_ref, row_a_ref, row_b_ref, col_a_ref, col_b_ref, grid_ref, react_ref = refs[:7]
    along_ref, across_ref = refs[7:9]
    new_ref, active_ref, south, north = refs[-4:]
    tracers, levels, rows, tile = state_ref.shape
    cells = tracers * rows
    half, side = rows // 2, tile // 2
    odd_band, odd_tile = info[BAND] % 2 == 1, info[ME] % 2 == 1
    first = ((info[ME] ^ k) * pl.num_programs(0) + pl.program_id(0)) * levels

    def column(value):
        pad = jnp.zeros((LANES - value.shape[0], cells), F32)
        turn = lax.rem(LANES - first, LANES)
        return pltpu.roll(jnp.concatenate([value, pad], axis=0).T, turn, 1)

    a, b = col_a_ref[...].astype(F32), col_b_ref[...].astype(F32)
    west, east = column(jnp.where(odd_tile, a, b)), column(jnp.where(odd_tile, b, a))
    row = lax.broadcasted_iota(jnp.int32, (rows, tile), 0)
    lane = lax.broadcasted_iota(jnp.int32, (rows, tile), 1)
    ids, points = IDS, IDS + active_ref.shape[0]
    count = jnp.full((rows, tile), info[points], jnp.int32)
    for j in range(1, rows):
        count = jnp.where(row == j, info[points + j], count)
    mask = jnp.where(info[ME] * tile + lane < count, 1.0, 0.0)
    nn = ((1,), (0,))

    def three(v):
        return v.reshape(tracers, rows, tile)

    for l in range(levels):
        x = state_ref[:, l].reshape(cells, tile)
        lon = dot(x, along_ref[...], nn)
        lat = dot(across_ref[...], x, nn)
        wind_u = grid_ref[0, l].astype(F32) * (scale * 0.1)
        wind_v = grid_ref[1, l].astype(F32) * (scale * 0.1)
        temper = grid_ref[2, l].astype(F32) * scale
        moved = (
            three(x.astype(F32))
            - wind_u * three(lon[:, :tile])
            - wind_v * three(lat[:cells])
            + 0.05 * three(lon[:, tile:] + lat[cells:])
        )
        a, b = row_a_ref[l].astype(F32), row_b_ref[l].astype(F32)
        south[l] = jnp.where(odd_band, a, b)
        north[l] = jnp.where(odd_band, b, a)
        in_row = jnp.where(row == 0, 0.05 + wind_v, jnp.where(row == rows - 1, 0.05 - wind_v, 0.0))
        in_col = jnp.where(lane == 0, 0.05 + wind_u, jnp.where(lane == tile - 1, 0.05 - wind_u, 0.0))
        outer = []
        for t in range(tracers):
            up = [jnp.broadcast_to(ref[l, t : t + 1], (half, tile)) for ref in (south, north)]
            cell = slice(t * rows, (t + 1) * rows)
            across = [
                jnp.broadcast_to(col[cell, l : l + 1], (rows, side)) for col in (west, east)
            ]
            outer.append(
                in_row * jnp.concatenate(up, axis=0) + in_col * jnp.concatenate(across, axis=1)
            )
        moved = moved + jnp.stack(outer, axis=0)
        high = moved.reshape(cells, tile).astype(BF16)
        terms = dot(react_ref[...], jnp.concatenate([high, high], axis=0), nn)
        reacted = (moved + three(terms[:cells]) + temper * three(terms[cells:])) * mask
        new_ref[:, l] = reacted.astype(BF16)
    for a in range(active_ref.shape[0]):
        active_ref[a] = new_ref[info[ids + a]]


def chemistry(state, halos, grid, react, info, k, actives, waves, before):
    tracers, levels, rows, tile = state.shape
    fields, own = grid.shape[:2]
    some = 4 if own % 4 == 0 else own
    steps = own // some
    cells = tracers * rows
    eye, one = np.eye(tracers), np.eye(tile)
    along = np.concatenate(
        [np.eye(tile, k=-1) - np.eye(tile, k=1), np.eye(tile, k=-1) + np.eye(tile, k=1) - 4 * one], 1
    )
    down, up = np.eye(rows, k=-1), np.eye(rows, k=1)
    across = np.concatenate([np.kron(eye, up - down), np.kron(eye, up + down)], 0)
    scale = 1.0 / float(np.sqrt(np.float32(waves)))

    def whole(shape):
        return pl.BlockSpec(shape, lambda i, info: (0,) * len(shape))

    row_spec = pl.BlockSpec((some, tracers, tile), lambda i, info: ((info[ME] ^ k) * steps + i, 0, 0))
    state_spec = pl.BlockSpec(
        (tracers, some, rows, tile), lambda i, info: (0, (info[ME] ^ k) * steps + i, 0, 0)
    )
    operands = [
        state, *halos, grid, react, jnp.asarray(along, BF16), jnp.asarray(across, BF16),
    ]
    in_specs = [
        state_spec,
        row_spec,
        row_spec,
        whole(halos[2].shape),
        whole(halos[3].shape),
        pl.BlockSpec((fields, some, rows, tile), lambda i, info: (0, i, 0, 0)),
        whole(react.shape),
        whole(along.shape),
        whole(across.shape),
    ]
    aliases = {}
    if before is not None:
        aliases = {1 + len(operands): 0}
        operands.append(before)
        in_specs.append(pl.BlockSpec(memory_space=pl.ANY))
    return pl.pallas_call(
        functools.partial(chem_kernel, scale, k),
        grid_spec=pltpu.PrefetchScalarGridSpec(
            num_scalar_prefetch=1,
            grid=(steps,),
            in_specs=in_specs,
            out_specs=[
                state_spec,
                pl.BlockSpec((actives, some, rows, tile), lambda i, info: (0, i, 0, 0)),
            ],
            scratch_shapes=[pltpu.VMEM((some, tracers, tile), F32)] * 2,
        ),
        out_shape=[
            jax.ShapeDtypeStruct(state.shape, BF16),
            jax.ShapeDtypeStruct((actives, own, rows, tile), BF16),
        ],
        input_output_aliases=aliases,
        compiler_params=pltpu.CompilerParams(vmem_limit_bytes=16 * MIB),
        cost_estimate=cost(own * cells * tile, own * tile),
        name="chemistry",
    )(info, *operands)


def spread_kernel(info, recv_ref, *refs):
    refs[-1][...] = recv_ref[...].astype(F32)


def spread(recv, info, k, sources, before):
    actives, own, rows, tile = recv.shape
    each = 2 if actives % 2 == 0 else 1
    operands = [recv]
    in_specs = [pl.BlockSpec((each, own, rows, tile), lambda a, info: (a, 0, 0, 0))]
    aliases = {}
    if before is not None:
        operands.append(before)
        in_specs.append(pl.BlockSpec(memory_space=pl.ANY))
        aliases = {2: 0}
    return pl.pallas_call(
        spread_kernel,
        grid_spec=pltpu.PrefetchScalarGridSpec(
            num_scalar_prefetch=1,
            grid=(actives // each,),
            in_specs=in_specs,
            out_specs=pl.BlockSpec((each, own, rows, tile), lambda a, info: (a, 0, 0, info[ME] ^ k)),
        ),
        out_shape=jax.ShapeDtypeStruct((actives, own, rows, sources * tile), F32),
        input_output_aliases=aliases,
        compiler_params=pltpu.CompilerParams(vmem_limit_bytes=8 * MIB),
        cost_estimate=cost(recv.size, recv.shape[0]),
        name="spread",
    )(info, *operands)


def legendre_kernel(spectral_ref, legendre_ref, out_ref, rows_of, sums):
    parts, own, block, size = spectral_ref.shape
    bands, _, rows, pitch = out_ref.shape
    share = block * pl.num_programs(0)
    step = pl.program_id(0)
    lines = parts * own
    apart, stretch = block + 1, pitch + 1

    @pl.when(step == 0)
    def _():
        for h in range(sums.shape[0]):
            for l in range(own):
                tail = pl.ds(l * stretch + parts * share, pitch - parts * share)
                sums[h, tail, :] = jnp.zeros((pitch - parts * share, LANES), F32)

    for v in range(size // LANES):
        part = spectral_ref[:, :, :, v * LANES : (v + 1) * LANES].astype(F32)
        part = part.reshape(lines, block, LANES)
        for i in range(lines):
            rows_of[v, pl.ds(i * apart, block), :] = part[i]
    for m in range(block):
        x = [rows_of[v, pl.ds(m, lines, stride=apart), :] for v in range(size // LANES)]
        x = jnp.concatenate(x, axis=1).astype(BF16)
        result = dot(x, legendre_ref[m], ((1,), (0,)))
        for r in range(parts):
            at = r * share + step * block + m
            for h in range(sums.shape[0]):
                piece = result[r * own : (r + 1) * own, h * LANES : (h + 1) * LANES]
                sums[h, pl.ds(at, own, stride=stretch), :] = piece

    @pl.when(step == pl.num_programs(0) - 1)
    def _():
        some = LANES // rows
        for l in range(own):
            for h in range(sums.shape[0]):
                turned = sums[h, pl.ds(l * stretch, pitch), :].T.astype(BF16)
                out_ref[h * some : (h + 1) * some, l] = turned.reshape(some, rows, pitch)


def legendre_sums(spectral, legendre, bands):
    parts, own, share, size = spectral.shape
    rows = legendre.shape[2] // bands
    pitch = -(-parts * share // LANES) * LANES
    block = 16 if share % 16 == 0 else 8
    shape = (bands, own, rows, pitch)
    return pl.pallas_call(
        legendre_kernel,
        grid=(share // block,),
        in_specs=[
            pl.BlockSpec((parts, own, block, size), lambda i: (0, 0, i, 0)),
            pl.BlockSpec((block,) + legendre.shape[1:], lambda i: (i, 0, 0)),
        ],
        out_specs=pl.BlockSpec(shape, lambda i: (0, 0, 0, 0)),
        out_shape=jax.ShapeDtypeStruct(shape, BF16),
        scratch_shapes=[
            pltpu.VMEM((size // LANES, parts * own * (block + 1), LANES), F32),
            pltpu.VMEM((legendre.shape[2] // LANES, own * (pitch + 1), LANES), F32),
        ],
        compiler_params=pltpu.CompilerParams(vmem_limit_bytes=56 * MIB),
        cost_estimate=cost(2 * parts * own * legendre.size, 2 * (spectral.size + legendre.size)),
        name="legendre",
    )(spectral, legendre)


def exchange(value, axis, pairs):
    return lax.ppermute(value, axis, [p for a, b in pairs for p in ((a, b), (b, a))])


def neighbours(axis, first):
    size = lax.axis_size(axis)
    return [(i, i + 1) for i in range(first, size - 1, 2)]


def partners(axis, k):
    return [(i, i ^ k) for i in range(lax.axis_size(axis)) if i < i ^ k]


def body(spectral, legendre, wave_ids, points, tracers, react_base, react_temp, active_ids):
    bands, tiles = lax.axis_size("lat"), lax.axis_size("lon")
    tile = tracers.shape[3]
    waves = wave_ids.shape[0]
    band, me = lax.axis_index("lat"), lax.axis_index("lon")

    sent = legendre_sums(spectral, legendre, bands)

    rows = points.shape[0]
    info = jnp.concatenate([jnp.stack([band, me]), active_ids, points]).astype(jnp.int32)
    sent, info = lax.optimization_barrier((sent, info))
    recv = lax.all_to_all(sent, "lat", split_axis=0, concat_axis=0, tiled=True)
    *ends, react = edges(tracers, react_base, react_temp, info)
    halos = (
        exchange(ends[0], "lat", neighbours("lat", 0)),
        exchange(ends[1], "lat", neighbours("lat", 1)),
        exchange(ends[2], "lon", neighbours("lon", 0)),
        exchange(ends[3], "lon", neighbours("lon", 1)),
    )
    react, wave_ids = lax.optimization_barrier((react, wave_ids))
    table, twiddle = tables(info, wave_ids, rows, tiles * tile // LANES)
    recv, table, twiddle, halos, react = lax.optimization_barrier(
        (recv, table, twiddle, halos, react)
    )
    grids = synthesis(recv, table, twiddle, info, tiles, tile)

    middle = list(range(tiles // 2, tiles))
    soon, late = middle[: tiles // 4], middle[tiles // 4 :]
    inner = list(range(1, tiles // 2))

    def send(value, k):
        return exchange(value, "lon", partners("lon", k))

    moved = {0: grids[0]} | {k: send(grids[k], k) for k in soon + inner}
    new, active = None, {}
    order = [0] + inner + soon + late
    for k in order:
        new, active[k] = chemistry(
            tracers, halos, moved[k], react, info, k, active_ids.shape[0], waves, new
        )
        if k:
            active[k] = send(active[k], k)
        else:
            held, active[0] = lax.optimization_barrier(([grids[i] for i in late], active[0]))
            moved |= {i: send(value, i) for i, value in zip(late, held)}
    spreaded = None
    for k in order:
        spreaded = spread(active[k], info, k, tiles, spreaded)
    return new, spreaded


def solution(mesh):
    return jax.shard_map(
        body,
        mesh=mesh,
        in_specs=(
            P(None, "lon", "lat", None),
            P("lat", None, None),
            P(),
            P("lat"),
            P(None, None, "lat", "lon"),
            P(),
            P(),
            P(),
        ),
        out_specs=(P(None, None, "lat", "lon"), P(None, "lon", "lat", None)),
        check_vma=False,
    )
```

```python
import functools

import jax
import jax.numpy as jnp
import numpy as np
from jax import lax
from jax.experimental import pallas as pl
from jax.experimental.pallas import tpu as pltpu
from jax.sharding import PartitionSpec as P

F32 = jnp.float32
BF16 = jnp.bfloat16
LANES = 128
LOW = 16
STEP = 4
MIB = 1024 * 1024

COS = (
    0.9999999890590228,
    -19.739204499454026,
    64.93911745990036,
    -85.45013953095037,
    60.16763095136588,
    -25.96759924965491,
    6.528658162567069,
)
SIN = (
    6.283185302511503,
    -41.34170040531769,
    81.60513138580204,
    -76.7030153539128,
    42.02592698618416,
    -14.899846668691637,
    3.238137510515757,
)


def dot(a, b, dims):
    return lax.dot_general(a, b, (dims, ((), ())), preferred_element_type=F32)


BAND, ME, IDS = 0, 1, 2


def cost(flops, moved):
    return pl.CostEstimate(flops=int(flops), bytes_accessed=int(moved), transcendentals=0)


def unit_circle(step, rows, waves, count):
    index = lax.broadcasted_iota(jnp.int32, (rows, waves.shape[1]), 0) * step
    product = index.astype(F32) * waves
    inverse = 1.0 / count
    turns = (product - jnp.floor(product * inverse) * count) * inverse
    y = turns - jnp.floor(turns + 0.5)
    z = y * y
    cosine = jnp.full_like(z, COS[-1])
    sine = jnp.full_like(z, SIN[-1])
    for c, s in zip(COS[-2::-1], SIN[-2::-1]):
        cosine = cosine * z + c
        sine = sine * z + s
    return cosine, sine * y


def table_kernel(first, info, waves_ref, table_ref, twiddle_ref):
    size, turns = waves_ref.shape[1], twiddle_ref.shape[2]
    waves = waves_ref[...].astype(F32)
    for k in range(table_ref.shape[0]):
        row = pl.program_id(0) * table_ref.shape[0] + k
        count = jnp.full(waves.shape, info[first + row], jnp.int32).astype(F32)
        cos_low, sin_low = unit_circle(1, LOW, waves, count)
        cos_high, sin_high = unit_circle(LOW, LANES // LOW, waves, count)
        cosine, sine = [], []
        for a in range(LANES // LOW):
            ch, sh = cos_high[a : a + 1], sin_high[a : a + 1]
            cosine.append(ch * cos_low - sh * sin_low)
            sine.append(-sh * cos_low - ch * sin_low)
        table_ref[k, :size, :] = jnp.concatenate(cosine, axis=0).T.astype(BF16)
        table_ref[k, size:, :] = jnp.concatenate(sine, axis=0).T.astype(BF16)
        cos_turn, sin_turn = unit_circle(LANES, turns, waves, count)
        twiddle_ref[k, 0] = cos_turn
        twiddle_ref[k, 1] = sin_turn


def tables(info, wave_ids, rows, turns):
    waves = wave_ids.shape[0]
    each = STEP if rows % STEP == 0 else 1
    return pl.pallas_call(
        functools.partial(table_kernel, info.shape[0] - rows),
        grid_spec=pltpu.PrefetchScalarGridSpec(
            num_scalar_prefetch=1,
            grid=(rows // each,),
            in_specs=[pl.BlockSpec((1, waves), lambda j, p: (0, 0))],
            out_specs=[
                pl.BlockSpec((each, 2 * waves, LANES), lambda j, p: (j, 0, 0)),
                pl.BlockSpec((each, 2, turns, waves), lambda j, p: (j, 0, 0, 0)),
            ],
        ),
        out_shape=[
            jax.ShapeDtypeStruct((rows, 2 * waves, LANES), BF16),
            jax.ShapeDtypeStruct((rows, 2, turns, waves), F32),
        ],
        compiler_params=pltpu.CompilerParams(vmem_limit_bytes=55 * MIB),
        cost_estimate=cost(rows * waves * LANES * 8, rows * waves * LANES * 4),
        name="tables",
    )(info, wave_ids[None, :])


def place(pieces, width):
    out = [None] * (width // LANES)
    lane = lax.broadcasted_iota(jnp.int32, (pieces[0][0].shape[0], LANES), 1)
    for value, start, count, here in pieces:
        shift = (here - start) % LANES
        for a in range(start // LANES, (start + count - 1) // LANES + 1):
            part = value[:, a * LANES : (a + 1) * LANES]
            if shift:
                part = pltpu.roll(part, shift, 1)
            first = max(start, a * LANES) - start + here
            last = min(start + count, (a + 1) * LANES) - start + here
            for v in range(first // LANES, (last - 1) // LANES + 1):
                low, high = max(first - v * LANES, 0), min(last - v * LANES, LANES)
                if out[v] is None:
                    out[v] = part
                else:
                    out[v] = jnp.where((lane >= low) & (lane < high), part, out[v])
    return out


def synth_kernel(info, recv_ref, table_ref, twiddle_ref, *refs):
    *out_refs, coef, grid = refs
    sources, levels, rows, _ = recv_ref.shape
    fields, waves = coef.shape[0] // 2, coef.shape[1] * LANES
    share = waves // sources
    each, _, turns = twiddle_ref.shape[:3]
    pitch = rows + 1
    step = pl.program_id(0)

    @pl.when(step == 0)
    def _():
        def level(l, carry):
            values = [recv_ref[s, l].astype(F32) for s in range(sources)]
            for r in range(2 * fields):
                windows = [
                    (values[s], r * share, share, s * share) for s in range(sources)
                ]
                for v, part in enumerate(place(windows, waves)):
                    coef[r, v, pl.ds(l * pitch, rows), :] = part
            return carry

        lax.fori_loop(0, levels, level, 0)

    for k in range(each):
        j = step * each + k

        def own_row(r):
            parts = [coef[r, v, pl.ds(j, levels, stride=pitch), :] for v in range(waves // LANES)]
            return jnp.concatenate(parts, axis=1)

        values = [own_row(r) for r in range(2 * fields)]
        real, imag = [], []
        for t in range(turns):
            c, s = twiddle_ref[k, 0, t : t + 1], twiddle_ref[k, 1, t : t + 1]
            for f in range(fields):
                re, im = values[2 * f], values[2 * f + 1]
                real.append(re * c - im * s)
                imag.append(re * s + im * c)
        both = [jnp.concatenate(part, axis=0).astype(BF16) for part in (real, imag)]
        result = dot(jnp.concatenate(both, axis=1), table_ref[k], ((1,), (0,)))
        grid[pl.ds(j, turns * fields * levels, stride=pitch), :] = result

    @pl.when(step == pl.num_programs(0) - 1)
    def _():
        tiles = turns // len(out_refs)
        for k, out_ref in enumerate(out_refs):
            for t in range(tiles):
                for f in range(fields):
                    start = (((info[ME] ^ k) * tiles + t) * fields + f) * levels
                    for l in range(levels):
                        block = grid[pl.ds((start + l) * pitch, rows), :].astype(BF16)
                        out_ref[f, l, :, t * LANES : (t + 1) * LANES] = block


def synthesis(recv, table, twiddle, info, dests, tile):
    sources, levels, rows, lanes = recv.shape
    turns, waves = twiddle.shape[2:]
    fields = 3
    each = STEP if rows % STEP == 0 else 1
    shape = (fields, levels, rows, tile)
    return pl.pallas_call(
        synth_kernel,
        grid_spec=pltpu.PrefetchScalarGridSpec(
            num_scalar_prefetch=1,
            grid=(rows // each,),
            in_specs=[
                pl.BlockSpec(recv.shape, lambda j, info: (0, 0, 0, 0)),
                pl.BlockSpec((each, 2 * waves, LANES), lambda j, info: (j, 0, 0)),
                pl.BlockSpec((each, 2, turns, waves), lambda j, info: (j, 0, 0, 0)),
            ],
            out_specs=[pl.BlockSpec(shape, lambda j, info: (0, 0, 0, 0))] * dests,
            scratch_shapes=[
                pltpu.VMEM((2 * fields, waves // LANES, levels * (rows + 1), LANES), F32),
                pltpu.VMEM((turns * fields * levels * (rows + 1), LANES), F32),
            ],
        ),
        out_shape=[jax.ShapeDtypeStruct(shape, BF16)] * dests,
        compiler_params=pltpu.CompilerParams(vmem_limit_bytes=50 * MIB),
        cost_estimate=cost(4 * rows * waves * fields * levels * turns * LANES, 4 * rows * waves * LANES),
        name="synthesis",
    )(info, recv, table, twiddle)


def edge_kernel(
    info, state_ref, base_ref, temp_ref, row_a_ref, row_b_ref, col_a_ref, col_b_ref, react_ref
):
    tracers, levels, rows, tile = state_ref.shape
    cells = tracers * rows

    @pl.when(pl.program_id(0) == 0)
    def _():
        rates = jnp.concatenate([base_ref[...], temp_ref[...]], axis=0)
        high = rates.astype(BF16)
        low = (rates - high.astype(F32)).astype(BF16)

        def iota(shape, axis):
            return lax.broadcasted_iota(jnp.int32, shape, axis)

        shape = (2 * cells, 2 * tracers)
        down = jnp.where(iota(shape, 0) // rows == iota(shape, 1), 1.0, 0.0).astype(BF16)
        shape = (tracers, cells)
        over = jnp.where(iota(shape, 0) == iota(shape, 1) // rows, 1.0, 0.0).astype(BF16)
        shape = (2 * cells, cells)
        same = iota(shape, 0) % rows == iota(shape, 1) % rows
        for k, part in enumerate((high, low)):
            wide = dot(dot(down, part, ((1,), (0,))).astype(BF16), over, ((1,), (0,)))
            react_ref[:, k * cells : (k + 1) * cells] = jnp.where(same, wide, 0.0).astype(BF16)

    def iota(shape, axis):
        return lax.broadcasted_iota(jnp.int32, shape, axis)

    odd = info[BAND] % 2, info[ME] % 2
    far, near = (1 - odd[0]) * (rows - 1), odd[0] * (rows - 1)
    shape = (2 * tracers, cells)
    end = jnp.where(iota(shape, 0) < tracers, far, near)
    pick = iota(shape, 1) == (iota(shape, 0) % tracers) * rows + end
    pick = jnp.where(pick, 1.0, 0.0).astype(BF16)
    shape = (tile, 2 * LANES)
    far, near = (1 - odd[1]) * (tile - 1), odd[1] * (tile - 1)
    is_end = iota(shape, 0) == jnp.where(iota(shape, 1) < LANES, far, near)
    level = iota(shape, 1) % LANES - pl.program_id(0) * levels
    columns = jnp.zeros((cells, 2 * LANES), F32)
    for l in range(levels):
        x = state_ref[:, l].reshape(cells, tile)
        picked = dot(pick, x, ((1,), (0,)))
        row_a_ref[l] = picked[:tracers].astype(BF16)
        row_b_ref[l] = picked[tracers:].astype(BF16)
        mark = jnp.where(is_end & (level == l), 1.0, 0.0).astype(BF16)
        columns = columns + dot(x, mark, ((1,), (0,)))

    @pl.when(pl.program_id(0) == 0)
    def _():
        col_a_ref[...] = columns[:, :LANES].astype(BF16)
        col_b_ref[...] = columns[:, LANES:].astype(BF16)

    @pl.when(pl.program_id(0) > 0)
    def _():
        col_a_ref[...] = (col_a_ref[...].astype(F32) + columns[:, :LANES]).astype(BF16)
        col_b_ref[...] = (col_b_ref[...].astype(F32) + columns[:, LANES:]).astype(BF16)


def edges(state, react_base, react_temp, info):
    tracers, levels, rows, tile = state.shape
    block = 16
    cells = tracers * rows
    rowed = jax.ShapeDtypeStruct((levels, tracers, tile), BF16)
    columned = jax.ShapeDtypeStruct((cells, LANES), BF16)
    row_spec = pl.BlockSpec((block, tracers, tile), lambda i, info: (i, 0, 0))
    col_spec = pl.BlockSpec((cells, LANES), lambda i, info: (0, 0))
    wide = (2 * cells, 2 * cells)
    return pl.pallas_call(
        edge_kernel,
        grid_spec=pltpu.PrefetchScalarGridSpec(
            num_scalar_prefetch=1,
            grid=(levels // block,),
            in_specs=[
                pl.BlockSpec((tracers, block, rows, tile), lambda i, info: (0, i, 0, 0)),
                pl.BlockSpec(react_base.shape, lambda i, info: (0, 0)),
                pl.BlockSpec(react_temp.shape, lambda i, info: (0, 0)),
            ],
            out_specs=[
                row_spec, row_spec, col_spec, col_spec, pl.BlockSpec(wide, lambda i, info: (0, 0)),
            ],
        ),
        out_shape=[rowed, rowed, columned, columned, jax.ShapeDtypeStruct(wide, BF16)],
        compiler_params=pltpu.CompilerParams(vmem_limit_bytes=52 * MIB),
        cost_estimate=cost(4 * state.size * 32, 2 * state.size),
        name="edges",
    )(info, state, react_base, react_temp)


def chem_kernel(scale, k, info, *refs):
    state_ref, row_a_ref, row_b_ref, col_a_ref, col_b_ref, grid_ref, react_ref = refs[:7]
    along_ref, across_ref = refs[7:9]
    new_ref, active_ref, south, north = refs[-4:]
    tracers, levels, rows, tile = state_ref.shape
    cells = tracers * rows
    half, side = rows // 2, tile // 2
    odd_band, odd_tile = info[BAND] % 2 == 1, info[ME] % 2 == 1
    first = ((info[ME] ^ k) * pl.num_programs(0) + pl.program_id(0)) * levels

    def column(value):
        return pltpu.roll(value, lax.rem(LANES - first, LANES), 1)

    a, b = col_a_ref[...].astype(F32), col_b_ref[...].astype(F32)
    west, east = column(jnp.where(odd_tile, a, b)), column(jnp.where(odd_tile, b, a))
    row = lax.broadcasted_iota(jnp.int32, (rows, tile), 0)
    lane = lax.broadcasted_iota(jnp.int32, (rows, tile), 1)
    ids, points = IDS, IDS + active_ref.shape[0]
    count = jnp.full((rows, tile), info[points], jnp.int32)
    for j in range(1, rows):
        count = jnp.where(row == j, info[points + j], count)
    mask = jnp.where(info[ME] * tile + lane < count, 1.0, 0.0)
    nn = ((1,), (0,))

    def three(v):
        return v.reshape(tracers, rows, tile)

    for l in range(levels):
        x = state_ref[:, l].reshape(cells, tile)
        lon = dot(x, along_ref[...], nn)
        lat = dot(across_ref[...], x, nn)
        wind_u = grid_ref[0, l].astype(F32) * (scale * 0.1)
        wind_v = grid_ref[1, l].astype(F32) * (scale * 0.1)
        temper = grid_ref[2, l].astype(F32) * scale
        moved = (
            three(x.astype(F32))
            - wind_u * three(lon[:, :tile])
            - wind_v * three(lat[:cells])
            + 0.05 * three(lon[:, tile:] + lat[cells:])
        )
        a, b = row_a_ref[l].astype(F32), row_b_ref[l].astype(F32)
        south[l] = jnp.where(odd_band, a, b)
        north[l] = jnp.where(odd_band, b, a)
        in_row = jnp.where(row == 0, 0.05 + wind_v, jnp.where(row == rows - 1, 0.05 - wind_v, 0.0))
        in_col = jnp.where(lane == 0, 0.05 + wind_u, jnp.where(lane == tile - 1, 0.05 - wind_u, 0.0))
        outer = []
        for t in range(tracers):
            up = [jnp.broadcast_to(ref[l, t : t + 1], (half, tile)) for ref in (south, north)]
            cell = slice(t * rows, (t + 1) * rows)
            across = [
                jnp.broadcast_to(col[cell, l : l + 1], (rows, side)) for col in (west, east)
            ]
            outer.append(
                in_row * jnp.concatenate(up, axis=0) + in_col * jnp.concatenate(across, axis=1)
            )
        moved = moved + jnp.stack(outer, axis=0)
        high = moved.reshape(cells, tile).astype(BF16)
        terms = dot(react_ref[...], jnp.concatenate([high, high], axis=0), nn)
        reacted = (moved + three(terms[:cells]) + temper * three(terms[cells:])) * mask
        new_ref[:, l] = reacted.astype(BF16)
    for a in range(active_ref.shape[0]):
        active_ref[a] = new_ref[info[ids + a]]


def chemistry(state, halos, grid, react, info, k, actives, waves, before):
    tracers, levels, rows, tile = state.shape
    fields, own = grid.shape[:2]
    some = 4 if own % 4 == 0 else own
    steps = own // some
    cells = tracers * rows
    eye, one = np.eye(tracers), np.eye(tile)
    along = np.concatenate(
        [np.eye(tile, k=-1) - np.eye(tile, k=1), np.eye(tile, k=-1) + np.eye(tile, k=1) - 4 * one], 1
    )
    down, up = np.eye(rows, k=-1), np.eye(rows, k=1)
    across = np.concatenate([np.kron(eye, up - down), np.kron(eye, up + down)], 0)
    scale = 1.0 / float(np.sqrt(np.float32(waves)))

    def whole(shape):
        return pl.BlockSpec(shape, lambda i, info: (0,) * len(shape))

    row_spec = pl.BlockSpec((some, tracers, tile), lambda i, info: ((info[ME] ^ k) * steps + i, 0, 0))
    state_spec = pl.BlockSpec(
        (tracers, some, rows, tile), lambda i, info: (0, (info[ME] ^ k) * steps + i, 0, 0)
    )
    operands = [
        state, *halos, grid, react, jnp.asarray(along, BF16), jnp.asarray(across, BF16),
    ]
    in_specs = [
        state_spec,
        row_spec,
        row_spec,
        whole(halos[2].shape),
        whole(halos[3].shape),
        pl.BlockSpec((fields, some, rows, tile), lambda i, info: (0, i, 0, 0)),
        whole(react.shape),
        whole(along.shape),
        whole(across.shape),
    ]
    aliases = {}
    if before is not None:
        aliases = {1 + len(operands): 0}
        operands.append(before)
        in_specs.append(pl.BlockSpec(memory_space=pl.ANY))
    return pl.pallas_call(
        functools.partial(chem_kernel, scale, k),
        grid_spec=pltpu.PrefetchScalarGridSpec(
            num_scalar_prefetch=1,
            grid=(steps,),
            in_specs=in_specs,
            out_specs=[
                state_spec,
                pl.BlockSpec((actives, some, rows, tile), lambda i, info: (0, i, 0, 0)),
            ],
            scratch_shapes=[pltpu.VMEM((some, tracers, tile), F32)] * 2,
        ),
        out_shape=[
            jax.ShapeDtypeStruct(state.shape, BF16),
            jax.ShapeDtypeStruct((actives, own, rows, tile), BF16),
        ],
        input_output_aliases=aliases,
        compiler_params=pltpu.CompilerParams(vmem_limit_bytes=16 * MIB),
        cost_estimate=cost(own * cells * tile, own * tile),
        name="chemistry",
    )(info, *operands)


def spread_kernel(info, recv_ref, *refs):
    refs[-1][...] = recv_ref[...].astype(F32)


def spread(recv, info, k, sources, before):
    actives, own, rows, tile = recv.shape
    each = 2 if actives % 2 == 0 else 1
    operands = [recv]
    in_specs = [pl.BlockSpec((each, own, rows, tile), lambda a, info: (a, 0, 0, 0))]
    aliases = {}
    if before is not None:
        operands.append(before)
        in_specs.append(pl.BlockSpec(memory_space=pl.ANY))
        aliases = {2: 0}
    return pl.pallas_call(
        spread_kernel,
        grid_spec=pltpu.PrefetchScalarGridSpec(
            num_scalar_prefetch=1,
            grid=(actives // each,),
            in_specs=in_specs,
            out_specs=pl.BlockSpec((each, own, rows, tile), lambda a, info: (a, 0, 0, info[ME] ^ k)),
        ),
        out_shape=jax.ShapeDtypeStruct((actives, own, rows, sources * tile), F32),
        input_output_aliases=aliases,
        compiler_params=pltpu.CompilerParams(vmem_limit_bytes=8 * MIB),
        cost_estimate=cost(recv.size, recv.shape[0]),
        name="spread",
    )(info, *operands)


def legendre_kernel(spectral_ref, legendre_ref, out_ref, rows_of, sums):
    parts, own, block, size = spectral_ref.shape
    bands, _, rows, pitch = out_ref.shape
    share = block * pl.num_programs(0)
    step = pl.program_id(0)
    lines = parts * own
    apart, stretch = block + 1, pitch + 1

    @pl.when(step == 0)
    def _():
        for h in range(sums.shape[0]):
            for l in range(own):
                tail = pl.ds(l * stretch + parts * share, pitch - parts * share)
                sums[h, tail, :] = jnp.zeros((pitch - parts * share, LANES), F32)

    for v in range(size // LANES):
        part = spectral_ref[:, :, :, v * LANES : (v + 1) * LANES].astype(F32)
        part = part.reshape(lines, block, LANES)
        for i in range(lines):
            rows_of[v, pl.ds(i * apart, block), :] = part[i]
    for m in range(block):
        x = [rows_of[v, pl.ds(m, lines, stride=apart), :] for v in range(size // LANES)]
        x = jnp.concatenate(x, axis=1).astype(BF16)
        result = dot(x, legendre_ref[m], ((1,), (0,)))
        for r in range(parts):
            at = r * share + step * block + m
            for h in range(sums.shape[0]):
                piece = result[r * own : (r + 1) * own, h * LANES : (h + 1) * LANES]
                sums[h, pl.ds(at, own, stride=stretch), :] = piece

    @pl.when(step == pl.num_programs(0) - 1)
    def _():
        some = LANES // rows
        for l in range(own):
            for h in range(sums.shape[0]):
                turned = sums[h, pl.ds(l * stretch, pitch), :].T.astype(BF16)
                out_ref[h * some : (h + 1) * some, l] = turned.reshape(some, rows, pitch)


def legendre_sums(spectral, legendre, bands):
    parts, own, share, size = spectral.shape
    rows = legendre.shape[2] // bands
    pitch = -(-parts * share // LANES) * LANES
    block = 16 if share % 16 == 0 else 8
    shape = (bands, own, rows, pitch)
    return pl.pallas_call(
        legendre_kernel,
        grid=(share // block,),
        in_specs=[
            pl.BlockSpec((parts, own, block, size), lambda i: (0, 0, i, 0)),
            pl.BlockSpec((block,) + legendre.shape[1:], lambda i: (i, 0, 0)),
        ],
        out_specs=pl.BlockSpec(shape, lambda i: (0, 0, 0, 0)),
        out_shape=jax.ShapeDtypeStruct(shape, BF16),
        scratch_shapes=[
            pltpu.VMEM((size // LANES, parts * own * (block + 1), LANES), F32),
            pltpu.VMEM((legendre.shape[2] // LANES, own * (pitch + 1), LANES), F32),
        ],
        compiler_params=pltpu.CompilerParams(vmem_limit_bytes=56 * MIB),
        cost_estimate=cost(2 * parts * own * legendre.size, 2 * (spectral.size + legendre.size)),
        name="legendre",
    )(spectral, legendre)


def exchange(value, axis, pairs):
    return lax.ppermute(value, axis, [p for a, b in pairs for p in ((a, b), (b, a))])


def neighbours(axis, first):
    size = lax.axis_size(axis)
    return [(i, i + 1) for i in range(first, size - 1, 2)]


def partners(axis, k):
    return [(i, i ^ k) for i in range(lax.axis_size(axis)) if i < i ^ k]


def body(spectral, legendre, wave_ids, points, tracers, react_base, react_temp, active_ids):
    bands, tiles = lax.axis_size("lat"), lax.axis_size("lon")
    tile = tracers.shape[3]
    waves = wave_ids.shape[0]
    band, me = lax.axis_index("lat"), lax.axis_index("lon")

    sent = legendre_sums(spectral, legendre, bands)

    rows = points.shape[0]
    info = jnp.concatenate([jnp.stack([band, me]), active_ids, points]).astype(jnp.int32)
    sent, info = lax.optimization_barrier((sent, info))
    recv = lax.all_to_all(sent, "lat", split_axis=0, concat_axis=0, tiled=True)
    *ends, react = edges(tracers, react_base, react_temp, info)
    halos = (
        exchange(ends[0], "lat", neighbours("lat", 0)),
        exchange(ends[1], "lat", neighbours("lat", 1)),
        exchange(ends[2], "lon", neighbours("lon", 0)),
        exchange(ends[3], "lon", neighbours("lon", 1)),
    )
    react, wave_ids = lax.optimization_barrier((react, wave_ids))
    table, twiddle = tables(info, wave_ids, rows, tiles * tile // LANES)
    recv, table, twiddle, halos, react = lax.optimization_barrier(
        (recv, table, twiddle, halos, react)
    )
    grids = synthesis(recv, table, twiddle, info, tiles, tile)

    middle = list(range(tiles // 2, tiles))
    soon, late = middle[: tiles // 4], middle[tiles // 4 :]
    inner = list(range(1, tiles // 2))

    def send(value, k):
        return exchange(value, "lon", partners("lon", k))

    moved = {0: grids[0]} | {k: send(grids[k], k) for k in inner + soon}
    new, active = None, {}
    order = [0] + inner + soon + late
    for k in order:
        new, active[k] = chemistry(
            tracers, halos, moved[k], react, info, k, active_ids.shape[0], waves, new
        )
        if k:
            active[k] = send(active[k], k)
        else:
            held, active[0] = lax.optimization_barrier(([grids[i] for i in late], active[0]))
            moved |= {i: send(value, i) for i, value in zip(late, held)}
    spreaded = None
    for k in order:
        spreaded = spread(active[k], info, k, tiles, spreaded)
    return new, spreaded


def solution(mesh):
    return jax.shard_map(
        body,
        mesh=mesh,
        in_specs=(
            P(None, "lon", "lat", None),
            P("lat", None, None),
            P(),
            P("lat"),
            P(None, None, "lat", "lon"),
            P(),
            P(),
            P(),
        ),
        out_specs=(P(None, None, "lat", "lon"), P(None, "lon", "lat", None)),
        check_vma=False,
    )
```

```python
import functools

import jax
import jax.numpy as jnp
import numpy as np
from jax import lax
from jax.experimental import pallas as pl
from jax.experimental.pallas import tpu as pltpu
from jax.sharding import PartitionSpec as P

F32 = jnp.float32
BF16 = jnp.bfloat16
LANES = 128
SUBLANES = 8
LOW = 16
STEP = 4
MIB = 1024 * 1024

COS = (
    0.9999999890590228,
    -19.739204499454026,
    64.93911745990036,
    -85.45013953095037,
    60.16763095136588,
    -25.96759924965491,
    6.528658162567069,
)
SIN = (
    6.283185302511503,
    -41.34170040531769,
    81.60513138580204,
    -76.7030153539128,
    42.02592698618416,
    -14.899846668691637,
    3.238137510515757,
)


def dot(a, b, dims):
    return lax.dot_general(a, b, (dims, ((), ())), preferred_element_type=F32)


BAND, ME, IDS = 0, 1, 2


def cost(flops, moved):
    return pl.CostEstimate(flops=int(flops), bytes_accessed=int(moved), transcendentals=0)


def unit_circle(step, rows, waves, count):
    index = lax.broadcasted_iota(jnp.int32, (rows, waves.shape[1]), 0) * step
    product = index.astype(F32) * waves
    inverse = 1.0 / count
    turns = (product - jnp.floor(product * inverse) * count) * inverse
    y = turns - jnp.floor(turns + 0.5)
    z = y * y
    cosine = jnp.full_like(z, COS[-1])
    sine = jnp.full_like(z, SIN[-1])
    for c, s in zip(COS[-2::-1], SIN[-2::-1]):
        cosine = cosine * z + c
        sine = sine * z + s
    return cosine, sine * y


def table_kernel(first, info, waves_ref, table_ref, twiddle_ref):
    size, turns = waves_ref.shape[1], twiddle_ref.shape[2]
    waves = waves_ref[...].astype(F32)
    for k in range(table_ref.shape[0]):
        row = pl.program_id(0) * table_ref.shape[0] + k
        count = jnp.full(waves.shape, info[first + row], jnp.int32).astype(F32)
        cos_low, sin_low = unit_circle(1, LOW, waves, count)
        cos_high, sin_high = unit_circle(LOW, LANES // LOW, waves, count)
        cosine, sine = [], []
        for a in range(LANES // LOW):
            ch, sh = cos_high[a : a + 1], sin_high[a : a + 1]
            cosine.append(ch * cos_low - sh * sin_low)
            sine.append(-sh * cos_low - ch * sin_low)
        table_ref[k, :size, :] = jnp.concatenate(cosine, axis=0).T.astype(BF16)
        table_ref[k, size:, :] = jnp.concatenate(sine, axis=0).T.astype(BF16)
        cos_turn, sin_turn = unit_circle(LANES, turns, waves, count)
        twiddle_ref[k, 0] = cos_turn
        twiddle_ref[k, 1] = sin_turn


def tables(info, wave_ids, rows, turns):
    waves = wave_ids.shape[0]
    each = STEP if rows % STEP == 0 else 1
    return pl.pallas_call(
        functools.partial(table_kernel, info.shape[0] - rows),
        grid_spec=pltpu.PrefetchScalarGridSpec(
            num_scalar_prefetch=1,
            grid=(rows // each,),
            in_specs=[pl.BlockSpec((1, waves), lambda j, p: (0, 0))],
            out_specs=[
                pl.BlockSpec((each, 2 * waves, LANES), lambda j, p: (j, 0, 0)),
                pl.BlockSpec((each, 2, turns, waves), lambda j, p: (j, 0, 0, 0)),
            ],
        ),
        out_shape=[
            pltpu.VMEM((rows, 2 * waves, LANES), BF16),
            pltpu.VMEM((rows, 2, turns, waves), F32),
        ],
        compiler_params=pltpu.CompilerParams(vmem_limit_bytes=20 * MIB),
        cost_estimate=cost(rows * waves * LANES * 8, rows * waves * LANES * 4),
        name="tables",
    )(info, wave_ids[None, :])


def place(pieces, width):
    out = [None] * (width // LANES)
    lane = lax.broadcasted_iota(jnp.int32, (pieces[0][0].shape[0], LANES), 1)
    for value, start, count, here in pieces:
        shift = (here - start) % LANES
        for a in range(start // LANES, (start + count - 1) // LANES + 1):
            part = value[:, a * LANES : (a + 1) * LANES]
            if shift:
                part = pltpu.roll(part, shift, 1)
            first = max(start, a * LANES) - start + here
            last = min(start + count, (a + 1) * LANES) - start + here
            for v in range(first // LANES, (last - 1) // LANES + 1):
                low, high = max(first - v * LANES, 0), min(last - v * LANES, LANES)
                if out[v] is None:
                    out[v] = part
                else:
                    out[v] = jnp.where((lane >= low) & (lane < high), part, out[v])
    return out


def synth_kernel(info, recv_ref, table_ref, twiddle_ref, *refs):
    *out_refs, coef, grid = refs
    sources, levels, rows, _ = recv_ref.shape
    fields, waves = coef.shape[0] // 2, coef.shape[1] * LANES
    share = waves // sources
    each, _, turns = twiddle_ref.shape[:3]
    pitch = rows + 1
    step = pl.program_id(0)

    @pl.when(step == 0)
    def _():
        def level(l, carry):
            values = [recv_ref[s, l].astype(F32) for s in range(sources)]
            for r in range(2 * fields):
                windows = [
                    (values[s], r * share, share, s * share) for s in range(sources)
                ]
                for v, part in enumerate(place(windows, waves)):
                    coef[r, v, pl.ds(l * pitch, rows), :] = part
            return carry

        lax.fori_loop(0, levels, level, 0)

    for k in range(each):
        j = step * each + k

        def own_row(r):
            parts = [coef[r, v, pl.ds(j, levels, stride=pitch), :] for v in range(waves // LANES)]
            return jnp.concatenate(parts, axis=1)

        values = [own_row(r) for r in range(2 * fields)]
        real, imag = [], []
        for t in range(turns):
            c, s = twiddle_ref[k, 0, t : t + 1], twiddle_ref[k, 1, t : t + 1]
            for f in range(fields):
                re, im = values[2 * f], values[2 * f + 1]
                real.append(re * c - im * s)
                imag.append(re * s + im * c)
        both = [jnp.concatenate(part, axis=0).astype(BF16) for part in (real, imag)]
        result = dot(jnp.concatenate(both, axis=1), table_ref[k], ((1,), (0,)))
        grid[pl.ds(j, turns * fields * levels, stride=pitch), :] = result

    @pl.when(step == pl.num_programs(0) - 1)
    def _():
        tiles = turns // len(out_refs)
        for k, out_ref in enumerate(out_refs):
            for t in range(tiles):
                for f in range(fields):
                    start = (((info[ME] ^ k) * tiles + t) * fields + f) * levels
                    for l in range(levels):
                        block = grid[pl.ds((start + l) * pitch, rows), :].astype(BF16)
                        out_ref[f, l, :, t * LANES : (t + 1) * LANES] = block


def synthesis(recv, table, twiddle, info, dests, tile):
    sources, levels, rows, lanes = recv.shape
    turns, waves = twiddle.shape[2:]
    fields = 3
    each = STEP if rows % STEP == 0 else 1
    shape = (fields, levels, rows, tile)
    return pl.pallas_call(
        synth_kernel,
        grid_spec=pltpu.PrefetchScalarGridSpec(
            num_scalar_prefetch=1,
            grid=(rows // each,),
            in_specs=[
                pl.BlockSpec(recv.shape, lambda j, info: (0, 0, 0, 0)),
                pl.BlockSpec((each, 2 * waves, LANES), lambda j, info: (j, 0, 0)),
                pl.BlockSpec((each, 2, turns, waves), lambda j, info: (j, 0, 0, 0)),
            ],
            out_specs=[pl.BlockSpec(shape, lambda j, info: (0, 0, 0, 0))] * dests,
            scratch_shapes=[
                pltpu.VMEM((2 * fields, waves // LANES, levels * (rows + 1), LANES), F32),
                pltpu.VMEM((turns * fields * levels * (rows + 1), LANES), F32),
            ],
        ),
        out_shape=[jax.ShapeDtypeStruct(shape, BF16)] * dests,
        compiler_params=pltpu.CompilerParams(vmem_limit_bytes=24 * MIB),
        cost_estimate=cost(4 * rows * waves * fields * levels * turns * LANES, 4 * rows * waves * LANES),
        name="synthesis",
    )(info, recv, table, twiddle)


def edge_kernel(
    info, state_ref, base_ref, temp_ref, row_a_ref, row_b_ref, col_a_ref, col_b_ref, react_ref
):
    tracers, levels, rows, tile = state_ref.shape
    cells = tracers * rows

    @pl.when(pl.program_id(0) == 0)
    def _():
        rates = jnp.concatenate([base_ref[...], temp_ref[...]], axis=0)
        high = rates.astype(BF16)
        low = (rates - high.astype(F32)).astype(BF16)

        def iota(shape, axis):
            return lax.broadcasted_iota(jnp.int32, shape, axis)

        shape = (2 * cells, 2 * tracers)
        down = jnp.where(iota(shape, 0) // rows == iota(shape, 1), 1.0, 0.0).astype(BF16)
        shape = (tracers, cells)
        over = jnp.where(iota(shape, 0) == iota(shape, 1) // rows, 1.0, 0.0).astype(BF16)
        shape = (2 * cells, cells)
        same = iota(shape, 0) % rows == iota(shape, 1) % rows
        for k, part in enumerate((high, low)):
            wide = dot(dot(down, part, ((1,), (0,))).astype(BF16), over, ((1,), (0,)))
            react_ref[:, k * cells : (k + 1) * cells] = jnp.where(same, wide, 0.0).astype(BF16)

    def iota(shape, axis):
        return lax.broadcasted_iota(jnp.int32, shape, axis)

    odd = info[BAND] % 2, info[ME] % 2
    far, near = (1 - odd[0]) * (rows - 1), odd[0] * (rows - 1)
    shape = (2 * tracers, cells)
    end = jnp.where(iota(shape, 0) < tracers, far, near)
    pick = iota(shape, 1) == (iota(shape, 0) % tracers) * rows + end
    pick = jnp.where(pick, 1.0, 0.0).astype(BF16)
    shape = (tile, 2 * LANES)
    far, near = (1 - odd[1]) * (tile - 1), odd[1] * (tile - 1)
    is_end = iota(shape, 0) == jnp.where(iota(shape, 1) < LANES, far, near)
    level = iota(shape, 1) % LANES - pl.program_id(0) * levels
    columns = jnp.zeros((cells, 2 * LANES), F32)
    for l in range(levels):
        x = state_ref[:, l].reshape(cells, tile)
        picked = dot(pick, x, ((1,), (0,)))
        row_a_ref[l] = picked[:tracers].astype(BF16)
        row_b_ref[l] = picked[tracers:].astype(BF16)
        mark = jnp.where(is_end & (level == l), 1.0, 0.0).astype(BF16)
        columns = columns + dot(x, mark, ((1,), (0,)))

    @pl.when(pl.program_id(0) == 0)
    def _():
        col_a_ref[...] = columns[:, :LANES].astype(BF16)
        col_b_ref[...] = columns[:, LANES:].astype(BF16)

    @pl.when(pl.program_id(0) > 0)
    def _():
        col_a_ref[...] = (col_a_ref[...].astype(F32) + columns[:, :LANES]).astype(BF16)
        col_b_ref[...] = (col_b_ref[...].astype(F32) + columns[:, LANES:]).astype(BF16)


def edges(state, react_base, react_temp, info):
    tracers, levels, rows, tile = state.shape
    block = 16
    cells = tracers * rows
    rowed = jax.ShapeDtypeStruct((levels, tracers, tile), BF16)
    columned = jax.ShapeDtypeStruct((cells, LANES), BF16)
    row_spec = pl.BlockSpec((block, tracers, tile), lambda i, info: (i, 0, 0))
    col_spec = pl.BlockSpec((cells, LANES), lambda i, info: (0, 0))
    wide = (2 * cells, 2 * cells)
    return pl.pallas_call(
        edge_kernel,
        grid_spec=pltpu.PrefetchScalarGridSpec(
            num_scalar_prefetch=1,
            grid=(levels // block,),
            in_specs=[
                pl.BlockSpec((tracers, block, rows, tile), lambda i, info: (0, i, 0, 0)),
                pl.BlockSpec(react_base.shape, lambda i, info: (0, 0)),
                pl.BlockSpec(react_temp.shape, lambda i, info: (0, 0)),
            ],
            out_specs=[
                row_spec, row_spec, col_spec, col_spec, pl.BlockSpec(wide, lambda i, info: (0, 0)),
            ],
        ),
        out_shape=[rowed, rowed, columned, columned, jax.ShapeDtypeStruct(wide, BF16)],
        compiler_params=pltpu.CompilerParams(vmem_limit_bytes=52 * MIB),
        cost_estimate=cost(4 * state.size * 32, 2 * state.size),
        name="edges",
    )(info, state, react_base, react_temp)


def shifted(value, outer, axis, step):
    size = value[0].shape[axis]
    turned = [pltpu.roll(v, -step % size, axis) for v in value]
    place = lax.broadcasted_iota(jnp.int32, value[0].shape, axis)
    at_end = place == (size - 1 if step == 1 else 0)
    following = turned[1:] + [outer] if step == 1 else [outer] + turned[:-1]
    return [jnp.where(at_end, f, t) for f, t in zip(following, turned)]


def chem_kernel(scale, k, info, *refs):
    state_ref, row_a_ref, row_b_ref, col_a_ref, col_b_ref, grid_ref, react_ref = refs[:7]
    new_ref, active_ref, south, north, advected, rounded = refs[-6:]
    tracers, levels, rows, tile = state_ref.shape
    cells = tracers * rows
    odd_band, odd_tile = info[BAND] % 2 == 1, info[ME] % 2 == 1
    first = ((info[ME] ^ k) * pl.num_programs(0) + pl.program_id(0)) * levels

    def column(value):
        return pltpu.roll(value, lax.rem(LANES - first, LANES), 1)

    a, b = col_a_ref[...].astype(F32), col_b_ref[...].astype(F32)
    west, east = column(jnp.where(odd_tile, a, b)), column(jnp.where(odd_tile, b, a))
    row = lax.broadcasted_iota(jnp.int32, (rows, tile), 0)
    lane = lax.broadcasted_iota(jnp.int32, (rows, tile), 1)
    ids, points = IDS, IDS + active_ref.shape[0]
    count = jnp.full((rows, tile), info[points], jnp.int32)
    for j in range(1, rows):
        count = jnp.where(row == j, info[points + j], count)
    mask = jnp.where(info[ME] * tile + lane < count, 1.0, 0.0)
    across = [slice(v * LANES, (v + 1) * LANES) for v in range(tile // LANES)]
    along = [slice(v * SUBLANES, (v + 1) * SUBLANES) for v in range(rows // SUBLANES)]

    for l in range(levels):
        wind_u = grid_ref[0, l].astype(F32) * (scale * 0.1)
        wind_v = grid_ref[1, l].astype(F32) * (scale * 0.1)
        from_east, from_west = 0.05 - wind_u, 0.05 + wind_u
        from_north, from_south = 0.05 - wind_v, 0.05 + wind_v
        a, b = row_a_ref[l].astype(F32), row_b_ref[l].astype(F32)
        south[l] = jnp.where(odd_band, a, b)
        north[l] = jnp.where(odd_band, b, a)
        for t in range(tracers):
            cell = slice(t * rows, (t + 1) * rows)
            x = state_ref[t, l].astype(F32)
            outer = [jnp.broadcast_to(col[cell, l : l + 1], (rows, LANES)) for col in (east, west)]
            parts = [x[:, v] for v in across]
            qe = jnp.concatenate(shifted(parts, outer[0], 1, 1), axis=1)
            qw = jnp.concatenate(shifted(parts, outer[1], 1, -1), axis=1)
            shape = (SUBLANES, tile)
            outer = [jnp.broadcast_to(ref[l, t : t + 1], shape) for ref in (north, south)]
            parts = [x[v] for v in along]
            qn = jnp.concatenate(shifted(parts, outer[0], 0, 1), axis=0)
            qs = jnp.concatenate(shifted(parts, outer[1], 0, -1), axis=0)
            moved = 0.8 * x + from_east * qe + from_west * qw + from_north * qn + from_south * qs
            advected[l, cell] = moved
            rounded[l, cell] = moved.astype(BF16)
    for l in range(levels):
        temper = grid_ref[2, l].astype(F32) * scale
        high = rounded[l]
        terms = dot(react_ref[...], jnp.concatenate([high, high], axis=0), ((1,), (0,)))
        for t in range(tracers):
            cell = slice(t * rows, (t + 1) * rows)
            warm = slice(cells + t * rows, cells + (t + 1) * rows)
            reacted = (advected[l, cell] + terms[cell] + temper * terms[warm]) * mask
            new_ref[t, l] = reacted.astype(BF16)
    for a in range(active_ref.shape[0]):
        active_ref[a] = new_ref[info[ids + a]]


def chemistry(state, halos, grid, react, info, k, actives, waves, before):
    tracers, levels, rows, tile = state.shape
    fields, own = grid.shape[:2]
    some = 4 if own % 4 == 0 else own
    steps = own // some
    cells = tracers * rows
    scale = 1.0 / float(np.sqrt(np.float32(waves)))

    def whole(shape):
        return pl.BlockSpec(shape, lambda i, info: (0,) * len(shape))

    row_spec = pl.BlockSpec((some, tracers, tile), lambda i, info: ((info[ME] ^ k) * steps + i, 0, 0))
    state_spec = pl.BlockSpec(
        (tracers, some, rows, tile), lambda i, info: (0, (info[ME] ^ k) * steps + i, 0, 0)
    )
    operands = [state, *halos, grid, react]
    in_specs = [
        state_spec,
        row_spec,
        row_spec,
        whole(halos[2].shape),
        whole(halos[3].shape),
        pl.BlockSpec((fields, some, rows, tile), lambda i, info: (0, i, 0, 0)),
        whole(react.shape),
    ]
    aliases = {}
    if before is not None:
        aliases = {1 + len(operands): 0}
        operands.append(before)
        in_specs.append(pl.BlockSpec(memory_space=pl.ANY))
    return pl.pallas_call(
        functools.partial(chem_kernel, scale, k),
        grid_spec=pltpu.PrefetchScalarGridSpec(
            num_scalar_prefetch=1,
            grid=(steps,),
            in_specs=in_specs,
            out_specs=[
                state_spec,
                pl.BlockSpec((actives, some, rows, tile), lambda i, info: (0, i, 0, 0)),
            ],
            scratch_shapes=[
                pltpu.VMEM((some, tracers, tile), F32),
                pltpu.VMEM((some, tracers, tile), F32),
                pltpu.VMEM((some, cells, tile), F32),
                pltpu.VMEM((some, cells, tile), BF16),
            ],
        ),
        out_shape=[
            jax.ShapeDtypeStruct(state.shape, BF16),
            jax.ShapeDtypeStruct((actives, own, rows, tile), BF16),
        ],
        input_output_aliases=aliases,
        compiler_params=pltpu.CompilerParams(vmem_limit_bytes=16 * MIB),
        cost_estimate=cost(own * cells * tile, own * tile),
        name="chemistry",
    )(info, *operands)


def spread_kernel(info, recv_ref, *refs):
    refs[-1][...] = recv_ref[...].astype(F32)


def spread(recv, info, k, sources, before):
    actives, own, rows, tile = recv.shape
    each = 2 if actives % 2 == 0 else 1
    operands = [recv]
    in_specs = [pl.BlockSpec((each, own, rows, tile), lambda a, info: (a, 0, 0, 0))]
    aliases = {}
    if before is not None:
        operands.append(before)
        in_specs.append(pl.BlockSpec(memory_space=pl.ANY))
        aliases = {2: 0}
    return pl.pallas_call(
        spread_kernel,
        grid_spec=pltpu.PrefetchScalarGridSpec(
            num_scalar_prefetch=1,
            grid=(actives // each,),
            in_specs=in_specs,
            out_specs=pl.BlockSpec((each, own, rows, tile), lambda a, info: (a, 0, 0, info[ME] ^ k)),
        ),
        out_shape=jax.ShapeDtypeStruct((actives, own, rows, sources * tile), F32),
        input_output_aliases=aliases,
        compiler_params=pltpu.CompilerParams(vmem_limit_bytes=8 * MIB),
        cost_estimate=cost(recv.size, recv.shape[0]),
        name="spread",
    )(info, *operands)


def legendre_kernel(spectral_ref, legendre_ref, out_ref, rows_of, sums):
    parts, own, block, size = spectral_ref.shape
    bands, _, rows, pitch = out_ref.shape
    share = block * pl.num_programs(0)
    step = pl.program_id(0)
    lines = parts * own
    apart, stretch = block + 1, pitch + 1

    @pl.when(step == 0)
    def _():
        for h in range(sums.shape[0]):
            for l in range(own):
                tail = pl.ds(l * stretch + parts * share, pitch - parts * share)
                sums[h, tail, :] = jnp.zeros((pitch - parts * share, LANES), F32)

    for v in range(size // LANES):
        part = spectral_ref[:, :, :, v * LANES : (v + 1) * LANES].astype(F32)
        part = part.reshape(lines, block, LANES)
        for i in range(lines):
            rows_of[v, pl.ds(i * apart, block), :] = part[i]
    for m in range(block):
        x = [rows_of[v, pl.ds(m, lines, stride=apart), :] for v in range(size // LANES)]
        x = jnp.concatenate(x, axis=1).astype(BF16)
        result = dot(x, legendre_ref[m], ((1,), (0,)))
        for r in range(parts):
            at = r * share + step * block + m
            for h in range(sums.shape[0]):
                piece = result[r * own : (r + 1) * own, h * LANES : (h + 1) * LANES]
                sums[h, pl.ds(at, own, stride=stretch), :] = piece

    @pl.when(step == pl.num_programs(0) - 1)
    def _():
        some = LANES // rows
        for l in range(own):
            for h in range(sums.shape[0]):
                turned = sums[h, pl.ds(l * stretch, pitch), :].T.astype(BF16)
                out_ref[h * some : (h + 1) * some, l] = turned.reshape(some, rows, pitch)


def legendre_sums(spectral, legendre, bands):
    parts, own, share, size = spectral.shape
    rows = legendre.shape[2] // bands
    pitch = -(-parts * share // LANES) * LANES
    block = 16 if share % 16 == 0 else 8
    shape = (bands, own, rows, pitch)
    return pl.pallas_call(
        legendre_kernel,
        grid=(share // block,),
        in_specs=[
            pl.BlockSpec((parts, own, block, size), lambda i: (0, 0, i, 0)),
            pl.BlockSpec((block,) + legendre.shape[1:], lambda i: (i, 0, 0)),
        ],
        out_specs=pl.BlockSpec(shape, lambda i: (0, 0, 0, 0)),
        out_shape=jax.ShapeDtypeStruct(shape, BF16),
        scratch_shapes=[
            pltpu.VMEM((size // LANES, parts * own * (block + 1), LANES), F32),
            pltpu.VMEM((legendre.shape[2] // LANES, own * (pitch + 1), LANES), F32),
        ],
        compiler_params=pltpu.CompilerParams(vmem_limit_bytes=56 * MIB),
        cost_estimate=cost(2 * parts * own * legendre.size, 2 * (spectral.size + legendre.size)),
        name="legendre",
    )(spectral, legendre)


def exchange(value, axis, pairs):
    return lax.ppermute(value, axis, [p for a, b in pairs for p in ((a, b), (b, a))])


def neighbours(axis, first):
    size = lax.axis_size(axis)
    return [(i, i + 1) for i in range(first, size - 1, 2)]


def partners(axis, k):
    return [(i, i ^ k) for i in range(lax.axis_size(axis)) if i < i ^ k]


def body(spectral, legendre, wave_ids, points, tracers, react_base, react_temp, active_ids):
    bands, tiles = lax.axis_size("lat"), lax.axis_size("lon")
    tile = tracers.shape[3]
    waves = wave_ids.shape[0]
    band, me = lax.axis_index("lat"), lax.axis_index("lon")

    sent = legendre_sums(spectral, legendre, bands)

    rows = points.shape[0]
    info = jnp.concatenate([jnp.stack([band, me]), active_ids, points]).astype(jnp.int32)
    sent, info = lax.optimization_barrier((sent, info))
    recv = lax.all_to_all(sent, "lat", split_axis=0, concat_axis=0, tiled=True)
    *ends, react = edges(tracers, react_base, react_temp, info)
    halos = (
        exchange(ends[0], "lat", neighbours("lat", 0)),
        exchange(ends[1], "lat", neighbours("lat", 1)),
        exchange(ends[2], "lon", neighbours("lon", 0)),
        exchange(ends[3], "lon", neighbours("lon", 1)),
    )
    react, wave_ids = lax.optimization_barrier((react, wave_ids))
    table, twiddle = tables(info, wave_ids, rows, tiles * tile // LANES)
    recv, table, twiddle, halos, react = lax.optimization_barrier(
        (recv, table, twiddle, halos, react)
    )
    grids = synthesis(recv, table, twiddle, info, tiles, tile)

    middle = list(range(tiles // 2, tiles))
    soon, late = middle[: tiles // 4], middle[tiles // 4 :]
    inner = list(range(1, tiles // 2))

    def send(value, k):
        return exchange(value, "lon", partners("lon", k))

    moved = {0: grids[0]} | {k: send(grids[k], k) for k in inner + soon}
    new, active = None, {}
    order = [0] + inner + soon + late
    for k in order:
        new, active[k] = chemistry(
            tracers, halos, moved[k], react, info, k, active_ids.shape[0], waves, new
        )
        if k:
            active[k] = send(active[k], k)
        else:
            held, active[0] = lax.optimization_barrier(([grids[i] for i in late], active[0]))
            moved |= {i: send(value, i) for i, value in zip(late, held)}
    spreaded = None
    for k in order:
        spreaded = spread(active[k], info, k, tiles, spreaded)
    return new, spreaded


def solution(mesh):
    return jax.shard_map(
        body,
        mesh=mesh,
        in_specs=(
            P(None, "lon", "lat", None),
            P("lat", None, None),
            P(),
            P("lat"),
            P(None, None, "lat", "lon"),
            P(),
            P(),
            P(),
        ),
        out_specs=(P(None, None, "lat", "lon"), P(None, "lon", "lat", None)),
        check_vma=False,
    )
```

```python
import functools

import jax
import jax.numpy as jnp
import numpy as np
from jax import lax
from jax.experimental import pallas as pl
from jax.experimental.pallas import tpu as pltpu
from jax.sharding import PartitionSpec as P

F32 = jnp.float32
BF16 = jnp.bfloat16
LANES = 128
SUBLANES = 8
LOW = 16
STEP = 4
MIB = 1024 * 1024

COS = (
    0.9999999890590228,
    -19.739204499454026,
    64.93911745990036,
    -85.45013953095037,
    60.16763095136588,
    -25.96759924965491,
    6.528658162567069,
)
SIN = (
    6.283185302511503,
    -41.34170040531769,
    81.60513138580204,
    -76.7030153539128,
    42.02592698618416,
    -14.899846668691637,
    3.238137510515757,
)


def dot(a, b, dims):
    return lax.dot_general(a, b, (dims, ((), ())), preferred_element_type=F32)


BAND, ME, IDS = 0, 1, 2


def cost(flops, moved):
    return pl.CostEstimate(flops=int(flops), bytes_accessed=int(moved), transcendentals=0)


def unit_circle(step, rows, waves, count):
    index = lax.broadcasted_iota(jnp.int32, (rows, waves.shape[1]), 0) * step
    product = index.astype(F32) * waves
    inverse = 1.0 / count
    turns = (product - jnp.floor(product * inverse) * count) * inverse
    y = turns - jnp.floor(turns + 0.5)
    z = y * y
    cosine = jnp.full_like(z, COS[-1])
    sine = jnp.full_like(z, SIN[-1])
    for c, s in zip(COS[-2::-1], SIN[-2::-1]):
        cosine = cosine * z + c
        sine = sine * z + s
    return cosine, sine * y


def table_kernel(first, info, waves_ref, table_ref, twiddle_ref):
    size, turns = waves_ref.shape[1], twiddle_ref.shape[2]
    waves = waves_ref[...].astype(F32)
    for k in range(table_ref.shape[0]):
        row = pl.program_id(0) * table_ref.shape[0] + k
        count = jnp.full(waves.shape, info[first + row], jnp.int32).astype(F32)
        cos_low, sin_low = unit_circle(1, LOW, waves, count)
        cos_high, sin_high = unit_circle(LOW, LANES // LOW, waves, count)
        cosine, sine = [], []
        for a in range(LANES // LOW):
            ch, sh = cos_high[a : a + 1], sin_high[a : a + 1]
            cosine.append(ch * cos_low - sh * sin_low)
            sine.append(-sh * cos_low - ch * sin_low)
        table_ref[k, :size, :] = jnp.concatenate(cosine, axis=0).T.astype(BF16)
        table_ref[k, size:, :] = jnp.concatenate(sine, axis=0).T.astype(BF16)
        cos_turn, sin_turn = unit_circle(LANES, turns, waves, count)
        twiddle_ref[k, 0] = cos_turn
        twiddle_ref[k, 1] = sin_turn


def tables(info, wave_ids, rows, turns):
    waves = wave_ids.shape[0]
    each = STEP if rows % STEP == 0 else 1
    return pl.pallas_call(
        functools.partial(table_kernel, info.shape[0] - rows),
        grid_spec=pltpu.PrefetchScalarGridSpec(
            num_scalar_prefetch=1,
            grid=(rows // each,),
            in_specs=[pl.BlockSpec((1, waves), lambda j, p: (0, 0))],
            out_specs=[
                pl.BlockSpec((each, 2 * waves, LANES), lambda j, p: (j, 0, 0)),
                pl.BlockSpec((each, 2, turns, waves), lambda j, p: (j, 0, 0, 0)),
            ],
        ),
        out_shape=[
            pltpu.VMEM((rows, 2 * waves, LANES), BF16),
            pltpu.VMEM((rows, 2, turns, waves), F32),
        ],
        compiler_params=pltpu.CompilerParams(vmem_limit_bytes=20 * MIB),
        cost_estimate=cost(rows * waves * LANES * 8, rows * waves * LANES * 4),
        name="tables",
    )(info, wave_ids[None, :])


def place(pieces, width):
    out = [None] * (width // LANES)
    lane = lax.broadcasted_iota(jnp.int32, (pieces[0][0].shape[0], LANES), 1)
    for value, start, count, here in pieces:
        shift = (here - start) % LANES
        for a in range(start // LANES, (start + count - 1) // LANES + 1):
            part = value[:, a * LANES : (a + 1) * LANES]
            if shift:
                part = pltpu.roll(part, shift, 1)
            first = max(start, a * LANES) - start + here
            last = min(start + count, (a + 1) * LANES) - start + here
            for v in range(first // LANES, (last - 1) // LANES + 1):
                low, high = max(first - v * LANES, 0), min(last - v * LANES, LANES)
                if out[v] is None:
                    out[v] = part
                else:
                    out[v] = jnp.where((lane >= low) & (lane < high), part, out[v])
    return out


def synth_kernel(info, recv_ref, table_ref, twiddle_ref, *refs):
    *out_refs, coef, grid = refs
    sources, levels, rows, _ = recv_ref.shape
    fields, waves = coef.shape[0] // 2, coef.shape[1] * LANES
    share = waves // sources
    each, _, turns = twiddle_ref.shape[:3]
    pitch = rows + 1
    step = pl.program_id(0)

    @pl.when(step == 0)
    def _():
        def level(l, carry):
            values = [recv_ref[s, l].astype(F32) for s in range(sources)]
            for r in range(2 * fields):
                windows = [
                    (values[s], r * share, share, s * share) for s in range(sources)
                ]
                for v, part in enumerate(place(windows, waves)):
                    coef[r, v, pl.ds(l * pitch, rows), :] = part
            return carry

        lax.fori_loop(0, levels, level, 0)

    for k in range(each):
        j = step * each + k

        def own_row(r):
            parts = [coef[r, v, pl.ds(j, levels, stride=pitch), :] for v in range(waves // LANES)]
            return jnp.concatenate(parts, axis=1)

        values = [own_row(r) for r in range(2 * fields)]
        real, imag = [], []
        for t in range(turns):
            c, s = twiddle_ref[k, 0, t : t + 1], twiddle_ref[k, 1, t : t + 1]
            for f in range(fields):
                re, im = values[2 * f], values[2 * f + 1]
                real.append(re * c - im * s)
                imag.append(re * s + im * c)
        both = [jnp.concatenate(part, axis=0).astype(BF16) for part in (real, imag)]
        result = dot(jnp.concatenate(both, axis=1), table_ref[k], ((1,), (0,)))
        grid[pl.ds(j, turns * fields * levels, stride=pitch), :] = result

    @pl.when(step == pl.num_programs(0) - 1)
    def _():
        tiles = turns // len(out_refs)
        for k, out_ref in enumerate(out_refs):
            for t in range(tiles):
                for f in range(fields):
                    start = (((info[ME] ^ k) * tiles + t) * fields + f) * levels
                    for l in range(levels):
                        block = grid[pl.ds((start + l) * pitch, rows), :].astype(BF16)
                        out_ref[f, l, :, t * LANES : (t + 1) * LANES] = block


def synthesis(recv, table, twiddle, info, dests, tile):
    sources, levels, rows, lanes = recv.shape
    turns, waves = twiddle.shape[2:]
    fields = 3
    each = STEP if rows % STEP == 0 else 1
    shape = (fields, levels, rows, tile)
    return pl.pallas_call(
        synth_kernel,
        grid_spec=pltpu.PrefetchScalarGridSpec(
            num_scalar_prefetch=1,
            grid=(rows // each,),
            in_specs=[
                pl.BlockSpec(recv.shape, lambda j, info: (0, 0, 0, 0)),
                pl.BlockSpec((each, 2 * waves, LANES), lambda j, info: (j, 0, 0)),
                pl.BlockSpec((each, 2, turns, waves), lambda j, info: (j, 0, 0, 0)),
            ],
            out_specs=[pl.BlockSpec(shape, lambda j, info: (0, 0, 0, 0))] * dests,
            scratch_shapes=[
                pltpu.VMEM((2 * fields, waves // LANES, levels * (rows + 1), LANES), F32),
                pltpu.VMEM((turns * fields * levels * (rows + 1), LANES), F32),
            ],
        ),
        out_shape=[jax.ShapeDtypeStruct(shape, BF16)] * dests,
        compiler_params=pltpu.CompilerParams(vmem_limit_bytes=24 * MIB),
        cost_estimate=cost(4 * rows * waves * fields * levels * turns * LANES, 4 * rows * waves * LANES),
        name="synthesis",
    )(info, recv, *[pltpu.with_memory_space_constraint(v, pltpu.VMEM) for v in (table, twiddle)])


def edge_kernel(
    info, state_ref, base_ref, temp_ref, row_a_ref, row_b_ref, col_a_ref, col_b_ref, react_ref
):
    tracers, levels, rows, tile = state_ref.shape
    cells = tracers * rows

    @pl.when(pl.program_id(0) == 0)
    def _():
        rates = jnp.concatenate([base_ref[...], temp_ref[...]], axis=0)
        high = rates.astype(BF16)
        low = (rates - high.astype(F32)).astype(BF16)

        def iota(shape, axis):
            return lax.broadcasted_iota(jnp.int32, shape, axis)

        shape = (2 * cells, 2 * tracers)
        down = jnp.where(iota(shape, 0) // rows == iota(shape, 1), 1.0, 0.0).astype(BF16)
        shape = (tracers, cells)
        over = jnp.where(iota(shape, 0) == iota(shape, 1) // rows, 1.0, 0.0).astype(BF16)
        shape = (2 * cells, cells)
        same = iota(shape, 0) % rows == iota(shape, 1) % rows
        for k, part in enumerate((high, low)):
            wide = dot(dot(down, part, ((1,), (0,))).astype(BF16), over, ((1,), (0,)))
            react_ref[:, k * cells : (k + 1) * cells] = jnp.where(same, wide, 0.0).astype(BF16)

    def iota(shape, axis):
        return lax.broadcasted_iota(jnp.int32, shape, axis)

    odd = info[BAND] % 2, info[ME] % 2
    far, near = (1 - odd[0]) * (rows - 1), odd[0] * (rows - 1)
    shape = (2 * tracers, cells)
    end = jnp.where(iota(shape, 0) < tracers, far, near)
    pick = iota(shape, 1) == (iota(shape, 0) % tracers) * rows + end
    pick = jnp.where(pick, 1.0, 0.0).astype(BF16)
    shape = (tile, 2 * LANES)
    far, near = (1 - odd[1]) * (tile - 1), odd[1] * (tile - 1)
    is_end = iota(shape, 0) == jnp.where(iota(shape, 1) < LANES, far, near)
    level = iota(shape, 1) % LANES - pl.program_id(0) * levels
    columns = jnp.zeros((cells, 2 * LANES), F32)
    for l in range(levels):
        x = state_ref[:, l].reshape(cells, tile)
        picked = dot(pick, x, ((1,), (0,)))
        row_a_ref[l] = picked[:tracers].astype(BF16)
        row_b_ref[l] = picked[tracers:].astype(BF16)
        mark = jnp.where(is_end & (level == l), 1.0, 0.0).astype(BF16)
        columns = columns + dot(x, mark, ((1,), (0,)))

    @pl.when(pl.program_id(0) == 0)
    def _():
        col_a_ref[...] = columns[:, :LANES].astype(BF16)
        col_b_ref[...] = columns[:, LANES:].astype(BF16)

    @pl.when(pl.program_id(0) > 0)
    def _():
        col_a_ref[...] = (col_a_ref[...].astype(F32) + columns[:, :LANES]).astype(BF16)
        col_b_ref[...] = (col_b_ref[...].astype(F32) + columns[:, LANES:]).astype(BF16)


def edges(state, react_base, react_temp, info):
    tracers, levels, rows, tile = state.shape
    block = 16
    cells = tracers * rows
    rowed = jax.ShapeDtypeStruct((levels, tracers, tile), BF16)
    columned = jax.ShapeDtypeStruct((cells, LANES), BF16)
    row_spec = pl.BlockSpec((block, tracers, tile), lambda i, info: (i, 0, 0))
    col_spec = pl.BlockSpec((cells, LANES), lambda i, info: (0, 0))
    wide = (2 * cells, 2 * cells)
    return pl.pallas_call(
        edge_kernel,
        grid_spec=pltpu.PrefetchScalarGridSpec(
            num_scalar_prefetch=1,
            grid=(levels // block,),
            in_specs=[
                pl.BlockSpec((tracers, block, rows, tile), lambda i, info: (0, i, 0, 0)),
                pl.BlockSpec(react_base.shape, lambda i, info: (0, 0)),
                pl.BlockSpec(react_temp.shape, lambda i, info: (0, 0)),
            ],
            out_specs=[
                row_spec, row_spec, col_spec, col_spec, pl.BlockSpec(wide, lambda i, info: (0, 0)),
            ],
        ),
        out_shape=[rowed, rowed, columned, columned, jax.ShapeDtypeStruct(wide, BF16)],
        compiler_params=pltpu.CompilerParams(vmem_limit_bytes=52 * MIB),
        cost_estimate=cost(4 * state.size * 32, 2 * state.size),
        name="edges",
    )(info, state, react_base, react_temp)


def shifted(value, outer, axis, step):
    size = value[0].shape[axis]
    turned = [pltpu.roll(v, -step % size, axis) for v in value]
    place = lax.broadcasted_iota(jnp.int32, value[0].shape, axis)
    at_end = place == (size - 1 if step == 1 else 0)
    following = turned[1:] + [outer] if step == 1 else [outer] + turned[:-1]
    return [jnp.where(at_end, f, t) for f, t in zip(following, turned)]


def chem_kernel(scale, k, info, *refs):
    state_ref, row_a_ref, row_b_ref, col_a_ref, col_b_ref, grid_ref, react_ref = refs[:7]
    new_ref, active_ref, south, north, advected, rounded = refs[-6:]
    tracers, levels, rows, tile = state_ref.shape
    cells = tracers * rows
    odd_band, odd_tile = info[BAND] % 2 == 1, info[ME] % 2 == 1
    first = ((info[ME] ^ k) * pl.num_programs(0) + pl.program_id(0)) * levels

    def column(value):
        return pltpu.roll(value, lax.rem(LANES - first, LANES), 1)

    a, b = col_a_ref[...].astype(F32), col_b_ref[...].astype(F32)
    west, east = column(jnp.where(odd_tile, a, b)), column(jnp.where(odd_tile, b, a))
    row = lax.broadcasted_iota(jnp.int32, (rows, tile), 0)
    lane = lax.broadcasted_iota(jnp.int32, (rows, tile), 1)
    ids, points = IDS, IDS + active_ref.shape[0]
    count = jnp.full((rows, tile), info[points], jnp.int32)
    for j in range(1, rows):
        count = jnp.where(row == j, info[points + j], count)
    mask = jnp.where(info[ME] * tile + lane < count, 1.0, 0.0)
    across = [slice(v * LANES, (v + 1) * LANES) for v in range(tile // LANES)]
    along = [slice(v * SUBLANES, (v + 1) * SUBLANES) for v in range(rows // SUBLANES)]

    for l in range(levels):
        wind_u = grid_ref[0, l].astype(F32) * (scale * 0.1)
        wind_v = grid_ref[1, l].astype(F32) * (scale * 0.1)
        from_east, from_west = 0.05 - wind_u, 0.05 + wind_u
        from_north, from_south = 0.05 - wind_v, 0.05 + wind_v
        a, b = row_a_ref[l].astype(F32), row_b_ref[l].astype(F32)
        south[l] = jnp.where(odd_band, a, b)
        north[l] = jnp.where(odd_band, b, a)
        for t in range(tracers):
            cell = slice(t * rows, (t + 1) * rows)
            x = state_ref[t, l].astype(F32)
            outer = [jnp.broadcast_to(col[cell, l : l + 1], (rows, LANES)) for col in (east, west)]
            parts = [x[:, v] for v in across]
            qe = jnp.concatenate(shifted(parts, outer[0], 1, 1), axis=1)
            qw = jnp.concatenate(shifted(parts, outer[1], 1, -1), axis=1)
            shape = (SUBLANES, tile)
            outer = [jnp.broadcast_to(ref[l, t : t + 1], shape) for ref in (north, south)]
            parts = [x[v] for v in along]
            qn = jnp.concatenate(shifted(parts, outer[0], 0, 1), axis=0)
            qs = jnp.concatenate(shifted(parts, outer[1], 0, -1), axis=0)
            moved = 0.8 * x + from_east * qe + from_west * qw + from_north * qn + from_south * qs
            advected[l, cell] = moved
            rounded[l, cell] = moved.astype(BF16)
    for l in range(levels):
        temper = grid_ref[2, l].astype(F32) * scale
        high = rounded[l]
        terms = dot(react_ref[...], jnp.concatenate([high, high], axis=0), ((1,), (0,)))
        for t in range(tracers):
            cell = slice(t * rows, (t + 1) * rows)
            warm = slice(cells + t * rows, cells + (t + 1) * rows)
            reacted = (advected[l, cell] + terms[cell] + temper * terms[warm]) * mask
            new_ref[t, l] = reacted.astype(BF16)
    for a in range(active_ref.shape[0]):
        active_ref[a] = new_ref[info[ids + a]]


def chemistry(state, halos, grid, react, info, k, actives, waves, before):
    tracers, levels, rows, tile = state.shape
    fields, own = grid.shape[:2]
    some = 4 if own % 4 == 0 else own
    steps = own // some
    cells = tracers * rows
    scale = 1.0 / float(np.sqrt(np.float32(waves)))

    def whole(shape):
        return pl.BlockSpec(shape, lambda i, info: (0,) * len(shape))

    row_spec = pl.BlockSpec((some, tracers, tile), lambda i, info: ((info[ME] ^ k) * steps + i, 0, 0))
    state_spec = pl.BlockSpec(
        (tracers, some, rows, tile), lambda i, info: (0, (info[ME] ^ k) * steps + i, 0, 0)
    )
    operands = [state, *halos, grid, react]
    in_specs = [
        state_spec,
        row_spec,
        row_spec,
        whole(halos[2].shape),
        whole(halos[3].shape),
        pl.BlockSpec((fields, some, rows, tile), lambda i, info: (0, i, 0, 0)),
        whole(react.shape),
    ]
    aliases = {}
    if before is not None:
        aliases = {1 + len(operands): 0}
        operands.append(before)
        in_specs.append(pl.BlockSpec(memory_space=pl.ANY))
    return pl.pallas_call(
        functools.partial(chem_kernel, scale, k),
        grid_spec=pltpu.PrefetchScalarGridSpec(
            num_scalar_prefetch=1,
            grid=(steps,),
            in_specs=in_specs,
            out_specs=[
                state_spec,
                pl.BlockSpec((actives, some, rows, tile), lambda i, info: (0, i, 0, 0)),
            ],
            scratch_shapes=[
                pltpu.VMEM((some, tracers, tile), F32),
                pltpu.VMEM((some, tracers, tile), F32),
                pltpu.VMEM((some, cells, tile), F32),
                pltpu.VMEM((some, cells, tile), BF16),
            ],
        ),
        out_shape=[
            jax.ShapeDtypeStruct(state.shape, BF16),
            jax.ShapeDtypeStruct((actives, own, rows, tile), BF16),
        ],
        input_output_aliases=aliases,
        compiler_params=pltpu.CompilerParams(vmem_limit_bytes=16 * MIB),
        cost_estimate=cost(own * cells * tile, own * tile),
        name="chemistry",
    )(info, *operands)


def spread_kernel(info, recv_ref, *refs):
    refs[-1][...] = recv_ref[...].astype(F32)


def spread(recv, info, k, sources, before):
    actives, own, rows, tile = recv.shape
    each = 2 if actives % 2 == 0 else 1
    operands = [recv]
    in_specs = [pl.BlockSpec((each, own, rows, tile), lambda a, info: (a, 0, 0, 0))]
    aliases = {}
    if before is not None:
        operands.append(before)
        in_specs.append(pl.BlockSpec(memory_space=pl.ANY))
        aliases = {2: 0}
    return pl.pallas_call(
        spread_kernel,
        grid_spec=pltpu.PrefetchScalarGridSpec(
            num_scalar_prefetch=1,
            grid=(actives // each,),
            in_specs=in_specs,
            out_specs=pl.BlockSpec((each, own, rows, tile), lambda a, info: (a, 0, 0, info[ME] ^ k)),
        ),
        out_shape=jax.ShapeDtypeStruct((actives, own, rows, sources * tile), F32),
        input_output_aliases=aliases,
        compiler_params=pltpu.CompilerParams(vmem_limit_bytes=8 * MIB),
        cost_estimate=cost(recv.size, recv.shape[0]),
        name="spread",
    )(info, *operands)


def legendre_kernel(spectral_ref, legendre_ref, out_ref, rows_of, sums):
    parts, own, block, size = spectral_ref.shape
    bands, _, rows, pitch = out_ref.shape
    share = block * pl.num_programs(0)
    step = pl.program_id(0)
    lines = parts * own
    apart, stretch = block + 1, pitch + 1

    @pl.when(step == 0)
    def _():
        for h in range(sums.shape[0]):
            for l in range(own):
                tail = pl.ds(l * stretch + parts * share, pitch - parts * share)
                sums[h, tail, :] = jnp.zeros((pitch - parts * share, LANES), F32)

    for v in range(size // LANES):
        part = spectral_ref[:, :, :, v * LANES : (v + 1) * LANES].astype(F32)
        part = part.reshape(lines, block, LANES)
        for i in range(lines):
            rows_of[v, pl.ds(i * apart, block), :] = part[i]
    for m in range(block):
        x = [rows_of[v, pl.ds(m, lines, stride=apart), :] for v in range(size // LANES)]
        x = jnp.concatenate(x, axis=1).astype(BF16)
        result = dot(x, legendre_ref[m], ((1,), (0,)))
        for r in range(parts):
            at = r * share + step * block + m
            for h in range(sums.shape[0]):
                piece = result[r * own : (r + 1) * own, h * LANES : (h + 1) * LANES]
                sums[h, pl.ds(at, own, stride=stretch), :] = piece

    @pl.when(step == pl.num_programs(0) - 1)
    def _():
        some = LANES // rows
        for l in range(own):
            for h in range(sums.shape[0]):
                turned = sums[h, pl.ds(l * stretch, pitch), :].T.astype(BF16)
                out_ref[h * some : (h + 1) * some, l] = turned.reshape(some, rows, pitch)


def legendre_sums(spectral, legendre, bands):
    parts, own, share, size = spectral.shape
    rows = legendre.shape[2] // bands
    pitch = -(-parts * share // LANES) * LANES
    block = 16 if share % 16 == 0 else 8
    shape = (bands, own, rows, pitch)
    return pl.pallas_call(
        legendre_kernel,
        grid=(share // block,),
        in_specs=[
            pl.BlockSpec((parts, own, block, size), lambda i: (0, 0, i, 0)),
            pl.BlockSpec((block,) + legendre.shape[1:], lambda i: (i, 0, 0)),
        ],
        out_specs=pl.BlockSpec(shape, lambda i: (0, 0, 0, 0)),
        out_shape=jax.ShapeDtypeStruct(shape, BF16),
        scratch_shapes=[
            pltpu.VMEM((size // LANES, parts * own * (block + 1), LANES), F32),
            pltpu.VMEM((legendre.shape[2] // LANES, own * (pitch + 1), LANES), F32),
        ],
        compiler_params=pltpu.CompilerParams(vmem_limit_bytes=56 * MIB),
        cost_estimate=cost(2 * parts * own * legendre.size, 2 * (spectral.size + legendre.size)),
        name="legendre",
    )(spectral, legendre)


def exchange(value, axis, pairs):
    return lax.ppermute(value, axis, [p for a, b in pairs for p in ((a, b), (b, a))])


def neighbours(axis, first):
    size = lax.axis_size(axis)
    return [(i, i + 1) for i in range(first, size - 1, 2)]


def partners(axis, k):
    return [(i, i ^ k) for i in range(lax.axis_size(axis)) if i < i ^ k]


def body(spectral, legendre, wave_ids, points, tracers, react_base, react_temp, active_ids):
    bands, tiles = lax.axis_size("lat"), lax.axis_size("lon")
    tile = tracers.shape[3]
    waves = wave_ids.shape[0]
    band, me = lax.axis_index("lat"), lax.axis_index("lon")

    sent = legendre_sums(spectral, legendre, bands)

    rows = points.shape[0]
    info = jnp.concatenate([jnp.stack([band, me]), active_ids, points]).astype(jnp.int32)
    sent, info = lax.optimization_barrier((sent, info))
    recv = lax.all_to_all(sent, "lat", split_axis=0, concat_axis=0, tiled=True)
    *ends, react = edges(tracers, react_base, react_temp, info)
    halos = (
        exchange(ends[0], "lat", neighbours("lat", 0)),
        exchange(ends[1], "lat", neighbours("lat", 1)),
        exchange(ends[2], "lon", neighbours("lon", 0)),
        exchange(ends[3], "lon", neighbours("lon", 1)),
    )
    react, wave_ids = lax.optimization_barrier((react, wave_ids))
    table, twiddle = tables(info, wave_ids, rows, tiles * tile // LANES)
    recv, table, twiddle, halos, react = lax.optimization_barrier(
        (recv, table, twiddle, halos, react)
    )
    grids = synthesis(recv, table, twiddle, info, tiles, tile)

    middle, inner = list(range(tiles // 2, tiles)), list(range(1, tiles // 2))
    soon, late = middle[: tiles // 4], middle[tiles // 4 :]

    def send(value, k):
        return exchange(value, "lon", partners("lon", k))

    moved = {0: grids[0]} | {k: send(grids[k], k) for k in soon}
    new, active = None, {}
    for k in [0] + soon + late + inner:
        new, active[k] = chemistry(
            tracers, halos, moved[k], react, info, k, active_ids.shape[0], waves, new
        )
        if k:
            active[k] = send(active[k], k)
        else:
            rest = late + inner
            held, active[0] = lax.optimization_barrier(([grids[i] for i in rest], active[0]))
            moved |= {i: send(value, i) for i, value in zip(rest, held)}
    spreaded = None
    for k in [0] + soon + inner + late:
        spreaded = spread(active[k], info, k, tiles, spreaded)
    return new, spreaded


def solution(mesh):
    return jax.shard_map(
        body,
        mesh=mesh,
        in_specs=(
            P(None, "lon", "lat", None),
            P("lat", None, None),
            P(),
            P("lat"),
            P(None, None, "lat", "lon"),
            P(),
            P(),
            P(),
        ),
        out_specs=(P(None, None, "lat", "lon"), P(None, "lon", "lat", None)),
        check_vma=False,
    )
```

```python
import functools

import jax
import jax.numpy as jnp
import numpy as np
from jax import lax
from jax.experimental import pallas as pl
from jax.experimental.pallas import tpu as pltpu
from jax.sharding import PartitionSpec as P

F32 = jnp.float32
BF16 = jnp.bfloat16
LANES = 128
HALF = LANES // 2
LOW = 16
STEP = 4
MIB = 1024 * 1024

COS = (
    0.9999999890590228,
    -19.739204499454026,
    64.93911745990036,
    -85.45013953095037,
    60.16763095136588,
    -25.96759924965491,
    6.528658162567069,
)
SIN = (
    6.283185302511503,
    -41.34170040531769,
    81.60513138580204,
    -76.7030153539128,
    42.02592698618416,
    -14.899846668691637,
    3.238137510515757,
)


def dot(a, b, dims):
    return lax.dot_general(a, b, (dims, ((), ())), preferred_element_type=F32)


BAND, ME, IDS = 0, 1, 2


def cost(flops, moved):
    return pl.CostEstimate(flops=int(flops), bytes_accessed=int(moved), transcendentals=0)


def unit_circle(step, rows, waves, count):
    index = lax.broadcasted_iota(jnp.int32, (rows, waves.shape[1]), 0) * step
    product = index.astype(F32) * waves
    inverse = 1.0 / count
    turns = (product - jnp.floor(product * inverse) * count) * inverse
    y = turns - jnp.floor(turns + 0.5)
    z = y * y
    cosine = jnp.full_like(z, COS[-1])
    sine = jnp.full_like(z, SIN[-1])
    for c, s in zip(COS[-2::-1], SIN[-2::-1]):
        cosine = cosine * z + c
        sine = sine * z + s
    return cosine, sine * y


def table_kernel(first, info, waves_ref, table_ref, twiddle_ref):
    size, turns = waves_ref.shape[1], twiddle_ref.shape[2]
    waves = waves_ref[...].astype(F32)
    for k in range(table_ref.shape[0]):
        row = pl.program_id(0) * table_ref.shape[0] + k
        count = jnp.full(waves.shape, info[first + row], jnp.int32).astype(F32)
        cos_low, sin_low = unit_circle(1, LOW, waves, count)
        cos_high, sin_high = unit_circle(LOW, LANES // LOW, waves, count)
        cosine, sine = [], []
        for a in range(LANES // LOW):
            ch, sh = cos_high[a : a + 1], sin_high[a : a + 1]
            cosine.append(ch * cos_low - sh * sin_low)
            sine.append(-sh * cos_low - ch * sin_low)
        table_ref[k, :size, :] = jnp.concatenate(cosine, axis=0).T.astype(BF16)
        table_ref[k, size:, :] = jnp.concatenate(sine, axis=0).T.astype(BF16)
        cos_turn, sin_turn = unit_circle(LANES, turns, waves, count)
        twiddle_ref[k, 0] = cos_turn
        twiddle_ref[k, 1] = sin_turn


def tables(info, wave_ids, rows, turns):
    waves = wave_ids.shape[0]
    each = STEP if rows % STEP == 0 else 1
    return pl.pallas_call(
        functools.partial(table_kernel, info.shape[0] - rows),
        grid_spec=pltpu.PrefetchScalarGridSpec(
            num_scalar_prefetch=1,
            grid=(rows // each,),
            in_specs=[pl.BlockSpec((1, waves), lambda j, p: (0, 0))],
            out_specs=[
                pl.BlockSpec((each, 2 * waves, LANES), lambda j, p: (j, 0, 0)),
                pl.BlockSpec((each, 2, turns, waves), lambda j, p: (j, 0, 0, 0)),
            ],
        ),
        out_shape=[
            pltpu.VMEM((rows, 2 * waves, LANES), BF16),
            pltpu.VMEM((rows, 2, turns, waves), F32),
        ],
        compiler_params=pltpu.CompilerParams(vmem_limit_bytes=20 * MIB),
        cost_estimate=cost(rows * waves * LANES * 8, rows * waves * LANES * 4),
        name="tables",
    )(info, wave_ids[None, :])


def place(pieces, width):
    out = [None] * (width // LANES)
    lane = lax.broadcasted_iota(jnp.int32, (pieces[0][0].shape[0], LANES), 1)
    for value, start, count, here in pieces:
        shift = (here - start) % LANES
        for a in range(start // LANES, (start + count - 1) // LANES + 1):
            part = value[:, a * LANES : (a + 1) * LANES]
            if shift:
                part = pltpu.roll(part, shift, 1)
            first = max(start, a * LANES) - start + here
            last = min(start + count, (a + 1) * LANES) - start + here
            for v in range(first // LANES, (last - 1) // LANES + 1):
                low, high = max(first - v * LANES, 0), min(last - v * LANES, LANES)
                if out[v] is None:
                    out[v] = part
                else:
                    out[v] = jnp.where((lane >= low) & (lane < high), part, out[v])
    return out


def synth_kernel(info, recv_ref, table_ref, twiddle_ref, *refs):
    *out_refs, coef, grid = refs
    sources, levels, rows, _ = recv_ref.shape
    fields, waves = coef.shape[0] // 2, coef.shape[1] * LANES
    share = waves // sources
    each, _, turns = twiddle_ref.shape[:3]
    pitch = rows + 1
    step = pl.program_id(0)

    @pl.when(step == 0)
    def _():
        def level(l, carry):
            values = [recv_ref[s, l].astype(F32) for s in range(sources)]
            for r in range(2 * fields):
                windows = [
                    (values[s], r * share, share, s * share) for s in range(sources)
                ]
                for v, part in enumerate(place(windows, waves)):
                    coef[r, v, pl.ds(l * pitch, rows), :] = part
            return carry

        lax.fori_loop(0, levels, level, 0)

    for k in range(each):
        j = step * each + k

        def own_row(r):
            parts = [coef[r, v, pl.ds(j, levels, stride=pitch), :] for v in range(waves // LANES)]
            return jnp.concatenate(parts, axis=1)

        values = [own_row(r) for r in range(2 * fields)]
        real, imag = [], []
        for t in range(turns):
            c, s = twiddle_ref[k, 0, t : t + 1], twiddle_ref[k, 1, t : t + 1]
            for f in range(fields):
                re, im = values[2 * f], values[2 * f + 1]
                real.append(re * c - im * s)
                imag.append(re * s + im * c)
        both = [jnp.concatenate(part, axis=0).astype(BF16) for part in (real, imag)]
        result = dot(jnp.concatenate(both, axis=1), table_ref[k], ((1,), (0,)))
        grid[pl.ds(j, turns * fields * levels, stride=pitch), :] = result

    @pl.when(step == pl.num_programs(0) - 1)
    def _():
        tiles = turns // len(out_refs)
        for k, out_ref in enumerate(out_refs):
            for t in range(tiles):
                for f in range(fields):
                    start = (((info[ME] ^ k) * tiles + t) * fields + f) * levels
                    for l in range(levels):
                        block = grid[pl.ds((start + l) * pitch, rows), :].astype(BF16)
                        out_ref[f, l, :, t * LANES : (t + 1) * LANES] = block


def synthesis(recv, table, twiddle, info, dests, tile):
    sources, levels, rows, lanes = recv.shape
    turns, waves = twiddle.shape[2:]
    fields = 3
    each = STEP if rows % STEP == 0 else 1
    shape = (fields, levels, rows, tile)
    return pl.pallas_call(
        synth_kernel,
        grid_spec=pltpu.PrefetchScalarGridSpec(
            num_scalar_prefetch=1,
            grid=(rows // each,),
            in_specs=[
                pl.BlockSpec(recv.shape, lambda j, info: (0, 0, 0, 0)),
                pl.BlockSpec((each, 2 * waves, LANES), lambda j, info: (j, 0, 0)),
                pl.BlockSpec((each, 2, turns, waves), lambda j, info: (j, 0, 0, 0)),
            ],
            out_specs=[pl.BlockSpec(shape, lambda j, info: (0, 0, 0, 0))] * dests,
            scratch_shapes=[
                pltpu.VMEM((2 * fields, waves // LANES, levels * (rows + 1), LANES), F32),
                pltpu.VMEM((turns * fields * levels * (rows + 1), LANES), F32),
            ],
        ),
        out_shape=[jax.ShapeDtypeStruct(shape, BF16)] * dests,
        compiler_params=pltpu.CompilerParams(vmem_limit_bytes=24 * MIB),
        cost_estimate=cost(4 * rows * waves * fields * levels * turns * LANES, 4 * rows * waves * LANES),
        name="synthesis",
    )(info, recv, *[pltpu.with_memory_space_constraint(v, pltpu.VMEM) for v in (table, twiddle)])


def edge_kernel(
    info, state_ref, base_ref, temp_ref, row_a_ref, row_b_ref, column_ref, react_ref
):
    tracers, levels, rows, tile = state_ref.shape
    cells = tracers * rows

    @pl.when(pl.program_id(0) == 0)
    def _():
        rates = jnp.concatenate([base_ref[...], temp_ref[...]], axis=0)
        high = rates.astype(BF16)
        low = (rates - high.astype(F32)).astype(BF16)

        def iota(shape, axis):
            return lax.broadcasted_iota(jnp.int32, shape, axis)

        shape = (2 * cells, 2 * tracers)
        down = jnp.where(iota(shape, 0) // rows == iota(shape, 1), 1.0, 0.0).astype(BF16)
        shape = (tracers, cells)
        over = jnp.where(iota(shape, 0) == iota(shape, 1) // rows, 1.0, 0.0).astype(BF16)
        shape = (2 * cells, cells)
        same = iota(shape, 0) % rows == iota(shape, 1) % rows
        for k, part in enumerate((high, low)):
            wide = dot(dot(down, part, ((1,), (0,))).astype(BF16), over, ((1,), (0,)))
            react_ref[:, k * cells : (k + 1) * cells] = jnp.where(same, wide, 0.0).astype(BF16)

    def iota(shape, axis):
        return lax.broadcasted_iota(jnp.int32, shape, axis)

    odd = info[BAND] % 2
    far, near = (1 - odd) * (rows - 1), odd * (rows - 1)
    shape = (2 * tracers, cells)
    end = jnp.where(iota(shape, 0) < tracers, far, near)
    pick = iota(shape, 1) == (iota(shape, 0) % tracers) * rows + end
    pick = jnp.where(pick, 1.0, 0.0).astype(BF16)
    shape = (tile, LANES)
    is_end = iota(shape, 0) == jnp.where(iota(shape, 1) < HALF, 0, tile - 1)
    level = iota(shape, 1) % HALF - pl.program_id(0) * levels
    columns = jnp.zeros((cells, LANES), F32)
    for l in range(levels):
        x = state_ref[:, l].reshape(cells, tile)
        picked = dot(pick, x, ((1,), (0,)))
        row_a_ref[l] = picked[:tracers].astype(BF16)
        row_b_ref[l] = picked[tracers:].astype(BF16)
        mark = jnp.where(is_end & (level == l), 1.0, 0.0).astype(BF16)
        columns = columns + dot(x, mark, ((1,), (0,)))

    @pl.when(pl.program_id(0) == 0)
    def _():
        column_ref[...] = columns.astype(BF16)

    @pl.when(pl.program_id(0) > 0)
    def _():
        column_ref[...] = (column_ref[...].astype(F32) + columns).astype(BF16)


def edges(state, react_base, react_temp, info):
    tracers, levels, rows, tile = state.shape
    block = 16
    cells = tracers * rows
    rowed = jax.ShapeDtypeStruct((levels, tracers, tile), BF16)
    columned = jax.ShapeDtypeStruct((cells, LANES), BF16)
    row_spec = pl.BlockSpec((block, tracers, tile), lambda i, info: (i, 0, 0))
    col_spec = pl.BlockSpec((cells, LANES), lambda i, info: (0, 0))
    wide = (2 * cells, 2 * cells)
    return pl.pallas_call(
        edge_kernel,
        grid_spec=pltpu.PrefetchScalarGridSpec(
            num_scalar_prefetch=1,
            grid=(levels // block,),
            in_specs=[
                pl.BlockSpec((tracers, block, rows, tile), lambda i, info: (0, i, 0, 0)),
                pl.BlockSpec(react_base.shape, lambda i, info: (0, 0)),
                pl.BlockSpec(react_temp.shape, lambda i, info: (0, 0)),
            ],
            out_specs=[
                row_spec, row_spec, col_spec, pl.BlockSpec(wide, lambda i, info: (0, 0)),
            ],
        ),
        out_shape=[rowed, rowed, columned, jax.ShapeDtypeStruct(wide, BF16)],
        compiler_params=pltpu.CompilerParams(vmem_limit_bytes=52 * MIB),
        cost_estimate=cost(4 * state.size * 32, 2 * state.size),
        name="edges",
    )(info, state, react_base, react_temp)


def beside(parts, outer, step):
    turned = [pltpu.roll(v, -step % LANES, 1) for v in parts]
    lane = lax.broadcasted_iota(jnp.int32, parts[0].shape, 1)
    at_end = lane == (LANES - 1 if step == 1 else 0)
    following = turned[1:] + [outer] if step == 1 else [outer] + turned[:-1]
    return [jnp.where(at_end, f, t) for f, t in zip(following, turned)]


def chem_kernel(scale, k, info, *refs):
    state_ref, row_a_ref, row_b_ref, column_ref, grid_ref, react_ref = refs[:6]
    new_ref, active_ref, column, padded, advected, rounded = refs[-6:]
    tracers, levels, rows, tile = state_ref.shape
    tiles = column_ref.shape[0]
    cells = tracers * rows
    me, odd = info[ME], info[BAND] % 2 == 1
    first = ((me ^ k) * pl.num_programs(0) + pl.program_id(0)) * levels
    west = column_ref[jnp.maximum(me - 1, 0)].astype(F32) * jnp.where(me > 0, 1.0, 0.0)
    east = column_ref[jnp.minimum(me + 1, tiles - 1)].astype(F32) * jnp.where(me < tiles - 1, 1.0, 0.0)
    column[0] = pltpu.roll(west, lax.rem(LANES + HALF - first, LANES), 1)
    column[1] = pltpu.roll(east, lax.rem(LANES - first, LANES), 1)
    row = lax.broadcasted_iota(jnp.int32, (rows, tile), 0)
    lane = lax.broadcasted_iota(jnp.int32, (rows, tile), 1)
    ids, points = IDS, IDS + active_ref.shape[0]
    count = jnp.full((rows, tile), info[points], jnp.int32)
    for j in range(1, rows):
        count = jnp.where(row == j, info[points + j], count)
    mask = jnp.where(me * tile + lane < count, 1.0, 0.0)
    across = [slice(v * LANES, (v + 1) * LANES) for v in range(tile // LANES)]
    pitch = rows + 3

    for l in range(levels):
        a, b = row_a_ref[l].astype(F32), row_b_ref[l].astype(F32)
        south, north = jnp.where(odd, a, b), jnp.where(odd, b, a)
        for v, lanes in enumerate(across):
            padded[l, v, pl.ds(0, tracers, stride=pitch), :] = south[:, lanes]
            padded[l, v, pl.ds(rows + 1, tracers, stride=pitch), :] = north[:, lanes]
            for t in range(tracers):
                padded[l, v, pl.ds(t * pitch + 1, rows), :] = state_ref[t, l, :, lanes].astype(F32)
    for l in range(levels):
        wind_u = grid_ref[0, l].astype(F32) * (scale * 0.1)
        wind_v = grid_ref[1, l].astype(F32) * (scale * 0.1)
        from_east, from_west = 0.05 - wind_u, 0.05 + wind_u
        from_north, from_south = 0.05 - wind_v, 0.05 + wind_v
        for t in range(tracers):
            cell = slice(t * rows, (t + 1) * rows)
            outer = [jnp.broadcast_to(column[i, cell, l : l + 1], (rows, LANES)) for i in (0, 1)]
            x = [state_ref[t, l, :, lanes].astype(F32) for lanes in across]
            qw, qe = beside(x, outer[0], -1), beside(x, outer[1], 1)
            for v, lanes in enumerate(across):
                qs = padded[l, v, pl.ds(t * pitch, rows), :]
                qn = padded[l, v, pl.ds(t * pitch + 2, rows), :]
                moved = 0.8 * x[v] + from_east[:, lanes] * qe[v] + from_west[:, lanes] * qw[v]
                moved = moved + from_north[:, lanes] * qn + from_south[:, lanes] * qs
                advected[l, cell, lanes] = moved
                rounded[l, cell, lanes] = moved.astype(BF16)
    for l in range(levels):
        temper = grid_ref[2, l].astype(F32) * scale
        high = rounded[l]
        terms = dot(react_ref[...], jnp.concatenate([high, high], axis=0), ((1,), (0,)))
        for t in range(tracers):
            cell = slice(t * rows, (t + 1) * rows)
            warm = slice(cells + t * rows, cells + (t + 1) * rows)
            reacted = (advected[l, cell] + terms[cell] + temper * terms[warm]) * mask
            new_ref[t, l] = reacted.astype(BF16)
    for a in range(active_ref.shape[0]):
        active_ref[a] = new_ref[info[ids + a]]


def chemistry(state, halos, grid, react, info, k, actives, waves, before):
    tracers, levels, rows, tile = state.shape
    fields, own = grid.shape[:2]
    some = 4 if own % 4 == 0 else own
    steps = own // some
    cells = tracers * rows
    scale = 1.0 / float(np.sqrt(np.float32(waves)))

    def whole(shape):
        return pl.BlockSpec(shape, lambda i, info: (0,) * len(shape))

    row_spec = pl.BlockSpec((some, tracers, tile), lambda i, info: ((info[ME] ^ k) * steps + i, 0, 0))
    state_spec = pl.BlockSpec(
        (tracers, some, rows, tile), lambda i, info: (0, (info[ME] ^ k) * steps + i, 0, 0)
    )
    operands = [state, *halos, grid, react]
    in_specs = [
        state_spec,
        row_spec,
        row_spec,
        whole(halos[2].shape),
        pl.BlockSpec((fields, some, rows, tile), lambda i, info: (0, i, 0, 0)),
        whole(react.shape),
    ]
    aliases = {}
    if before is not None:
        aliases = {1 + len(operands): 0}
        operands.append(before)
        in_specs.append(pl.BlockSpec(memory_space=pl.ANY))
    return pl.pallas_call(
        functools.partial(chem_kernel, scale, k),
        grid_spec=pltpu.PrefetchScalarGridSpec(
            num_scalar_prefetch=1,
            grid=(steps,),
            in_specs=in_specs,
            out_specs=[
                state_spec,
                pl.BlockSpec((actives, some, rows, tile), lambda i, info: (0, i, 0, 0)),
            ],
            scratch_shapes=[
                pltpu.VMEM((2, cells, LANES), F32),
                pltpu.VMEM((some, tile // LANES, tracers * (rows + 3), LANES), F32),
                pltpu.VMEM((some, cells, tile), F32),
                pltpu.VMEM((some, cells, tile), BF16),
            ],
        ),
        out_shape=[
            jax.ShapeDtypeStruct(state.shape, BF16),
            jax.ShapeDtypeStruct((actives, own, rows, tile), BF16),
        ],
        input_output_aliases=aliases,
        compiler_params=pltpu.CompilerParams(vmem_limit_bytes=16 * MIB),
        cost_estimate=cost(own * cells * tile, own * tile),
        name="chemistry",
    )(info, *operands)


def spread_kernel(info, recv_ref, *refs):
    refs[-1][...] = recv_ref[...].astype(F32)


def spread(recv, info, k, sources, before):
    actives, own, rows, tile = recv.shape
    each = 2 if actives % 2 == 0 else 1
    operands = [recv]
    in_specs = [pl.BlockSpec((each, own, rows, tile), lambda a, info: (a, 0, 0, 0))]
    aliases = {}
    if before is not None:
        operands.append(before)
        in_specs.append(pl.BlockSpec(memory_space=pl.ANY))
        aliases = {2: 0}
    return pl.pallas_call(
        spread_kernel,
        grid_spec=pltpu.PrefetchScalarGridSpec(
            num_scalar_prefetch=1,
            grid=(actives // each,),
            in_specs=in_specs,
            out_specs=pl.BlockSpec((each, own, rows, tile), lambda a, info: (a, 0, 0, info[ME] ^ k)),
        ),
        out_shape=jax.ShapeDtypeStruct((actives, own, rows, sources * tile), F32),
        input_output_aliases=aliases,
        compiler_params=pltpu.CompilerParams(vmem_limit_bytes=8 * MIB),
        cost_estimate=cost(recv.size, recv.shape[0]),
        name="spread",
    )(info, *operands)


def legendre_kernel(spectral_ref, legendre_ref, out_ref, rows_of, sums):
    parts, own, block, size = spectral_ref.shape
    bands, _, rows, pitch = out_ref.shape
    share = block * pl.num_programs(0)
    step = pl.program_id(0)
    lines = parts * own
    apart, stretch = block + 1, pitch + 1

    @pl.when(step == 0)
    def _():
        for h in range(sums.shape[0]):
            for l in range(own):
                tail = pl.ds(l * stretch + parts * share, pitch - parts * share)
                sums[h, tail, :] = jnp.zeros((pitch - parts * share, LANES), F32)

    for v in range(size // LANES):
        part = spectral_ref[:, :, :, v * LANES : (v + 1) * LANES].astype(F32)
        part = part.reshape(lines, block, LANES)
        for i in range(lines):
            rows_of[v, pl.ds(i * apart, block), :] = part[i]
    for m in range(block):
        x = [rows_of[v, pl.ds(m, lines, stride=apart), :] for v in range(size // LANES)]
        x = jnp.concatenate(x, axis=1).astype(BF16)
        result = dot(x, legendre_ref[m], ((1,), (0,)))
        for r in range(parts):
            at = r * share + step * block + m
            for h in range(sums.shape[0]):
                piece = result[r * own : (r + 1) * own, h * LANES : (h + 1) * LANES]
                sums[h, pl.ds(at, own, stride=stretch), :] = piece

    @pl.when(step == pl.num_programs(0) - 1)
    def _():
        some = LANES // rows
        for l in range(own):
            for h in range(sums.shape[0]):
                turned = sums[h, pl.ds(l * stretch, pitch), :].T.astype(BF16)
                out_ref[h * some : (h + 1) * some, l] = turned.reshape(some, rows, pitch)


def legendre_sums(spectral, legendre, bands):
    parts, own, share, size = spectral.shape
    rows = legendre.shape[2] // bands
    pitch = -(-parts * share // LANES) * LANES
    block = 16 if share % 16 == 0 else 8
    shape = (bands, own, rows, pitch)
    return pl.pallas_call(
        legendre_kernel,
        grid=(share // block,),
        in_specs=[
            pl.BlockSpec((parts, own, block, size), lambda i: (0, 0, i, 0)),
            pl.BlockSpec((block,) + legendre.shape[1:], lambda i: (i, 0, 0)),
        ],
        out_specs=pl.BlockSpec(shape, lambda i: (0, 0, 0, 0)),
        out_shape=jax.ShapeDtypeStruct(shape, BF16),
        scratch_shapes=[
            pltpu.VMEM((size // LANES, parts * own * (block + 1), LANES), F32),
            pltpu.VMEM((legendre.shape[2] // LANES, own * (pitch + 1), LANES), F32),
        ],
        compiler_params=pltpu.CompilerParams(vmem_limit_bytes=56 * MIB),
        cost_estimate=cost(2 * parts * own * legendre.size, 2 * (spectral.size + legendre.size)),
        name="legendre",
    )(spectral, legendre)


def exchange(value, axis, pairs):
    return lax.ppermute(value, axis, [p for a, b in pairs for p in ((a, b), (b, a))])


def neighbours(axis, first):
    size = lax.axis_size(axis)
    return [(i, i + 1) for i in range(first, size - 1, 2)]


def partners(axis, k):
    return [(i, i ^ k) for i in range(lax.axis_size(axis)) if i < i ^ k]


def body(spectral, legendre, wave_ids, points, tracers, react_base, react_temp, active_ids):
    bands, tiles = lax.axis_size("lat"), lax.axis_size("lon")
    tile = tracers.shape[3]
    waves = wave_ids.shape[0]
    band, me = lax.axis_index("lat"), lax.axis_index("lon")

    sent = legendre_sums(spectral, legendre, bands)

    rows = points.shape[0]
    info = jnp.concatenate([jnp.stack([band, me]), active_ids, points]).astype(jnp.int32)
    sent, info = lax.optimization_barrier((sent, info))
    recv = lax.all_to_all(sent, "lat", split_axis=0, concat_axis=0, tiled=True)
    row_a, row_b, column, react = edges(tracers, react_base, react_temp, info)
    halos = (
        exchange(row_a, "lat", neighbours("lat", 0)),
        exchange(row_b, "lat", neighbours("lat", 1)),
        lax.all_gather(column, "lon", axis=0),
    )
    react, wave_ids = lax.optimization_barrier((react, wave_ids))
    table, twiddle = tables(info, wave_ids, rows, tiles * tile // LANES)
    recv, table, twiddle, react, halos = lax.optimization_barrier(
        (recv, table, twiddle, react, halos)
    )
    grids = synthesis(recv, table, twiddle, info, tiles, tile)

    middle, inner = list(range(tiles // 2, tiles)), list(range(1, tiles // 2))
    soon, late = middle[: tiles // 4], middle[tiles // 4 :]

    def send(value, k):
        return exchange(value, "lon", partners("lon", k))

    moved = {0: grids[0]} | {k: send(grids[k], k) for k in soon}
    new, active = None, {}
    for k in [0] + soon + late + inner:
        new, active[k] = chemistry(
            tracers, halos, moved[k], react, info, k, active_ids.shape[0], waves, new
        )
        if k:
            active[k] = send(active[k], k)
        else:
            rest = late + inner
            held, active[0] = lax.optimization_barrier(([grids[i] for i in rest], active[0]))
            moved |= {i: send(value, i) for i, value in zip(rest, held)}
    spreaded = None
    for k in [0] + soon + inner + late:
        spreaded = spread(active[k], info, k, tiles, spreaded)
    return new, spreaded


def solution(mesh):
    return jax.shard_map(
        body,
        mesh=mesh,
        in_specs=(
            P(None, "lon", "lat", None),
            P("lat", None, None),
            P(),
            P("lat"),
            P(None, None, "lat", "lon"),
            P(),
            P(),
            P(),
        ),
        out_specs=(P(None, None, "lat", "lon"), P(None, "lon", "lat", None)),
        check_vma=False,
    )
```

```python
import functools

import jax
import jax.numpy as jnp
import numpy as np
from jax import lax
from jax.experimental import pallas as pl
from jax.experimental.pallas import tpu as pltpu
from jax.sharding import PartitionSpec as P

F32 = jnp.float32
BF16 = jnp.bfloat16
LANES = 128
SUBLANES = 8
LOW = 16
STEP = 4
MIB = 1024 * 1024

COS = (
    0.9999999890590228,
    -19.739204499454026,
    64.93911745990036,
    -85.45013953095037,
    60.16763095136588,
    -25.96759924965491,
    6.528658162567069,
)
SIN = (
    6.283185302511503,
    -41.34170040531769,
    81.60513138580204,
    -76.7030153539128,
    42.02592698618416,
    -14.899846668691637,
    3.238137510515757,
)


def dot(a, b, dims):
    return lax.dot_general(a, b, (dims, ((), ())), preferred_element_type=F32)


BAND, ME, IDS = 0, 1, 2


def cost(flops, moved):
    return pl.CostEstimate(flops=int(flops), bytes_accessed=int(moved), transcendentals=0)


def unit_circle(step, rows, waves, count):
    index = lax.broadcasted_iota(jnp.int32, (rows, waves.shape[1]), 0) * step
    product = index.astype(F32) * waves
    inverse = 1.0 / count
    turns = (product - jnp.floor(product * inverse) * count) * inverse
    y = turns - jnp.floor(turns + 0.5)
    z = y * y
    cosine = jnp.full_like(z, COS[-1])
    sine = jnp.full_like(z, SIN[-1])
    for c, s in zip(COS[-2::-1], SIN[-2::-1]):
        cosine = cosine * z + c
        sine = sine * z + s
    return cosine, sine * y


def table_kernel(first, info, waves_ref, table_ref, twiddle_ref):
    size, turns = waves_ref.shape[1], twiddle_ref.shape[2]
    waves = waves_ref[...].astype(F32)
    for k in range(table_ref.shape[0]):
        row = pl.program_id(0) * table_ref.shape[0] + k
        count = jnp.full(waves.shape, info[first + row], jnp.int32).astype(F32)
        cos_low, sin_low = unit_circle(1, LOW, waves, count)
        cos_high, sin_high = unit_circle(LOW, LANES // LOW, waves, count)
        cosine, sine = [], []
        for a in range(LANES // LOW):
            ch, sh = cos_high[a : a + 1], sin_high[a : a + 1]
            cosine.append(ch * cos_low - sh * sin_low)
            sine.append(-sh * cos_low - ch * sin_low)
        table_ref[k, :size, :] = jnp.concatenate(cosine, axis=0).T.astype(BF16)
        table_ref[k, size:, :] = jnp.concatenate(sine, axis=0).T.astype(BF16)
        cos_turn, sin_turn = unit_circle(LANES, turns, waves, count)
        twiddle_ref[k, 0] = cos_turn
        twiddle_ref[k, 1] = sin_turn


def tables(info, wave_ids, rows, turns):
    waves = wave_ids.shape[0]
    each = STEP if rows % STEP == 0 else 1
    return pl.pallas_call(
        functools.partial(table_kernel, info.shape[0] - rows),
        grid_spec=pltpu.PrefetchScalarGridSpec(
            num_scalar_prefetch=1,
            grid=(rows // each,),
            in_specs=[pl.BlockSpec((1, waves), lambda j, p: (0, 0))],
            out_specs=[
                pl.BlockSpec((each, 2 * waves, LANES), lambda j, p: (j, 0, 0)),
                pl.BlockSpec((each, 2, turns, waves), lambda j, p: (j, 0, 0, 0)),
            ],
        ),
        out_shape=[
            pltpu.VMEM((rows, 2 * waves, LANES), BF16),
            pltpu.VMEM((rows, 2, turns, waves), F32),
        ],
        compiler_params=pltpu.CompilerParams(vmem_limit_bytes=20 * MIB),
        cost_estimate=cost(rows * waves * LANES * 8, rows * waves * LANES * 4),
        name="tables",
    )(info, wave_ids[None, :])


def place(pieces, width):
    out = [None] * (width // LANES)
    lane = lax.broadcasted_iota(jnp.int32, (pieces[0][0].shape[0], LANES), 1)
    for value, start, count, here in pieces:
        shift = (here - start) % LANES
        for a in range(start // LANES, (start + count - 1) // LANES + 1):
            part = value[:, a * LANES : (a + 1) * LANES]
            if shift:
                part = pltpu.roll(part, shift, 1)
            first = max(start, a * LANES) - start + here
            last = min(start + count, (a + 1) * LANES) - start + here
            for v in range(first // LANES, (last - 1) // LANES + 1):
                low, high = max(first - v * LANES, 0), min(last - v * LANES, LANES)
                if out[v] is None:
                    out[v] = part
                else:
                    out[v] = jnp.where((lane >= low) & (lane < high), part, out[v])
    return out


def synth_kernel(info, recv_ref, table_ref, twiddle_ref, *refs):
    *out_refs, coef, grid = refs
    sources, levels, rows, _ = recv_ref.shape
    fields, waves = coef.shape[0] // 2, coef.shape[1] * LANES
    share = waves // sources
    each, _, turns = twiddle_ref.shape[:3]
    pitch = rows + 1
    step = pl.program_id(0)

    @pl.when(step == 0)
    def _():
        def level(l, carry):
            values = [recv_ref[s, l].astype(F32) for s in range(sources)]
            for r in range(2 * fields):
                windows = [
                    (values[s], r * share, share, s * share) for s in range(sources)
                ]
                for v, part in enumerate(place(windows, waves)):
                    coef[r, v, pl.ds(l * pitch, rows), :] = part
            return carry

        lax.fori_loop(0, levels, level, 0)

    for k in range(each):
        j = step * each + k

        def own_row(r):
            parts = [coef[r, v, pl.ds(j, levels, stride=pitch), :] for v in range(waves // LANES)]
            return jnp.concatenate(parts, axis=1)

        values = [own_row(r) for r in range(2 * fields)]
        real, imag = [], []
        for t in range(turns):
            c, s = twiddle_ref[k, 0, t : t + 1], twiddle_ref[k, 1, t : t + 1]
            for f in range(fields):
                re, im = values[2 * f], values[2 * f + 1]
                real.append(re * c - im * s)
                imag.append(re * s + im * c)
        both = [jnp.concatenate(part, axis=0).astype(BF16) for part in (real, imag)]
        result = dot(jnp.concatenate(both, axis=1), table_ref[k], ((1,), (0,)))
        grid[pl.ds(j, turns * fields * levels, stride=pitch), :] = result

    @pl.when(step == pl.num_programs(0) - 1)
    def _():
        tiles = turns // len(out_refs)
        for k, out_ref in enumerate(out_refs):
            for t in range(tiles):
                for f in range(fields):
                    start = (((info[ME] ^ k) * tiles + t) * fields + f) * levels
                    for l in range(levels):
                        block = grid[pl.ds((start + l) * pitch, rows), :].astype(BF16)
                        out_ref[f, l, :, t * LANES : (t + 1) * LANES] = block


def synthesis(recv, table, twiddle, info, dests, tile):
    sources, levels, rows, lanes = recv.shape
    turns, waves = twiddle.shape[2:]
    fields = 3
    each = STEP if rows % STEP == 0 else 1
    shape = (fields, levels, rows, tile)
    return pl.pallas_call(
        synth_kernel,
        grid_spec=pltpu.PrefetchScalarGridSpec(
            num_scalar_prefetch=1,
            grid=(rows // each,),
            in_specs=[
                pl.BlockSpec(recv.shape, lambda j, info: (0, 0, 0, 0)),
                pl.BlockSpec((each, 2 * waves, LANES), lambda j, info: (j, 0, 0)),
                pl.BlockSpec((each, 2, turns, waves), lambda j, info: (j, 0, 0, 0)),
            ],
            out_specs=[pl.BlockSpec(shape, lambda j, info: (0, 0, 0, 0))] * dests,
            scratch_shapes=[
                pltpu.VMEM((2 * fields, waves // LANES, levels * (rows + 1), LANES), F32),
                pltpu.VMEM((turns * fields * levels * (rows + 1), LANES), F32),
            ],
        ),
        out_shape=[jax.ShapeDtypeStruct(shape, BF16)] * dests,
        compiler_params=pltpu.CompilerParams(vmem_limit_bytes=24 * MIB),
        cost_estimate=cost(4 * rows * waves * fields * levels * turns * LANES, 4 * rows * waves * LANES),
        name="synthesis",
    )(info, recv, *[pltpu.with_memory_space_constraint(v, pltpu.VMEM) for v in (table, twiddle)])


def edge_kernel(
    info, state_ref, base_ref, temp_ref, row_a_ref, row_b_ref, col_a_ref, col_b_ref, react_ref
):
    tracers, levels, rows, tile = state_ref.shape
    cells = tracers * rows

    @pl.when(pl.program_id(0) == 0)
    def _():
        rates = jnp.concatenate([base_ref[...], temp_ref[...]], axis=0)
        high = rates.astype(BF16)
        low = (rates - high.astype(F32)).astype(BF16)

        def iota(shape, axis):
            return lax.broadcasted_iota(jnp.int32, shape, axis)

        shape = (2 * cells, 2 * tracers)
        down = jnp.where(iota(shape, 0) // rows == iota(shape, 1), 1.0, 0.0).astype(BF16)
        shape = (tracers, cells)
        over = jnp.where(iota(shape, 0) == iota(shape, 1) // rows, 1.0, 0.0).astype(BF16)
        shape = (2 * cells, cells)
        same = iota(shape, 0) % rows == iota(shape, 1) % rows
        for k, part in enumerate((high, low)):
            wide = dot(dot(down, part, ((1,), (0,))).astype(BF16), over, ((1,), (0,)))
            react_ref[:, k * cells : (k + 1) * cells] = jnp.where(same, wide, 0.0).astype(BF16)

    def iota(shape, axis):
        return lax.broadcasted_iota(jnp.int32, shape, axis)

    odd = info[BAND] % 2, info[ME] % 2
    far, near = (1 - odd[0]) * (rows - 1), odd[0] * (rows - 1)
    shape = (2 * tracers, cells)
    end = jnp.where(iota(shape, 0) < tracers, far, near)
    pick = iota(shape, 1) == (iota(shape, 0) % tracers) * rows + end
    pick = jnp.where(pick, 1.0, 0.0).astype(BF16)
    shape = (tile, 2 * LANES)
    far, near = (1 - odd[1]) * (tile - 1), odd[1] * (tile - 1)
    is_end = iota(shape, 0) == jnp.where(iota(shape, 1) < LANES, far, near)
    level = iota(shape, 1) % LANES - pl.program_id(0) * levels
    columns = jnp.zeros((cells, 2 * LANES), F32)
    for l in range(levels):
        x = state_ref[:, l].reshape(cells, tile)
        picked = dot(pick, x, ((1,), (0,)))
        row_a_ref[l] = picked[:tracers].astype(BF16)
        row_b_ref[l] = picked[tracers:].astype(BF16)
        mark = jnp.where(is_end & (level == l), 1.0, 0.0).astype(BF16)
        columns = columns + dot(x, mark, ((1,), (0,)))

    @pl.when(pl.program_id(0) == 0)
    def _():
        col_a_ref[...] = columns[:, :LANES].astype(BF16)
        col_b_ref[...] = columns[:, LANES:].astype(BF16)

    @pl.when(pl.program_id(0) > 0)
    def _():
        col_a_ref[...] = (col_a_ref[...].astype(F32) + columns[:, :LANES]).astype(BF16)
        col_b_ref[...] = (col_b_ref[...].astype(F32) + columns[:, LANES:]).astype(BF16)


def edges(state, react_base, react_temp, info):
    tracers, levels, rows, tile = state.shape
    block = 16
    cells = tracers * rows
    rowed = jax.ShapeDtypeStruct((levels, tracers, tile), BF16)
    columned = jax.ShapeDtypeStruct((cells, LANES), BF16)
    row_spec = pl.BlockSpec((block, tracers, tile), lambda i, info: (i, 0, 0))
    col_spec = pl.BlockSpec((cells, LANES), lambda i, info: (0, 0))
    wide = (2 * cells, 2 * cells)
    return pl.pallas_call(
        edge_kernel,
        grid_spec=pltpu.PrefetchScalarGridSpec(
            num_scalar_prefetch=1,
            grid=(levels // block,),
            in_specs=[
                pl.BlockSpec((tracers, block, rows, tile), lambda i, info: (0, i, 0, 0)),
                pl.BlockSpec(react_base.shape, lambda i, info: (0, 0)),
                pl.BlockSpec(react_temp.shape, lambda i, info: (0, 0)),
            ],
            out_specs=[
                row_spec, row_spec, col_spec, col_spec, pl.BlockSpec(wide, lambda i, info: (0, 0)),
            ],
        ),
        out_shape=[rowed, rowed, columned, columned, jax.ShapeDtypeStruct(wide, BF16)],
        compiler_params=pltpu.CompilerParams(vmem_limit_bytes=52 * MIB),
        cost_estimate=cost(4 * state.size * 32, 2 * state.size),
        name="edges",
    )(info, state, react_base, react_temp)


def shifted(value, outer, axis, step):
    size = value[0].shape[axis]
    turned = [pltpu.roll(v, -step % size, axis) for v in value]
    place = lax.broadcasted_iota(jnp.int32, value[0].shape, axis)
    at_end = place == (size - 1 if step == 1 else 0)
    following = turned[1:] + [outer] if step == 1 else [outer] + turned[:-1]
    return [jnp.where(at_end, f, t) for f, t in zip(following, turned)]


def chem_kernel(scale, k, info, *refs):
    state_ref, row_a_ref, row_b_ref, col_a_ref, col_b_ref, grid_ref, react_ref = refs[:7]
    new_ref, active_ref, south, north, advected, rounded = refs[-6:]
    tracers, levels, rows, tile = state_ref.shape
    cells = tracers * rows
    odd_band, odd_tile = info[BAND] % 2 == 1, info[ME] % 2 == 1
    first = ((info[ME] ^ k) * pl.num_programs(0) + pl.program_id(0)) * levels

    def column(value):
        return pltpu.roll(value, lax.rem(LANES - first, LANES), 1)

    a, b = col_a_ref[...].astype(F32), col_b_ref[...].astype(F32)
    west, east = column(jnp.where(odd_tile, a, b)), column(jnp.where(odd_tile, b, a))
    row = lax.broadcasted_iota(jnp.int32, (rows, tile), 0)
    lane = lax.broadcasted_iota(jnp.int32, (rows, tile), 1)
    ids, points = IDS, IDS + active_ref.shape[0]
    count = jnp.full((rows, tile), info[points], jnp.int32)
    for j in range(1, rows):
        count = jnp.where(row == j, info[points + j], count)
    mask = jnp.where(info[ME] * tile + lane < count, 1.0, 0.0)
    across = [slice(v * LANES, (v + 1) * LANES) for v in range(tile // LANES)]
    along = [slice(v * SUBLANES, (v + 1) * SUBLANES) for v in range(rows // SUBLANES)]

    for l in range(levels):
        wind_u = grid_ref[0, l].astype(F32) * (scale * 0.1)
        wind_v = grid_ref[1, l].astype(F32) * (scale * 0.1)
        from_east, from_west = 0.05 - wind_u, 0.05 + wind_u
        from_north, from_south = 0.05 - wind_v, 0.05 + wind_v
        a, b = row_a_ref[l].astype(F32), row_b_ref[l].astype(F32)
        south[l] = jnp.where(odd_band, a, b)
        north[l] = jnp.where(odd_band, b, a)
        for t in range(tracers):
            cell = slice(t * rows, (t + 1) * rows)
            x = state_ref[t, l].astype(F32)
            outer = [jnp.broadcast_to(col[cell, l : l + 1], (rows, LANES)) for col in (east, west)]
            parts = [x[:, v] for v in across]
            qe = jnp.concatenate(shifted(parts, outer[0], 1, 1), axis=1)
            qw = jnp.concatenate(shifted(parts, outer[1], 1, -1), axis=1)
            shape = (SUBLANES, tile)
            outer = [jnp.broadcast_to(ref[l, t : t + 1], shape) for ref in (north, south)]
            parts = [x[v] for v in along]
            qn = jnp.concatenate(shifted(parts, outer[0], 0, 1), axis=0)
            qs = jnp.concatenate(shifted(parts, outer[1], 0, -1), axis=0)
            moved = 0.8 * x + from_east * qe + from_west * qw + from_north * qn + from_south * qs
            advected[l, cell] = moved
            rounded[l, cell] = moved.astype(BF16)
    for l in range(levels):
        temper = grid_ref[2, l].astype(F32) * scale
        high = rounded[l]
        terms = dot(react_ref[...], jnp.concatenate([high, high], axis=0), ((1,), (0,)))
        for t in range(tracers):
            cell = slice(t * rows, (t + 1) * rows)
            warm = slice(cells + t * rows, cells + (t + 1) * rows)
            reacted = (advected[l, cell] + terms[cell] + temper * terms[warm]) * mask
            new_ref[t, l] = reacted.astype(BF16)
    for a in range(active_ref.shape[0]):
        active_ref[a] = new_ref[info[ids + a]]


def chemistry(state, halos, grid, react, info, k, actives, waves, before):
    tracers, levels, rows, tile = state.shape
    fields, own = grid.shape[:2]
    some = 4 if own % 4 == 0 else own
    steps = own // some
    cells = tracers * rows
    scale = 1.0 / float(np.sqrt(np.float32(waves)))

    def whole(shape):
        return pl.BlockSpec(shape, lambda i, info: (0,) * len(shape))

    row_spec = pl.BlockSpec((some, tracers, tile), lambda i, info: ((info[ME] ^ k) * steps + i, 0, 0))
    state_spec = pl.BlockSpec(
        (tracers, some, rows, tile), lambda i, info: (0, (info[ME] ^ k) * steps + i, 0, 0)
    )
    operands = [state, *halos, grid, react]
    in_specs = [
        state_spec,
        row_spec,
        row_spec,
        whole(halos[2].shape),
        whole(halos[3].shape),
        pl.BlockSpec((fields, some, rows, tile), lambda i, info: (0, i, 0, 0)),
        whole(react.shape),
    ]
    aliases = {}
    if before is not None:
        aliases = {1 + len(operands): 0}
        operands.append(before)
        in_specs.append(pl.BlockSpec(memory_space=pl.ANY))
    return pl.pallas_call(
        functools.partial(chem_kernel, scale, k),
        grid_spec=pltpu.PrefetchScalarGridSpec(
            num_scalar_prefetch=1,
            grid=(steps,),
            in_specs=in_specs,
            out_specs=[
                state_spec,
                pl.BlockSpec((actives, some, rows, tile), lambda i, info: (0, i, 0, 0)),
            ],
            scratch_shapes=[
                pltpu.VMEM((some, tracers, tile), F32),
                pltpu.VMEM((some, tracers, tile), F32),
                pltpu.VMEM((some, cells, tile), F32),
                pltpu.VMEM((some, cells, tile), BF16),
            ],
        ),
        out_shape=[
            jax.ShapeDtypeStruct(state.shape, BF16),
            jax.ShapeDtypeStruct((actives, own, rows, tile), BF16),
        ],
        input_output_aliases=aliases,
        compiler_params=pltpu.CompilerParams(vmem_limit_bytes=16 * MIB),
        cost_estimate=cost(own * cells * tile, own * tile),
        name="chemistry",
    )(info, *operands)


def spread_kernel(info, recv_ref, *refs):
    refs[-1][...] = recv_ref[...].astype(F32)


def spread(recv, info, k, sources, before):
    actives, own, rows, tile = recv.shape
    each = 2 if actives % 2 == 0 else 1
    operands = [recv]
    in_specs = [pl.BlockSpec((each, own, rows, tile), lambda a, info: (a, 0, 0, 0))]
    aliases = {}
    if before is not None:
        operands.append(before)
        in_specs.append(pl.BlockSpec(memory_space=pl.ANY))
        aliases = {2: 0}
    return pl.pallas_call(
        spread_kernel,
        grid_spec=pltpu.PrefetchScalarGridSpec(
            num_scalar_prefetch=1,
            grid=(actives // each,),
            in_specs=in_specs,
            out_specs=pl.BlockSpec((each, own, rows, tile), lambda a, info: (a, 0, 0, info[ME] ^ k)),
        ),
        out_shape=jax.ShapeDtypeStruct((actives, own, rows, sources * tile), F32),
        input_output_aliases=aliases,
        compiler_params=pltpu.CompilerParams(vmem_limit_bytes=8 * MIB),
        cost_estimate=cost(recv.size, recv.shape[0]),
        name="spread",
    )(info, *operands)


def legendre_kernel(spectral_ref, legendre_ref, out_ref, rows_of, sums):
    parts, own, block, size = spectral_ref.shape
    bands, _, rows, pitch = out_ref.shape
    share = block * pl.num_programs(0)
    step = pl.program_id(0)
    lines = parts * own
    apart, stretch = block + 1, pitch + 1

    @pl.when(step == 0)
    def _():
        for h in range(sums.shape[0]):
            for l in range(own):
                tail = pl.ds(l * stretch + parts * share, pitch - parts * share)
                sums[h, tail, :] = jnp.zeros((pitch - parts * share, LANES), F32)

    for v in range(size // LANES):
        part = spectral_ref[:, :, :, v * LANES : (v + 1) * LANES].astype(F32)
        part = part.reshape(lines, block, LANES)
        for i in range(lines):
            rows_of[v, pl.ds(i * apart, block), :] = part[i]
    for m in range(block):
        x = [rows_of[v, pl.ds(m, lines, stride=apart), :] for v in range(size // LANES)]
        x = jnp.concatenate(x, axis=1).astype(BF16)
        result = dot(x, legendre_ref[m], ((1,), (0,)))
        for r in range(parts):
            at = r * share + step * block + m
            for h in range(sums.shape[0]):
                piece = result[r * own : (r + 1) * own, h * LANES : (h + 1) * LANES]
                sums[h, pl.ds(at, own, stride=stretch), :] = piece

    @pl.when(step == pl.num_programs(0) - 1)
    def _():
        some = LANES // rows
        for l in range(own):
            for h in range(sums.shape[0]):
                turned = sums[h, pl.ds(l * stretch, pitch), :].T.astype(BF16)
                out_ref[h * some : (h + 1) * some, l] = turned.reshape(some, rows, pitch)


def legendre_sums(spectral, legendre, bands):
    parts, own, share, size = spectral.shape
    rows = legendre.shape[2] // bands
    pitch = -(-parts * share // LANES) * LANES
    block = 16 if share % 16 == 0 else 8
    shape = (bands, own, rows, pitch)
    return pl.pallas_call(
        legendre_kernel,
        grid=(share // block,),
        in_specs=[
            pl.BlockSpec((parts, own, block, size), lambda i: (0, 0, i, 0)),
            pl.BlockSpec((block,) + legendre.shape[1:], lambda i: (i, 0, 0)),
        ],
        out_specs=pl.BlockSpec(shape, lambda i: (0, 0, 0, 0)),
        out_shape=jax.ShapeDtypeStruct(shape, BF16),
        scratch_shapes=[
            pltpu.VMEM((size // LANES, parts * own * (block + 1), LANES), F32),
            pltpu.VMEM((legendre.shape[2] // LANES, own * (pitch + 1), LANES), F32),
        ],
        compiler_params=pltpu.CompilerParams(vmem_limit_bytes=56 * MIB),
        cost_estimate=cost(2 * parts * own * legendre.size, 2 * (spectral.size + legendre.size)),
        name="legendre",
    )(spectral, legendre)


def exchange(value, axis, pairs):
    return lax.ppermute(value, axis, [p for a, b in pairs for p in ((a, b), (b, a))])


def neighbours(axis, first):
    size = lax.axis_size(axis)
    return [(i, i + 1) for i in range(first, size - 1, 2)]


def partners(axis, k):
    return [(i, i ^ k) for i in range(lax.axis_size(axis)) if i < i ^ k]


def body(spectral, legendre, wave_ids, points, tracers, react_base, react_temp, active_ids):
    bands, tiles = lax.axis_size("lat"), lax.axis_size("lon")
    tile = tracers.shape[3]
    waves = wave_ids.shape[0]
    band, me = lax.axis_index("lat"), lax.axis_index("lon")

    sent = legendre_sums(spectral, legendre, bands)

    rows = points.shape[0]
    info = jnp.concatenate([jnp.stack([band, me]), active_ids, points]).astype(jnp.int32)
    sent, info = lax.optimization_barrier((sent, info))
    recv = lax.all_to_all(sent, "lat", split_axis=0, concat_axis=0, tiled=True)
    *ends, react = edges(tracers, react_base, react_temp, info)
    react, wave_ids = lax.optimization_barrier((react, wave_ids))
    table, twiddle = tables(info, wave_ids, rows, tiles * tile // LANES)
    recv, table, twiddle, react, ends = lax.optimization_barrier(
        (recv, table, twiddle, react, ends)
    )
    halos = (
        exchange(ends[0], "lat", neighbours("lat", 0)),
        exchange(ends[1], "lat", neighbours("lat", 1)),
        exchange(ends[2], "lon", neighbours("lon", 0)),
        exchange(ends[3], "lon", neighbours("lon", 1)),
    )
    grids = synthesis(recv, table, twiddle, info, tiles, tile)

    middle, inner = list(range(tiles // 2, tiles)), list(range(1, tiles // 2))
    soon, late = middle[: tiles // 4], middle[tiles // 4 :]

    def send(value, k):
        return exchange(value, "lon", partners("lon", k))

    moved = {0: grids[0]} | {k: send(grids[k], k) for k in soon}
    new, active = None, {}
    for k in [0] + soon + late + inner:
        new, active[k] = chemistry(
            tracers, halos, moved[k], react, info, k, active_ids.shape[0], waves, new
        )
        if k:
            active[k] = send(active[k], k)
        else:
            rest = late + inner
            held, active[0] = lax.optimization_barrier(([grids[i] for i in rest], active[0]))
            moved |= {i: send(value, i) for i, value in zip(rest, held)}
    spreaded = None
    for k in [0] + soon + inner + late:
        spreaded = spread(active[k], info, k, tiles, spreaded)
    return new, spreaded


def solution(mesh):
    return jax.shard_map(
        body,
        mesh=mesh,
        in_specs=(
            P(None, "lon", "lat", None),
            P("lat", None, None),
            P(),
            P("lat"),
            P(None, None, "lat", "lon"),
            P(),
            P(),
            P(),
        ),
        out_specs=(P(None, None, "lat", "lon"), P(None, "lon", "lat", None)),
        check_vma=False,
    )
```

```python
import functools

import jax
import jax.numpy as jnp
import numpy as np
from jax import lax
from jax.experimental import pallas as pl
from jax.experimental.pallas import tpu as pltpu
from jax.sharding import PartitionSpec as P

F32 = jnp.float32
BF16 = jnp.bfloat16
LANES = 128
SUBLANES = 8
LOW = 16
STEP = 4
MIB = 1024 * 1024

COS = (
    0.9999999890590228,
    -19.739204499454026,
    64.93911745990036,
    -85.45013953095037,
    60.16763095136588,
    -25.96759924965491,
    6.528658162567069,
)
SIN = (
    6.283185302511503,
    -41.34170040531769,
    81.60513138580204,
    -76.7030153539128,
    42.02592698618416,
    -14.899846668691637,
    3.238137510515757,
)


def dot(a, b, dims):
    return lax.dot_general(a, b, (dims, ((), ())), preferred_element_type=F32)


BAND, ME, IDS = 0, 1, 2


def cost(flops, moved):
    return pl.CostEstimate(flops=int(flops), bytes_accessed=int(moved), transcendentals=0)


def unit_circle(step, rows, waves, count):
    index = lax.broadcasted_iota(jnp.int32, (rows, waves.shape[1]), 0) * step
    product = index.astype(F32) * waves
    inverse = 1.0 / count
    turns = (product - jnp.floor(product * inverse) * count) * inverse
    y = turns - jnp.floor(turns + 0.5)
    z = y * y
    cosine = jnp.full_like(z, COS[-1])
    sine = jnp.full_like(z, SIN[-1])
    for c, s in zip(COS[-2::-1], SIN[-2::-1]):
        cosine = cosine * z + c
        sine = sine * z + s
    return cosine, sine * y


def make_tables(points, first, waves, table_ref, twiddle_ref):
    size, turns = waves.shape[1], twiddle_ref.shape[2]
    for k in range(table_ref.shape[0]):
        count = jnp.full(waves.shape, points[first + k], jnp.int32).astype(F32)
        cos_low, sin_low = unit_circle(1, LOW, waves, count)
        cos_high, sin_high = unit_circle(LOW, LANES // LOW, waves, count)
        cosine, sine = [], []
        for a in range(LANES // LOW):
            ch, sh = cos_high[a : a + 1], sin_high[a : a + 1]
            cosine.append(ch * cos_low - sh * sin_low)
            sine.append(-sh * cos_low - ch * sin_low)
        table_ref[k, :size, :] = jnp.concatenate(cosine, axis=0).T.astype(BF16)
        table_ref[k, size:, :] = jnp.concatenate(sine, axis=0).T.astype(BF16)
        cos_turn, sin_turn = unit_circle(LANES, turns, waves, count)
        twiddle_ref[k, 0] = cos_turn
        twiddle_ref[k, 1] = sin_turn


def place(pieces, width):
    out = [None] * (width // LANES)
    lane = lax.broadcasted_iota(jnp.int32, (pieces[0][0].shape[0], LANES), 1)
    for value, start, count, here in pieces:
        shift = (here - start) % LANES
        for a in range(start // LANES, (start + count - 1) // LANES + 1):
            part = value[:, a * LANES : (a + 1) * LANES]
            if shift:
                part = pltpu.roll(part, shift, 1)
            first = max(start, a * LANES) - start + here
            last = min(start + count, (a + 1) * LANES) - start + here
            for v in range(first // LANES, (last - 1) // LANES + 1):
                low, high = max(first - v * LANES, 0), min(last - v * LANES, LANES)
                if out[v] is None:
                    out[v] = part
                else:
                    out[v] = jnp.where((lane >= low) & (lane < high), part, out[v])
    return out


def synth_kernel(info, recv_ref, table_ref, twiddle_ref, *refs):
    *out_refs, coef, grid = refs
    sources, levels, rows, _ = recv_ref.shape
    fields, waves = coef.shape[0] // 2, coef.shape[1] * LANES
    share = waves // sources
    each, _, turns = twiddle_ref.shape[:3]
    pitch = rows + 1
    step = pl.program_id(0)

    @pl.when(step == 0)
    def _():
        def level(l, carry):
            values = [recv_ref[s, l].astype(F32) for s in range(sources)]
            for r in range(2 * fields):
                windows = [
                    (values[s], r * share, share, s * share) for s in range(sources)
                ]
                for v, part in enumerate(place(windows, waves)):
                    coef[r, v, pl.ds(l * pitch, rows), :] = part
            return carry

        lax.fori_loop(0, levels, level, 0)

    for k in range(each):
        j = step * each + k

        def own_row(r):
            parts = [coef[r, v, pl.ds(j, levels, stride=pitch), :] for v in range(waves // LANES)]
            return jnp.concatenate(parts, axis=1)

        values = [own_row(r) for r in range(2 * fields)]
        real, imag = [], []
        for t in range(turns):
            c, s = twiddle_ref[k, 0, t : t + 1], twiddle_ref[k, 1, t : t + 1]
            for f in range(fields):
                re, im = values[2 * f], values[2 * f + 1]
                real.append(re * c - im * s)
                imag.append(re * s + im * c)
        both = [jnp.concatenate(part, axis=0).astype(BF16) for part in (real, imag)]
        result = dot(jnp.concatenate(both, axis=1), table_ref[k], ((1,), (0,)))
        grid[pl.ds(j, turns * fields * levels, stride=pitch), :] = result

    @pl.when(step == pl.num_programs(0) - 1)
    def _():
        tiles = turns // len(out_refs)
        for k, out_ref in enumerate(out_refs):
            for t in range(tiles):
                for f in range(fields):
                    start = (((info[ME] ^ k) * tiles + t) * fields + f) * levels
                    for l in range(levels):
                        block = grid[pl.ds((start + l) * pitch, rows), :].astype(BF16)
                        out_ref[f, l, :, t * LANES : (t + 1) * LANES] = block


def synthesis(recv, table, twiddle, info, dests, tile):
    sources, levels, rows, lanes = recv.shape
    turns, waves = twiddle.shape[2:]
    fields = 3
    each = STEP if rows % STEP == 0 else 1
    shape = (fields, levels, rows, tile)
    return pl.pallas_call(
        synth_kernel,
        grid_spec=pltpu.PrefetchScalarGridSpec(
            num_scalar_prefetch=1,
            grid=(rows // each,),
            in_specs=[
                pl.BlockSpec(recv.shape, lambda j, info: (0, 0, 0, 0)),
                pl.BlockSpec((each, 2 * waves, LANES), lambda j, info: (j, 0, 0)),
                pl.BlockSpec((each, 2, turns, waves), lambda j, info: (j, 0, 0, 0)),
            ],
            out_specs=[pl.BlockSpec(shape, lambda j, info: (0, 0, 0, 0))] * dests,
            scratch_shapes=[
                pltpu.VMEM((2 * fields, waves // LANES, levels * (rows + 1), LANES), F32),
                pltpu.VMEM((turns * fields * levels * (rows + 1), LANES), F32),
            ],
        ),
        out_shape=[jax.ShapeDtypeStruct(shape, BF16)] * dests,
        compiler_params=pltpu.CompilerParams(vmem_limit_bytes=24 * MIB),
        cost_estimate=cost(4 * rows * waves * fields * levels * turns * LANES, 4 * rows * waves * LANES),
        name="synthesis",
    )(info, recv, table, twiddle)


def edge_kernel(
    info, state_ref, base_ref, temp_ref, row_a_ref, row_b_ref, col_a_ref, col_b_ref, react_ref
):
    tracers, levels, rows, tile = state_ref.shape
    cells = tracers * rows

    @pl.when(pl.program_id(0) == 0)
    def _():
        rates = jnp.concatenate([base_ref[...], temp_ref[...]], axis=0)
        high = rates.astype(BF16)
        low = (rates - high.astype(F32)).astype(BF16)

        def iota(shape, axis):
            return lax.broadcasted_iota(jnp.int32, shape, axis)

        shape = (2 * cells, 2 * tracers)
        down = jnp.where(iota(shape, 0) // rows == iota(shape, 1), 1.0, 0.0).astype(BF16)
        shape = (tracers, cells)
        over = jnp.where(iota(shape, 0) == iota(shape, 1) // rows, 1.0, 0.0).astype(BF16)
        shape = (2 * cells, cells)
        same = iota(shape, 0) % rows == iota(shape, 1) % rows
        for k, part in enumerate((high, low)):
            wide = dot(dot(down, part, ((1,), (0,))).astype(BF16), over, ((1,), (0,)))
            react_ref[:, k * cells : (k + 1) * cells] = jnp.where(same, wide, 0.0).astype(BF16)

    def iota(shape, axis):
        return lax.broadcasted_iota(jnp.int32, shape, axis)

    odd = info[BAND] % 2, info[ME] % 2
    far, near = (1 - odd[0]) * (rows - 1), odd[0] * (rows - 1)
    shape = (2 * tracers, cells)
    end = jnp.where(iota(shape, 0) < tracers, far, near)
    pick = iota(shape, 1) == (iota(shape, 0) % tracers) * rows + end
    pick = jnp.where(pick, 1.0, 0.0).astype(BF16)
    shape = (tile, 2 * LANES)
    far, near = (1 - odd[1]) * (tile - 1), odd[1] * (tile - 1)
    is_end = iota(shape, 0) == jnp.where(iota(shape, 1) < LANES, far, near)
    level = iota(shape, 1) % LANES - pl.program_id(0) * levels
    columns = jnp.zeros((cells, 2 * LANES), F32)
    for l in range(levels):
        x = state_ref[:, l].reshape(cells, tile)
        picked = dot(pick, x, ((1,), (0,)))
        row_a_ref[l] = picked[:tracers].astype(BF16)
        row_b_ref[l] = picked[tracers:].astype(BF16)
        mark = jnp.where(is_end & (level == l), 1.0, 0.0).astype(BF16)
        columns = columns + dot(x, mark, ((1,), (0,)))

    @pl.when(pl.program_id(0) == 0)
    def _():
        col_a_ref[...] = columns[:, :LANES].astype(BF16)
        col_b_ref[...] = columns[:, LANES:].astype(BF16)

    @pl.when(pl.program_id(0) > 0)
    def _():
        col_a_ref[...] = (col_a_ref[...].astype(F32) + columns[:, :LANES]).astype(BF16)
        col_b_ref[...] = (col_b_ref[...].astype(F32) + columns[:, LANES:]).astype(BF16)


def edges(state, react_base, react_temp, info):
    tracers, levels, rows, tile = state.shape
    block = 16
    cells = tracers * rows
    rowed = jax.ShapeDtypeStruct((levels, tracers, tile), BF16)
    columned = jax.ShapeDtypeStruct((cells, LANES), BF16)
    row_spec = pl.BlockSpec((block, tracers, tile), lambda i, info: (i, 0, 0))
    col_spec = pl.BlockSpec((cells, LANES), lambda i, info: (0, 0))
    wide = (2 * cells, 2 * cells)
    return pl.pallas_call(
        edge_kernel,
        grid_spec=pltpu.PrefetchScalarGridSpec(
            num_scalar_prefetch=1,
            grid=(levels // block,),
            in_specs=[
                pl.BlockSpec((tracers, block, rows, tile), lambda i, info: (0, i, 0, 0)),
                pl.BlockSpec(react_base.shape, lambda i, info: (0, 0)),
                pl.BlockSpec(react_temp.shape, lambda i, info: (0, 0)),
            ],
            out_specs=[
                row_spec, row_spec, col_spec, col_spec, pl.BlockSpec(wide, lambda i, info: (0, 0)),
            ],
        ),
        out_shape=[rowed, rowed, columned, columned, jax.ShapeDtypeStruct(wide, BF16)],
        compiler_params=pltpu.CompilerParams(vmem_limit_bytes=52 * MIB),
        cost_estimate=cost(4 * state.size * 32, 2 * state.size),
        name="edges",
    )(info, state, react_base, react_temp)


def shifted(value, outer, axis, step):
    size = value[0].shape[axis]
    turned = [pltpu.roll(v, -step % size, axis) for v in value]
    place = lax.broadcasted_iota(jnp.int32, value[0].shape, axis)
    at_end = place == (size - 1 if step == 1 else 0)
    following = turned[1:] + [outer] if step == 1 else [outer] + turned[:-1]
    return [jnp.where(at_end, f, t) for f, t in zip(following, turned)]


def chem_kernel(scale, k, info, *refs):
    state_ref, row_a_ref, row_b_ref, col_a_ref, col_b_ref, grid_ref, react_ref = refs[:7]
    new_ref, active_ref, south, north, advected, rounded = refs[-6:]
    tracers, levels, rows, tile = state_ref.shape
    cells = tracers * rows
    odd_band, odd_tile = info[BAND] % 2 == 1, info[ME] % 2 == 1
    first = ((info[ME] ^ k) * pl.num_programs(0) + pl.program_id(0)) * levels

    def column(value):
        return pltpu.roll(value, lax.rem(LANES - first, LANES), 1)

    a, b = col_a_ref[...].astype(F32), col_b_ref[...].astype(F32)
    west, east = column(jnp.where(odd_tile, a, b)), column(jnp.where(odd_tile, b, a))
    row = lax.broadcasted_iota(jnp.int32, (rows, tile), 0)
    lane = lax.broadcasted_iota(jnp.int32, (rows, tile), 1)
    ids, points = IDS, IDS + active_ref.shape[0]
    count = jnp.full((rows, tile), info[points], jnp.int32)
    for j in range(1, rows):
        count = jnp.where(row == j, info[points + j], count)
    mask = jnp.where(info[ME] * tile + lane < count, 1.0, 0.0)
    across = [slice(v * LANES, (v + 1) * LANES) for v in range(tile // LANES)]
    along = [slice(v * SUBLANES, (v + 1) * SUBLANES) for v in range(rows // SUBLANES)]

    for l in range(levels):
        wind_u = grid_ref[0, l].astype(F32) * (scale * 0.1)
        wind_v = grid_ref[1, l].astype(F32) * (scale * 0.1)
        from_east, from_west = 0.05 - wind_u, 0.05 + wind_u
        from_north, from_south = 0.05 - wind_v, 0.05 + wind_v
        a, b = row_a_ref[l].astype(F32), row_b_ref[l].astype(F32)
        south[l] = jnp.where(odd_band, a, b)
        north[l] = jnp.where(odd_band, b, a)
        for t in range(tracers):
            cell = slice(t * rows, (t + 1) * rows)
            x = state_ref[t, l].astype(F32)
            outer = [jnp.broadcast_to(col[cell, l : l + 1], (rows, LANES)) for col in (east, west)]
            parts = [x[:, v] for v in across]
            qe = jnp.concatenate(shifted(parts, outer[0], 1, 1), axis=1)
            qw = jnp.concatenate(shifted(parts, outer[1], 1, -1), axis=1)
            shape = (SUBLANES, tile)
            outer = [jnp.broadcast_to(ref[l, t : t + 1], shape) for ref in (north, south)]
            parts = [x[v] for v in along]
            qn = jnp.concatenate(shifted(parts, outer[0], 0, 1), axis=0)
            qs = jnp.concatenate(shifted(parts, outer[1], 0, -1), axis=0)
            moved = 0.8 * x + from_east * qe + from_west * qw + from_north * qn + from_south * qs
            advected[l, cell] = moved
            rounded[l, cell] = moved.astype(BF16)
    for l in range(levels):
        temper = grid_ref[2, l].astype(F32) * scale
        high = rounded[l]
        terms = dot(react_ref[...], jnp.concatenate([high, high], axis=0), ((1,), (0,)))
        for t in range(tracers):
            cell = slice(t * rows, (t + 1) * rows)
            warm = slice(cells + t * rows, cells + (t + 1) * rows)
            reacted = (advected[l, cell] + terms[cell] + temper * terms[warm]) * mask
            new_ref[t, l] = reacted.astype(BF16)
    for a in range(active_ref.shape[0]):
        active_ref[a] = new_ref[info[ids + a]]


def chemistry(state, halos, grid, react, info, k, actives, waves, before):
    tracers, levels, rows, tile = state.shape
    fields, own = grid.shape[:2]
    some = 4 if own % 4 == 0 else own
    steps = own // some
    cells = tracers * rows
    scale = 1.0 / float(np.sqrt(np.float32(waves)))

    def whole(shape):
        return pl.BlockSpec(shape, lambda i, info: (0,) * len(shape))

    row_spec = pl.BlockSpec((some, tracers, tile), lambda i, info: ((info[ME] ^ k) * steps + i, 0, 0))
    state_spec = pl.BlockSpec(
        (tracers, some, rows, tile), lambda i, info: (0, (info[ME] ^ k) * steps + i, 0, 0)
    )
    operands = [state, *halos, grid, react]
    in_specs = [
        state_spec,
        row_spec,
        row_spec,
        whole(halos[2].shape),
        whole(halos[3].shape),
        pl.BlockSpec((fields, some, rows, tile), lambda i, info: (0, i, 0, 0)),
        whole(react.shape),
    ]
    aliases = {}
    if before is not None:
        aliases = {1 + len(operands): 0}
        operands.append(before)
        in_specs.append(pl.BlockSpec(memory_space=pl.ANY))
    return pl.pallas_call(
        functools.partial(chem_kernel, scale, k),
        grid_spec=pltpu.PrefetchScalarGridSpec(
            num_scalar_prefetch=1,
            grid=(steps,),
            in_specs=in_specs,
            out_specs=[
                state_spec,
                pl.BlockSpec((actives, some, rows, tile), lambda i, info: (0, i, 0, 0)),
            ],
            scratch_shapes=[
                pltpu.VMEM((some, tracers, tile), F32),
                pltpu.VMEM((some, tracers, tile), F32),
                pltpu.VMEM((some, cells, tile), F32),
                pltpu.VMEM((some, cells, tile), BF16),
            ],
        ),
        out_shape=[
            jax.ShapeDtypeStruct(state.shape, BF16),
            jax.ShapeDtypeStruct((actives, own, rows, tile), BF16),
        ],
        input_output_aliases=aliases,
        compiler_params=pltpu.CompilerParams(vmem_limit_bytes=16 * MIB),
        cost_estimate=cost(own * cells * tile, own * tile),
        name="chemistry",
    )(info, *operands)


def spread_kernel(info, recv_ref, *refs):
    refs[-1][...] = recv_ref[...].astype(F32)


def spread(recv, info, k, sources, before):
    actives, own, rows, tile = recv.shape
    each = 2 if actives % 2 == 0 else 1
    operands = [recv]
    in_specs = [pl.BlockSpec((each, own, rows, tile), lambda a, info: (a, 0, 0, 0))]
    aliases = {}
    if before is not None:
        operands.append(before)
        in_specs.append(pl.BlockSpec(memory_space=pl.ANY))
        aliases = {2: 0}
    return pl.pallas_call(
        spread_kernel,
        grid_spec=pltpu.PrefetchScalarGridSpec(
            num_scalar_prefetch=1,
            grid=(actives // each,),
            in_specs=in_specs,
            out_specs=pl.BlockSpec((each, own, rows, tile), lambda a, info: (a, 0, 0, info[ME] ^ k)),
        ),
        out_shape=jax.ShapeDtypeStruct((actives, own, rows, sources * tile), F32),
        input_output_aliases=aliases,
        compiler_params=pltpu.CompilerParams(vmem_limit_bytes=8 * MIB),
        cost_estimate=cost(recv.size, recv.shape[0]),
        name="spread",
    )(info, *operands)


def legendre_kernel(points, waves_ref, spectral_ref, legendre_ref, *refs):
    out_ref, table_ref, twiddle_ref, rows_of, sums = refs
    parts, own, block, size = spectral_ref.shape
    bands, _, rows, pitch = out_ref.shape
    share = block * pl.num_programs(0)
    step = pl.program_id(0)
    lines = parts * own
    apart, stretch = block + 1, pitch + 1

    @pl.when(step == 0)
    def _():
        for h in range(sums.shape[0]):
            for l in range(own):
                tail = pl.ds(l * stretch + parts * share, pitch - parts * share)
                sums[h, tail, :] = jnp.zeros((pitch - parts * share, LANES), F32)

    each = table_ref.shape[0]
    first = jnp.minimum(step, points.shape[0] // each - 1) * each
    make_tables(points, first, waves_ref[...].astype(F32), table_ref, twiddle_ref)

    for v in range(size // LANES):
        part = spectral_ref[:, :, :, v * LANES : (v + 1) * LANES].astype(F32)
        part = part.reshape(lines, block, LANES)
        for i in range(lines):
            rows_of[v, pl.ds(i * apart, block), :] = part[i]
    for m in range(block):
        x = [rows_of[v, pl.ds(m, lines, stride=apart), :] for v in range(size // LANES)]
        x = jnp.concatenate(x, axis=1).astype(BF16)
        result = dot(x, legendre_ref[m], ((1,), (0,)))
        for r in range(parts):
            at = r * share + step * block + m
            for h in range(sums.shape[0]):
                piece = result[r * own : (r + 1) * own, h * LANES : (h + 1) * LANES]
                sums[h, pl.ds(at, own, stride=stretch), :] = piece

    @pl.when(step == pl.num_programs(0) - 1)
    def _():
        some = LANES // rows
        for l in range(own):
            for h in range(sums.shape[0]):
                turned = sums[h, pl.ds(l * stretch, pitch), :].T.astype(BF16)
                out_ref[h * some : (h + 1) * some, l] = turned.reshape(some, rows, pitch)


def legendre_sums(spectral, legendre, points, wave_ids, bands, turns):
    parts, own, share, size = spectral.shape
    waves, count = wave_ids.shape[0], points.shape[0]
    rows = legendre.shape[2] // bands
    pitch = -(-parts * share // LANES) * LANES
    block = 16 if share % 16 == 0 else 8
    steps = share // block
    each = min(e for e in range(1, count + 1) if count % e == 0 and e * steps >= count)
    shape = (bands, own, rows, pitch)

    def of_rows(i, points):
        return jnp.minimum(i, count // each - 1)

    return pl.pallas_call(
        legendre_kernel,
        grid_spec=pltpu.PrefetchScalarGridSpec(
            num_scalar_prefetch=1,
            grid=(steps,),
            in_specs=[
                pl.BlockSpec((1, waves), lambda i, points: (0, 0)),
                pl.BlockSpec((parts, own, block, size), lambda i, points: (0, 0, i, 0)),
                pl.BlockSpec((block,) + legendre.shape[1:], lambda i, points: (i, 0, 0)),
            ],
            out_specs=[
                pl.BlockSpec(shape, lambda i, points: (0, 0, 0, 0)),
                pl.BlockSpec((each, 2 * waves, LANES), lambda i, p: (of_rows(i, p), 0, 0)),
                pl.BlockSpec((each, 2, turns, waves), lambda i, p: (of_rows(i, p), 0, 0, 0)),
            ],
            scratch_shapes=[
                pltpu.VMEM((size // LANES, parts * own * (block + 1), LANES), F32),
                pltpu.VMEM((legendre.shape[2] // LANES, own * (pitch + 1), LANES), F32),
            ],
        ),
        out_shape=[
            jax.ShapeDtypeStruct(shape, BF16),
            jax.ShapeDtypeStruct((count, 2 * waves, LANES), BF16),
            jax.ShapeDtypeStruct((count, 2, turns, waves), F32),
        ],
        compiler_params=pltpu.CompilerParams(vmem_limit_bytes=56 * MIB),
        cost_estimate=cost(2 * parts * own * legendre.size, 2 * (spectral.size + legendre.size)),
        name="legendre",
    )(points, wave_ids[None, :], spectral, legendre)


def exchange(value, axis, pairs):
    return lax.ppermute(value, axis, [p for a, b in pairs for p in ((a, b), (b, a))])


def neighbours(axis, first):
    size = lax.axis_size(axis)
    return [(i, i + 1) for i in range(first, size - 1, 2)]


def partners(axis, k):
    return [(i, i ^ k) for i in range(lax.axis_size(axis)) if i < i ^ k]


def body(spectral, legendre, wave_ids, points, tracers, react_base, react_temp, active_ids):
    bands, tiles = lax.axis_size("lat"), lax.axis_size("lon")
    tile = tracers.shape[3]
    waves, rows = wave_ids.shape[0], points.shape[0]
    band, me = lax.axis_index("lat"), lax.axis_index("lon")

    sent, table, twiddle = legendre_sums(
        spectral, legendre, points, wave_ids, bands, tiles * tile // LANES
    )
    info = jnp.concatenate([jnp.stack([band, me]), active_ids, points]).astype(jnp.int32)
    sent, info = lax.optimization_barrier((sent, info))
    recv = lax.all_to_all(sent, "lat", split_axis=0, concat_axis=0, tiled=True)
    *ends, react = edges(tracers, react_base, react_temp, info)
    halos = [
        exchange(ends[0], "lat", neighbours("lat", 0)),
        exchange(ends[1], "lat", neighbours("lat", 1)),
        exchange(ends[2], "lon", neighbours("lon", 0)),
        exchange(ends[3], "lon", neighbours("lon", 1)),
    ]
    recv, react, halos = lax.optimization_barrier((recv, react, halos))
    grids = synthesis(recv, table, twiddle, info, tiles, tile)

    middle, inner = list(range(tiles // 2, tiles)), list(range(1, tiles // 2))
    soon, late = middle[: tiles // 4], middle[tiles // 4 :]

    def send(value, k):
        return exchange(value, "lon", partners("lon", k))

    moved = {0: grids[0]} | {k: send(grids[k], k) for k in soon}
    new, active = None, {}
    for k in [0] + soon + late + inner:
        new, active[k] = chemistry(
            tracers, halos, moved[k], react, info, k, active_ids.shape[0], waves, new
        )
        if k:
            active[k] = send(active[k], k)
        else:
            rest = late + inner
            held, active[0] = lax.optimization_barrier(([grids[i] for i in rest], active[0]))
            moved |= {i: send(value, i) for i, value in zip(rest, held)}
    spreaded = None
    for k in [0] + soon + inner + late:
        spreaded = spread(active[k], info, k, tiles, spreaded)
    return new, spreaded


def solution(mesh):
    return jax.shard_map(
        body,
        mesh=mesh,
        in_specs=(
            P(None, "lon", "lat", None),
            P("lat", None, None),
            P(),
            P("lat"),
            P(None, None, "lat", "lon"),
            P(),
            P(),
            P(),
        ),
        out_specs=(P(None, None, "lat", "lon"), P(None, "lon", "lat", None)),
        check_vma=False,
    )
```

```python
import functools

import jax
import jax.numpy as jnp
import numpy as np
from jax import lax
from jax.experimental import pallas as pl
from jax.experimental.pallas import tpu as pltpu
from jax.sharding import PartitionSpec as P

F32 = jnp.float32
BF16 = jnp.bfloat16
LANES = 128
SUBLANES = 8
LOW = 16
STEP = 4
MIB = 1024 * 1024

COS = (
    0.9999999890590228,
    -19.739204499454026,
    64.93911745990036,
    -85.45013953095037,
    60.16763095136588,
    -25.96759924965491,
    6.528658162567069,
)
SIN = (
    6.283185302511503,
    -41.34170040531769,
    81.60513138580204,
    -76.7030153539128,
    42.02592698618416,
    -14.899846668691637,
    3.238137510515757,
)


def dot(a, b, dims):
    return lax.dot_general(a, b, (dims, ((), ())), preferred_element_type=F32)


BAND, ME, IDS = 0, 1, 2


def cost(flops, moved):
    return pl.CostEstimate(flops=int(flops), bytes_accessed=int(moved), transcendentals=0)


def unit_circle(step, rows, waves, count):
    index = lax.broadcasted_iota(jnp.int32, (rows, waves.shape[1]), 0) * step
    product = index.astype(F32) * waves
    inverse = 1.0 / count
    turns = (product - jnp.floor(product * inverse) * count) * inverse
    y = turns - jnp.floor(turns + 0.5)
    z = y * y
    cosine = jnp.full_like(z, COS[-1])
    sine = jnp.full_like(z, SIN[-1])
    for c, s in zip(COS[-2::-1], SIN[-2::-1]):
        cosine = cosine * z + c
        sine = sine * z + s
    return cosine, sine * y


def table_kernel(first, info, waves_ref, table_ref, twiddle_ref):
    size, turns = waves_ref.shape[1], twiddle_ref.shape[2]
    waves = waves_ref[...].astype(F32)
    for k in range(table_ref.shape[0]):
        row = pl.program_id(0) * table_ref.shape[0] + k
        count = jnp.full(waves.shape, info[first + row], jnp.int32).astype(F32)
        cos_low, sin_low = unit_circle(1, LOW, waves, count)
        cos_high, sin_high = unit_circle(LOW, LANES // LOW, waves, count)
        cosine, sine = [], []
        for a in range(LANES // LOW):
            ch, sh = cos_high[a : a + 1], sin_high[a : a + 1]
            cosine.append(ch * cos_low - sh * sin_low)
            sine.append(-sh * cos_low - ch * sin_low)
        table_ref[k, :size, :] = jnp.concatenate(cosine, axis=0).T.astype(BF16)
        table_ref[k, size:, :] = jnp.concatenate(sine, axis=0).T.astype(BF16)
        cos_turn, sin_turn = unit_circle(LANES, turns, waves, count)
        twiddle_ref[k, 0] = cos_turn
        twiddle_ref[k, 1] = sin_turn


def tables(info, wave_ids, rows, turns):
    waves = wave_ids.shape[0]
    each = STEP if rows % STEP == 0 else 1
    return pl.pallas_call(
        functools.partial(table_kernel, info.shape[0] - rows),
        grid_spec=pltpu.PrefetchScalarGridSpec(
            num_scalar_prefetch=1,
            grid=(rows // each,),
            in_specs=[pl.BlockSpec((1, waves), lambda j, p: (0, 0))],
            out_specs=[
                pl.BlockSpec((each, 2 * waves, LANES), lambda j, p: (j, 0, 0)),
                pl.BlockSpec((each, 2, turns, waves), lambda j, p: (j, 0, 0, 0)),
            ],
        ),
        out_shape=[
            pltpu.VMEM((rows, 2 * waves, LANES), BF16),
            pltpu.VMEM((rows, 2, turns, waves), F32),
        ],
        compiler_params=pltpu.CompilerParams(vmem_limit_bytes=20 * MIB),
        cost_estimate=cost(rows * waves * LANES * 8, rows * waves * LANES * 4),
        name="tables",
    )(info, wave_ids[None, :])


def place(pieces, width):
    out = [None] * (width // LANES)
    lane = lax.broadcasted_iota(jnp.int32, (pieces[0][0].shape[0], LANES), 1)
    for value, start, count, here in pieces:
        shift = (here - start) % LANES
        for a in range(start // LANES, (start + count - 1) // LANES + 1):
            part = value[:, a * LANES : (a + 1) * LANES]
            if shift:
                part = pltpu.roll(part, shift, 1)
            first = max(start, a * LANES) - start + here
            last = min(start + count, (a + 1) * LANES) - start + here
            for v in range(first // LANES, (last - 1) // LANES + 1):
                low, high = max(first - v * LANES, 0), min(last - v * LANES, LANES)
                if out[v] is None:
                    out[v] = part
                else:
                    out[v] = jnp.where((lane >= low) & (lane < high), part, out[v])
    return out


def synth_kernel(info, recv_ref, table_ref, twiddle_ref, *refs):
    *out_refs, coef, grid = refs
    sources, levels, rows, _ = recv_ref.shape
    fields, waves = coef.shape[0] // 2, coef.shape[1] * LANES
    share = waves // sources
    each, _, turns = twiddle_ref.shape[:3]
    pitch = rows + 1
    step = pl.program_id(0)

    @pl.when(step == 0)
    def _():
        def level(l, carry):
            values = [recv_ref[s, l].astype(F32) for s in range(sources)]
            for r in range(2 * fields):
                windows = [
                    (values[s], r * share, share, s * share) for s in range(sources)
                ]
                for v, part in enumerate(place(windows, waves)):
                    coef[r, v, pl.ds(l * pitch, rows), :] = part
            return carry

        lax.fori_loop(0, levels, level, 0)

    for k in range(each):
        j = step * each + k

        def own_row(r):
            parts = [coef[r, v, pl.ds(j, levels, stride=pitch), :] for v in range(waves // LANES)]
            return jnp.concatenate(parts, axis=1)

        values = [own_row(r) for r in range(2 * fields)]
        real, imag = [], []
        for t in range(turns):
            c, s = twiddle_ref[k, 0, t : t + 1], twiddle_ref[k, 1, t : t + 1]
            for f in range(fields):
                re, im = values[2 * f], values[2 * f + 1]
                real.append(re * c - im * s)
                imag.append(re * s + im * c)
        both = [jnp.concatenate(part, axis=0).astype(BF16) for part in (real, imag)]
        result = dot(jnp.concatenate(both, axis=1), table_ref[k], ((1,), (0,)))
        grid[pl.ds(j, turns * fields * levels, stride=pitch), :] = result

    @pl.when(step == pl.num_programs(0) - 1)
    def _():
        tiles = turns // len(out_refs)
        for k, out_ref in enumerate(out_refs):
            for t in range(tiles):
                for f in range(fields):
                    start = (((info[ME] ^ k) * tiles + t) * fields + f) * levels
                    for l in range(levels):
                        block = grid[pl.ds((start + l) * pitch, rows), :].astype(BF16)
                        out_ref[f, l, :, t * LANES : (t + 1) * LANES] = block


def synthesis(recv, table, twiddle, info, dests, tile):
    sources, levels, rows, lanes = recv.shape
    turns, waves = twiddle.shape[2:]
    fields = 3
    each = STEP if rows % STEP == 0 else 1
    shape = (fields, levels, rows, tile)
    return pl.pallas_call(
        synth_kernel,
        grid_spec=pltpu.PrefetchScalarGridSpec(
            num_scalar_prefetch=1,
            grid=(rows // each,),
            in_specs=[
                pl.BlockSpec(recv.shape, lambda j, info: (0, 0, 0, 0)),
                pl.BlockSpec((each, 2 * waves, LANES), lambda j, info: (j, 0, 0)),
                pl.BlockSpec((each, 2, turns, waves), lambda j, info: (j, 0, 0, 0)),
            ],
            out_specs=[pl.BlockSpec(shape, lambda j, info: (0, 0, 0, 0))] * dests,
            scratch_shapes=[
                pltpu.VMEM((2 * fields, waves // LANES, levels * (rows + 1), LANES), F32),
                pltpu.VMEM((turns * fields * levels * (rows + 1), LANES), F32),
            ],
        ),
        out_shape=[jax.ShapeDtypeStruct(shape, BF16)] * dests,
        compiler_params=pltpu.CompilerParams(vmem_limit_bytes=24 * MIB),
        cost_estimate=cost(4 * rows * waves * fields * levels * turns * LANES, 4 * rows * waves * LANES),
        name="synthesis",
    )(info, recv, *[pltpu.with_memory_space_constraint(v, pltpu.VMEM) for v in (table, twiddle)])


def edge_kernel(
    info, state_ref, base_ref, temp_ref, row_a_ref, row_b_ref, col_a_ref, col_b_ref, react_ref
):
    tracers, levels, rows, tile = state_ref.shape
    cells = tracers * rows

    @pl.when(pl.program_id(0) == 0)
    def _():
        rates = jnp.concatenate([base_ref[...], temp_ref[...]], axis=0)
        high = rates.astype(BF16)
        low = (rates - high.astype(F32)).astype(BF16)

        def iota(shape, axis):
            return lax.broadcasted_iota(jnp.int32, shape, axis)

        shape = (2 * cells, 2 * tracers)
        down = jnp.where(iota(shape, 0) // rows == iota(shape, 1), 1.0, 0.0).astype(BF16)
        shape = (tracers, cells)
        over = jnp.where(iota(shape, 0) == iota(shape, 1) // rows, 1.0, 0.0).astype(BF16)
        shape = (2 * cells, cells)
        same = iota(shape, 0) % rows == iota(shape, 1) % rows
        for k, part in enumerate((high, low)):
            wide = dot(dot(down, part, ((1,), (0,))).astype(BF16), over, ((1,), (0,)))
            react_ref[:, k * cells : (k + 1) * cells] = jnp.where(same, wide, 0.0).astype(BF16)

    def iota(shape, axis):
        return lax.broadcasted_iota(jnp.int32, shape, axis)

    odd = info[BAND] % 2, info[ME] % 2
    far, near = (1 - odd[0]) * (rows - 1), odd[0] * (rows - 1)
    shape = (2 * tracers, cells)
    end = jnp.where(iota(shape, 0) < tracers, far, near)
    pick = iota(shape, 1) == (iota(shape, 0) % tracers) * rows + end
    pick = jnp.where(pick, 1.0, 0.0).astype(BF16)
    shape = (tile, 2 * LANES)
    far, near = (1 - odd[1]) * (tile - 1), odd[1] * (tile - 1)
    is_end = iota(shape, 0) == jnp.where(iota(shape, 1) < LANES, far, near)
    level = iota(shape, 1) % LANES - pl.program_id(0) * levels
    columns = jnp.zeros((cells, 2 * LANES), F32)
    for l in range(levels):
        x = state_ref[:, l].reshape(cells, tile)
        picked = dot(pick, x, ((1,), (0,)))
        row_a_ref[l] = picked[:tracers].astype(BF16)
        row_b_ref[l] = picked[tracers:].astype(BF16)
        mark = jnp.where(is_end & (level == l), 1.0, 0.0).astype(BF16)
        columns = columns + dot(x, mark, ((1,), (0,)))

    @pl.when(pl.program_id(0) == 0)
    def _():
        col_a_ref[...] = columns[:, :LANES].astype(BF16)
        col_b_ref[...] = columns[:, LANES:].astype(BF16)

    @pl.when(pl.program_id(0) > 0)
    def _():
        col_a_ref[...] = (col_a_ref[...].astype(F32) + columns[:, :LANES]).astype(BF16)
        col_b_ref[...] = (col_b_ref[...].astype(F32) + columns[:, LANES:]).astype(BF16)


def edges(state, react_base, react_temp, info):
    tracers, levels, rows, tile = state.shape
    block = 16
    cells = tracers * rows
    rowed = jax.ShapeDtypeStruct((levels, tracers, tile), BF16)
    columned = jax.ShapeDtypeStruct((cells, LANES), BF16)
    row_spec = pl.BlockSpec((block, tracers, tile), lambda i, info: (i, 0, 0))
    col_spec = pl.BlockSpec((cells, LANES), lambda i, info: (0, 0))
    wide = (2 * cells, 2 * cells)
    return pl.pallas_call(
        edge_kernel,
        grid_spec=pltpu.PrefetchScalarGridSpec(
            num_scalar_prefetch=1,
            grid=(levels // block,),
            in_specs=[
                pl.BlockSpec((tracers, block, rows, tile), lambda i, info: (0, i, 0, 0)),
                pl.BlockSpec(react_base.shape, lambda i, info: (0, 0)),
                pl.BlockSpec(react_temp.shape, lambda i, info: (0, 0)),
            ],
            out_specs=[
                row_spec, row_spec, col_spec, col_spec, pl.BlockSpec(wide, lambda i, info: (0, 0)),
            ],
        ),
        out_shape=[rowed, rowed, columned, columned, jax.ShapeDtypeStruct(wide, BF16)],
        compiler_params=pltpu.CompilerParams(vmem_limit_bytes=52 * MIB),
        cost_estimate=cost(4 * state.size * 32, 2 * state.size),
        name="edges",
    )(info, state, react_base, react_temp)


def shifted(value, outer, axis, step):
    size = value[0].shape[axis]
    turned = [pltpu.roll(v, -step % size, axis) for v in value]
    place = lax.broadcasted_iota(jnp.int32, value[0].shape, axis)
    at_end = place == (size - 1 if step == 1 else 0)
    following = turned[1:] + [outer] if step == 1 else [outer] + turned[:-1]
    return [jnp.where(at_end, f, t) for f, t in zip(following, turned)]


def chem_kernel(scale, k, info, *refs):
    state_ref, row_a_ref, row_b_ref, col_a_ref, col_b_ref, grid_ref, react_ref = refs[:7]
    new_ref, active_ref, south, north, advected, rounded = refs[-6:]
    tracers, levels, rows, tile = state_ref.shape
    cells = tracers * rows
    odd_band, odd_tile = info[BAND] % 2 == 1, info[ME] % 2 == 1
    first = ((info[ME] ^ k) * pl.num_programs(0) + pl.program_id(0)) * levels

    def column(value):
        return pltpu.roll(value, lax.rem(LANES - first, LANES), 1)

    a, b = col_a_ref[...].astype(F32), col_b_ref[...].astype(F32)
    west, east = column(jnp.where(odd_tile, a, b)), column(jnp.where(odd_tile, b, a))
    row = lax.broadcasted_iota(jnp.int32, (rows, tile), 0)
    lane = lax.broadcasted_iota(jnp.int32, (rows, tile), 1)
    ids, points = IDS, IDS + active_ref.shape[0]
    count = jnp.full((rows, tile), info[points], jnp.int32)
    for j in range(1, rows):
        count = jnp.where(row == j, info[points + j], count)
    mask = jnp.where(info[ME] * tile + lane < count, 1.0, 0.0)
    across = [slice(v * LANES, (v + 1) * LANES) for v in range(tile // LANES)]
    along = [slice(v * SUBLANES, (v + 1) * SUBLANES) for v in range(rows // SUBLANES)]

    for l in range(levels):
        wind_u = grid_ref[0, l].astype(F32) * (scale * 0.1)
        wind_v = grid_ref[1, l].astype(F32) * (scale * 0.1)
        from_east, from_west = 0.05 - wind_u, 0.05 + wind_u
        from_north, from_south = 0.05 - wind_v, 0.05 + wind_v
        a, b = row_a_ref[l].astype(F32), row_b_ref[l].astype(F32)
        south[l] = jnp.where(odd_band, a, b)
        north[l] = jnp.where(odd_band, b, a)
        for t in range(tracers):
            cell = slice(t * rows, (t + 1) * rows)
            x = state_ref[t, l].astype(F32)
            outer = [jnp.broadcast_to(col[cell, l : l + 1], (rows, LANES)) for col in (east, west)]
            parts = [x[:, v] for v in across]
            qe = jnp.concatenate(shifted(parts, outer[0], 1, 1), axis=1)
            qw = jnp.concatenate(shifted(parts, outer[1], 1, -1), axis=1)
            shape = (SUBLANES, tile)
            outer = [jnp.broadcast_to(ref[l, t : t + 1], shape) for ref in (north, south)]
            parts = [x[v] for v in along]
            qn = jnp.concatenate(shifted(parts, outer[0], 0, 1), axis=0)
            qs = jnp.concatenate(shifted(parts, outer[1], 0, -1), axis=0)
            moved = 0.8 * x + from_east * qe + from_west * qw + from_north * qn + from_south * qs
            advected[l, cell] = moved
            rounded[l, cell] = moved.astype(BF16)
    for l in range(levels):
        temper = grid_ref[2, l].astype(F32) * scale
        high = rounded[l]
        terms = dot(react_ref[...], jnp.concatenate([high, high], axis=0), ((1,), (0,)))
        for t in range(tracers):
            cell = slice(t * rows, (t + 1) * rows)
            warm = slice(cells + t * rows, cells + (t + 1) * rows)
            reacted = (advected[l, cell] + terms[cell] + temper * terms[warm]) * mask
            new_ref[t, l] = reacted.astype(BF16)
    for a in range(active_ref.shape[0]):
        active_ref[a] = new_ref[info[ids + a]]


def chemistry(state, halos, grid, react, info, k, actives, waves, before):
    tracers, levels, rows, tile = state.shape
    fields, own = grid.shape[:2]
    some = 4 if own % 4 == 0 else own
    steps = own // some
    cells = tracers * rows
    scale = 1.0 / float(np.sqrt(np.float32(waves)))

    def whole(shape):
        return pl.BlockSpec(shape, lambda i, info: (0,) * len(shape))

    row_spec = pl.BlockSpec((some, tracers, tile), lambda i, info: ((info[ME] ^ k) * steps + i, 0, 0))
    state_spec = pl.BlockSpec(
        (tracers, some, rows, tile), lambda i, info: (0, (info[ME] ^ k) * steps + i, 0, 0)
    )
    operands = [state, *halos, grid, react]
    in_specs = [
        state_spec,
        row_spec,
        row_spec,
        whole(halos[2].shape),
        whole(halos[3].shape),
        pl.BlockSpec((fields, some, rows, tile), lambda i, info: (0, i, 0, 0)),
        whole(react.shape),
    ]
    aliases = {}
    if before is not None:
        aliases = {1 + len(operands): 0}
        operands.append(before)
        in_specs.append(pl.BlockSpec(memory_space=pl.ANY))
    return pl.pallas_call(
        functools.partial(chem_kernel, scale, k),
        grid_spec=pltpu.PrefetchScalarGridSpec(
            num_scalar_prefetch=1,
            grid=(steps,),
            in_specs=in_specs,
            out_specs=[
                state_spec,
                pl.BlockSpec((actives, some, rows, tile), lambda i, info: (0, i, 0, 0)),
            ],
            scratch_shapes=[
                pltpu.VMEM((some, tracers, tile), F32),
                pltpu.VMEM((some, tracers, tile), F32),
                pltpu.VMEM((some, cells, tile), F32),
                pltpu.VMEM((some, cells, tile), BF16),
            ],
        ),
        out_shape=[
            jax.ShapeDtypeStruct(state.shape, BF16),
            jax.ShapeDtypeStruct((actives, own, rows, tile), BF16),
        ],
        input_output_aliases=aliases,
        compiler_params=pltpu.CompilerParams(vmem_limit_bytes=16 * MIB),
        cost_estimate=cost(own * cells * tile, own * tile),
        name="chemistry",
    )(info, *operands)


def spread_kernel(info, recv_ref, *refs):
    refs[-1][...] = recv_ref[...].astype(F32)


def spread(recv, info, k, sources, before):
    actives, own, rows, tile = recv.shape
    each = 2 if actives % 2 == 0 else 1
    operands = [recv]
    in_specs = [pl.BlockSpec((each, own, rows, tile), lambda a, info: (a, 0, 0, 0))]
    aliases = {}
    if before is not None:
        operands.append(before)
        in_specs.append(pl.BlockSpec(memory_space=pl.ANY))
        aliases = {2: 0}
    return pl.pallas_call(
        spread_kernel,
        grid_spec=pltpu.PrefetchScalarGridSpec(
            num_scalar_prefetch=1,
            grid=(actives // each,),
            in_specs=in_specs,
            out_specs=pl.BlockSpec((each, own, rows, tile), lambda a, info: (a, 0, 0, info[ME] ^ k)),
        ),
        out_shape=jax.ShapeDtypeStruct((actives, own, rows, sources * tile), F32),
        input_output_aliases=aliases,
        compiler_params=pltpu.CompilerParams(vmem_limit_bytes=8 * MIB),
        cost_estimate=cost(recv.size, recv.shape[0]),
        name="spread",
    )(info, *operands)


def legendre_kernel(spectral_ref, legendre_ref, out_ref, rows_of, sums):
    parts, own, block, size = spectral_ref.shape
    bands, _, rows, pitch = out_ref.shape
    share = block * pl.num_programs(0)
    step = pl.program_id(0)
    lines = parts * own
    apart, stretch = block + 1, pitch + 1

    @pl.when(step == 0)
    def _():
        for h in range(sums.shape[0]):
            for l in range(own):
                tail = pl.ds(l * stretch + parts * share, pitch - parts * share)
                sums[h, tail, :] = jnp.zeros((pitch - parts * share, LANES), F32)

    for v in range(size // LANES):
        part = spectral_ref[:, :, :, v * LANES : (v + 1) * LANES].astype(F32)
        part = part.reshape(lines, block, LANES)
        for i in range(lines):
            rows_of[v, pl.ds(i * apart, block), :] = part[i]
    def line(m):
        x = [rows_of[v, pl.ds(m, lines, stride=apart), :] for v in range(size // LANES)]
        return jnp.concatenate(x, axis=1).astype(BF16)

    wide = legendre_ref.shape[2]
    group = max(1, 2 * LANES // wide)
    for m in range(0, block, group):
        both = range(m, m + group)
        x = jnp.concatenate([line(i) for i in both], axis=0)
        y = jnp.concatenate([legendre_ref[i] for i in both], axis=1)
        product = dot(x, y, ((1,), (0,)))
        for i in both:
            result = product[(i - m) * lines : (i - m + 1) * lines, (i - m) * wide : (i - m + 1) * wide]
            for r in range(parts):
                at = r * share + step * block + i
                for h in range(sums.shape[0]):
                    piece = result[r * own : (r + 1) * own, h * LANES : (h + 1) * LANES]
                    sums[h, pl.ds(at, own, stride=stretch), :] = piece

    @pl.when(step == pl.num_programs(0) - 1)
    def _():
        some = LANES // rows
        for l in range(own):
            for h in range(sums.shape[0]):
                turned = sums[h, pl.ds(l * stretch, pitch), :].T.astype(BF16)
                out_ref[h * some : (h + 1) * some, l] = turned.reshape(some, rows, pitch)


def legendre_sums(spectral, legendre, bands):
    parts, own, share, size = spectral.shape
    rows = legendre.shape[2] // bands
    pitch = -(-parts * share // LANES) * LANES
    block = 16 if share % 16 == 0 else 8
    shape = (bands, own, rows, pitch)
    return pl.pallas_call(
        legendre_kernel,
        grid=(share // block,),
        in_specs=[
            pl.BlockSpec((parts, own, block, size), lambda i: (0, 0, i, 0)),
            pl.BlockSpec((block,) + legendre.shape[1:], lambda i: (i, 0, 0)),
        ],
        out_specs=pl.BlockSpec(shape, lambda i: (0, 0, 0, 0)),
        out_shape=jax.ShapeDtypeStruct(shape, BF16),
        scratch_shapes=[
            pltpu.VMEM((size // LANES, parts * own * (block + 1), LANES), F32),
            pltpu.VMEM((legendre.shape[2] // LANES, own * (pitch + 1), LANES), F32),
        ],
        compiler_params=pltpu.CompilerParams(vmem_limit_bytes=56 * MIB),
        cost_estimate=cost(2 * parts * own * legendre.size, 2 * (spectral.size + legendre.size)),
        name="legendre",
    )(spectral, legendre)


def exchange(value, axis, pairs):
    return lax.ppermute(value, axis, [p for a, b in pairs for p in ((a, b), (b, a))])


def neighbours(axis, first):
    size = lax.axis_size(axis)
    return [(i, i + 1) for i in range(first, size - 1, 2)]


def partners(axis, k):
    return [(i, i ^ k) for i in range(lax.axis_size(axis)) if i < i ^ k]


def body(spectral, legendre, wave_ids, points, tracers, react_base, react_temp, active_ids):
    bands, tiles = lax.axis_size("lat"), lax.axis_size("lon")
    tile = tracers.shape[3]
    waves = wave_ids.shape[0]
    band, me = lax.axis_index("lat"), lax.axis_index("lon")

    sent = legendre_sums(spectral, legendre, bands)

    rows = points.shape[0]
    info = jnp.concatenate([jnp.stack([band, me]), active_ids, points]).astype(jnp.int32)
    sent, info = lax.optimization_barrier((sent, info))
    recv = lax.all_to_all(sent, "lat", split_axis=0, concat_axis=0, tiled=True)
    *ends, react = edges(tracers, react_base, react_temp, info)
    halos = [
        exchange(ends[0], "lat", neighbours("lat", 0)),
        exchange(ends[2], "lon", neighbours("lon", 0)),
        exchange(ends[3], "lon", neighbours("lon", 1)),
    ]
    react, wave_ids = lax.optimization_barrier((react, wave_ids))
    table, twiddle = tables(info, wave_ids, rows, tiles * tile // LANES)
    recv, table, twiddle, react, halos, last = lax.optimization_barrier(
        (recv, table, twiddle, react, halos, ends[1])
    )
    halos.insert(1, exchange(last, "lat", neighbours("lat", 1)))
    grids = synthesis(recv, table, twiddle, info, tiles, tile)

    middle, inner = list(range(tiles // 2, tiles)), list(range(1, tiles // 2))
    soon, late = middle[: tiles // 4], middle[tiles // 4 :]

    def send(value, k):
        return exchange(value, "lon", partners("lon", k))

    moved = {0: grids[0]} | {k: send(grids[k], k) for k in soon}
    new, active = None, {}
    for k in [0] + soon + late + inner:
        new, active[k] = chemistry(
            tracers, halos, moved[k], react, info, k, active_ids.shape[0], waves, new
        )
        if k:
            active[k] = send(active[k], k)
        else:
            rest = late + inner
            held, active[0] = lax.optimization_barrier(([grids[i] for i in rest], active[0]))
            moved |= {i: send(value, i) for i, value in zip(rest, held)}
    spreaded = None
    for k in [0] + soon + inner + late:
        spreaded = spread(active[k], info, k, tiles, spreaded)
    return new, spreaded


def solution(mesh):
    return jax.shard_map(
        body,
        mesh=mesh,
        in_specs=(
            P(None, "lon", "lat", None),
            P("lat", None, None),
            P(),
            P("lat"),
            P(None, None, "lat", "lon"),
            P(),
            P(),
            P(),
        ),
        out_specs=(P(None, None, "lat", "lon"), P(None, "lon", "lat", None)),
        check_vma=False,
    )
```

```python
import functools

import jax
import jax.numpy as jnp
import numpy as np
from jax import lax
from jax.experimental import pallas as pl
from jax.experimental.pallas import tpu as pltpu
from jax.sharding import PartitionSpec as P

F32 = jnp.float32
BF16 = jnp.bfloat16
LANES = 128
SUBLANES = 8
LOW = 16
STEP = 4
MIB = 1024 * 1024

COS = (
    0.9999999890590228,
    -19.739204499454026,
    64.93911745990036,
    -85.45013953095037,
    60.16763095136588,
    -25.96759924965491,
    6.528658162567069,
)
SIN = (
    6.283185302511503,
    -41.34170040531769,
    81.60513138580204,
    -76.7030153539128,
    42.02592698618416,
    -14.899846668691637,
    3.238137510515757,
)


def dot(a, b, dims):
    return lax.dot_general(a, b, (dims, ((), ())), preferred_element_type=F32)


BAND, ME, IDS = 0, 1, 2


def cost(flops, moved):
    return pl.CostEstimate(flops=int(flops), bytes_accessed=int(moved), transcendentals=0)


def unit_circle(step, rows, waves, count):
    index = lax.broadcasted_iota(jnp.int32, (rows, waves.shape[1]), 0) * step
    product = index.astype(F32) * waves
    inverse = 1.0 / count
    turns = (product - jnp.floor(product * inverse) * count) * inverse
    y = turns - jnp.floor(turns + 0.5)
    z = y * y
    cosine = jnp.full_like(z, COS[-1])
    sine = jnp.full_like(z, SIN[-1])
    for c, s in zip(COS[-2::-1], SIN[-2::-1]):
        cosine = cosine * z + c
        sine = sine * z + s
    return cosine, sine * y


def table_kernel(first, info, waves_ref, table_ref, twiddle_ref):
    size, turns = waves_ref.shape[1], twiddle_ref.shape[2]
    waves = waves_ref[...].astype(F32)
    for k in range(table_ref.shape[0]):
        row = pl.program_id(0) * table_ref.shape[0] + k
        count = jnp.full(waves.shape, info[first + row], jnp.int32).astype(F32)
        cos_low, sin_low = unit_circle(1, LOW, waves, count)
        cos_high, sin_high = unit_circle(LOW, LANES // LOW, waves, count)
        cosine, sine = [], []
        for a in range(LANES // LOW):
            ch, sh = cos_high[a : a + 1], sin_high[a : a + 1]
            cosine.append(ch * cos_low - sh * sin_low)
            sine.append(-sh * cos_low - ch * sin_low)
        table_ref[k, :size, :] = jnp.concatenate(cosine, axis=0).T.astype(BF16)
        table_ref[k, size:, :] = jnp.concatenate(sine, axis=0).T.astype(BF16)
        cos_turn, sin_turn = unit_circle(LANES, turns, waves, count)
        twiddle_ref[k, 0] = cos_turn
        twiddle_ref[k, 1] = sin_turn


def tables(info, wave_ids, rows, turns):
    waves = wave_ids.shape[0]
    each = STEP if rows % STEP == 0 else 1
    return pl.pallas_call(
        functools.partial(table_kernel, info.shape[0] - rows),
        grid_spec=pltpu.PrefetchScalarGridSpec(
            num_scalar_prefetch=1,
            grid=(rows // each,),
            in_specs=[pl.BlockSpec((1, waves), lambda j, p: (0, 0))],
            out_specs=[
                pl.BlockSpec((each, 2 * waves, LANES), lambda j, p: (j, 0, 0)),
                pl.BlockSpec((each, 2, turns, waves), lambda j, p: (j, 0, 0, 0)),
            ],
        ),
        out_shape=[
            pltpu.VMEM((rows, 2 * waves, LANES), BF16),
            pltpu.VMEM((rows, 2, turns, waves), F32),
        ],
        compiler_params=pltpu.CompilerParams(vmem_limit_bytes=20 * MIB),
        cost_estimate=cost(rows * waves * LANES * 8, rows * waves * LANES * 4),
        name="tables",
    )(info, wave_ids[None, :])


def place(pieces, width):
    out = [None] * (width // LANES)
    lane = lax.broadcasted_iota(jnp.int32, (pieces[0][0].shape[0], LANES), 1)
    for value, start, count, here in pieces:
        shift = (here - start) % LANES
        for a in range(start // LANES, (start + count - 1) // LANES + 1):
            part = value[:, a * LANES : (a + 1) * LANES]
            if shift:
                part = pltpu.roll(part, shift, 1)
            first = max(start, a * LANES) - start + here
            last = min(start + count, (a + 1) * LANES) - start + here
            for v in range(first // LANES, (last - 1) // LANES + 1):
                low, high = max(first - v * LANES, 0), min(last - v * LANES, LANES)
                if out[v] is None:
                    out[v] = part
                else:
                    out[v] = jnp.where((lane >= low) & (lane < high), part, out[v])
    return out


def synth_kernel(info, recv_ref, table_ref, twiddle_ref, *refs):
    *out_refs, coef, grid = refs
    sources, levels, rows, _ = recv_ref.shape
    fields, waves = coef.shape[0] // 2, coef.shape[1] * LANES
    share = waves // sources
    each, _, turns = twiddle_ref.shape[:3]
    pitch = rows + 1
    step = pl.program_id(0)

    @pl.when(step == 0)
    def _():
        def level(l, carry):
            values = [recv_ref[s, l].astype(F32) for s in range(sources)]
            for r in range(2 * fields):
                windows = [
                    (values[s], r * share, share, s * share) for s in range(sources)
                ]
                for v, part in enumerate(place(windows, waves)):
                    coef[r, v, pl.ds(l * pitch, rows), :] = part
            return carry

        lax.fori_loop(0, levels, level, 0)

    for k in range(each):
        j = step * each + k

        def own_row(r):
            parts = [coef[r, v, pl.ds(j, levels, stride=pitch), :] for v in range(waves // LANES)]
            return jnp.concatenate(parts, axis=1)

        values = [own_row(r) for r in range(2 * fields)]
        real, imag = [], []
        for t in range(turns):
            c, s = twiddle_ref[k, 0, t : t + 1], twiddle_ref[k, 1, t : t + 1]
            for f in range(fields):
                re, im = values[2 * f], values[2 * f + 1]
                real.append(re * c - im * s)
                imag.append(re * s + im * c)
        both = [jnp.concatenate(part, axis=0).astype(BF16) for part in (real, imag)]
        result = dot(jnp.concatenate(both, axis=1), table_ref[k], ((1,), (0,)))
        grid[pl.ds(j, turns * fields * levels, stride=pitch), :] = result

    @pl.when(step == pl.num_programs(0) - 1)
    def _():
        tiles = turns // len(out_refs)
        for k, out_ref in enumerate(out_refs):
            for t in range(tiles):
                for f in range(fields):
                    start = (((info[ME] ^ k) * tiles + t) * fields + f) * levels
                    for l in range(levels):
                        block = grid[pl.ds((start + l) * pitch, rows), :].astype(BF16)
                        out_ref[f, l, :, t * LANES : (t + 1) * LANES] = block


def synthesis(recv, table, twiddle, info, dests, tile):
    sources, levels, rows, lanes = recv.shape
    turns, waves = twiddle.shape[2:]
    fields = 3
    each = STEP if rows % STEP == 0 else 1
    shape = (fields, levels, rows, tile)
    return pl.pallas_call(
        synth_kernel,
        grid_spec=pltpu.PrefetchScalarGridSpec(
            num_scalar_prefetch=1,
            grid=(rows // each,),
            in_specs=[
                pl.BlockSpec(recv.shape, lambda j, info: (0, 0, 0, 0)),
                pl.BlockSpec((each, 2 * waves, LANES), lambda j, info: (j, 0, 0)),
                pl.BlockSpec((each, 2, turns, waves), lambda j, info: (j, 0, 0, 0)),
            ],
            out_specs=[pl.BlockSpec(shape, lambda j, info: (0, 0, 0, 0))] * dests,
            scratch_shapes=[
                pltpu.VMEM((2 * fields, waves // LANES, levels * (rows + 1), LANES), F32),
                pltpu.VMEM((turns * fields * levels * (rows + 1), LANES), F32),
            ],
        ),
        out_shape=[jax.ShapeDtypeStruct(shape, BF16)] * dests,
        compiler_params=pltpu.CompilerParams(vmem_limit_bytes=24 * MIB),
        cost_estimate=cost(4 * rows * waves * fields * levels * turns * LANES, 4 * rows * waves * LANES),
        name="synthesis",
    )(info, recv, *[pltpu.with_memory_space_constraint(v, pltpu.VMEM) for v in (table, twiddle)])


def edge_kernel(
    info, state_ref, base_ref, temp_ref, row_a_ref, row_b_ref, col_a_ref, col_b_ref, react_ref
):
    tracers, levels, rows, tile = state_ref.shape
    cells = tracers * rows

    @pl.when(pl.program_id(0) == 0)
    def _():
        rates = jnp.concatenate([base_ref[...], temp_ref[...]], axis=0)
        high = rates.astype(BF16)
        low = (rates - high.astype(F32)).astype(BF16)

        def iota(shape, axis):
            return lax.broadcasted_iota(jnp.int32, shape, axis)

        shape = (2 * cells, 2 * tracers)
        down = jnp.where(iota(shape, 0) // rows == iota(shape, 1), 1.0, 0.0).astype(BF16)
        shape = (tracers, cells)
        over = jnp.where(iota(shape, 0) == iota(shape, 1) // rows, 1.0, 0.0).astype(BF16)
        shape = (2 * cells, cells)
        same = iota(shape, 0) % rows == iota(shape, 1) % rows
        for k, part in enumerate((high, low)):
            wide = dot(dot(down, part, ((1,), (0,))).astype(BF16), over, ((1,), (0,)))
            react_ref[:, k * cells : (k + 1) * cells] = jnp.where(same, wide, 0.0).astype(BF16)

    def iota(shape, axis):
        return lax.broadcasted_iota(jnp.int32, shape, axis)

    odd = info[BAND] % 2, info[ME] % 2
    far, near = (1 - odd[0]) * (rows - 1), odd[0] * (rows - 1)
    shape = (2 * tracers, cells)
    end = jnp.where(iota(shape, 0) < tracers, far, near)
    pick = iota(shape, 1) == (iota(shape, 0) % tracers) * rows + end
    pick = jnp.where(pick, 1.0, 0.0).astype(BF16)
    shape = (tile, 2 * LANES)
    far, near = (1 - odd[1]) * (tile - 1), odd[1] * (tile - 1)
    is_end = iota(shape, 0) == jnp.where(iota(shape, 1) < LANES, far, near)
    level = iota(shape, 1) % LANES - pl.program_id(0) * levels
    columns = jnp.zeros((cells, 2 * LANES), F32)
    for l in range(levels):
        x = state_ref[:, l].reshape(cells, tile)
        picked = dot(pick, x, ((1,), (0,)))
        row_a_ref[l] = picked[:tracers].astype(BF16)
        row_b_ref[l] = picked[tracers:].astype(BF16)
        mark = jnp.where(is_end & (level == l), 1.0, 0.0).astype(BF16)
        columns = columns + dot(x, mark, ((1,), (0,)))

    @pl.when(pl.program_id(0) == 0)
    def _():
        col_a_ref[...] = columns[:, :LANES].astype(BF16)
        col_b_ref[...] = columns[:, LANES:].astype(BF16)

    @pl.when(pl.program_id(0) > 0)
    def _():
        col_a_ref[...] = (col_a_ref[...].astype(F32) + columns[:, :LANES]).astype(BF16)
        col_b_ref[...] = (col_b_ref[...].astype(F32) + columns[:, LANES:]).astype(BF16)


def edges(state, react_base, react_temp, info):
    tracers, levels, rows, tile = state.shape
    block = 16
    cells = tracers * rows
    rowed = jax.ShapeDtypeStruct((levels, tracers, tile), BF16)
    columned = jax.ShapeDtypeStruct((cells, LANES), BF16)
    row_spec = pl.BlockSpec((block, tracers, tile), lambda i, info: (i, 0, 0))
    col_spec = pl.BlockSpec((cells, LANES), lambda i, info: (0, 0))
    wide = (2 * cells, 2 * cells)
    return pl.pallas_call(
        edge_kernel,
        grid_spec=pltpu.PrefetchScalarGridSpec(
            num_scalar_prefetch=1,
            grid=(levels // block,),
            in_specs=[
                pl.BlockSpec((tracers, block, rows, tile), lambda i, info: (0, i, 0, 0)),
                pl.BlockSpec(react_base.shape, lambda i, info: (0, 0)),
                pl.BlockSpec(react_temp.shape, lambda i, info: (0, 0)),
            ],
            out_specs=[
                row_spec, row_spec, col_spec, col_spec, pl.BlockSpec(wide, lambda i, info: (0, 0)),
            ],
        ),
        out_shape=[rowed, rowed, columned, columned, jax.ShapeDtypeStruct(wide, BF16)],
        compiler_params=pltpu.CompilerParams(vmem_limit_bytes=52 * MIB),
        cost_estimate=cost(4 * state.size * 32, 2 * state.size),
        name="edges",
    )(info, state, react_base, react_temp)


def shifted(value, outer, axis, step):
    size = value[0].shape[axis]
    turned = [pltpu.roll(v, -step % size, axis) for v in value]
    place = lax.broadcasted_iota(jnp.int32, value[0].shape, axis)
    at_end = place == (size - 1 if step == 1 else 0)
    following = turned[1:] + [outer] if step == 1 else [outer] + turned[:-1]
    return [jnp.where(at_end, f, t) for f, t in zip(following, turned)]


def chem_kernel(scale, k, info, *refs):
    state_ref, row_a_ref, row_b_ref, col_a_ref, col_b_ref, grid_ref, react_ref = refs[:7]
    new_ref, active_ref, south, north, advected, rounded = refs[-6:]
    tracers, levels, rows, tile = state_ref.shape
    cells = tracers * rows
    odd_band, odd_tile = info[BAND] % 2 == 1, info[ME] % 2 == 1
    first = ((info[ME] ^ k) * pl.num_programs(0) + pl.program_id(0)) * levels

    def column(value):
        return pltpu.roll(value, lax.rem(LANES - first, LANES), 1)

    a, b = col_a_ref[...].astype(F32), col_b_ref[...].astype(F32)
    west, east = column(jnp.where(odd_tile, a, b)), column(jnp.where(odd_tile, b, a))
    row = lax.broadcasted_iota(jnp.int32, (rows, tile), 0)
    lane = lax.broadcasted_iota(jnp.int32, (rows, tile), 1)
    ids, points = IDS, IDS + active_ref.shape[0]
    count = jnp.full((rows, tile), info[points], jnp.int32)
    for j in range(1, rows):
        count = jnp.where(row == j, info[points + j], count)
    mask = jnp.where(info[ME] * tile + lane < count, 1.0, 0.0)
    across = [slice(v * LANES, (v + 1) * LANES) for v in range(tile // LANES)]
    along = [slice(v * SUBLANES, (v + 1) * SUBLANES) for v in range(rows // SUBLANES)]

    for l in range(levels):
        wind_u = grid_ref[0, l].astype(F32) * (scale * 0.1)
        wind_v = grid_ref[1, l].astype(F32) * (scale * 0.1)
        from_east, from_west = 0.05 - wind_u, 0.05 + wind_u
        from_north, from_south = 0.05 - wind_v, 0.05 + wind_v
        a, b = row_a_ref[l].astype(F32), row_b_ref[l].astype(F32)
        south[l] = jnp.where(odd_band, a, b)
        north[l] = jnp.where(odd_band, b, a)
        for t in range(tracers):
            cell = slice(t * rows, (t + 1) * rows)
            x = state_ref[t, l].astype(F32)
            outer = [jnp.broadcast_to(col[cell, l : l + 1], (rows, LANES)) for col in (east, west)]
            parts = [x[:, v] for v in across]
            qe = jnp.concatenate(shifted(parts, outer[0], 1, 1), axis=1)
            qw = jnp.concatenate(shifted(parts, outer[1], 1, -1), axis=1)
            shape = (SUBLANES, tile)
            outer = [jnp.broadcast_to(ref[l, t : t + 1], shape) for ref in (north, south)]
            parts = [x[v] for v in along]
            qn = jnp.concatenate(shifted(parts, outer[0], 0, 1), axis=0)
            qs = jnp.concatenate(shifted(parts, outer[1], 0, -1), axis=0)
            moved = 0.8 * x + from_east * qe + from_west * qw + from_north * qn + from_south * qs
            advected[l, cell] = moved
            rounded[l, cell] = moved.astype(BF16)
    for l in range(levels):
        temper = grid_ref[2, l].astype(F32) * scale
        high = rounded[l]
        terms = dot(react_ref[...], jnp.concatenate([high, high], axis=0), ((1,), (0,)))
        for t in range(tracers):
            cell = slice(t * rows, (t + 1) * rows)
            warm = slice(cells + t * rows, cells + (t + 1) * rows)
            reacted = (advected[l, cell] + terms[cell] + temper * terms[warm]) * mask
            new_ref[t, l] = reacted.astype(BF16)
    for a in range(active_ref.shape[0]):
        active_ref[a] = new_ref[info[ids + a]]


def chemistry(state, halos, grid, react, info, k, actives, waves, before):
    tracers, levels, rows, tile = state.shape
    fields, own = grid.shape[:2]
    some = 4 if own % 4 == 0 else own
    steps = own // some
    cells = tracers * rows
    scale = 1.0 / float(np.sqrt(np.float32(waves)))

    def whole(shape):
        return pl.BlockSpec(shape, lambda i, info: (0,) * len(shape))

    row_spec = pl.BlockSpec((some, tracers, tile), lambda i, info: ((info[ME] ^ k) * steps + i, 0, 0))
    state_spec = pl.BlockSpec(
        (tracers, some, rows, tile), lambda i, info: (0, (info[ME] ^ k) * steps + i, 0, 0)
    )
    operands = [state, *halos, grid, react]
    in_specs = [
        state_spec,
        row_spec,
        row_spec,
        whole(halos[2].shape),
        whole(halos[3].shape),
        pl.BlockSpec((fields, some, rows, tile), lambda i, info: (0, i, 0, 0)),
        whole(react.shape),
    ]
    aliases = {}
    if before is not None:
        aliases = {1 + len(operands): 0}
        operands.append(before)
        in_specs.append(pl.BlockSpec(memory_space=pl.ANY))
    return pl.pallas_call(
        functools.partial(chem_kernel, scale, k),
        grid_spec=pltpu.PrefetchScalarGridSpec(
            num_scalar_prefetch=1,
            grid=(steps,),
            in_specs=in_specs,
            out_specs=[
                state_spec,
                pl.BlockSpec((actives, some, rows, tile), lambda i, info: (0, i, 0, 0)),
            ],
            scratch_shapes=[
                pltpu.VMEM((some, tracers, tile), F32),
                pltpu.VMEM((some, tracers, tile), F32),
                pltpu.VMEM((some, cells, tile), F32),
                pltpu.VMEM((some, cells, tile), BF16),
            ],
        ),
        out_shape=[
            jax.ShapeDtypeStruct(state.shape, BF16),
            jax.ShapeDtypeStruct((actives, own, rows, tile), BF16),
        ],
        input_output_aliases=aliases,
        compiler_params=pltpu.CompilerParams(vmem_limit_bytes=16 * MIB),
        cost_estimate=cost(own * cells * tile, own * tile),
        name="chemistry",
    )(info, *operands)


def spread_kernel(order, info, *refs):
    *recv_refs, out_ref = refs
    tile = recv_refs[0].shape[3]
    for k, recv_ref in zip(order, recv_refs):
        start = pl.multiple_of((info[ME] ^ k) * tile, LANES)
        out_ref[:, :, :, pl.ds(start, tile)] = recv_ref[...].astype(F32)


def spread(parts, order, info):
    actives, own, rows, tile = parts[0].shape
    wide = len(parts) * tile
    return pl.pallas_call(
        functools.partial(spread_kernel, order),
        grid_spec=pltpu.PrefetchScalarGridSpec(
            num_scalar_prefetch=1,
            grid=(actives,),
            in_specs=[pl.BlockSpec((1, own, rows, tile), lambda a, info: (a, 0, 0, 0))] * len(parts),
            out_specs=pl.BlockSpec((1, own, rows, wide), lambda a, info: (a, 0, 0, 0)),
        ),
        out_shape=jax.ShapeDtypeStruct((actives, own, rows, wide), F32),
        compiler_params=pltpu.CompilerParams(vmem_limit_bytes=8 * MIB),
        cost_estimate=cost(actives, actives),
        name="spread",
    )(info, *parts)


def legendre_kernel(spectral_ref, legendre_ref, out_ref, rows_of, sums):
    parts, own, block, size = spectral_ref.shape
    bands, _, rows, pitch = out_ref.shape
    share = block * pl.num_programs(0)
    step = pl.program_id(0)
    lines = parts * own
    apart, stretch = block + 1, pitch + 1

    @pl.when(step == 0)
    def _():
        for h in range(sums.shape[0]):
            for l in range(own):
                tail = pl.ds(l * stretch + parts * share, pitch - parts * share)
                sums[h, tail, :] = jnp.zeros((pitch - parts * share, LANES), F32)

    for v in range(size // LANES):
        part = spectral_ref[:, :, :, v * LANES : (v + 1) * LANES].astype(F32)
        part = part.reshape(lines, block, LANES)
        for i in range(lines):
            rows_of[v, pl.ds(i * apart, block), :] = part[i]
    def line(m):
        x = [rows_of[v, pl.ds(m, lines, stride=apart), :] for v in range(size // LANES)]
        return jnp.concatenate(x, axis=1).astype(BF16)

    wide = legendre_ref.shape[2]
    group = max(1, 2 * LANES // wide)
    for m in range(0, block, group):
        both = range(m, m + group)
        x = jnp.concatenate([line(i) for i in both], axis=0)
        y = jnp.concatenate([legendre_ref[i] for i in both], axis=1)
        product = dot(x, y, ((1,), (0,)))
        for i in both:
            result = product[(i - m) * lines : (i - m + 1) * lines, (i - m) * wide : (i - m + 1) * wide]
            for r in range(parts):
                at = r * share + step * block + i
                for h in range(sums.shape[0]):
                    piece = result[r * own : (r + 1) * own, h * LANES : (h + 1) * LANES]
                    sums[h, pl.ds(at, own, stride=stretch), :] = piece

    @pl.when(step == pl.num_programs(0) - 1)
    def _():
        some = LANES // rows
        for l in range(own):
            for h in range(sums.shape[0]):
                turned = sums[h, pl.ds(l * stretch, pitch), :].T.astype(BF16)
                out_ref[h * some : (h + 1) * some, l] = turned.reshape(some, rows, pitch)


def legendre_sums(spectral, legendre, bands):
    parts, own, share, size = spectral.shape
    rows = legendre.shape[2] // bands
    pitch = -(-parts * share // LANES) * LANES
    block = 16 if share % 16 == 0 else 8
    shape = (bands, own, rows, pitch)
    return pl.pallas_call(
        legendre_kernel,
        grid=(share // block,),
        in_specs=[
            pl.BlockSpec((parts, own, block, size), lambda i: (0, 0, i, 0)),
            pl.BlockSpec((block,) + legendre.shape[1:], lambda i: (i, 0, 0)),
        ],
        out_specs=pl.BlockSpec(shape, lambda i: (0, 0, 0, 0)),
        out_shape=jax.ShapeDtypeStruct(shape, BF16),
        scratch_shapes=[
            pltpu.VMEM((size // LANES, parts * own * (block + 1), LANES), F32),
            pltpu.VMEM((legendre.shape[2] // LANES, own * (pitch + 1), LANES), F32),
        ],
        compiler_params=pltpu.CompilerParams(vmem_limit_bytes=56 * MIB),
        cost_estimate=cost(2 * parts * own * legendre.size, 2 * (spectral.size + legendre.size)),
        name="legendre",
    )(spectral, legendre)


def exchange(value, axis, pairs):
    return lax.ppermute(value, axis, [p for a, b in pairs for p in ((a, b), (b, a))])


def neighbours(axis, first):
    size = lax.axis_size(axis)
    return [(i, i + 1) for i in range(first, size - 1, 2)]


def partners(axis, k):
    return [(i, i ^ k) for i in range(lax.axis_size(axis)) if i < i ^ k]


def body(spectral, legendre, wave_ids, points, tracers, react_base, react_temp, active_ids):
    bands, tiles = lax.axis_size("lat"), lax.axis_size("lon")
    tile = tracers.shape[3]
    waves = wave_ids.shape[0]
    band, me = lax.axis_index("lat"), lax.axis_index("lon")

    sent = legendre_sums(spectral, legendre, bands)

    rows = points.shape[0]
    info = jnp.concatenate([jnp.stack([band, me]), active_ids, points]).astype(jnp.int32)
    sent, info = lax.optimization_barrier((sent, info))
    recv = lax.all_to_all(sent, "lat", split_axis=0, concat_axis=0, tiled=True)
    *ends, react = edges(tracers, react_base, react_temp, info)
    halos = [
        exchange(ends[0], "lat", neighbours("lat", 0)),
        exchange(ends[2], "lon", neighbours("lon", 0)),
        exchange(ends[3], "lon", neighbours("lon", 1)),
    ]
    react, wave_ids = lax.optimization_barrier((react, wave_ids))
    table, twiddle = tables(info, wave_ids, rows, tiles * tile // LANES)
    recv, table, twiddle, react, halos, last = lax.optimization_barrier(
        (recv, table, twiddle, react, halos, ends[1])
    )
    halos.insert(1, exchange(last, "lat", neighbours("lat", 1)))
    grids = synthesis(recv, table, twiddle, info, tiles, tile)

    middle, inner = list(range(tiles // 2, tiles)), list(range(1, tiles // 2))
    soon, late = middle[: tiles // 4], middle[tiles // 4 :]

    def send(value, k):
        return exchange(value, "lon", partners("lon", k))

    moved = {0: grids[0]} | {k: send(grids[k], k) for k in soon}
    new, active = None, {}
    for k in [0] + soon + late + inner:
        new, active[k] = chemistry(
            tracers, halos, moved[k], react, info, k, active_ids.shape[0], waves, new
        )
        if k:
            active[k] = send(active[k], k)
        else:
            rest = late + inner
            held, active[0] = lax.optimization_barrier(([grids[i] for i in rest], active[0]))
            moved |= {i: send(value, i) for i, value in zip(rest, held)}
    order = [0] + soon + late + inner
    through = lax.optimization_barrier([active[k] for k in soon + late])
    active |= zip(soon + late, through)
    active = dict(zip(order, lax.optimization_barrier([active[k] for k in order])))
    return new, spread([active[k] for k in order], order, info)


def solution(mesh):
    return jax.shard_map(
        body,
        mesh=mesh,
        in_specs=(
            P(None, "lon", "lat", None),
            P("lat", None, None),
            P(),
            P("lat"),
            P(None, None, "lat", "lon"),
            P(),
            P(),
            P(),
        ),
        out_specs=(P(None, None, "lat", "lon"), P(None, "lon", "lat", None)),
        check_vma=False,
    )
```

```python
import functools

import jax
import jax.numpy as jnp
import numpy as np
from jax import lax
from jax.experimental import pallas as pl
from jax.experimental.pallas import tpu as pltpu
from jax.sharding import PartitionSpec as P

F32 = jnp.float32
BF16 = jnp.bfloat16
LANES = 128
SUBLANES = 8
LOW = 16
STEP = 4
MIB = 1024 * 1024

COS = (
    0.9999999890590228,
    -19.739204499454026,
    64.93911745990036,
    -85.45013953095037,
    60.16763095136588,
    -25.96759924965491,
    6.528658162567069,
)
SIN = (
    6.283185302511503,
    -41.34170040531769,
    81.60513138580204,
    -76.7030153539128,
    42.02592698618416,
    -14.899846668691637,
    3.238137510515757,
)


def dot(a, b, dims):
    return lax.dot_general(a, b, (dims, ((), ())), preferred_element_type=F32)


BAND, ME, IDS = 0, 1, 2


def cost(flops, moved):
    return pl.CostEstimate(flops=int(flops), bytes_accessed=int(moved), transcendentals=0)


def unit_circle(step, rows, waves, count):
    index = lax.broadcasted_iota(jnp.int32, (rows, waves.shape[1]), 0) * step
    product = index.astype(F32) * waves
    inverse = 1.0 / count
    turns = (product - jnp.floor(product * inverse) * count) * inverse
    y = turns - jnp.floor(turns + 0.5)
    z = y * y
    cosine = jnp.full_like(z, COS[-1])
    sine = jnp.full_like(z, SIN[-1])
    for c, s in zip(COS[-2::-1], SIN[-2::-1]):
        cosine = cosine * z + c
        sine = sine * z + s
    return cosine, sine * y


def row_tables(count, waves, turns):
    cos_low, sin_low = unit_circle(1, LOW, waves, count)
    cos_high, sin_high = unit_circle(LOW, LANES // LOW, waves, count)
    cosine, sine = [], []
    for a in range(LANES // LOW):
        ch, sh = cos_high[a : a + 1], sin_high[a : a + 1]
        cosine.append(ch * cos_low - sh * sin_low)
        sine.append(-sh * cos_low - ch * sin_low)
    table = [jnp.concatenate(part, axis=0).T.astype(BF16) for part in (cosine, sine)]
    return jnp.concatenate(table, axis=0), *unit_circle(LANES, turns, waves, count)


def place(pieces, width):
    out = [None] * (width // LANES)
    lane = lax.broadcasted_iota(jnp.int32, (pieces[0][0].shape[0], LANES), 1)
    for value, start, count, here in pieces:
        shift = (here - start) % LANES
        for a in range(start // LANES, (start + count - 1) // LANES + 1):
            part = value[:, a * LANES : (a + 1) * LANES]
            if shift:
                part = pltpu.roll(part, shift, 1)
            first = max(start, a * LANES) - start + here
            last = min(start + count, (a + 1) * LANES) - start + here
            for v in range(first // LANES, (last - 1) // LANES + 1):
                low, high = max(first - v * LANES, 0), min(last - v * LANES, LANES)
                if out[v] is None:
                    out[v] = part
                else:
                    out[v] = jnp.where((lane >= low) & (lane < high), part, out[v])
    return out


def synth_kernel(info, waves_ref, recv_ref, *refs):
    *out_refs, coef, grid = refs
    pieces, levels, rows, _ = recv_ref.shape
    fields, waves = coef.shape[0] // 2, coef.shape[1] * LANES
    share = waves // pieces
    turns = grid.shape[0] // (fields * levels * (rows + 1))
    pitch = rows + 1
    step, steps = pl.program_id(0), pl.num_programs(0)
    each = rows // steps

    @pl.when(step == 0)
    def _():
        def level(l, carry):
            values = [recv_ref[s, l].astype(F32) for s in range(pieces)]
            for r in range(2 * fields):
                windows = [(values[s], r * share, share, s * share) for s in range(pieces)]
                for v, part in enumerate(place(windows, waves)):
                    coef[r, v, pl.ds(l * pitch, rows), :] = part
            return carry

        lax.fori_loop(0, levels, level, 0)

    wave_line = waves_ref[...].astype(F32)
    first = info.shape[0] - rows
    for k in range(each):
        j = step * each + k
        count = jnp.full(wave_line.shape, info[first + j], jnp.int32).astype(F32)
        table, cos_turn, sin_turn = row_tables(count, wave_line, turns)

        def own_row(r):
            parts = [coef[r, v, pl.ds(j, levels, stride=pitch), :] for v in range(waves // LANES)]
            return jnp.concatenate(parts, axis=1)

        values = [own_row(r) for r in range(2 * fields)]
        real, imag = [], []
        for t in range(turns):
            c, s = cos_turn[t : t + 1], sin_turn[t : t + 1]
            for f in range(fields):
                re, im = values[2 * f], values[2 * f + 1]
                real.append(re * c - im * s)
                imag.append(re * s + im * c)
        both = [jnp.concatenate(part, axis=0).astype(BF16) for part in (real, imag)]
        result = dot(jnp.concatenate(both, axis=1), table, ((1,), (0,)))
        grid[pl.ds(j, turns * fields * levels, stride=pitch), :] = result

    @pl.when(step == steps - 1)
    def _():
        tiles = turns // len(out_refs)
        for k, out_ref in enumerate(out_refs):
            for t in range(tiles):
                for f in range(fields):
                    start = (((info[ME] ^ k) * tiles + t) * fields + f) * levels
                    for l in range(levels):
                        block = grid[pl.ds((start + l) * pitch, rows), :].astype(BF16)
                        out_ref[f, l, :, t * LANES : (t + 1) * LANES] = block


def synthesis(recv, wave_ids, info, dests, tile):
    levels, rows = recv.shape[1:3]
    waves = wave_ids.shape[0]
    turns, fields = dests * tile // LANES, 3
    each = STEP if rows % STEP == 0 else 1
    shape = (fields, levels, rows, tile)
    return pl.pallas_call(
        synth_kernel,
        grid_spec=pltpu.PrefetchScalarGridSpec(
            num_scalar_prefetch=1,
            grid=(rows // each,),
            in_specs=[
                pl.BlockSpec((1, waves), lambda j, info: (0, 0)),
                pl.BlockSpec(recv.shape, lambda j, info: (0, 0, 0, 0)),
            ],
            out_specs=[pl.BlockSpec(shape, lambda j, info: (0, 0, 0, 0))] * dests,
            scratch_shapes=[
                pltpu.VMEM((2 * fields, waves // LANES, levels * (rows + 1), LANES), F32),
                pltpu.VMEM((turns * fields * levels * (rows + 1), LANES), F32),
            ],
        ),
        out_shape=[jax.ShapeDtypeStruct(shape, BF16)] * dests,
        compiler_params=pltpu.CompilerParams(vmem_limit_bytes=24 * MIB),
        cost_estimate=cost(4 * rows * waves * fields * levels * turns * LANES, 4 * rows * waves * LANES),
        name="synthesis",
    )(info, wave_ids[None, :], recv)


def edge_kernel(
    info, state_ref, base_ref, temp_ref, row_a_ref, row_b_ref, col_a_ref, col_b_ref, react_ref
):
    tracers, levels, rows, tile = state_ref.shape
    cells = tracers * rows

    @pl.when(pl.program_id(0) == 0)
    def _():
        rates = jnp.concatenate([base_ref[...], temp_ref[...]], axis=0)
        high = rates.astype(BF16)
        low = (rates - high.astype(F32)).astype(BF16)

        def iota(shape, axis):
            return lax.broadcasted_iota(jnp.int32, shape, axis)

        shape = (2 * cells, 2 * tracers)
        down = jnp.where(iota(shape, 0) // rows == iota(shape, 1), 1.0, 0.0).astype(BF16)
        shape = (tracers, cells)
        over = jnp.where(iota(shape, 0) == iota(shape, 1) // rows, 1.0, 0.0).astype(BF16)
        shape = (2 * cells, cells)
        same = iota(shape, 0) % rows == iota(shape, 1) % rows
        for k, part in enumerate((high, low)):
            wide = dot(dot(down, part, ((1,), (0,))).astype(BF16), over, ((1,), (0,)))
            react_ref[:, k * cells : (k + 1) * cells] = jnp.where(same, wide, 0.0).astype(BF16)

    def iota(shape, axis):
        return lax.broadcasted_iota(jnp.int32, shape, axis)

    odd = info[BAND] % 2, info[ME] % 2
    far, near = (1 - odd[0]) * (rows - 1), odd[0] * (rows - 1)
    shape = (2 * tracers, cells)
    end = jnp.where(iota(shape, 0) < tracers, far, near)
    pick = iota(shape, 1) == (iota(shape, 0) % tracers) * rows + end
    pick = jnp.where(pick, 1.0, 0.0).astype(BF16)
    shape = (tile, 2 * LANES)
    far, near = (1 - odd[1]) * (tile - 1), odd[1] * (tile - 1)
    is_end = iota(shape, 0) == jnp.where(iota(shape, 1) < LANES, far, near)
    level = iota(shape, 1) % LANES - pl.program_id(0) * levels
    columns = jnp.zeros((cells, 2 * LANES), F32)
    for l in range(levels):
        x = state_ref[:, l].reshape(cells, tile)
        picked = dot(pick, x, ((1,), (0,)))
        row_a_ref[l] = picked[:tracers].astype(BF16)
        row_b_ref[l] = picked[tracers:].astype(BF16)
        mark = jnp.where(is_end & (level == l), 1.0, 0.0).astype(BF16)
        columns = columns + dot(x, mark, ((1,), (0,)))

    @pl.when(pl.program_id(0) == 0)
    def _():
        col_a_ref[...] = columns[:, :LANES].astype(BF16)
        col_b_ref[...] = columns[:, LANES:].astype(BF16)

    @pl.when(pl.program_id(0) > 0)
    def _():
        col_a_ref[...] = (col_a_ref[...].astype(F32) + columns[:, :LANES]).astype(BF16)
        col_b_ref[...] = (col_b_ref[...].astype(F32) + columns[:, LANES:]).astype(BF16)


def edges(state, react_base, react_temp, info):
    tracers, levels, rows, tile = state.shape
    block = 16
    cells = tracers * rows
    rowed = jax.ShapeDtypeStruct((levels, tracers, tile), BF16)
    columned = jax.ShapeDtypeStruct((cells, LANES), BF16)
    row_spec = pl.BlockSpec((block, tracers, tile), lambda i, info: (i, 0, 0))
    col_spec = pl.BlockSpec((cells, LANES), lambda i, info: (0, 0))
    wide = (2 * cells, 2 * cells)
    return pl.pallas_call(
        edge_kernel,
        grid_spec=pltpu.PrefetchScalarGridSpec(
            num_scalar_prefetch=1,
            grid=(levels // block,),
            in_specs=[
                pl.BlockSpec((tracers, block, rows, tile), lambda i, info: (0, i, 0, 0)),
                pl.BlockSpec(react_base.shape, lambda i, info: (0, 0)),
                pl.BlockSpec(react_temp.shape, lambda i, info: (0, 0)),
            ],
            out_specs=[
                row_spec, row_spec, col_spec, col_spec, pl.BlockSpec(wide, lambda i, info: (0, 0)),
            ],
        ),
        out_shape=[rowed, rowed, columned, columned, jax.ShapeDtypeStruct(wide, BF16)],
        compiler_params=pltpu.CompilerParams(vmem_limit_bytes=52 * MIB),
        cost_estimate=cost(4 * state.size * 32, 2 * state.size),
        name="edges",
    )(info, state, react_base, react_temp)


def shifted(value, outer, axis, step):
    size = value[0].shape[axis]
    turned = [pltpu.roll(v, -step % size, axis) for v in value]
    place = lax.broadcasted_iota(jnp.int32, value[0].shape, axis)
    at_end = place == (size - 1 if step == 1 else 0)
    following = turned[1:] + [outer] if step == 1 else [outer] + turned[:-1]
    return [jnp.where(at_end, f, t) for f, t in zip(following, turned)]


def chem_kernel(scale, k, info, *refs):
    state_ref, row_a_ref, row_b_ref, col_a_ref, col_b_ref, grid_ref, react_ref = refs[:7]
    new_ref, active_ref, south, north, advected, rounded = refs[-6:]
    tracers, levels, rows, tile = state_ref.shape
    cells = tracers * rows
    odd_band, odd_tile = info[BAND] % 2 == 1, info[ME] % 2 == 1
    first = ((info[ME] ^ k) * pl.num_programs(0) + pl.program_id(0)) * levels

    def column(value):
        return pltpu.roll(value, lax.rem(LANES - first, LANES), 1)

    a, b = col_a_ref[...].astype(F32), col_b_ref[...].astype(F32)
    west, east = column(jnp.where(odd_tile, a, b)), column(jnp.where(odd_tile, b, a))
    row = lax.broadcasted_iota(jnp.int32, (rows, tile), 0)
    lane = lax.broadcasted_iota(jnp.int32, (rows, tile), 1)
    ids, points = IDS, IDS + active_ref.shape[0]
    count = jnp.full((rows, tile), info[points], jnp.int32)
    for j in range(1, rows):
        count = jnp.where(row == j, info[points + j], count)
    mask = jnp.where(info[ME] * tile + lane < count, 1.0, 0.0)
    across = [slice(v * LANES, (v + 1) * LANES) for v in range(tile // LANES)]
    along = [slice(v * SUBLANES, (v + 1) * SUBLANES) for v in range(rows // SUBLANES)]

    for l in range(levels):
        wind_u = grid_ref[0, l].astype(F32) * (scale * 0.1)
        wind_v = grid_ref[1, l].astype(F32) * (scale * 0.1)
        from_east, from_west = 0.05 - wind_u, 0.05 + wind_u
        from_north, from_south = 0.05 - wind_v, 0.05 + wind_v
        a, b = row_a_ref[l].astype(F32), row_b_ref[l].astype(F32)
        south[l] = jnp.where(odd_band, a, b)
        north[l] = jnp.where(odd_band, b, a)
        for t in range(tracers):
            cell = slice(t * rows, (t + 1) * rows)
            x = state_ref[t, l].astype(F32)
            outer = [jnp.broadcast_to(col[cell, l : l + 1], (rows, LANES)) for col in (east, west)]
            parts = [x[:, v] for v in across]
            qe = jnp.concatenate(shifted(parts, outer[0], 1, 1), axis=1)
            qw = jnp.concatenate(shifted(parts, outer[1], 1, -1), axis=1)
            shape = (SUBLANES, tile)
            outer = [jnp.broadcast_to(ref[l, t : t + 1], shape) for ref in (north, south)]
            parts = [x[v] for v in along]
            qn = jnp.concatenate(shifted(parts, outer[0], 0, 1), axis=0)
            qs = jnp.concatenate(shifted(parts, outer[1], 0, -1), axis=0)
            moved = 0.8 * x + from_east * qe + from_west * qw + from_north * qn + from_south * qs
            advected[l, cell] = moved
            rounded[l, cell] = moved.astype(BF16)
    for l in range(levels):
        temper = grid_ref[2, l].astype(F32) * scale
        high = rounded[l]
        terms = dot(react_ref[...], jnp.concatenate([high, high], axis=0), ((1,), (0,)))
        for t in range(tracers):
            cell = slice(t * rows, (t + 1) * rows)
            warm = slice(cells + t * rows, cells + (t + 1) * rows)
            reacted = (advected[l, cell] + terms[cell] + temper * terms[warm]) * mask
            new_ref[t, l] = reacted.astype(BF16)
    for a in range(active_ref.shape[0]):
        active_ref[a] = new_ref[info[ids + a]]


def chemistry(state, halos, grid, react, info, k, actives, waves, before):
    tracers, levels, rows, tile = state.shape
    fields, own = grid.shape[:2]
    some = 4 if own % 4 == 0 else own
    steps = own // some
    cells = tracers * rows
    scale = 1.0 / float(np.sqrt(np.float32(waves)))

    def whole(shape):
        return pl.BlockSpec(shape, lambda i, info: (0,) * len(shape))

    row_spec = pl.BlockSpec((some, tracers, tile), lambda i, info: ((info[ME] ^ k) * steps + i, 0, 0))
    state_spec = pl.BlockSpec(
        (tracers, some, rows, tile), lambda i, info: (0, (info[ME] ^ k) * steps + i, 0, 0)
    )
    operands = [state, *halos, grid, react]
    in_specs = [
        state_spec,
        row_spec,
        row_spec,
        whole(halos[2].shape),
        whole(halos[3].shape),
        pl.BlockSpec((fields, some, rows, tile), lambda i, info: (0, i, 0, 0)),
        whole(react.shape),
    ]
    aliases = {}
    if before is not None:
        aliases = {1 + len(operands): 0}
        operands.append(before)
        in_specs.append(pl.BlockSpec(memory_space=pl.ANY))
    return pl.pallas_call(
        functools.partial(chem_kernel, scale, k),
        grid_spec=pltpu.PrefetchScalarGridSpec(
            num_scalar_prefetch=1,
            grid=(steps,),
            in_specs=in_specs,
            out_specs=[
                state_spec,
                pl.BlockSpec((actives, some, rows, tile), lambda i, info: (0, i, 0, 0)),
            ],
            scratch_shapes=[
                pltpu.VMEM((some, tracers, tile), F32),
                pltpu.VMEM((some, tracers, tile), F32),
                pltpu.VMEM((some, cells, tile), F32),
                pltpu.VMEM((some, cells, tile), BF16),
            ],
        ),
        out_shape=[
            jax.ShapeDtypeStruct(state.shape, BF16),
            jax.ShapeDtypeStruct((actives, own, rows, tile), BF16),
        ],
        input_output_aliases=aliases,
        compiler_params=pltpu.CompilerParams(vmem_limit_bytes=16 * MIB),
        cost_estimate=cost(own * cells * tile, own * tile),
        name="chemistry",
    )(info, *operands)


def spread_kernel(order, info, *refs):
    *recv_refs, out_ref = refs
    tile = recv_refs[0].shape[3]
    for k, recv_ref in zip(order, recv_refs):
        start = pl.multiple_of((info[ME] ^ k) * tile, LANES)
        out_ref[:, :, :, pl.ds(start, tile)] = recv_ref[...].astype(F32)


def spread(parts, order, info):
    actives, own, rows, tile = parts[0].shape
    wide = len(parts) * tile
    return pl.pallas_call(
        functools.partial(spread_kernel, order),
        grid_spec=pltpu.PrefetchScalarGridSpec(
            num_scalar_prefetch=1,
            grid=(actives,),
            in_specs=[pl.BlockSpec((1, own, rows, tile), lambda a, info: (a, 0, 0, 0))] * len(parts),
            out_specs=pl.BlockSpec((1, own, rows, wide), lambda a, info: (a, 0, 0, 0)),
        ),
        out_shape=jax.ShapeDtypeStruct((actives, own, rows, wide), F32),
        compiler_params=pltpu.CompilerParams(vmem_limit_bytes=8 * MIB),
        cost_estimate=cost(actives, actives),
        name="spread",
    )(info, *parts)


def legendre_kernel(spectral_ref, legendre_ref, out_ref, rows_of, sums):
    parts, own, block, size = spectral_ref.shape
    bands, _, rows, pitch = out_ref.shape
    share = block * pl.num_programs(0)
    step = pl.program_id(0)
    lines = parts * own
    apart, stretch = block + 1, pitch + 1

    @pl.when(step == 0)
    def _():
        for h in range(sums.shape[0]):
            for l in range(own):
                tail = pl.ds(l * stretch + parts * share, pitch - parts * share)
                sums[h, tail, :] = jnp.zeros((pitch - parts * share, LANES), F32)

    for v in range(size // LANES):
        part = spectral_ref[:, :, :, v * LANES : (v + 1) * LANES].astype(F32)
        part = part.reshape(lines, block, LANES)
        for i in range(lines):
            rows_of[v, pl.ds(i * apart, block), :] = part[i]
    def line(m):
        x = [rows_of[v, pl.ds(m, lines, stride=apart), :] for v in range(size // LANES)]
        return jnp.concatenate(x, axis=1).astype(BF16)

    wide = legendre_ref.shape[2]
    group = max(1, 2 * LANES // wide)
    for m in range(0, block, group):
        both = range(m, m + group)
        x = jnp.concatenate([line(i) for i in both], axis=0)
        y = jnp.concatenate([legendre_ref[i] for i in both], axis=1)
        product = dot(x, y, ((1,), (0,)))
        for i in both:
            result = product[(i - m) * lines : (i - m + 1) * lines, (i - m) * wide : (i - m + 1) * wide]
            for r in range(parts):
                at = r * share + step * block + i
                for h in range(sums.shape[0]):
                    piece = result[r * own : (r + 1) * own, h * LANES : (h + 1) * LANES]
                    sums[h, pl.ds(at, own, stride=stretch), :] = piece

    @pl.when(step == pl.num_programs(0) - 1)
    def _():
        some = LANES // rows
        for l in range(own):
            for h in range(sums.shape[0]):
                turned = sums[h, pl.ds(l * stretch, pitch), :].T.astype(BF16)
                out_ref[h * some : (h + 1) * some, l] = turned.reshape(some, rows, pitch)


def legendre_sums(spectral, legendre, bands):
    parts, own, share, size = spectral.shape
    rows = legendre.shape[2] // bands
    pitch = -(-parts * share // LANES) * LANES
    block = 16 if share % 16 == 0 else 8
    shape = (bands, own, rows, pitch)
    return pl.pallas_call(
        legendre_kernel,
        grid=(share // block,),
        in_specs=[
            pl.BlockSpec((parts, own, block, size), lambda i: (0, 0, i, 0)),
            pl.BlockSpec((block,) + legendre.shape[1:], lambda i: (i, 0, 0)),
        ],
        out_specs=pl.BlockSpec(shape, lambda i: (0, 0, 0, 0)),
        out_shape=jax.ShapeDtypeStruct(shape, BF16),
        scratch_shapes=[
            pltpu.VMEM((size // LANES, parts * own * (block + 1), LANES), F32),
            pltpu.VMEM((legendre.shape[2] // LANES, own * (pitch + 1), LANES), F32),
        ],
        compiler_params=pltpu.CompilerParams(vmem_limit_bytes=56 * MIB),
        cost_estimate=cost(2 * parts * own * legendre.size, 2 * (spectral.size + legendre.size)),
        name="legendre",
    )(spectral, legendre)


def exchange(value, axis, pairs):
    return lax.ppermute(value, axis, [p for a, b in pairs for p in ((a, b), (b, a))])


def neighbours(axis, first):
    size = lax.axis_size(axis)
    return [(i, i + 1) for i in range(first, size - 1, 2)]


def partners(axis, k):
    return [(i, i ^ k) for i in range(lax.axis_size(axis)) if i < i ^ k]


def body(spectral, legendre, wave_ids, points, tracers, react_base, react_temp, active_ids):
    bands, tiles = lax.axis_size("lat"), lax.axis_size("lon")
    tile = tracers.shape[3]
    waves = wave_ids.shape[0]
    band, me = lax.axis_index("lat"), lax.axis_index("lon")

    sent = legendre_sums(spectral, legendre, bands)

    rows = points.shape[0]
    info = jnp.concatenate([jnp.stack([band, me]), active_ids, points]).astype(jnp.int32)
    sent, info = lax.optimization_barrier((sent, info))
    recv = lax.all_to_all(sent, "lat", split_axis=0, concat_axis=0, tiled=True)
    *ends, react = edges(tracers, react_base, react_temp, info)
    halos = [
        exchange(ends[0], "lat", neighbours("lat", 0)),
        exchange(ends[2], "lon", neighbours("lon", 0)),
        exchange(ends[3], "lon", neighbours("lon", 1)),
    ]
    recv, react, halos, last = lax.optimization_barrier((recv, react, halos, ends[1]))
    halos.insert(1, exchange(last, "lat", neighbours("lat", 1)))
    grids = synthesis(recv, wave_ids, info, tiles, tile)

    middle, inner = list(range(tiles // 2, tiles)), list(range(1, tiles // 2))
    soon, late = middle[: tiles // 4], middle[tiles // 4 :]

    def send(value, k):
        return exchange(value, "lon", partners("lon", k))

    moved = {0: grids[0]} | {k: send(grids[k], k) for k in soon}
    new, active = None, {}
    for k in [0] + soon + late + inner:
        new, active[k] = chemistry(
            tracers, halos, moved[k], react, info, k, active_ids.shape[0], waves, new
        )
        if k:
            active[k] = send(active[k], k)
        else:
            rest = late + inner
            held, active[0] = lax.optimization_barrier(([grids[i] for i in rest], active[0]))
            moved |= {i: send(value, i) for i, value in zip(rest, held)}
    order = [0] + soon + late + inner
    through = lax.optimization_barrier([active[k] for k in soon + late])
    active |= zip(soon + late, through)
    active = dict(zip(order, lax.optimization_barrier([active[k] for k in order])))
    return new, spread([active[k] for k in order], order, info)


def solution(mesh):
    return jax.shard_map(
        body,
        mesh=mesh,
        in_specs=(
            P(None, "lon", "lat", None),
            P("lat", None, None),
            P(),
            P("lat"),
            P(None, None, "lat", "lon"),
            P(),
            P(),
            P(),
        ),
        out_specs=(P(None, None, "lat", "lon"), P(None, "lon", "lat", None)),
        check_vma=False,
    )
```

```python
import functools

import jax
import jax.numpy as jnp
import numpy as np
from jax import lax
from jax.experimental import pallas as pl
from jax.experimental.pallas import tpu as pltpu
from jax.sharding import PartitionSpec as P

F32 = jnp.float32
BF16 = jnp.bfloat16
LANES = 128
SUBLANES = 8
LOW = 16
STEP = 4
MIB = 1024 * 1024

COS = (
    0.9999999890590228,
    -19.739204499454026,
    64.93911745990036,
    -85.45013953095037,
    60.16763095136588,
    -25.96759924965491,
    6.528658162567069,
)
SIN = (
    6.283185302511503,
    -41.34170040531769,
    81.60513138580204,
    -76.7030153539128,
    42.02592698618416,
    -14.899846668691637,
    3.238137510515757,
)


def dot(a, b, dims):
    return lax.dot_general(a, b, (dims, ((), ())), preferred_element_type=F32)


BAND, ME, IDS = 0, 1, 2


def cost(flops, moved):
    return pl.CostEstimate(flops=int(flops), bytes_accessed=int(moved), transcendentals=0)


def unit_circle(step, rows, waves, count):
    index = lax.broadcasted_iota(jnp.int32, (rows, waves.shape[1]), 0) * step
    product = index.astype(F32) * waves
    inverse = 1.0 / count
    turns = (product - jnp.floor(product * inverse) * count) * inverse
    y = turns - jnp.floor(turns + 0.5)
    z = y * y
    cosine = jnp.full_like(z, COS[-1])
    sine = jnp.full_like(z, SIN[-1])
    for c, s in zip(COS[-2::-1], SIN[-2::-1]):
        cosine = cosine * z + c
        sine = sine * z + s
    return cosine, sine * y


def table_kernel(first, info, waves_ref, table_ref, twiddle_ref):
    size, turns = waves_ref.shape[1], twiddle_ref.shape[2]
    waves = waves_ref[...].astype(F32)
    for k in range(table_ref.shape[0]):
        row = pl.program_id(0) * table_ref.shape[0] + k
        count = jnp.full(waves.shape, info[first + row], jnp.int32).astype(F32)
        cos_low, sin_low = unit_circle(1, LOW, waves, count)
        cos_high, sin_high = unit_circle(LOW, LANES // LOW, waves, count)
        cosine, sine = [], []
        for a in range(LANES // LOW):
            ch, sh = cos_high[a : a + 1], sin_high[a : a + 1]
            cosine.append(ch * cos_low - sh * sin_low)
            sine.append(-sh * cos_low - ch * sin_low)
        table_ref[k, :size, :] = jnp.concatenate(cosine, axis=0).T.astype(BF16)
        table_ref[k, size:, :] = jnp.concatenate(sine, axis=0).T.astype(BF16)
        cos_turn, sin_turn = unit_circle(LANES, turns, waves, count)
        twiddle_ref[k, 0] = cos_turn
        twiddle_ref[k, 1] = sin_turn


def tables(info, wave_ids, rows, turns):
    waves = wave_ids.shape[0]
    each = STEP if rows % STEP == 0 else 1
    return pl.pallas_call(
        functools.partial(table_kernel, info.shape[0] - rows),
        grid_spec=pltpu.PrefetchScalarGridSpec(
            num_scalar_prefetch=1,
            grid=(rows // each,),
            in_specs=[pl.BlockSpec((1, waves), lambda j, p: (0, 0))],
            out_specs=[
                pl.BlockSpec((each, 2 * waves, LANES), lambda j, p: (j, 0, 0)),
                pl.BlockSpec((each, 2, turns, waves), lambda j, p: (j, 0, 0, 0)),
            ],
        ),
        out_shape=[
            pltpu.HBM((rows, 2 * waves, LANES), BF16),
            pltpu.HBM((rows, 2, turns, waves), F32),
        ],
        compiler_params=pltpu.CompilerParams(vmem_limit_bytes=20 * MIB),
        cost_estimate=cost(rows * waves * LANES * 8, rows * waves * LANES * 4),
        name="tables",
    )(info, wave_ids[None, :])


def place(pieces, width):
    out = [None] * (width // LANES)
    lane = lax.broadcasted_iota(jnp.int32, (pieces[0][0].shape[0], LANES), 1)
    for value, start, count, here in pieces:
        shift = (here - start) % LANES
        for a in range(start // LANES, (start + count - 1) // LANES + 1):
            part = value[:, a * LANES : (a + 1) * LANES]
            if shift:
                part = pltpu.roll(part, shift, 1)
            first = max(start, a * LANES) - start + here
            last = min(start + count, (a + 1) * LANES) - start + here
            for v in range(first // LANES, (last - 1) // LANES + 1):
                low, high = max(first - v * LANES, 0), min(last - v * LANES, LANES)
                if out[v] is None:
                    out[v] = part
                else:
                    out[v] = jnp.where((lane >= low) & (lane < high), part, out[v])
    return out


def synth_kernel(info, recv_ref, table_ref, twiddle_ref, *refs):
    *out_refs, coef, grid = refs
    sources, levels, rows, _ = recv_ref.shape
    fields, waves = coef.shape[0] // 2, coef.shape[1] * LANES
    share = waves // sources
    each, _, turns = twiddle_ref.shape[:3]
    pitch = rows + 1
    step = pl.program_id(0)

    @pl.when(step == 0)
    def _():
        def level(l, carry):
            values = [recv_ref[s, l].astype(F32) for s in range(sources)]
            for r in range(2 * fields):
                windows = [
                    (values[s], r * share, share, s * share) for s in range(sources)
                ]
                for v, part in enumerate(place(windows, waves)):
                    coef[r, v, pl.ds(l * pitch, rows), :] = part
            return carry

        lax.fori_loop(0, levels, level, 0)

    for k in range(each):
        j = step * each + k

        def own_row(r):
            parts = [coef[r, v, pl.ds(j, levels, stride=pitch), :] for v in range(waves // LANES)]
            return jnp.concatenate(parts, axis=1)

        values = [own_row(r) for r in range(2 * fields)]
        real, imag = [], []
        for t in range(turns):
            c, s = twiddle_ref[k, 0, t : t + 1], twiddle_ref[k, 1, t : t + 1]
            for f in range(fields):
                re, im = values[2 * f], values[2 * f + 1]
                real.append(re * c - im * s)
                imag.append(re * s + im * c)
        both = [jnp.concatenate(part, axis=0).astype(BF16) for part in (real, imag)]
        result = dot(jnp.concatenate(both, axis=1), table_ref[k], ((1,), (0,)))
        grid[pl.ds(j, turns * fields * levels, stride=pitch), :] = result

    @pl.when(step == pl.num_programs(0) - 1)
    def _():
        tiles = turns // len(out_refs)
        for k, out_ref in enumerate(out_refs):
            for t in range(tiles):
                for f in range(fields):
                    start = (((info[ME] ^ k) * tiles + t) * fields + f) * levels
                    for l in range(levels):
                        block = grid[pl.ds((start + l) * pitch, rows), :].astype(BF16)
                        out_ref[f, l, :, t * LANES : (t + 1) * LANES] = block


def synthesis(recv, table, twiddle, info, dests, tile):
    sources, levels, rows, lanes = recv.shape
    turns, waves = twiddle.shape[2:]
    fields = 3
    each = STEP if rows % STEP == 0 else 1
    shape = (fields, levels, rows, tile)
    return pl.pallas_call(
        synth_kernel,
        grid_spec=pltpu.PrefetchScalarGridSpec(
            num_scalar_prefetch=1,
            grid=(rows // each,),
            in_specs=[
                pl.BlockSpec(recv.shape, lambda j, info: (0, 0, 0, 0)),
                pl.BlockSpec((each, 2 * waves, LANES), lambda j, info: (j, 0, 0)),
                pl.BlockSpec((each, 2, turns, waves), lambda j, info: (j, 0, 0, 0)),
            ],
            out_specs=[pl.BlockSpec(shape, lambda j, info: (0, 0, 0, 0))] * dests,
            scratch_shapes=[
                pltpu.VMEM((2 * fields, waves // LANES, levels * (rows + 1), LANES), F32),
                pltpu.VMEM((turns * fields * levels * (rows + 1), LANES), F32),
            ],
        ),
        out_shape=[jax.ShapeDtypeStruct(shape, BF16)] * dests,
        compiler_params=pltpu.CompilerParams(vmem_limit_bytes=24 * MIB),
        cost_estimate=cost(4 * rows * waves * fields * levels * turns * LANES, 4 * rows * waves * LANES),
        name="synthesis",
    )(info, recv, *[pltpu.with_memory_space_constraint(v, pltpu.HBM) for v in (table, twiddle)])


def edge_kernel(
    info, state_ref, base_ref, temp_ref, row_a_ref, row_b_ref, col_a_ref, col_b_ref, react_ref
):
    tracers, levels, rows, tile = state_ref.shape
    cells = tracers * rows

    @pl.when(pl.program_id(0) == 0)
    def _():
        rates = jnp.concatenate([base_ref[...], temp_ref[...]], axis=0)
        high = rates.astype(BF16)
        low = (rates - high.astype(F32)).astype(BF16)

        def iota(shape, axis):
            return lax.broadcasted_iota(jnp.int32, shape, axis)

        shape = (2 * cells, 2 * tracers)
        down = jnp.where(iota(shape, 0) // rows == iota(shape, 1), 1.0, 0.0).astype(BF16)
        shape = (tracers, cells)
        over = jnp.where(iota(shape, 0) == iota(shape, 1) // rows, 1.0, 0.0).astype(BF16)
        shape = (2 * cells, cells)
        same = iota(shape, 0) % rows == iota(shape, 1) % rows
        for k, part in enumerate((high, low)):
            wide = dot(dot(down, part, ((1,), (0,))).astype(BF16), over, ((1,), (0,)))
            react_ref[:, k * cells : (k + 1) * cells] = jnp.where(same, wide, 0.0).astype(BF16)

    def iota(shape, axis):
        return lax.broadcasted_iota(jnp.int32, shape, axis)

    odd = info[BAND] % 2, info[ME] % 2
    far, near = (1 - odd[0]) * (rows - 1), odd[0] * (rows - 1)
    shape = (2 * tracers, cells)
    end = jnp.where(iota(shape, 0) < tracers, far, near)
    pick = iota(shape, 1) == (iota(shape, 0) % tracers) * rows + end
    pick = jnp.where(pick, 1.0, 0.0).astype(BF16)
    shape = (tile, 2 * LANES)
    far, near = (1 - odd[1]) * (tile - 1), odd[1] * (tile - 1)
    is_end = iota(shape, 0) == jnp.where(iota(shape, 1) < LANES, far, near)
    level = iota(shape, 1) % LANES - pl.program_id(0) * levels
    columns = jnp.zeros((cells, 2 * LANES), F32)
    for l in range(levels):
        x = state_ref[:, l].reshape(cells, tile)
        picked = dot(pick, x, ((1,), (0,)))
        row_a_ref[l] = picked[:tracers].astype(BF16)
        row_b_ref[l] = picked[tracers:].astype(BF16)
        mark = jnp.where(is_end & (level == l), 1.0, 0.0).astype(BF16)
        columns = columns + dot(x, mark, ((1,), (0,)))

    @pl.when(pl.program_id(0) == 0)
    def _():
        col_a_ref[...] = columns[:, :LANES].astype(BF16)
        col_b_ref[...] = columns[:, LANES:].astype(BF16)

    @pl.when(pl.program_id(0) > 0)
    def _():
        col_a_ref[...] = (col_a_ref[...].astype(F32) + columns[:, :LANES]).astype(BF16)
        col_b_ref[...] = (col_b_ref[...].astype(F32) + columns[:, LANES:]).astype(BF16)


def edges(state, react_base, react_temp, info):
    tracers, levels, rows, tile = state.shape
    block = 16
    cells = tracers * rows
    rowed = jax.ShapeDtypeStruct((levels, tracers, tile), BF16)
    columned = jax.ShapeDtypeStruct((cells, LANES), BF16)
    row_spec = pl.BlockSpec((block, tracers, tile), lambda i, info: (i, 0, 0))
    col_spec = pl.BlockSpec((cells, LANES), lambda i, info: (0, 0))
    wide = (2 * cells, 2 * cells)
    return pl.pallas_call(
        edge_kernel,
        grid_spec=pltpu.PrefetchScalarGridSpec(
            num_scalar_prefetch=1,
            grid=(levels // block,),
            in_specs=[
                pl.BlockSpec((tracers, block, rows, tile), lambda i, info: (0, i, 0, 0)),
                pl.BlockSpec(react_base.shape, lambda i, info: (0, 0)),
                pl.BlockSpec(react_temp.shape, lambda i, info: (0, 0)),
            ],
            out_specs=[
                row_spec, row_spec, col_spec, col_spec, pl.BlockSpec(wide, lambda i, info: (0, 0)),
            ],
        ),
        out_shape=[rowed, rowed, columned, columned, jax.ShapeDtypeStruct(wide, BF16)],
        compiler_params=pltpu.CompilerParams(vmem_limit_bytes=52 * MIB),
        cost_estimate=cost(4 * state.size * 32, 2 * state.size),
        name="edges",
    )(info, state, react_base, react_temp)


def shifted(value, outer, axis, step):
    size = value[0].shape[axis]
    turned = [pltpu.roll(v, -step % size, axis) for v in value]
    place = lax.broadcasted_iota(jnp.int32, value[0].shape, axis)
    at_end = place == (size - 1 if step == 1 else 0)
    following = turned[1:] + [outer] if step == 1 else [outer] + turned[:-1]
    return [jnp.where(at_end, f, t) for f, t in zip(following, turned)]


def chem_kernel(scale, k, info, *refs):
    state_ref, row_a_ref, row_b_ref, col_a_ref, col_b_ref, grid_ref, react_ref = refs[:7]
    new_ref, active_ref, south, north, advected, rounded = refs[-6:]
    tracers, levels, rows, tile = state_ref.shape
    cells = tracers * rows
    odd_band, odd_tile = info[BAND] % 2 == 1, info[ME] % 2 == 1
    first = ((info[ME] ^ k) * pl.num_programs(0) + pl.program_id(0)) * levels

    def column(value):
        return pltpu.roll(value, lax.rem(LANES - first, LANES), 1)

    a, b = col_a_ref[...].astype(F32), col_b_ref[...].astype(F32)
    west, east = column(jnp.where(odd_tile, a, b)), column(jnp.where(odd_tile, b, a))
    row = lax.broadcasted_iota(jnp.int32, (rows, tile), 0)
    lane = lax.broadcasted_iota(jnp.int32, (rows, tile), 1)
    ids, points = IDS, IDS + active_ref.shape[0]
    count = jnp.full((rows, tile), info[points], jnp.int32)
    for j in range(1, rows):
        count = jnp.where(row == j, info[points + j], count)
    mask = jnp.where(info[ME] * tile + lane < count, 1.0, 0.0)
    across = [slice(v * LANES, (v + 1) * LANES) for v in range(tile // LANES)]
    along = [slice(v * SUBLANES, (v + 1) * SUBLANES) for v in range(rows // SUBLANES)]

    for l in range(levels):
        wind_u = grid_ref[0, l].astype(F32) * (scale * 0.1)
        wind_v = grid_ref[1, l].astype(F32) * (scale * 0.1)
        from_east, from_west = 0.05 - wind_u, 0.05 + wind_u
        from_north, from_south = 0.05 - wind_v, 0.05 + wind_v
        a, b = row_a_ref[l].astype(F32), row_b_ref[l].astype(F32)
        south[l] = jnp.where(odd_band, a, b)
        north[l] = jnp.where(odd_band, b, a)
        for t in range(tracers):
            cell = slice(t * rows, (t + 1) * rows)
            x = state_ref[t, l].astype(F32)
            outer = [jnp.broadcast_to(col[cell, l : l + 1], (rows, LANES)) for col in (east, west)]
            parts = [x[:, v] for v in across]
            qe = jnp.concatenate(shifted(parts, outer[0], 1, 1), axis=1)
            qw = jnp.concatenate(shifted(parts, outer[1], 1, -1), axis=1)
            shape = (SUBLANES, tile)
            outer = [jnp.broadcast_to(ref[l, t : t + 1], shape) for ref in (north, south)]
            parts = [x[v] for v in along]
            qn = jnp.concatenate(shifted(parts, outer[0], 0, 1), axis=0)
            qs = jnp.concatenate(shifted(parts, outer[1], 0, -1), axis=0)
            moved = 0.8 * x + from_east * qe + from_west * qw + from_north * qn + from_south * qs
            advected[l, cell] = moved
            rounded[l, cell] = moved.astype(BF16)
    for l in range(levels):
        temper = grid_ref[2, l].astype(F32) * scale
        high = rounded[l]
        terms = dot(react_ref[...], jnp.concatenate([high, high], axis=0), ((1,), (0,)))
        for t in range(tracers):
            cell = slice(t * rows, (t + 1) * rows)
            warm = slice(cells + t * rows, cells + (t + 1) * rows)
            reacted = (advected[l, cell] + terms[cell] + temper * terms[warm]) * mask
            new_ref[t, l] = reacted.astype(BF16)
    for a in range(active_ref.shape[0]):
        active_ref[a] = new_ref[info[ids + a]]


def chemistry(state, halos, grid, react, info, k, actives, waves, before):
    tracers, levels, rows, tile = state.shape
    fields, own = grid.shape[:2]
    some = 4 if own % 4 == 0 else own
    steps = own // some
    cells = tracers * rows
    scale = 1.0 / float(np.sqrt(np.float32(waves)))

    def whole(shape):
        return pl.BlockSpec(shape, lambda i, info: (0,) * len(shape))

    row_spec = pl.BlockSpec((some, tracers, tile), lambda i, info: ((info[ME] ^ k) * steps + i, 0, 0))
    state_spec = pl.BlockSpec(
        (tracers, some, rows, tile), lambda i, info: (0, (info[ME] ^ k) * steps + i, 0, 0)
    )
    state = pltpu.with_memory_space_constraint(state, pltpu.HBM)
    operands = [state, *halos, grid, react]
    in_specs = [
        state_spec,
        row_spec,
        row_spec,
        whole(halos[2].shape),
        whole(halos[3].shape),
        pl.BlockSpec((fields, some, rows, tile), lambda i, info: (0, i, 0, 0)),
        whole(react.shape),
    ]
    aliases = {}
    if before is not None:
        aliases = {1 + len(operands): 0}
        operands.append(before)
        in_specs.append(pl.BlockSpec(memory_space=pl.ANY))
    return pl.pallas_call(
        functools.partial(chem_kernel, scale, k),
        grid_spec=pltpu.PrefetchScalarGridSpec(
            num_scalar_prefetch=1,
            grid=(steps,),
            in_specs=in_specs,
            out_specs=[
                state_spec,
                pl.BlockSpec((actives, some, rows, tile), lambda i, info: (0, i, 0, 0)),
            ],
            scratch_shapes=[
                pltpu.VMEM((some, tracers, tile), F32),
                pltpu.VMEM((some, tracers, tile), F32),
                pltpu.VMEM((some, cells, tile), F32),
                pltpu.VMEM((some, cells, tile), BF16),
            ],
        ),
        out_shape=[
            jax.ShapeDtypeStruct(state.shape, BF16),
            jax.ShapeDtypeStruct((actives, own, rows, tile), BF16),
        ],
        input_output_aliases=aliases,
        compiler_params=pltpu.CompilerParams(vmem_limit_bytes=16 * MIB),
        cost_estimate=cost(own * cells * tile, own * tile),
        name="chemistry",
    )(info, *operands)


def spread_kernel(order, info, *refs):
    *recv_refs, out_ref = refs
    tile = recv_refs[0].shape[3]
    for k, recv_ref in zip(order, recv_refs):
        start = pl.multiple_of((info[ME] ^ k) * tile, LANES)
        out_ref[:, :, :, pl.ds(start, tile)] = recv_ref[...].astype(F32)


def spread(parts, order, info):
    actives, own, rows, tile = parts[0].shape
    wide = len(parts) * tile
    return pl.pallas_call(
        functools.partial(spread_kernel, order),
        grid_spec=pltpu.PrefetchScalarGridSpec(
            num_scalar_prefetch=1,
            grid=(actives,),
            in_specs=[pl.BlockSpec((1, own, rows, tile), lambda a, info: (a, 0, 0, 0))] * len(parts),
            out_specs=pl.BlockSpec((1, own, rows, wide), lambda a, info: (a, 0, 0, 0)),
        ),
        out_shape=jax.ShapeDtypeStruct((actives, own, rows, wide), F32),
        compiler_params=pltpu.CompilerParams(vmem_limit_bytes=8 * MIB),
        cost_estimate=cost(actives, actives),
        name="spread",
    )(info, *parts)


def legendre_kernel(spectral_ref, legendre_ref, out_ref, rows_of, sums):
    parts, own, block, size = spectral_ref.shape
    bands, _, rows, pitch = out_ref.shape
    share = block * pl.num_programs(0)
    step = pl.program_id(0)
    lines = parts * own
    apart, stretch = block + 1, pitch + 1

    @pl.when(step == 0)
    def _():
        for h in range(sums.shape[0]):
            for l in range(own):
                tail = pl.ds(l * stretch + parts * share, pitch - parts * share)
                sums[h, tail, :] = jnp.zeros((pitch - parts * share, LANES), F32)

    for v in range(size // LANES):
        part = spectral_ref[:, :, :, v * LANES : (v + 1) * LANES].astype(F32)
        part = part.reshape(lines, block, LANES)
        for i in range(lines):
            rows_of[v, pl.ds(i * apart, block), :] = part[i]
    def line(m):
        x = [rows_of[v, pl.ds(m, lines, stride=apart), :] for v in range(size // LANES)]
        return jnp.concatenate(x, axis=1).astype(BF16)

    wide = legendre_ref.shape[2]
    group = max(1, 2 * LANES // wide)
    for m in range(0, block, group):
        both = range(m, m + group)
        x = jnp.concatenate([line(i) for i in both], axis=0)
        y = jnp.concatenate([legendre_ref[i] for i in both], axis=1)
        product = dot(x, y, ((1,), (0,)))
        for i in both:
            result = product[(i - m) * lines : (i - m + 1) * lines, (i - m) * wide : (i - m + 1) * wide]
            for r in range(parts):
                at = r * share + step * block + i
                for h in range(sums.shape[0]):
                    piece = result[r * own : (r + 1) * own, h * LANES : (h + 1) * LANES]
                    sums[h, pl.ds(at, own, stride=stretch), :] = piece

    @pl.when(step == pl.num_programs(0) - 1)
    def _():
        some = LANES // rows
        for l in range(own):
            for h in range(sums.shape[0]):
                turned = sums[h, pl.ds(l * stretch, pitch), :].T.astype(BF16)
                out_ref[h * some : (h + 1) * some, l] = turned.reshape(some, rows, pitch)


def legendre_sums(spectral, legendre, bands):
    parts, own, share, size = spectral.shape
    rows = legendre.shape[2] // bands
    pitch = -(-parts * share // LANES) * LANES
    block = 16 if share % 16 == 0 else 8
    shape = (bands, own, rows, pitch)
    return pl.pallas_call(
        legendre_kernel,
        grid=(share // block,),
        in_specs=[
            pl.BlockSpec((parts, own, block, size), lambda i: (0, 0, i, 0)),
            pl.BlockSpec((block,) + legendre.shape[1:], lambda i: (i, 0, 0)),
        ],
        out_specs=pl.BlockSpec(shape, lambda i: (0, 0, 0, 0)),
        out_shape=jax.ShapeDtypeStruct(shape, BF16),
        scratch_shapes=[
            pltpu.VMEM((size // LANES, parts * own * (block + 1), LANES), F32),
            pltpu.VMEM((legendre.shape[2] // LANES, own * (pitch + 1), LANES), F32),
        ],
        compiler_params=pltpu.CompilerParams(vmem_limit_bytes=56 * MIB),
        cost_estimate=cost(2 * parts * own * legendre.size, 2 * (spectral.size + legendre.size)),
        name="legendre",
    )(spectral, legendre)


def exchange(value, axis, pairs):
    return lax.ppermute(value, axis, [p for a, b in pairs for p in ((a, b), (b, a))])


def neighbours(axis, first):
    size = lax.axis_size(axis)
    return [(i, i + 1) for i in range(first, size - 1, 2)]


def partners(axis, k):
    return [(i, i ^ k) for i in range(lax.axis_size(axis)) if i < i ^ k]


def body(spectral, legendre, wave_ids, points, tracers, react_base, react_temp, active_ids):
    bands, tiles = lax.axis_size("lat"), lax.axis_size("lon")
    tile = tracers.shape[3]
    waves = wave_ids.shape[0]
    band, me = lax.axis_index("lat"), lax.axis_index("lon")

    sent = legendre_sums(spectral, legendre, bands)

    rows = points.shape[0]
    info = jnp.concatenate([jnp.stack([band, me]), active_ids, points]).astype(jnp.int32)
    sent, info = lax.optimization_barrier((sent, info))
    recv = lax.all_to_all(sent, "lat", split_axis=0, concat_axis=0, tiled=True)
    *ends, react = edges(tracers, react_base, react_temp, info)
    halos = [
        exchange(ends[0], "lat", neighbours("lat", 0)),
        exchange(ends[2], "lon", neighbours("lon", 0)),
        exchange(ends[3], "lon", neighbours("lon", 1)),
    ]
    react, wave_ids = lax.optimization_barrier((react, wave_ids))
    table, twiddle = tables(info, wave_ids, rows, tiles * tile // LANES)
    recv, table, twiddle, react, halos, last = lax.optimization_barrier(
        (recv, table, twiddle, react, halos, ends[1])
    )
    halos.insert(1, exchange(last, "lat", neighbours("lat", 1)))
    grids = synthesis(recv, table, twiddle, info, tiles, tile)

    middle, inner = list(range(tiles // 2, tiles)), list(range(1, tiles // 2))
    soon, late = middle[: tiles // 4], middle[tiles // 4 :]

    def send(value, k):
        return exchange(value, "lon", partners("lon", k))

    moved = {0: grids[0]} | {k: send(grids[k], k) for k in soon}
    new, active = None, {}
    for k in [0] + soon + late + inner:
        new, active[k] = chemistry(
            tracers, halos, moved[k], react, info, k, active_ids.shape[0], waves, new
        )
        if k:
            active[k] = send(active[k], k)
        else:
            rest = late + inner
            held, active[0] = lax.optimization_barrier(([grids[i] for i in rest], active[0]))
            moved |= {i: send(value, i) for i, value in zip(rest, held)}
    order = [0] + soon + late + inner
    through = lax.optimization_barrier([active[k] for k in soon + late])
    active |= zip(soon + late, through)
    active = dict(zip(order, lax.optimization_barrier([active[k] for k in order])))
    return new, spread([active[k] for k in order], order, info)


def solution(mesh):
    return jax.shard_map(
        body,
        mesh=mesh,
        in_specs=(
            P(None, "lon", "lat", None),
            P("lat", None, None),
            P(),
            P("lat"),
            P(None, None, "lat", "lon"),
            P(),
            P(),
            P(),
        ),
        out_specs=(P(None, None, "lat", "lon"), P(None, "lon", "lat", None)),
        check_vma=False,
    )
```

```python
import functools

import jax
import jax.numpy as jnp
import numpy as np
from jax import lax
from jax.experimental import pallas as pl
from jax.experimental.pallas import tpu as pltpu
from jax.sharding import PartitionSpec as P

F32 = jnp.float32
BF16 = jnp.bfloat16
LANES = 128
SUBLANES = 8
LOW = 16
STEP = 4
MIB = 1024 * 1024

COS = (
    0.9999999890590228,
    -19.739204499454026,
    64.93911745990036,
    -85.45013953095037,
    60.16763095136588,
    -25.96759924965491,
    6.528658162567069,
)
SIN = (
    6.283185302511503,
    -41.34170040531769,
    81.60513138580204,
    -76.7030153539128,
    42.02592698618416,
    -14.899846668691637,
    3.238137510515757,
)


def dot(a, b, dims):
    return lax.dot_general(a, b, (dims, ((), ())), preferred_element_type=F32)


BAND, ME, IDS = 0, 1, 2


def cost(flops, moved):
    return pl.CostEstimate(flops=int(flops), bytes_accessed=int(moved), transcendentals=0)


def unit_circle(step, rows, waves, count):
    index = lax.broadcasted_iota(jnp.int32, (rows, waves.shape[1]), 0) * step
    product = index.astype(F32) * waves
    inverse = 1.0 / count
    turns = (product - jnp.floor(product * inverse) * count) * inverse
    y = turns - jnp.floor(turns + 0.5)
    z = y * y
    cosine = jnp.full_like(z, COS[-1])
    sine = jnp.full_like(z, SIN[-1])
    for c, s in zip(COS[-2::-1], SIN[-2::-1]):
        cosine = cosine * z + c
        sine = sine * z + s
    return cosine, sine * y


def table_kernel(first, info, waves_ref, table_ref, twiddle_ref):
    size, turns = waves_ref.shape[1], twiddle_ref.shape[2]
    waves = waves_ref[...].astype(F32)
    for k in range(table_ref.shape[0]):
        row = pl.program_id(0) * table_ref.shape[0] + k
        count = jnp.full(waves.shape, info[first + row], jnp.int32).astype(F32)
        cos_low, sin_low = unit_circle(1, LOW, waves, count)
        cos_high, sin_high = unit_circle(LOW, LANES // LOW, waves, count)
        cosine, sine = [], []
        for a in range(LANES // LOW):
            ch, sh = cos_high[a : a + 1], sin_high[a : a + 1]
            cosine.append(ch * cos_low - sh * sin_low)
            sine.append(-sh * cos_low - ch * sin_low)
        table_ref[k, :size, :] = jnp.concatenate(cosine, axis=0).T.astype(BF16)
        table_ref[k, size:, :] = jnp.concatenate(sine, axis=0).T.astype(BF16)
        cos_turn, sin_turn = unit_circle(LANES, turns, waves, count)
        twiddle_ref[k, 0] = cos_turn
        twiddle_ref[k, 1] = sin_turn


def tables(info, wave_ids, rows, turns):
    waves = wave_ids.shape[0]
    each = STEP if rows % STEP == 0 else 1
    return pl.pallas_call(
        functools.partial(table_kernel, info.shape[0] - rows),
        grid_spec=pltpu.PrefetchScalarGridSpec(
            num_scalar_prefetch=1,
            grid=(rows // each,),
            in_specs=[pl.BlockSpec((1, waves), lambda j, p: (0, 0))],
            out_specs=[
                pl.BlockSpec((each, 2 * waves, LANES), lambda j, p: (j, 0, 0)),
                pl.BlockSpec((each, 2, turns, waves), lambda j, p: (j, 0, 0, 0)),
            ],
        ),
        out_shape=[
            pltpu.HBM((rows, 2 * waves, LANES), BF16),
            pltpu.HBM((rows, 2, turns, waves), F32),
        ],
        compiler_params=pltpu.CompilerParams(vmem_limit_bytes=20 * MIB),
        cost_estimate=cost(rows * waves * LANES * 8, rows * waves * LANES * 4),
        name="tables",
    )(info, wave_ids[None, :])


def place(pieces, width):
    out = [None] * (width // LANES)
    lane = lax.broadcasted_iota(jnp.int32, (pieces[0][0].shape[0], LANES), 1)
    for value, start, count, here in pieces:
        shift = (here - start) % LANES
        for a in range(start // LANES, (start + count - 1) // LANES + 1):
            part = value[:, a * LANES : (a + 1) * LANES]
            if shift:
                part = pltpu.roll(part, shift, 1)
            first = max(start, a * LANES) - start + here
            last = min(start + count, (a + 1) * LANES) - start + here
            for v in range(first // LANES, (last - 1) // LANES + 1):
                low, high = max(first - v * LANES, 0), min(last - v * LANES, LANES)
                if out[v] is None:
                    out[v] = part
                else:
                    out[v] = jnp.where((lane >= low) & (lane < high), part, out[v])
    return out


def synth_kernel(info, recv_ref, table_hbm, twiddle_hbm, *refs):
    *out_refs, coef, grid, table_ref, twiddle_ref, sems = refs
    sources, levels, rows, _ = recv_ref.shape
    fields, waves = coef.shape[0] // 2, coef.shape[1] * LANES
    share = waves // sources
    turns = twiddle_ref.shape[2]
    steps = sems.shape[1]
    each = rows // steps
    pitch = rows + 1

    def copies(step):
        some = pl.ds(step * each, each)
        pairs = ((table_hbm, table_ref), (twiddle_hbm, twiddle_ref))
        return [
            pltpu.make_async_copy(src.at[some], dst.at[some], sems.at[i, step])
            for i, (src, dst) in enumerate(pairs)
        ]

    for step in range(steps):
        for copy in copies(step):
            copy.start()

    def level(l, carry):
        values = [recv_ref[s, l].astype(F32) for s in range(sources)]
        for r in range(2 * fields):
            windows = [(values[s], r * share, share, s * share) for s in range(sources)]
            for v, part in enumerate(place(windows, waves)):
                coef[r, v, pl.ds(l * pitch, rows), :] = part
        return carry

    lax.fori_loop(0, levels, level, 0)

    def some_rows(step, carry):
        for copy in copies(step):
            copy.wait()
        for k in range(each):
            one_row(step * each + k)
        return carry

    def one_row(j):
        def own_row(r):
            parts = [coef[r, v, pl.ds(j, levels, stride=pitch), :] for v in range(waves // LANES)]
            return jnp.concatenate(parts, axis=1)

        values = [own_row(r) for r in range(2 * fields)]
        real, imag = [], []
        for t in range(turns):
            c, s = twiddle_ref[j, 0, t : t + 1], twiddle_ref[j, 1, t : t + 1]
            for f in range(fields):
                re, im = values[2 * f], values[2 * f + 1]
                real.append(re * c - im * s)
                imag.append(re * s + im * c)
        both = [jnp.concatenate(part, axis=0).astype(BF16) for part in (real, imag)]
        result = dot(jnp.concatenate(both, axis=1), table_ref[j], ((1,), (0,)))
        grid[pl.ds(j, turns * fields * levels, stride=pitch), :] = result

    lax.fori_loop(0, steps, some_rows, 0)
    tiles = turns // len(out_refs)
    for k, out_ref in enumerate(out_refs):
        for t in range(tiles):
            for f in range(fields):
                start = (((info[ME] ^ k) * tiles + t) * fields + f) * levels
                for l in range(levels):
                    block = grid[pl.ds((start + l) * pitch, rows), :].astype(BF16)
                    out_ref[f, l, :, t * LANES : (t + 1) * LANES] = block


def synthesis(recv, table, twiddle, info, dests, tile):
    sources, levels, rows, lanes = recv.shape
    turns, waves = twiddle.shape[2:]
    fields = 3
    each = STEP if rows % STEP == 0 else 1
    shape = (fields, levels, rows, tile)
    return pl.pallas_call(
        synth_kernel,
        grid_spec=pltpu.PrefetchScalarGridSpec(
            num_scalar_prefetch=1,
            grid=(1,),
            in_specs=[
                pl.BlockSpec(recv.shape, lambda j, info: (0, 0, 0, 0)),
                pl.BlockSpec(memory_space=pl.ANY),
                pl.BlockSpec(memory_space=pl.ANY),
            ],
            out_specs=[pl.BlockSpec(shape, lambda j, info: (0, 0, 0, 0))] * dests,
            scratch_shapes=[
                pltpu.VMEM((2 * fields, waves // LANES, levels * (rows + 1), LANES), F32),
                pltpu.VMEM((turns * fields * levels * (rows + 1), LANES), F32),
                pltpu.VMEM(table.shape, BF16),
                pltpu.VMEM(twiddle.shape, F32),
                pltpu.SemaphoreType.DMA((2, rows // each)),
            ],
        ),
        out_shape=[jax.ShapeDtypeStruct(shape, BF16)] * dests,
        compiler_params=pltpu.CompilerParams(vmem_limit_bytes=24 * MIB),
        cost_estimate=cost(4 * rows * waves * fields * levels * turns * LANES, 4 * rows * waves * LANES),
        name="synthesis",
    )(info, recv, *[pltpu.with_memory_space_constraint(v, pltpu.HBM) for v in (table, twiddle)])


def edge_kernel(
    info, state_ref, base_ref, temp_ref, row_a_ref, row_b_ref, col_a_ref, col_b_ref, react_ref
):
    tracers, levels, rows, tile = state_ref.shape
    cells = tracers * rows

    @pl.when(pl.program_id(0) == 0)
    def _():
        rates = jnp.concatenate([base_ref[...], temp_ref[...]], axis=0)
        high = rates.astype(BF16)
        low = (rates - high.astype(F32)).astype(BF16)

        def iota(shape, axis):
            return lax.broadcasted_iota(jnp.int32, shape, axis)

        shape = (2 * cells, 2 * tracers)
        down = jnp.where(iota(shape, 0) // rows == iota(shape, 1), 1.0, 0.0).astype(BF16)
        shape = (tracers, cells)
        over = jnp.where(iota(shape, 0) == iota(shape, 1) // rows, 1.0, 0.0).astype(BF16)
        shape = (2 * cells, cells)
        same = iota(shape, 0) % rows == iota(shape, 1) % rows
        for k, part in enumerate((high, low)):
            wide = dot(dot(down, part, ((1,), (0,))).astype(BF16), over, ((1,), (0,)))
            react_ref[:, k * cells : (k + 1) * cells] = jnp.where(same, wide, 0.0).astype(BF16)

    def iota(shape, axis):
        return lax.broadcasted_iota(jnp.int32, shape, axis)

    odd = info[BAND] % 2, info[ME] % 2
    far, near = (1 - odd[0]) * (rows - 1), odd[0] * (rows - 1)
    shape = (2 * tracers, cells)
    end = jnp.where(iota(shape, 0) < tracers, far, near)
    pick = iota(shape, 1) == (iota(shape, 0) % tracers) * rows + end
    pick = jnp.where(pick, 1.0, 0.0).astype(BF16)
    shape = (tile, 2 * LANES)
    far, near = (1 - odd[1]) * (tile - 1), odd[1] * (tile - 1)
    is_end = iota(shape, 0) == jnp.where(iota(shape, 1) < LANES, far, near)
    level = iota(shape, 1) % LANES - pl.program_id(0) * levels
    columns = jnp.zeros((cells, 2 * LANES), F32)
    for l in range(levels):
        x = state_ref[:, l].reshape(cells, tile)
        picked = dot(pick, x, ((1,), (0,)))
        row_a_ref[l] = picked[:tracers].astype(BF16)
        row_b_ref[l] = picked[tracers:].astype(BF16)
        mark = jnp.where(is_end & (level == l), 1.0, 0.0).astype(BF16)
        columns = columns + dot(x, mark, ((1,), (0,)))

    @pl.when(pl.program_id(0) == 0)
    def _():
        col_a_ref[...] = columns[:, :LANES].astype(BF16)
        col_b_ref[...] = columns[:, LANES:].astype(BF16)

    @pl.when(pl.program_id(0) > 0)
    def _():
        col_a_ref[...] = (col_a_ref[...].astype(F32) + columns[:, :LANES]).astype(BF16)
        col_b_ref[...] = (col_b_ref[...].astype(F32) + columns[:, LANES:]).astype(BF16)


def edges(state, react_base, react_temp, info):
    tracers, levels, rows, tile = state.shape
    block = 16
    cells = tracers * rows
    rowed = jax.ShapeDtypeStruct((levels, tracers, tile), BF16)
    columned = jax.ShapeDtypeStruct((cells, LANES), BF16)
    row_spec = pl.BlockSpec((block, tracers, tile), lambda i, info: (i, 0, 0))
    col_spec = pl.BlockSpec((cells, LANES), lambda i, info: (0, 0))
    wide = (2 * cells, 2 * cells)
    return pl.pallas_call(
        edge_kernel,
        grid_spec=pltpu.PrefetchScalarGridSpec(
            num_scalar_prefetch=1,
            grid=(levels // block,),
            in_specs=[
                pl.BlockSpec((tracers, block, rows, tile), lambda i, info: (0, i, 0, 0)),
                pl.BlockSpec(react_base.shape, lambda i, info: (0, 0)),
                pl.BlockSpec(react_temp.shape, lambda i, info: (0, 0)),
            ],
            out_specs=[
                row_spec, row_spec, col_spec, col_spec, pl.BlockSpec(wide, lambda i, info: (0, 0)),
            ],
        ),
        out_shape=[rowed, rowed, columned, columned, jax.ShapeDtypeStruct(wide, BF16)],
        compiler_params=pltpu.CompilerParams(vmem_limit_bytes=52 * MIB),
        cost_estimate=cost(4 * state.size * 32, 2 * state.size),
        name="edges",
    )(info, state, react_base, react_temp)


def shifted(value, outer, axis, step):
    size = value[0].shape[axis]
    turned = [pltpu.roll(v, -step % size, axis) for v in value]
    place = lax.broadcasted_iota(jnp.int32, value[0].shape, axis)
    at_end = place == (size - 1 if step == 1 else 0)
    following = turned[1:] + [outer] if step == 1 else [outer] + turned[:-1]
    return [jnp.where(at_end, f, t) for f, t in zip(following, turned)]


def chem_kernel(scale, k, info, *refs):
    state_ref, row_a_ref, row_b_ref, col_a_ref, col_b_ref, grid_ref, react_ref = refs[:7]
    new_ref, active_ref, south, north, advected, rounded = refs[-6:]
    tracers, levels, rows, tile = state_ref.shape
    cells = tracers * rows
    odd_band, odd_tile = info[BAND] % 2 == 1, info[ME] % 2 == 1
    first = ((info[ME] ^ k) * pl.num_programs(0) + pl.program_id(0)) * levels

    def column(value):
        return pltpu.roll(value, lax.rem(LANES - first, LANES), 1)

    a, b = col_a_ref[...].astype(F32), col_b_ref[...].astype(F32)
    west, east = column(jnp.where(odd_tile, a, b)), column(jnp.where(odd_tile, b, a))
    row = lax.broadcasted_iota(jnp.int32, (rows, tile), 0)
    lane = lax.broadcasted_iota(jnp.int32, (rows, tile), 1)
    ids, points = IDS, IDS + active_ref.shape[0]
    count = jnp.full((rows, tile), info[points], jnp.int32)
    for j in range(1, rows):
        count = jnp.where(row == j, info[points + j], count)
    mask = jnp.where(info[ME] * tile + lane < count, 1.0, 0.0)
    across = [slice(v * LANES, (v + 1) * LANES) for v in range(tile // LANES)]
    along = [slice(v * SUBLANES, (v + 1) * SUBLANES) for v in range(rows // SUBLANES)]

    for l in range(levels):
        wind_u = grid_ref[0, l].astype(F32) * (scale * 0.1)
        wind_v = grid_ref[1, l].astype(F32) * (scale * 0.1)
        from_east, from_west = 0.05 - wind_u, 0.05 + wind_u
        from_north, from_south = 0.05 - wind_v, 0.05 + wind_v
        a, b = row_a_ref[l].astype(F32), row_b_ref[l].astype(F32)
        south[l] = jnp.where(odd_band, a, b)
        north[l] = jnp.where(odd_band, b, a)
        for t in range(tracers):
            cell = slice(t * rows, (t + 1) * rows)
            x = state_ref[t, l].astype(F32)
            outer = [jnp.broadcast_to(col[cell, l : l + 1], (rows, LANES)) for col in (east, west)]
            parts = [x[:, v] for v in across]
            qe = jnp.concatenate(shifted(parts, outer[0], 1, 1), axis=1)
            qw = jnp.concatenate(shifted(parts, outer[1], 1, -1), axis=1)
            shape = (SUBLANES, tile)
            outer = [jnp.broadcast_to(ref[l, t : t + 1], shape) for ref in (north, south)]
            parts = [x[v] for v in along]
            qn = jnp.concatenate(shifted(parts, outer[0], 0, 1), axis=0)
            qs = jnp.concatenate(shifted(parts, outer[1], 0, -1), axis=0)
            moved = 0.8 * x + from_east * qe + from_west * qw + from_north * qn + from_south * qs
            advected[l, cell] = moved
            rounded[l, cell] = moved.astype(BF16)
    for l in range(levels):
        temper = grid_ref[2, l].astype(F32) * scale
        high = rounded[l]
        terms = dot(react_ref[...], jnp.concatenate([high, high], axis=0), ((1,), (0,)))
        for t in range(tracers):
            cell = slice(t * rows, (t + 1) * rows)
            warm = slice(cells + t * rows, cells + (t + 1) * rows)
            reacted = (advected[l, cell] + terms[cell] + temper * terms[warm]) * mask
            new_ref[t, l] = reacted.astype(BF16)
    for a in range(active_ref.shape[0]):
        active_ref[a] = new_ref[info[ids + a]]


def chemistry(state, halos, grid, react, info, k, actives, waves, before):
    tracers, levels, rows, tile = state.shape
    fields, own = grid.shape[:2]
    some = 4 if own % 4 == 0 else own
    steps = own // some
    cells = tracers * rows
    scale = 1.0 / float(np.sqrt(np.float32(waves)))

    def whole(shape):
        return pl.BlockSpec(shape, lambda i, info: (0,) * len(shape))

    row_spec = pl.BlockSpec((some, tracers, tile), lambda i, info: ((info[ME] ^ k) * steps + i, 0, 0))
    state_spec = pl.BlockSpec(
        (tracers, some, rows, tile), lambda i, info: (0, (info[ME] ^ k) * steps + i, 0, 0)
    )
    state = pltpu.with_memory_space_constraint(state, pltpu.HBM)
    operands = [state, *halos, grid, react]
    in_specs = [
        state_spec,
        row_spec,
        row_spec,
        whole(halos[2].shape),
        whole(halos[3].shape),
        pl.BlockSpec((fields, some, rows, tile), lambda i, info: (0, i, 0, 0)),
        whole(react.shape),
    ]
    aliases = {}
    if before is not None:
        aliases = {1 + len(operands): 0}
        operands.append(before)
        in_specs.append(pl.BlockSpec(memory_space=pl.ANY))
    return pl.pallas_call(
        functools.partial(chem_kernel, scale, k),
        grid_spec=pltpu.PrefetchScalarGridSpec(
            num_scalar_prefetch=1,
            grid=(steps,),
            in_specs=in_specs,
            out_specs=[
                state_spec,
                pl.BlockSpec((actives, some, rows, tile), lambda i, info: (0, i, 0, 0)),
            ],
            scratch_shapes=[
                pltpu.VMEM((some, tracers, tile), F32),
                pltpu.VMEM((some, tracers, tile), F32),
                pltpu.VMEM((some, cells, tile), F32),
                pltpu.VMEM((some, cells, tile), BF16),
            ],
        ),
        out_shape=[
            jax.ShapeDtypeStruct(state.shape, BF16),
            jax.ShapeDtypeStruct((actives, own, rows, tile), BF16),
        ],
        input_output_aliases=aliases,
        compiler_params=pltpu.CompilerParams(vmem_limit_bytes=16 * MIB),
        cost_estimate=cost(own * cells * tile, own * tile),
        name="chemistry",
    )(info, *operands)


def spread(parts, order, info, tiles, before):
    actives, own, rows, tile = parts[0].shape
    count = len(order)
    operands, aliases = list(parts), {}
    in_specs = [pl.BlockSpec(parts[0].shape, lambda i, info: (0, 0, 0, 0))] * count
    if before is not None:
        operands.append(before)
        in_specs.append(pl.BlockSpec(memory_space=pl.ANY))
        aliases = {1 + count: 0}

    def partner(i):
        k = order[0]
        for at in range(1, count):
            k = jnp.where(i == at, order[at], k)
        return k

    def kernel(info, *refs):
        for at in range(count):

            @pl.when(pl.program_id(0) == at)
            def _():
                refs[-1][...] = refs[at][...].astype(F32)

    return pl.pallas_call(
        kernel,
        grid_spec=pltpu.PrefetchScalarGridSpec(
            num_scalar_prefetch=1,
            grid=(count,),
            in_specs=in_specs,
            out_specs=pl.BlockSpec(
                (actives, own, rows, tile), lambda i, info: (0, 0, 0, info[ME] ^ partner(i))
            ),
        ),
        out_shape=jax.ShapeDtypeStruct((actives, own, rows, tiles * tile), F32),
        input_output_aliases=aliases,
        compiler_params=pltpu.CompilerParams(vmem_limit_bytes=12 * MIB),
        cost_estimate=cost(actives, actives),
        name="spread",
    )(info, *operands)


def legendre_kernel(spectral_ref, legendre_ref, out_ref, rows_of, sums):
    parts, own, block, size = spectral_ref.shape
    bands, _, rows, pitch = out_ref.shape
    share = block * pl.num_programs(0)
    step = pl.program_id(0)
    lines = parts * own
    apart, stretch = block + 1, pitch + 1

    @pl.when(step == 0)
    def _():
        for h in range(sums.shape[0]):
            for l in range(own):
                tail = pl.ds(l * stretch + parts * share, pitch - parts * share)
                sums[h, tail, :] = jnp.zeros((pitch - parts * share, LANES), F32)

    for v in range(size // LANES):
        part = spectral_ref[:, :, :, v * LANES : (v + 1) * LANES].astype(F32)
        part = part.reshape(lines, block, LANES)
        for i in range(lines):
            rows_of[v, pl.ds(i * apart, block), :] = part[i]
    def line(m):
        x = [rows_of[v, pl.ds(m, lines, stride=apart), :] for v in range(size // LANES)]
        return jnp.concatenate(x, axis=1).astype(BF16)

    wide = legendre_ref.shape[2]
    group = max(1, 2 * LANES // wide)
    for m in range(0, block, group):
        both = range(m, m + group)
        x = jnp.concatenate([line(i) for i in both], axis=0)
        y = jnp.concatenate([legendre_ref[i] for i in both], axis=1)
        product = dot(x, y, ((1,), (0,)))
        for i in both:
            result = product[(i - m) * lines : (i - m + 1) * lines, (i - m) * wide : (i - m + 1) * wide]
            for r in range(parts):
                at = r * share + step * block + i
                for h in range(sums.shape[0]):
                    piece = result[r * own : (r + 1) * own, h * LANES : (h + 1) * LANES]
                    sums[h, pl.ds(at, own, stride=stretch), :] = piece

    @pl.when(step == pl.num_programs(0) - 1)
    def _():
        some = LANES // rows
        for l in range(own):
            for h in range(sums.shape[0]):
                turned = sums[h, pl.ds(l * stretch, pitch), :].T.astype(BF16)
                out_ref[h * some : (h + 1) * some, l] = turned.reshape(some, rows, pitch)


def legendre_sums(spectral, legendre, bands):
    parts, own, share, size = spectral.shape
    rows = legendre.shape[2] // bands
    pitch = -(-parts * share // LANES) * LANES
    block = 16 if share % 16 == 0 else 8
    shape = (bands, own, rows, pitch)
    return pl.pallas_call(
        legendre_kernel,
        grid=(share // block,),
        in_specs=[
            pl.BlockSpec((parts, own, block, size), lambda i: (0, 0, i, 0)),
            pl.BlockSpec((block,) + legendre.shape[1:], lambda i: (i, 0, 0)),
        ],
        out_specs=pl.BlockSpec(shape, lambda i: (0, 0, 0, 0)),
        out_shape=jax.ShapeDtypeStruct(shape, BF16),
        scratch_shapes=[
            pltpu.VMEM((size // LANES, parts * own * (block + 1), LANES), F32),
            pltpu.VMEM((legendre.shape[2] // LANES, own * (pitch + 1), LANES), F32),
        ],
        compiler_params=pltpu.CompilerParams(vmem_limit_bytes=56 * MIB),
        cost_estimate=cost(2 * parts * own * legendre.size, 2 * (spectral.size + legendre.size)),
        name="legendre",
    )(spectral, legendre)


def exchange(value, axis, pairs):
    return lax.ppermute(value, axis, [p for a, b in pairs for p in ((a, b), (b, a))])


def neighbours(axis, first):
    size = lax.axis_size(axis)
    return [(i, i + 1) for i in range(first, size - 1, 2)]


def partners(axis, k):
    return [(i, i ^ k) for i in range(lax.axis_size(axis)) if i < i ^ k]


def body(spectral, legendre, wave_ids, points, tracers, react_base, react_temp, active_ids):
    bands, tiles = lax.axis_size("lat"), lax.axis_size("lon")
    tile = tracers.shape[3]
    waves = wave_ids.shape[0]
    band, me = lax.axis_index("lat"), lax.axis_index("lon")

    sent = legendre_sums(spectral, legendre, bands)

    rows = points.shape[0]
    info = jnp.concatenate([jnp.stack([band, me]), active_ids, points]).astype(jnp.int32)
    sent, info = lax.optimization_barrier((sent, info))
    recv = lax.all_to_all(sent, "lat", split_axis=0, concat_axis=0, tiled=True)
    *ends, react = edges(tracers, react_base, react_temp, info)
    halos = [
        exchange(ends[0], "lat", neighbours("lat", 0)),
        exchange(ends[2], "lon", neighbours("lon", 0)),
        exchange(ends[3], "lon", neighbours("lon", 1)),
    ]
    react, wave_ids = lax.optimization_barrier((react, wave_ids))
    table, twiddle = tables(info, wave_ids, rows, tiles * tile // LANES)
    recv, table, twiddle, react, halos, last = lax.optimization_barrier(
        (recv, table, twiddle, react, halos, ends[1])
    )
    halos.insert(1, exchange(last, "lat", neighbours("lat", 1)))
    grids = synthesis(recv, table, twiddle, info, tiles, tile)

    middle, inner = list(range(tiles // 2, tiles)), list(range(1, tiles // 2))
    soon, late = middle[: tiles // 4], middle[tiles // 4 :]

    def send(value, k):
        return exchange(value, "lon", partners("lon", k))

    moved = {0: grids[0]} | {k: send(grids[k], k) for k in soon}
    new, active = None, {}
    for k in [0] + soon + late + inner:
        new, active[k] = chemistry(
            tracers, halos, moved[k], react, info, k, active_ids.shape[0], waves, new
        )
        if k:
            active[k] = send(active[k], k)
        else:
            rest = late + inner
            held, active[0] = lax.optimization_barrier(([grids[i] for i in rest], active[0]))
            moved |= {i: send(value, i) for i, value in zip(rest, held)}
    early, last = [0] + soon, late + inner
    spreaded = spread([active[k] for k in early], early, info, tiles, None)
    through = lax.optimization_barrier([active[k] for k in late])
    parts = lax.optimization_barrier(through + [active[k] for k in inner])
    return new, spread(parts, last, info, tiles, spreaded)


def solution(mesh):
    return jax.shard_map(
        body,
        mesh=mesh,
        in_specs=(
            P(None, "lon", "lat", None),
            P("lat", None, None),
            P(),
            P("lat"),
            P(None, None, "lat", "lon"),
            P(),
            P(),
            P(),
        ),
        out_specs=(P(None, None, "lat", "lon"), P(None, "lon", "lat", None)),
        check_vma=False,
    )
```

```python
import functools

import jax
import jax.numpy as jnp
import numpy as np
from jax import lax
from jax.experimental import pallas as pl
from jax.experimental.pallas import tpu as pltpu
from jax.sharding import PartitionSpec as P

F32 = jnp.float32
BF16 = jnp.bfloat16
LANES = 128
SUBLANES = 8
LOW = 16
STEP = 4
MIB = 1024 * 1024

COS = (
    0.9999999890590228,
    -19.739204499454026,
    64.93911745990036,
    -85.45013953095037,
    60.16763095136588,
    -25.96759924965491,
    6.528658162567069,
)
SIN = (
    6.283185302511503,
    -41.34170040531769,
    81.60513138580204,
    -76.7030153539128,
    42.02592698618416,
    -14.899846668691637,
    3.238137510515757,
)

def dot(a, b, dims):
    return lax.dot_general(a, b, (dims, ((), ())), preferred_element_type=F32)

BAND, ME, IDS = 0, 1, 2

def cost(flops, moved):
    return pl.CostEstimate(flops=int(flops), bytes_accessed=int(moved), transcendentals=0)

def unit_circle(step, rows, waves, count):
    index = lax.broadcasted_iota(jnp.int32, (rows, waves.shape[1]), 0) * step
    product = index.astype(F32) * waves
    inverse = 1.0 / count
    turns = (product - jnp.floor(product * inverse) * count) * inverse
    y = turns - jnp.floor(turns + 0.5)
    z = y * y
    cosine = jnp.full_like(z, COS[-1])
    sine = jnp.full_like(z, SIN[-1])
    for c, s in zip(COS[-2::-1], SIN[-2::-1]):
        cosine = cosine * z + c
        sine = sine * z + s
    return cosine, sine * y

def table_kernel(first, info, waves_ref, table_ref, twiddle_ref):
    size, turns = waves_ref.shape[1], twiddle_ref.shape[2]
    waves = waves_ref[...].astype(F32)
    for k in range(table_ref.shape[0]):
        row = pl.program_id(0) * table_ref.shape[0] + k
        count = jnp.full(waves.shape, info[first + row], jnp.int32).astype(F32)
        cos_low, sin_low = unit_circle(1, LOW, waves, count)
        cos_high, sin_high = unit_circle(LOW, LANES // LOW, waves, count)
        cosine, sine = [], []
        for a in range(LANES // LOW):
            ch, sh = cos_high[a : a + 1], sin_high[a : a + 1]
            cosine.append(ch * cos_low - sh * sin_low)
            sine.append(-sh * cos_low - ch * sin_low)
        table_ref[k, :size, :] = jnp.concatenate(cosine, axis=0).T.astype(BF16)
        table_ref[k, size:, :] = jnp.concatenate(sine, axis=0).T.astype(BF16)
        cos_turn, sin_turn = unit_circle(LANES, turns, waves, count)
        twiddle_ref[k, 0] = cos_turn
        twiddle_ref[k, 1] = sin_turn

def tables(info, wave_ids, rows, turns):
    waves = wave_ids.shape[0]
    each = STEP if rows % STEP == 0 else 1
    return pl.pallas_call(
        functools.partial(table_kernel, info.shape[0] - rows),
        grid_spec=pltpu.PrefetchScalarGridSpec(
            num_scalar_prefetch=1,
            grid=(rows // each,),
            in_specs=[pl.BlockSpec((1, waves), lambda j, p: (0, 0))],
            out_specs=[
                pl.BlockSpec((each, 2 * waves, LANES), lambda j, p: (j, 0, 0)),
                pl.BlockSpec((each, 2, turns, waves), lambda j, p: (j, 0, 0, 0)),
            ],
        ),
        out_shape=[
            pltpu.HBM((rows, 2 * waves, LANES), BF16),
            pltpu.HBM((rows, 2, turns, waves), F32),
        ],
        compiler_params=pltpu.CompilerParams(vmem_limit_bytes=20 * MIB),
        cost_estimate=cost(rows * waves * LANES * 8, rows * waves * LANES * 4),
        name="tables",
    )(info, wave_ids[None, :])

def place(pieces, width):
    out = [None] * (width // LANES)
    lane = lax.broadcasted_iota(jnp.int32, (pieces[0][0].shape[0], LANES), 1)
    for value, start, count, here in pieces:
        shift = (here - start) % LANES
        for a in range(start // LANES, (start + count - 1) // LANES + 1):
            part = value[:, a * LANES : (a + 1) * LANES]
            if shift:
                part = pltpu.roll(part, shift, 1)
            first = max(start, a * LANES) - start + here
            last = min(start + count, (a + 1) * LANES) - start + here
            for v in range(first // LANES, (last - 1) // LANES + 1):
                low, high = max(first - v * LANES, 0), min(last - v * LANES, LANES)
                if out[v] is None:
                    out[v] = part
                else:
                    out[v] = jnp.where((lane >= low) & (lane < high), part, out[v])
    return out

def synth_kernel(info, recv_ref, table_hbm, twiddle_hbm, *refs):
    *out_refs, coef, grid, table_ref, twiddle_ref, sems = refs
    sources, levels, rows, _ = recv_ref.shape
    fields, waves = coef.shape[0] // 2, coef.shape[1] * LANES
    share = waves // sources
    turns = twiddle_ref.shape[2]
    steps = sems.shape[1]
    each = rows // steps
    pitch = rows + 1

    def copies(step):
        some = pl.ds(step * each, each)
        pairs = ((table_hbm, table_ref), (twiddle_hbm, twiddle_ref))
        return [
            pltpu.make_async_copy(src.at[some], dst.at[some], sems.at[i, step])
            for i, (src, dst) in enumerate(pairs)
        ]

    for step in range(steps):
        for copy in copies(step):
            copy.start()

    def level(l, carry):
        values = [recv_ref[s, l].astype(F32) for s in range(sources)]
        for r in range(2 * fields):
            windows = [(values[s], r * share, share, s * share) for s in range(sources)]
            for v, part in enumerate(place(windows, waves)):
                coef[r, v, pl.ds(l * pitch, rows), :] = part
        return carry

    lax.fori_loop(0, levels, level, 0)

    def some_rows(step, carry):
        for copy in copies(step):
            copy.wait()
        for k in range(each):
            one_row(step * each + k)
        return carry

    def one_row(j):
        def own_row(r):
            parts = [coef[r, v, pl.ds(j, levels, stride=pitch), :] for v in range(waves // LANES)]
            return jnp.concatenate(parts, axis=1)

        values = [own_row(r) for r in range(2 * fields)]
        real, imag = [], []
        for t in range(turns):
            c, s = twiddle_ref[j, 0, t : t + 1], twiddle_ref[j, 1, t : t + 1]
            for f in range(fields):
                re, im = values[2 * f], values[2 * f + 1]
                real.append(re * c - im * s)
                imag.append(re * s + im * c)
        both = [jnp.concatenate(part, axis=0).astype(BF16) for part in (real, imag)]
        result = dot(jnp.concatenate(both, axis=1), table_ref[j], ((1,), (0,)))
        grid[pl.ds(j, turns * fields * levels, stride=pitch), :] = result

    lax.fori_loop(0, steps, some_rows, 0)
    tiles = turns // len(out_refs)
    for k, out_ref in enumerate(out_refs):
        for t in range(tiles):
            for f in range(fields):
                start = (((info[ME] ^ k) * tiles + t) * fields + f) * levels
                for l in range(levels):
                    block = grid[pl.ds((start + l) * pitch, rows), :].astype(BF16)
                    out_ref[f, l, :, t * LANES : (t + 1) * LANES] = block

def synthesis(recv, table, twiddle, info, dests, tile):
    sources, levels, rows, lanes = recv.shape
    turns, waves = twiddle.shape[2:]
    fields = 3
    each = STEP if rows % STEP == 0 else 1
    shape = (fields, levels, rows, tile)
    return pl.pallas_call(
        synth_kernel,
        grid_spec=pltpu.PrefetchScalarGridSpec(
            num_scalar_prefetch=1,
            grid=(1,),
            in_specs=[
                pl.BlockSpec(recv.shape, lambda j, info: (0, 0, 0, 0)),
                pl.BlockSpec(memory_space=pl.ANY),
                pl.BlockSpec(memory_space=pl.ANY),
            ],
            out_specs=[pl.BlockSpec(shape, lambda j, info: (0, 0, 0, 0))] * dests,
            scratch_shapes=[
                pltpu.VMEM((2 * fields, waves // LANES, levels * (rows + 1), LANES), F32),
                pltpu.VMEM((turns * fields * levels * (rows + 1), LANES), F32),
                pltpu.VMEM(table.shape, BF16),
                pltpu.VMEM(twiddle.shape, F32),
                pltpu.SemaphoreType.DMA((2, rows // each)),
            ],
        ),
        out_shape=[jax.ShapeDtypeStruct(shape, BF16)] * dests,
        compiler_params=pltpu.CompilerParams(vmem_limit_bytes=24 * MIB),
        cost_estimate=cost(4 * rows * waves * fields * levels * turns * LANES, 4 * rows * waves * LANES),
        name="synthesis",
    )(info, recv, *[pltpu.with_memory_space_constraint(v, pltpu.HBM) for v in (table, twiddle)])

def edge_kernel(
    info, state_ref, base_ref, temp_ref, row_a_ref, row_b_ref, col_a_ref, col_b_ref, react_ref
):
    tracers, levels, rows, tile = state_ref.shape
    cells = tracers * rows

    @pl.when(pl.program_id(0) == 0)
    def _():
        rates = jnp.concatenate([base_ref[...], temp_ref[...]], axis=0)
        high = rates.astype(BF16)
        low = (rates - high.astype(F32)).astype(BF16)

        def iota(shape, axis):
            return lax.broadcasted_iota(jnp.int32, shape, axis)

        shape = (2 * cells, 2 * tracers)
        down = jnp.where(iota(shape, 0) // rows == iota(shape, 1), 1.0, 0.0).astype(BF16)
        shape = (tracers, cells)
        over = jnp.where(iota(shape, 0) == iota(shape, 1) // rows, 1.0, 0.0).astype(BF16)
        shape = (2 * cells, cells)
        same = iota(shape, 0) % rows == iota(shape, 1) % rows
        for k, part in enumerate((high, low)):
            wide = dot(dot(down, part, ((1,), (0,))).astype(BF16), over, ((1,), (0,)))
            react_ref[:, k * cells : (k + 1) * cells] = jnp.where(same, wide, 0.0).astype(BF16)

    def iota(shape, axis):
        return lax.broadcasted_iota(jnp.int32, shape, axis)

    odd = info[BAND] % 2, info[ME] % 2
    far, near = (1 - odd[0]) * (rows - 1), odd[0] * (rows - 1)
    shape = (2 * tracers, cells)
    end = jnp.where(iota(shape, 0) < tracers, far, near)
    pick = iota(shape, 1) == (iota(shape, 0) % tracers) * rows + end
    pick = jnp.where(pick, 1.0, 0.0).astype(BF16)
    shape = (tile, 2 * LANES)
    far, near = (1 - odd[1]) * (tile - 1), odd[1] * (tile - 1)
    is_end = iota(shape, 0) == jnp.where(iota(shape, 1) < LANES, far, near)
    level = iota(shape, 1) % LANES - pl.program_id(0) * levels
    columns = jnp.zeros((cells, 2 * LANES), F32)
    for l in range(levels):
        x = state_ref[:, l].reshape(cells, tile)
        picked = dot(pick, x, ((1,), (0,)))
        row_a_ref[l] = picked[:tracers].astype(BF16)
        row_b_ref[l] = picked[tracers:].astype(BF16)
        mark = jnp.where(is_end & (level == l), 1.0, 0.0).astype(BF16)
        columns = columns + dot(x, mark, ((1,), (0,)))

    @pl.when(pl.program_id(0) == 0)
    def _():
        col_a_ref[...] = columns[:, :LANES].astype(BF16)
        col_b_ref[...] = columns[:, LANES:].astype(BF16)

    @pl.when(pl.program_id(0) > 0)
    def _():
        col_a_ref[...] = (col_a_ref[...].astype(F32) + columns[:, :LANES]).astype(BF16)
        col_b_ref[...] = (col_b_ref[...].astype(F32) + columns[:, LANES:]).astype(BF16)

def edges(state, react_base, react_temp, info):
    tracers, levels, rows, tile = state.shape
    block = 16
    cells = tracers * rows
    rowed = jax.ShapeDtypeStruct((levels, tracers, tile), BF16)
    columned = jax.ShapeDtypeStruct((cells, LANES), BF16)
    row_spec = pl.BlockSpec((block, tracers, tile), lambda i, info: (i, 0, 0))
    col_spec = pl.BlockSpec((cells, LANES), lambda i, info: (0, 0))
    wide = (2 * cells, 2 * cells)
    return pl.pallas_call(
        edge_kernel,
        grid_spec=pltpu.PrefetchScalarGridSpec(
            num_scalar_prefetch=1,
            grid=(levels // block,),
            in_specs=[
                pl.BlockSpec((tracers, block, rows, tile), lambda i, info: (0, i, 0, 0)),
                pl.BlockSpec(react_base.shape, lambda i, info: (0, 0)),
                pl.BlockSpec(react_temp.shape, lambda i, info: (0, 0)),
            ],
            out_specs=[
                row_spec, row_spec, col_spec, col_spec, pl.BlockSpec(wide, lambda i, info: (0, 0)),
            ],
        ),
        out_shape=[rowed, rowed, columned, columned, jax.ShapeDtypeStruct(wide, BF16)],
        compiler_params=pltpu.CompilerParams(vmem_limit_bytes=52 * MIB),
        cost_estimate=cost(4 * state.size * 32, 2 * state.size),
        name="edges",
    )(info, state, react_base, react_temp)

def shifted(value, outer, axis, step):
    size = value[0].shape[axis]
    turned = [pltpu.roll(v, -step % size, axis) for v in value]
    place = lax.broadcasted_iota(jnp.int32, value[0].shape, axis)
    at_end = place == (size - 1 if step == 1 else 0)
    following = turned[1:] + [outer] if step == 1 else [outer] + turned[:-1]
    return [jnp.where(at_end, f, t) for f, t in zip(following, turned)]

def chem_kernel(scale, k, info, *refs):
    state_ref, row_a_ref, row_b_ref, col_a_ref, col_b_ref, grid_ref, react_ref = refs[:7]
    new_ref, active_ref, south, north, advected, rounded = refs[-6:]
    tracers, levels, rows, tile = state_ref.shape
    cells = tracers * rows
    odd_band, odd_tile = info[BAND] % 2 == 1, info[ME] % 2 == 1
    first = ((info[ME] ^ k) * pl.num_programs(0) + pl.program_id(0)) * levels

    def column(value):
        return pltpu.roll(value, lax.rem(LANES - first, LANES), 1)

    a, b = col_a_ref[...].astype(F32), col_b_ref[...].astype(F32)
    west, east = column(jnp.where(odd_tile, a, b)), column(jnp.where(odd_tile, b, a))
    row = lax.broadcasted_iota(jnp.int32, (rows, tile), 0)
    lane = lax.broadcasted_iota(jnp.int32, (rows, tile), 1)
    ids, points = IDS, IDS + active_ref.shape[0]
    count = jnp.full((rows, tile), info[points], jnp.int32)
    for j in range(1, rows):
        count = jnp.where(row == j, info[points + j], count)
    mask = jnp.where(info[ME] * tile + lane < count, 1.0, 0.0)
    across = [slice(v * LANES, (v + 1) * LANES) for v in range(tile // LANES)]
    along = [slice(v * SUBLANES, (v + 1) * SUBLANES) for v in range(rows // SUBLANES)]

    for l in range(levels):
        wind_u = grid_ref[0, l].astype(F32) * (scale * 0.1)
        wind_v = grid_ref[1, l].astype(F32) * (scale * 0.1)
        from_east, from_west = 0.05 - wind_u, 0.05 + wind_u
        from_north, from_south = 0.05 - wind_v, 0.05 + wind_v
        a, b = row_a_ref[l].astype(F32), row_b_ref[l].astype(F32)
        south[l] = jnp.where(odd_band, a, b)
        north[l] = jnp.where(odd_band, b, a)
        for t in range(tracers):
            cell = slice(t * rows, (t + 1) * rows)
            x = state_ref[t, l].astype(F32)
            outer = [jnp.broadcast_to(col[cell, l : l + 1], (rows, LANES)) for col in (east, west)]
            parts = [x[:, v] for v in across]
            qe = jnp.concatenate(shifted(parts, outer[0], 1, 1), axis=1)
            qw = jnp.concatenate(shifted(parts, outer[1], 1, -1), axis=1)
            shape = (SUBLANES, tile)
            outer = [jnp.broadcast_to(ref[l, t : t + 1], shape) for ref in (north, south)]
            parts = [x[v] for v in along]
            qn = jnp.concatenate(shifted(parts, outer[0], 0, 1), axis=0)
            qs = jnp.concatenate(shifted(parts, outer[1], 0, -1), axis=0)
            moved = 0.8 * x + from_east * qe + from_west * qw + from_north * qn + from_south * qs
            advected[l, cell] = moved
            rounded[l, cell] = moved.astype(BF16)
    for l in range(levels):
        temper = grid_ref[2, l].astype(F32) * scale
        high = rounded[l]
        terms = dot(react_ref[...], jnp.concatenate([high, high], axis=0), ((1,), (0,)))
        for t in range(tracers):
            cell = slice(t * rows, (t + 1) * rows)
            warm = slice(cells + t * rows, cells + (t + 1) * rows)
            reacted = (advected[l, cell] + terms[cell] + temper * terms[warm]) * mask
            new_ref[t, l] = reacted.astype(BF16)
    for a in range(active_ref.shape[0]):
        active_ref[a] = new_ref[info[ids + a]]

def chemistry(state, halos, grid, react, info, k, actives, waves, before):
    tracers, levels, rows, tile = state.shape
    fields, own = grid.shape[:2]
    some = 4 if own % 4 == 0 else own
    steps = own // some
    cells = tracers * rows
    scale = 1.0 / float(np.sqrt(np.float32(waves)))

    def whole(shape):
        return pl.BlockSpec(shape, lambda i, info: (0,) * len(shape))

    row_spec = pl.BlockSpec((some, tracers, tile), lambda i, info: ((info[ME] ^ k) * steps + i, 0, 0))
    state_spec = pl.BlockSpec(
        (tracers, some, rows, tile), lambda i, info: (0, (info[ME] ^ k) * steps + i, 0, 0)
    )

    operands = [state, *halos, grid, react]
    in_specs = [
        state_spec,
        row_spec,
        row_spec,
        whole(halos[2].shape),
        whole(halos[3].shape),
        pl.BlockSpec((fields, some, rows, tile), lambda i, info: (0, i, 0, 0)),
        whole(react.shape),
    ]
    aliases = {}
    if before is not None:
        aliases = {1 + len(operands): 0}
        operands.append(before)
        in_specs.append(pl.BlockSpec(memory_space=pl.ANY))
    return pl.pallas_call(
        functools.partial(chem_kernel, scale, k),
        grid_spec=pltpu.PrefetchScalarGridSpec(
            num_scalar_prefetch=1,
            grid=(steps,),
            in_specs=in_specs,
            out_specs=[
                state_spec,
                pl.BlockSpec((actives, some, rows, tile), lambda i, info: (0, i, 0, 0)),
            ],
            scratch_shapes=[
                pltpu.VMEM((some, tracers, tile), F32),
                pltpu.VMEM((some, tracers, tile), F32),
                pltpu.VMEM((some, cells, tile), F32),
                pltpu.VMEM((some, cells, tile), BF16),
            ],
        ),
        out_shape=[
            jax.ShapeDtypeStruct(state.shape, BF16),
            jax.ShapeDtypeStruct((actives, own, rows, tile), BF16),
        ],
        input_output_aliases=aliases,
        compiler_params=pltpu.CompilerParams(vmem_limit_bytes=16 * MIB),
        cost_estimate=cost(own * cells * tile, own * tile),
        name="chemistry",
    )(info, *operands)

def spread(parts, order, info, tiles, before):
    actives, own, rows, tile = parts[0].shape
    count = len(order)
    operands, aliases = list(parts), {}
    in_specs = [pl.BlockSpec(parts[0].shape, lambda i, info: (0, 0, 0, 0))] * count
    if before is not None:
        operands.append(before)
        in_specs.append(pl.BlockSpec(memory_space=pl.ANY))
        aliases = {1 + count: 0}

    def partner(i):
        k = order[0]
        for at in range(1, count):
            k = jnp.where(i == at, order[at], k)
        return k

    def kernel(info, *refs):
        for at in range(count):

            @pl.when(pl.program_id(0) == at)
            def _():
                refs[-1][...] = refs[at][...].astype(F32)

    return pl.pallas_call(
        kernel,
        grid_spec=pltpu.PrefetchScalarGridSpec(
            num_scalar_prefetch=1,
            grid=(count,),
            in_specs=in_specs,
            out_specs=pl.BlockSpec(
                (actives, own, rows, tile), lambda i, info: (0, 0, 0, info[ME] ^ partner(i))
            ),
        ),
        out_shape=jax.ShapeDtypeStruct((actives, own, rows, tiles * tile), F32),
        input_output_aliases=aliases,
        compiler_params=pltpu.CompilerParams(vmem_limit_bytes=12 * MIB),
        cost_estimate=cost(actives, actives),
        name="spread",
    )(info, *operands)

def legendre_kernel(spectral_ref, legendre_ref, out_ref, rows_of, sums):
    parts, own, block, size = spectral_ref.shape
    bands, _, rows, pitch = out_ref.shape
    share = block * pl.num_programs(0)
    step = pl.program_id(0)
    lines = parts * own
    apart, stretch = block + 1, pitch + 1

    @pl.when(step == 0)
    def _():
        for h in range(sums.shape[0]):
            for l in range(own):
                tail = pl.ds(l * stretch + parts * share, pitch - parts * share)
                sums[h, tail, :] = jnp.zeros((pitch - parts * share, LANES), F32)

    for v in range(size // LANES):
        part = spectral_ref[:, :, :, v * LANES : (v + 1) * LANES].astype(F32)
        part = part.reshape(lines, block, LANES)
        for i in range(lines):
            rows_of[v, pl.ds(i * apart, block), :] = part[i]
    def line(m):
        x = [rows_of[v, pl.ds(m, lines, stride=apart), :] for v in range(size // LANES)]
        return jnp.concatenate(x, axis=1).astype(BF16)

    wide = legendre_ref.shape[2]
    group = max(1, 2 * LANES // wide)
    for m in range(0, block, group):
        both = range(m, m + group)
        x = jnp.concatenate([line(i) for i in both], axis=0)
        y = jnp.concatenate([legendre_ref[i] for i in both], axis=1)
        product = dot(x, y, ((1,), (0,)))
        for i in both:
            result = product[(i - m) * lines : (i - m + 1) * lines, (i - m) * wide : (i - m + 1) * wide]
            for r in range(parts):
                at = r * share + step * block + i
                for h in range(sums.shape[0]):
                    piece = result[r * own : (r + 1) * own, h * LANES : (h + 1) * LANES]
                    sums[h, pl.ds(at, own, stride=stretch), :] = piece

    @pl.when(step == pl.num_programs(0) - 1)
    def _():
        some = LANES // rows
        for l in range(own):
            for h in range(sums.shape[0]):
                turned = sums[h, pl.ds(l * stretch, pitch), :].T.astype(BF16)
                out_ref[h * some : (h + 1) * some, l] = turned.reshape(some, rows, pitch)

def legendre_sums(spectral, legendre, bands):
    parts, own, share, size = spectral.shape
    rows = legendre.shape[2] // bands
    pitch = -(-parts * share // LANES) * LANES
    block = 16 if share % 16 == 0 else 8
    shape = (bands, own, rows, pitch)
    return pl.pallas_call(
        legendre_kernel,
        grid=(share // block,),
        in_specs=[
            pl.BlockSpec((parts, own, block, size), lambda i: (0, 0, i, 0)),
            pl.BlockSpec((block,) + legendre.shape[1:], lambda i: (i, 0, 0)),
        ],
        out_specs=pl.BlockSpec(shape, lambda i: (0, 0, 0, 0)),
        out_shape=pltpu.VMEM(shape, BF16),
        scratch_shapes=[
            pltpu.VMEM((size // LANES, parts * own * (block + 1), LANES), F32),
            pltpu.VMEM((legendre.shape[2] // LANES, own * (pitch + 1), LANES), F32),
        ],
        compiler_params=pltpu.CompilerParams(vmem_limit_bytes=54 * MIB),
        cost_estimate=cost(2 * parts * own * legendre.size, 2 * (spectral.size + legendre.size)),
        name="legendre",
    )(spectral, legendre)

def exchange(value, axis, pairs):
    return lax.ppermute(value, axis, [p for a, b in pairs for p in ((a, b), (b, a))])

def neighbours(axis, first):
    size = lax.axis_size(axis)
    return [(i, i + 1) for i in range(first, size - 1, 2)]

def partners(axis, k):
    return [(i, i ^ k) for i in range(lax.axis_size(axis)) if i < i ^ k]

def body(spectral, legendre, wave_ids, points, tracers, react_base, react_temp, active_ids):
    bands, tiles = lax.axis_size("lat"), lax.axis_size("lon")
    tile = tracers.shape[3]
    waves = wave_ids.shape[0]
    band, me = lax.axis_index("lat"), lax.axis_index("lon")

    sent = legendre_sums(spectral, legendre, bands)

    rows = points.shape[0]
    info = jnp.concatenate([jnp.stack([band, me]), active_ids, points]).astype(jnp.int32)
    sent, info = lax.optimization_barrier((sent, info))
    recv = lax.all_to_all(sent, "lat", split_axis=0, concat_axis=0, tiled=True)
    *ends, react = edges(tracers, react_base, react_temp, info)
    halos = [
        exchange(ends[0], "lat", neighbours("lat", 0)),
        exchange(ends[2], "lon", neighbours("lon", 0)),
        exchange(ends[3], "lon", neighbours("lon", 1)),
    ]
    react, wave_ids = lax.optimization_barrier((react, wave_ids))
    table, twiddle = tables(info, wave_ids, rows, tiles * tile // LANES)
    recv, table, twiddle, react, halos, last = lax.optimization_barrier(
        (recv, table, twiddle, react, halos, ends[1])
    )
    halos.insert(1, exchange(last, "lat", neighbours("lat", 1)))
    grids = synthesis(recv, table, twiddle, info, tiles, tile)

    middle, inner = list(range(tiles // 2, tiles)), list(range(1, tiles // 2))
    soon, late = middle[: tiles // 4], middle[tiles // 4 :]

    def send(value, k):
        return exchange(value, "lon", partners("lon", k))

    moved = {0: grids[0]} | {k: send(grids[k], k) for k in soon}
    new, active = None, {}
    for k in [0] + soon + late + inner:
        new, active[k] = chemistry(
            tracers, halos, moved[k], react, info, k, active_ids.shape[0], waves, new
        )
        if k:
            active[k] = send(active[k], k)
        else:
            rest = late + inner
            held, active[0] = lax.optimization_barrier(([grids[i] for i in rest], active[0]))
            moved |= {i: send(value, i) for i, value in zip(rest, held)}
    early, last = [0] + soon, late + inner
    spreaded = spread([active[k] for k in early], early, info, tiles, None)
    through = lax.optimization_barrier([active[k] for k in late])
    parts = lax.optimization_barrier(through + [active[k] for k in inner])
    return new, spread(parts, last, info, tiles, spreaded)

def solution(mesh):
    return jax.shard_map(
        body,
        mesh=mesh,
        in_specs=(
            P(None, "lon", "lat", None),
            P("lat", None, None),
            P(),
            P("lat"),
            P(None, None, "lat", "lon"),
            P(),
            P(),
            P(),
        ),
        out_specs=(P(None, None, "lat", "lon"), P(None, "lon", "lat", None)),
        check_vma=False,
    )
```

```python
import functools

import jax
import jax.numpy as jnp
import numpy as np
from jax import lax
from jax.experimental import pallas as pl
from jax.experimental.pallas import tpu as pltpu
from jax.sharding import PartitionSpec as P

F32 = jnp.float32
BF16 = jnp.bfloat16
LANES = 128
SUBLANES = 8
LOW = 16
STEP = 4
MIB = 1024 * 1024

COS = (
    0.9999999890590228,
    -19.739204499454026,
    64.93911745990036,
    -85.45013953095037,
    60.16763095136588,
    -25.96759924965491,
    6.528658162567069,
)
SIN = (
    6.283185302511503,
    -41.34170040531769,
    81.60513138580204,
    -76.7030153539128,
    42.02592698618416,
    -14.899846668691637,
    3.238137510515757,
)

def dot(a, b, dims):
    return lax.dot_general(a, b, (dims, ((), ())), preferred_element_type=F32)

BAND, ME, IDS = 0, 1, 2

def cost(flops, moved):
    return pl.CostEstimate(flops=int(flops), bytes_accessed=int(moved), transcendentals=0)

def unit_circle(step, rows, waves, count):
    index = lax.broadcasted_iota(jnp.int32, (rows, waves.shape[1]), 0) * step
    product = index.astype(F32) * waves
    inverse = 1.0 / count
    turns = (product - jnp.floor(product * inverse) * count) * inverse
    y = turns - jnp.floor(turns + 0.5)
    z = y * y
    cosine = jnp.full_like(z, COS[-1])
    sine = jnp.full_like(z, SIN[-1])
    for c, s in zip(COS[-2::-1], SIN[-2::-1]):
        cosine = cosine * z + c
        sine = sine * z + s
    return cosine, sine * y

def table_kernel(first, info, waves_ref, table_ref, twiddle_ref):
    size, turns = waves_ref.shape[1], twiddle_ref.shape[2]
    waves = waves_ref[...].astype(F32)
    for k in range(table_ref.shape[0]):
        row = pl.program_id(0) * table_ref.shape[0] + k
        count = jnp.full(waves.shape, info[first + row], jnp.int32).astype(F32)
        cos_low, sin_low = unit_circle(1, LOW, waves, count)
        cos_high, sin_high = unit_circle(LOW, LANES // LOW, waves, count)
        cosine, sine = [], []
        for a in range(LANES // LOW):
            ch, sh = cos_high[a : a + 1], sin_high[a : a + 1]
            cosine.append(ch * cos_low - sh * sin_low)
            sine.append(-sh * cos_low - ch * sin_low)
        table_ref[k, :size, :] = jnp.concatenate(cosine, axis=0).T.astype(BF16)
        table_ref[k, size:, :] = jnp.concatenate(sine, axis=0).T.astype(BF16)
        cos_turn, sin_turn = unit_circle(LANES, turns, waves, count)
        twiddle_ref[k, 0] = cos_turn
        twiddle_ref[k, 1] = sin_turn

def tables(info, wave_ids, rows, turns):
    waves = wave_ids.shape[0]
    each = STEP if rows % STEP == 0 else 1
    return pl.pallas_call(
        functools.partial(table_kernel, info.shape[0] - rows),
        grid_spec=pltpu.PrefetchScalarGridSpec(
            num_scalar_prefetch=1,
            grid=(rows // each,),
            in_specs=[pl.BlockSpec((1, waves), lambda j, p: (0, 0))],
            out_specs=[
                pl.BlockSpec((each, 2 * waves, LANES), lambda j, p: (j, 0, 0)),
                pl.BlockSpec((each, 2, turns, waves), lambda j, p: (j, 0, 0, 0)),
            ],
        ),
        out_shape=[
            pltpu.HBM((rows, 2 * waves, LANES), BF16),
            pltpu.HBM((rows, 2, turns, waves), F32),
        ],
        compiler_params=pltpu.CompilerParams(vmem_limit_bytes=20 * MIB),
        cost_estimate=cost(rows * waves * LANES * 8, rows * waves * LANES * 4),
        name="tables",
    )(info, wave_ids[None, :])

def place(pieces, width):
    out = [None] * (width // LANES)
    lane = lax.broadcasted_iota(jnp.int32, (pieces[0][0].shape[0], LANES), 1)
    for value, start, count, here in pieces:
        shift = (here - start) % LANES
        for a in range(start // LANES, (start + count - 1) // LANES + 1):
            part = value[:, a * LANES : (a + 1) * LANES]
            if shift:
                part = pltpu.roll(part, shift, 1)
            first = max(start, a * LANES) - start + here
            last = min(start + count, (a + 1) * LANES) - start + here
            for v in range(first // LANES, (last - 1) // LANES + 1):
                low, high = max(first - v * LANES, 0), min(last - v * LANES, LANES)
                if out[v] is None:
                    out[v] = part
                else:
                    out[v] = jnp.where((lane >= low) & (lane < high), part, out[v])
    return out

def synth_kernel(info, recv_ref, table_hbm, twiddle_hbm, *refs):
    *out_refs, coef, grid, table_ref, twiddle_ref, sems = refs
    sources, levels, rows, _ = recv_ref.shape
    fields, waves = coef.shape[0] // 2, coef.shape[1] * LANES
    share = waves // sources
    turns = twiddle_ref.shape[2]
    steps = sems.shape[1]
    each = rows // steps
    pitch = rows + 1

    def copies(step):
        some = pl.ds(step * each, each)
        pairs = ((table_hbm, table_ref), (twiddle_hbm, twiddle_ref))
        return [
            pltpu.make_async_copy(src.at[some], dst.at[some], sems.at[i, step])
            for i, (src, dst) in enumerate(pairs)
        ]

    for step in range(steps):
        for copy in copies(step):
            copy.start()

    def level(l, carry):
        values = [recv_ref[s, l].astype(F32) for s in range(sources)]
        for r in range(2 * fields):
            windows = [(values[s], r * share, share, s * share) for s in range(sources)]
            for v, part in enumerate(place(windows, waves)):
                coef[r, v, pl.ds(l * pitch, rows), :] = part
        return carry

    lax.fori_loop(0, levels, level, 0)

    def some_rows(step, carry):
        for copy in copies(step):
            copy.wait()
        for k in range(each):
            one_row(step * each + k)
        return carry

    def one_row(j):
        def own_row(r):
            parts = [coef[r, v, pl.ds(j, levels, stride=pitch), :] for v in range(waves // LANES)]
            return jnp.concatenate(parts, axis=1)

        values = [own_row(r) for r in range(2 * fields)]
        real, imag = [], []
        for t in range(turns):
            c, s = twiddle_ref[j, 0, t : t + 1], twiddle_ref[j, 1, t : t + 1]
            for f in range(fields):
                re, im = values[2 * f], values[2 * f + 1]
                real.append(re * c - im * s)
                imag.append(re * s + im * c)
        both = [jnp.concatenate(part, axis=0).astype(BF16) for part in (real, imag)]
        result = dot(jnp.concatenate(both, axis=1), table_ref[j], ((1,), (0,)))
        grid[pl.ds(j, turns * fields * levels, stride=pitch), :] = result

    lax.fori_loop(0, steps, some_rows, 0)
    tiles = turns // len(out_refs)
    for k, out_ref in enumerate(out_refs):
        for t in range(tiles):
            for f in range(fields):
                start = (((info[ME] ^ k) * tiles + t) * fields + f) * levels
                for l in range(levels):
                    block = grid[pl.ds((start + l) * pitch, rows), :].astype(BF16)
                    out_ref[f, l, :, t * LANES : (t + 1) * LANES] = block

def synthesis(recv, table, twiddle, info, dests, tile):
    sources, levels, rows, lanes = recv.shape
    turns, waves = twiddle.shape[2:]
    fields = 3
    each = STEP if rows % STEP == 0 else 1
    shape = (fields, levels, rows, tile)
    return pl.pallas_call(
        synth_kernel,
        grid_spec=pltpu.PrefetchScalarGridSpec(
            num_scalar_prefetch=1,
            grid=(1,),
            in_specs=[
                pl.BlockSpec(recv.shape, lambda j, info: (0, 0, 0, 0)),
                pl.BlockSpec(memory_space=pl.ANY),
                pl.BlockSpec(memory_space=pl.ANY),
            ],
            out_specs=[pl.BlockSpec(shape, lambda j, info: (0, 0, 0, 0))] * dests,
            scratch_shapes=[
                pltpu.VMEM((2 * fields, waves // LANES, levels * (rows + 1), LANES), F32),
                pltpu.VMEM((turns * fields * levels * (rows + 1), LANES), F32),
                pltpu.VMEM(table.shape, BF16),
                pltpu.VMEM(twiddle.shape, F32),
                pltpu.SemaphoreType.DMA((2, rows // each)),
            ],
        ),
        out_shape=[jax.ShapeDtypeStruct(shape, BF16)] * dests,
        compiler_params=pltpu.CompilerParams(vmem_limit_bytes=24 * MIB),
        cost_estimate=cost(4 * rows * waves * fields * levels * turns * LANES, 4 * rows * waves * LANES),
        name="synthesis",
    )(info, recv, *[pltpu.with_memory_space_constraint(v, pltpu.HBM) for v in (table, twiddle)])

def edge_kernel(
    info, state_ref, base_ref, temp_ref, row_a_ref, row_b_ref, col_a_ref, col_b_ref, react_ref
):
    tracers, levels, rows, tile = state_ref.shape
    cells = tracers * rows

    @pl.when(pl.program_id(0) == 0)
    def _():
        rates = jnp.concatenate([base_ref[...], temp_ref[...]], axis=0)
        high = rates.astype(BF16)
        low = (rates - high.astype(F32)).astype(BF16)

        def iota(shape, axis):
            return lax.broadcasted_iota(jnp.int32, shape, axis)

        shape = (2 * cells, 2 * tracers)
        down = jnp.where(iota(shape, 0) // rows == iota(shape, 1), 1.0, 0.0).astype(BF16)
        shape = (tracers, cells)
        over = jnp.where(iota(shape, 0) == iota(shape, 1) // rows, 1.0, 0.0).astype(BF16)
        shape = (2 * cells, cells)
        same = iota(shape, 0) % rows == iota(shape, 1) % rows
        for k, part in enumerate((high, low)):
            wide = dot(dot(down, part, ((1,), (0,))).astype(BF16), over, ((1,), (0,)))
            react_ref[:, k * cells : (k + 1) * cells] = jnp.where(same, wide, 0.0).astype(BF16)

    def iota(shape, axis):
        return lax.broadcasted_iota(jnp.int32, shape, axis)

    odd = info[BAND] % 2, info[ME] % 2
    far, near = (1 - odd[0]) * (rows - 1), odd[0] * (rows - 1)
    shape = (2 * tracers, cells)
    end = jnp.where(iota(shape, 0) < tracers, far, near)
    pick = iota(shape, 1) == (iota(shape, 0) % tracers) * rows + end
    pick = jnp.where(pick, 1.0, 0.0).astype(BF16)
    shape = (tile, 2 * LANES)
    far, near = (1 - odd[1]) * (tile - 1), odd[1] * (tile - 1)
    is_end = iota(shape, 0) == jnp.where(iota(shape, 1) < LANES, far, near)
    level = iota(shape, 1) % LANES - pl.program_id(0) * levels
    columns = jnp.zeros((cells, 2 * LANES), F32)
    for l in range(levels):
        x = state_ref[:, l].reshape(cells, tile)
        picked = dot(pick, x, ((1,), (0,)))
        row_a_ref[l] = picked[:tracers].astype(BF16)
        row_b_ref[l] = picked[tracers:].astype(BF16)
        mark = jnp.where(is_end & (level == l), 1.0, 0.0).astype(BF16)
        columns = columns + dot(x, mark, ((1,), (0,)))

    @pl.when(pl.program_id(0) == 0)
    def _():
        col_a_ref[...] = columns[:, :LANES].astype(BF16)
        col_b_ref[...] = columns[:, LANES:].astype(BF16)

    @pl.when(pl.program_id(0) > 0)
    def _():
        col_a_ref[...] = (col_a_ref[...].astype(F32) + columns[:, :LANES]).astype(BF16)
        col_b_ref[...] = (col_b_ref[...].astype(F32) + columns[:, LANES:]).astype(BF16)

def edges(state, react_base, react_temp, info):
    tracers, levels, rows, tile = state.shape
    block = 16
    cells = tracers * rows
    rowed = jax.ShapeDtypeStruct((levels, tracers, tile), BF16)
    columned = jax.ShapeDtypeStruct((cells, LANES), BF16)
    row_spec = pl.BlockSpec((block, tracers, tile), lambda i, info: (i, 0, 0))
    col_spec = pl.BlockSpec((cells, LANES), lambda i, info: (0, 0))
    wide = (2 * cells, 2 * cells)
    return pl.pallas_call(
        edge_kernel,
        grid_spec=pltpu.PrefetchScalarGridSpec(
            num_scalar_prefetch=1,
            grid=(levels // block,),
            in_specs=[
                pl.BlockSpec((tracers, block, rows, tile), lambda i, info: (0, i, 0, 0)),
                pl.BlockSpec(react_base.shape, lambda i, info: (0, 0)),
                pl.BlockSpec(react_temp.shape, lambda i, info: (0, 0)),
            ],
            out_specs=[
                row_spec, row_spec, col_spec, col_spec, pl.BlockSpec(wide, lambda i, info: (0, 0)),
            ],
        ),
        out_shape=[rowed, rowed, columned, columned, jax.ShapeDtypeStruct(wide, BF16)],
        compiler_params=pltpu.CompilerParams(vmem_limit_bytes=52 * MIB),
        cost_estimate=cost(4 * state.size * 32, 2 * state.size),
        name="edges",
    )(info, state, react_base, react_temp)

def shifted(value, outer, axis, step):
    size = value[0].shape[axis]
    turned = [pltpu.roll(v, -step % size, axis) for v in value]
    place = lax.broadcasted_iota(jnp.int32, value[0].shape, axis)
    at_end = place == (size - 1 if step == 1 else 0)
    following = turned[1:] + [outer] if step == 1 else [outer] + turned[:-1]
    return [jnp.where(at_end, f, t) for f, t in zip(following, turned)]

def chem_kernel(scale, k, info, *refs):
    state_ref, row_a_ref, row_b_ref, col_a_ref, col_b_ref, grid_ref, react_ref = refs[:7]
    new_ref, active_ref, south, north, advected, rounded = refs[-6:]
    tracers, levels, rows, tile = state_ref.shape
    cells = tracers * rows
    odd_band, odd_tile = info[BAND] % 2 == 1, info[ME] % 2 == 1
    first = ((info[ME] ^ k) * pl.num_programs(0) + pl.program_id(0)) * levels

    def column(value):
        return pltpu.roll(value, lax.rem(LANES - first, LANES), 1)

    a, b = col_a_ref[...].astype(F32), col_b_ref[...].astype(F32)
    west, east = column(jnp.where(odd_tile, a, b)), column(jnp.where(odd_tile, b, a))
    row = lax.broadcasted_iota(jnp.int32, (rows, tile), 0)
    lane = lax.broadcasted_iota(jnp.int32, (rows, tile), 1)
    ids, points = IDS, IDS + active_ref.shape[0]
    count = jnp.full((rows, tile), info[points], jnp.int32)
    for j in range(1, rows):
        count = jnp.where(row == j, info[points + j], count)
    mask = jnp.where(info[ME] * tile + lane < count, 1.0, 0.0)
    across = [slice(v * LANES, (v + 1) * LANES) for v in range(tile // LANES)]
    along = [slice(v * SUBLANES, (v + 1) * SUBLANES) for v in range(rows // SUBLANES)]

    for l in range(levels):
        wind_u = grid_ref[0, l].astype(F32) * (scale * 0.1)
        wind_v = grid_ref[1, l].astype(F32) * (scale * 0.1)
        from_east, from_west = 0.05 - wind_u, 0.05 + wind_u
        from_north, from_south = 0.05 - wind_v, 0.05 + wind_v
        a, b = row_a_ref[l].astype(F32), row_b_ref[l].astype(F32)
        south[l] = jnp.where(odd_band, a, b)
        north[l] = jnp.where(odd_band, b, a)
        for t in range(tracers):
            cell = slice(t * rows, (t + 1) * rows)
            x = state_ref[t, l].astype(F32)
            outer = [jnp.broadcast_to(col[cell, l : l + 1], (rows, LANES)) for col in (east, west)]
            parts = [x[:, v] for v in across]
            qe = jnp.concatenate(shifted(parts, outer[0], 1, 1), axis=1)
            qw = jnp.concatenate(shifted(parts, outer[1], 1, -1), axis=1)
            shape = (SUBLANES, tile)
            outer = [jnp.broadcast_to(ref[l, t : t + 1], shape) for ref in (north, south)]
            parts = [x[v] for v in along]
            qn = jnp.concatenate(shifted(parts, outer[0], 0, 1), axis=0)
            qs = jnp.concatenate(shifted(parts, outer[1], 0, -1), axis=0)
            moved = 0.8 * x + from_east * qe + from_west * qw + from_north * qn + from_south * qs
            advected[l, cell] = moved
            rounded[l, cell] = moved.astype(BF16)
    for l in range(levels):
        temper = grid_ref[2, l].astype(F32) * scale
        high = rounded[l]
        terms = dot(react_ref[...], jnp.concatenate([high, high], axis=0), ((1,), (0,)))
        for t in range(tracers):
            cell = slice(t * rows, (t + 1) * rows)
            warm = slice(cells + t * rows, cells + (t + 1) * rows)
            reacted = (advected[l, cell] + terms[cell] + temper * terms[warm]) * mask
            new_ref[t, l] = reacted.astype(BF16)
    for a in range(active_ref.shape[0]):
        active_ref[a] = new_ref[info[ids + a]]

def chemistry(state, halos, grid, react, info, k, actives, waves, before):
    tracers, levels, rows, tile = state.shape
    fields, own = grid.shape[:2]
    some = 4 if own % 4 == 0 else own
    steps = own // some
    cells = tracers * rows
    scale = 1.0 / float(np.sqrt(np.float32(waves)))

    def whole(shape):
        return pl.BlockSpec(shape, lambda i, info: (0,) * len(shape))

    row_spec = pl.BlockSpec((some, tracers, tile), lambda i, info: ((info[ME] ^ k) * steps + i, 0, 0))
    state_spec = pl.BlockSpec(
        (tracers, some, rows, tile), lambda i, info: (0, (info[ME] ^ k) * steps + i, 0, 0)
    )

    operands = [state, *halos, grid, react]
    in_specs = [
        state_spec,
        row_spec,
        row_spec,
        whole(halos[2].shape),
        whole(halos[3].shape),
        pl.BlockSpec((fields, some, rows, tile), lambda i, info: (0, i, 0, 0)),
        whole(react.shape),
    ]
    aliases = {}
    if before is not None:
        aliases = {1 + len(operands): 0}
        operands.append(before)
        in_specs.append(pl.BlockSpec(memory_space=pl.ANY))
    return pl.pallas_call(
        functools.partial(chem_kernel, scale, k),
        grid_spec=pltpu.PrefetchScalarGridSpec(
            num_scalar_prefetch=1,
            grid=(steps,),
            in_specs=in_specs,
            out_specs=[
                state_spec,
                pl.BlockSpec((actives, some, rows, tile), lambda i, info: (0, i, 0, 0)),
            ],
            scratch_shapes=[
                pltpu.VMEM((some, tracers, tile), F32),
                pltpu.VMEM((some, tracers, tile), F32),
                pltpu.VMEM((some, cells, tile), F32),
                pltpu.VMEM((some, cells, tile), BF16),
            ],
        ),
        out_shape=[
            jax.ShapeDtypeStruct(state.shape, BF16),
            jax.ShapeDtypeStruct((actives, own, rows, tile), BF16),
        ],
        input_output_aliases=aliases,
        compiler_params=pltpu.CompilerParams(vmem_limit_bytes=16 * MIB),
        cost_estimate=cost(own * cells * tile, own * tile),
        name="chemistry",
    )(info, *operands)

def spread(parts, order, info, tiles, before):
    actives, own, rows, tile = parts[0].shape
    count = len(order)
    operands, aliases = list(parts), {}
    in_specs = [pl.BlockSpec(parts[0].shape, lambda i, info: (0, 0, 0, 0))] * count
    if before is not None:
        operands.append(before)
        in_specs.append(pl.BlockSpec(memory_space=pl.ANY))
        aliases = {1 + count: 0}

    def partner(i):
        k = order[0]
        for at in range(1, count):
            k = jnp.where(i == at, order[at], k)
        return k

    def kernel(info, *refs):
        for at in range(count):

            @pl.when(pl.program_id(0) == at)
            def _():
                refs[-1][...] = refs[at][...].astype(F32)

    return pl.pallas_call(
        kernel,
        grid_spec=pltpu.PrefetchScalarGridSpec(
            num_scalar_prefetch=1,
            grid=(count,),
            in_specs=in_specs,
            out_specs=pl.BlockSpec(
                (actives, own, rows, tile), lambda i, info: (0, 0, 0, info[ME] ^ partner(i))
            ),
        ),
        out_shape=jax.ShapeDtypeStruct((actives, own, rows, tiles * tile), F32),
        input_output_aliases=aliases,
        compiler_params=pltpu.CompilerParams(vmem_limit_bytes=12 * MIB),
        cost_estimate=cost(actives, actives),
        name="spread",
    )(info, *operands)

def legendre_kernel(spectral_ref, legendre_ref, out_ref, rows_of, sums):
    parts, own, block, size = spectral_ref.shape
    bands, _, rows, pitch = out_ref.shape
    share = block * pl.num_programs(0)
    step, half = pl.program_id(0), pl.program_id(1)
    lines = parts * own
    apart, stretch = block + 1, pitch + 1

    @pl.when((step == 0) & (half == 0))
    def _():
        for h in range(sums.shape[0]):
            for l in range(own):
                tail = pl.ds(l * stretch + parts * share, pitch - parts * share)
                sums[h, tail, :] = jnp.zeros((pitch - parts * share, LANES), F32)

    for v in range(size // LANES):
        part = spectral_ref[:, :, :, v * LANES : (v + 1) * LANES].astype(F32)
        part = part.reshape(lines, block, LANES)
        for i in range(lines):
            rows_of[v, pl.ds(i * apart, block), :] = part[i]
    def line(m):
        x = [rows_of[v, pl.ds(m, lines, stride=apart), :] for v in range(size // LANES)]
        return jnp.concatenate(x, axis=1).astype(BF16)

    wide = legendre_ref.shape[2]
    group = max(1, 2 * LANES // wide)
    for m in range(0, block, group):
        both = range(m, m + group)
        x = jnp.concatenate([line(i) for i in both], axis=0)
        y = jnp.concatenate([legendre_ref[i] for i in both], axis=1)
        product = dot(x, y, ((1,), (0,)))
        for i in both:
            result = product[(i - m) * lines : (i - m + 1) * lines, (i - m) * wide : (i - m + 1) * wide]
            for r in range(parts):
                at = r * share + step * block + i
                for h in range(sums.shape[0]):
                    piece = result[r * own : (r + 1) * own, h * LANES : (h + 1) * LANES]
                    place_of = pl.ds(at, own, stride=stretch)
                    before = jnp.where(half > 0, sums[h, place_of, :], 0.0)
                    sums[h, place_of, :] = before + piece

    @pl.when((step == pl.num_programs(0) - 1) & (half == pl.num_programs(1) - 1))
    def _():
        some = LANES // rows
        for l in range(own):
            for h in range(sums.shape[0]):
                turned = sums[h, pl.ds(l * stretch, pitch), :].T.astype(BF16)
                out_ref[h * some : (h + 1) * some, l] = turned.reshape(some, rows, pitch)

def legendre_sums(spectral, legendre, bands):
    parts, own, share, size = spectral.shape
    rows = legendre.shape[2] // bands
    pitch = -(-parts * share // LANES) * LANES
    block = 16 if share % 16 == 0 else 8
    halves = 2 if size % (2 * LANES) == 0 else 1
    depth = size // halves
    shape = (bands, own, rows, pitch)
    return pl.pallas_call(
        legendre_kernel,
        grid=(share // block, halves),
        in_specs=[
            pl.BlockSpec((parts, own, block, depth), lambda i, n: (0, 0, i, n)),
            pl.BlockSpec((block, depth, legendre.shape[2]), lambda i, n: (i, n, 0)),
        ],
        out_specs=pl.BlockSpec(shape, lambda i, n: (0, 0, 0, 0)),
        out_shape=pltpu.VMEM(shape, BF16),
        scratch_shapes=[
            pltpu.VMEM((depth // LANES, parts * own * (block + 1), LANES), F32),
            pltpu.VMEM((legendre.shape[2] // LANES, own * (pitch + 1), LANES), F32),
        ],
        compiler_params=pltpu.CompilerParams(vmem_limit_bytes=54 * MIB),
        cost_estimate=cost(2 * parts * own * legendre.size, 2 * (spectral.size + legendre.size)),
        name="legendre",
    )(spectral, legendre)

def exchange(value, axis, pairs):
    return lax.ppermute(value, axis, [p for a, b in pairs for p in ((a, b), (b, a))])

def neighbours(axis, first):
    size = lax.axis_size(axis)
    return [(i, i + 1) for i in range(first, size - 1, 2)]

def partners(axis, k):
    return [(i, i ^ k) for i in range(lax.axis_size(axis)) if i < i ^ k]

def body(spectral, legendre, wave_ids, points, tracers, react_base, react_temp, active_ids):
    bands, tiles = lax.axis_size("lat"), lax.axis_size("lon")
    tile = tracers.shape[3]
    waves = wave_ids.shape[0]
    band, me = lax.axis_index("lat"), lax.axis_index("lon")

    sent = legendre_sums(spectral, legendre, bands)

    rows = points.shape[0]
    info = jnp.concatenate([jnp.stack([band, me]), active_ids, points]).astype(jnp.int32)
    sent, info = lax.optimization_barrier((sent, info))
    recv = lax.all_to_all(sent, "lat", split_axis=0, concat_axis=0, tiled=True)
    *ends, react = edges(tracers, react_base, react_temp, info)
    halos = [
        exchange(ends[0], "lat", neighbours("lat", 0)),
        exchange(ends[2], "lon", neighbours("lon", 0)),
        exchange(ends[3], "lon", neighbours("lon", 1)),
    ]
    react, wave_ids = lax.optimization_barrier((react, wave_ids))
    table, twiddle = tables(info, wave_ids, rows, tiles * tile // LANES)
    recv, table, twiddle, react, halos, last = lax.optimization_barrier(
        (recv, table, twiddle, react, halos, ends[1])
    )
    halos.insert(1, exchange(last, "lat", neighbours("lat", 1)))
    grids = synthesis(recv, table, twiddle, info, tiles, tile)

    middle, inner = list(range(tiles // 2, tiles)), list(range(1, tiles // 2))
    soon, late = middle[: tiles // 4], middle[tiles // 4 :]

    def send(value, k):
        return exchange(value, "lon", partners("lon", k))

    moved = {0: grids[0]} | {k: send(grids[k], k) for k in soon}
    new, active = None, {}
    for k in [0] + soon + late + inner:
        new, active[k] = chemistry(
            tracers, halos, moved[k], react, info, k, active_ids.shape[0], waves, new
        )
        if k:
            active[k] = send(active[k], k)
        else:
            rest = late + inner
            held, active[0] = lax.optimization_barrier(([grids[i] for i in rest], active[0]))
            moved |= {i: send(value, i) for i, value in zip(rest, held)}
    early, last = [0] + soon, late + inner
    spreaded = spread([active[k] for k in early], early, info, tiles, None)
    through = lax.optimization_barrier([active[k] for k in late])
    parts = lax.optimization_barrier(through + [active[k] for k in inner])
    return new, spread(parts, last, info, tiles, spreaded)

def solution(mesh):
    return jax.shard_map(
        body,
        mesh=mesh,
        in_specs=(
            P(None, "lon", "lat", None),
            P("lat", None, None),
            P(),
            P("lat"),
            P(None, None, "lat", "lon"),
            P(),
            P(),
            P(),
        ),
        out_specs=(P(None, None, "lat", "lon"), P(None, "lon", "lat", None)),
        check_vma=False,
    )
```

```python
import functools

import jax
import jax.numpy as jnp
import numpy as np
from jax import lax
from jax.experimental import pallas as pl
from jax.experimental.pallas import tpu as pltpu
from jax.sharding import PartitionSpec as P

F32 = jnp.float32
BF16 = jnp.bfloat16
LANES = 128
SUBLANES = 8
LOW = 16
STEP = 4
MIB = 1024 * 1024

COS = (
    0.9999999890590228,
    -19.739204499454026,
    64.93911745990036,
    -85.45013953095037,
    60.16763095136588,
    -25.96759924965491,
    6.528658162567069,
)
SIN = (
    6.283185302511503,
    -41.34170040531769,
    81.60513138580204,
    -76.7030153539128,
    42.02592698618416,
    -14.899846668691637,
    3.238137510515757,
)

def dot(a, b, dims):
    return lax.dot_general(a, b, (dims, ((), ())), preferred_element_type=F32)

BAND, ME, IDS = 0, 1, 2

def cost(flops, moved):
    return pl.CostEstimate(flops=int(flops), bytes_accessed=int(moved), transcendentals=0)

def unit_circle(step, rows, waves, count):
    index = lax.broadcasted_iota(jnp.int32, (rows, waves.shape[1]), 0) * step
    product = index.astype(F32) * waves
    inverse = 1.0 / count
    turns = (product - jnp.floor(product * inverse) * count) * inverse
    y = turns - jnp.floor(turns + 0.5)
    z = y * y
    cosine = jnp.full_like(z, COS[-1])
    sine = jnp.full_like(z, SIN[-1])
    for c, s in zip(COS[-2::-1], SIN[-2::-1]):
        cosine = cosine * z + c
        sine = sine * z + s
    return cosine, sine * y

def table_kernel(first, info, waves_ref, table_ref, twiddle_ref):
    size, turns = waves_ref.shape[1], twiddle_ref.shape[2]
    waves = waves_ref[...].astype(F32)
    for k in range(table_ref.shape[0]):
        row = pl.program_id(0) * table_ref.shape[0] + k
        count = jnp.full(waves.shape, info[first + row], jnp.int32).astype(F32)
        cos_low, sin_low = unit_circle(1, LOW, waves, count)
        cos_high, sin_high = unit_circle(LOW, LANES // LOW, waves, count)
        cosine, sine = [], []
        for a in range(LANES // LOW):
            ch, sh = cos_high[a : a + 1], sin_high[a : a + 1]
            cosine.append(ch * cos_low - sh * sin_low)
            sine.append(-sh * cos_low - ch * sin_low)
        table_ref[k, :size, :] = jnp.concatenate(cosine, axis=0).T.astype(BF16)
        table_ref[k, size:, :] = jnp.concatenate(sine, axis=0).T.astype(BF16)
        cos_turn, sin_turn = unit_circle(LANES, turns, waves, count)
        twiddle_ref[k, 0] = cos_turn
        twiddle_ref[k, 1] = sin_turn

def tables(info, wave_ids, rows, turns):
    waves = wave_ids.shape[0]
    each = STEP if rows % STEP == 0 else 1
    return pl.pallas_call(
        functools.partial(table_kernel, info.shape[0] - rows),
        grid_spec=pltpu.PrefetchScalarGridSpec(
            num_scalar_prefetch=1,
            grid=(rows // each,),
            in_specs=[pl.BlockSpec((1, waves), lambda j, p: (0, 0))],
            out_specs=[
                pl.BlockSpec((each, 2 * waves, LANES), lambda j, p: (j, 0, 0)),
                pl.BlockSpec((each, 2, turns, waves), lambda j, p: (j, 0, 0, 0)),
            ],
        ),
        out_shape=[
            pltpu.HBM((rows, 2 * waves, LANES), BF16),
            pltpu.HBM((rows, 2, turns, waves), F32),
        ],
        compiler_params=pltpu.CompilerParams(vmem_limit_bytes=20 * MIB),
        cost_estimate=cost(rows * waves * LANES * 8, rows * waves * LANES * 4),
        name="tables",
    )(info, wave_ids[None, :])

def place(pieces, width):
    out = [None] * (width // LANES)
    lane = lax.broadcasted_iota(jnp.int32, (pieces[0][0].shape[0], LANES), 1)
    for value, start, count, here in pieces:
        shift = (here - start) % LANES
        for a in range(start // LANES, (start + count - 1) // LANES + 1):
            part = value[:, a * LANES : (a + 1) * LANES]
            if shift:
                part = pltpu.roll(part, shift, 1)
            first = max(start, a * LANES) - start + here
            last = min(start + count, (a + 1) * LANES) - start + here
            for v in range(first // LANES, (last - 1) // LANES + 1):
                low, high = max(first - v * LANES, 0), min(last - v * LANES, LANES)
                if out[v] is None:
                    out[v] = part
                else:
                    out[v] = jnp.where((lane >= low) & (lane < high), part, out[v])
    return out

def synth_kernel(info, recv_ref, table_hbm, twiddle_hbm, *refs):
    *out_refs, coef, grid, table_ref, twiddle_ref, sems = refs
    sources, levels, rows, _ = recv_ref.shape
    fields, waves = coef.shape[0] // 2, coef.shape[1] * LANES
    share = waves // sources
    turns = twiddle_ref.shape[2]
    steps = sems.shape[1]
    each = rows // steps
    pitch = rows + 1

    def copies(step):
        some = pl.ds(step * each, each)
        pairs = ((table_hbm, table_ref), (twiddle_hbm, twiddle_ref))
        return [
            pltpu.make_async_copy(src.at[some], dst.at[some], sems.at[i, step])
            for i, (src, dst) in enumerate(pairs)
        ]

    for step in range(steps):
        for copy in copies(step):
            copy.start()

    def level(l, carry):
        values = [recv_ref[s, l].astype(F32) for s in range(sources)]
        for r in range(2 * fields):
            windows = [(values[s], r * share, share, s * share) for s in range(sources)]
            for v, part in enumerate(place(windows, waves)):
                coef[r, v, pl.ds(l * pitch, rows), :] = part
        return carry

    lax.fori_loop(0, levels, level, 0)

    def some_rows(step, carry):
        for copy in copies(step):
            copy.wait()
        for k in range(each):
            one_row(step * each + k)
        return carry

    def one_row(j):
        def own_row(r):
            parts = [coef[r, v, pl.ds(j, levels, stride=pitch), :] for v in range(waves // LANES)]
            return jnp.concatenate(parts, axis=1)

        values = [own_row(r) for r in range(2 * fields)]
        real, imag = [], []
        for t in range(turns):
            c, s = twiddle_ref[j, 0, t : t + 1], twiddle_ref[j, 1, t : t + 1]
            for f in range(fields):
                re, im = values[2 * f], values[2 * f + 1]
                real.append(re * c - im * s)
                imag.append(re * s + im * c)
        both = [jnp.concatenate(part, axis=0).astype(BF16) for part in (real, imag)]
        result = dot(jnp.concatenate(both, axis=1), table_ref[j], ((1,), (0,)))
        grid[pl.ds(j, turns * fields * levels, stride=pitch), :] = result

    lax.fori_loop(0, steps, some_rows, 0)
    tiles = turns // len(out_refs)
    for k, out_ref in enumerate(out_refs):
        for t in range(tiles):
            for f in range(fields):
                start = (((info[ME] ^ k) * tiles + t) * fields + f) * levels
                for l in range(levels):
                    block = grid[pl.ds((start + l) * pitch, rows), :].astype(BF16)
                    out_ref[f, l, :, t * LANES : (t + 1) * LANES] = block

def synthesis(recv, table, twiddle, info, dests, tile):
    sources, levels, rows, lanes = recv.shape
    turns, waves = twiddle.shape[2:]
    fields = 3
    each = STEP if rows % STEP == 0 else 1
    shape = (fields, levels, rows, tile)
    return pl.pallas_call(
        synth_kernel,
        grid_spec=pltpu.PrefetchScalarGridSpec(
            num_scalar_prefetch=1,
            grid=(1,),
            in_specs=[
                pl.BlockSpec(recv.shape, lambda j, info: (0, 0, 0, 0)),
                pl.BlockSpec(memory_space=pl.ANY),
                pl.BlockSpec(memory_space=pl.ANY),
            ],
            out_specs=[pl.BlockSpec(shape, lambda j, info: (0, 0, 0, 0))] * dests,
            scratch_shapes=[
                pltpu.VMEM((2 * fields, waves // LANES, levels * (rows + 1), LANES), F32),
                pltpu.VMEM((turns * fields * levels * (rows + 1), LANES), F32),
                pltpu.VMEM(table.shape, BF16),
                pltpu.VMEM(twiddle.shape, F32),
                pltpu.SemaphoreType.DMA((2, rows // each)),
            ],
        ),
        out_shape=[jax.ShapeDtypeStruct(shape, BF16)] * dests,
        compiler_params=pltpu.CompilerParams(vmem_limit_bytes=24 * MIB),
        cost_estimate=cost(4 * rows * waves * fields * levels * turns * LANES, 4 * rows * waves * LANES),
        name="synthesis",
    )(info, recv, *[pltpu.with_memory_space_constraint(v, pltpu.HBM) for v in (table, twiddle)])

def edge_kernel(
    info, state_ref, base_ref, temp_ref, row_a_ref, row_b_ref, col_a_ref, col_b_ref, react_ref
):
    tracers, levels, rows, tile = state_ref.shape
    cells = tracers * rows

    @pl.when(pl.program_id(0) == 0)
    def _():
        rates = jnp.concatenate([base_ref[...], temp_ref[...]], axis=0)
        high = rates.astype(BF16)
        low = (rates - high.astype(F32)).astype(BF16)

        def iota(shape, axis):
            return lax.broadcasted_iota(jnp.int32, shape, axis)

        shape = (2 * cells, 2 * tracers)
        down = jnp.where(iota(shape, 0) // rows == iota(shape, 1), 1.0, 0.0).astype(BF16)
        shape = (tracers, cells)
        over = jnp.where(iota(shape, 0) == iota(shape, 1) // rows, 1.0, 0.0).astype(BF16)
        shape = (2 * cells, cells)
        same = iota(shape, 0) % rows == iota(shape, 1) % rows
        for k, part in enumerate((high, low)):
            wide = dot(dot(down, part, ((1,), (0,))).astype(BF16), over, ((1,), (0,)))
            react_ref[:, k * cells : (k + 1) * cells] = jnp.where(same, wide, 0.0).astype(BF16)

    def iota(shape, axis):
        return lax.broadcasted_iota(jnp.int32, shape, axis)

    odd = info[BAND] % 2, info[ME] % 2
    far, near = (1 - odd[0]) * (rows - 1), odd[0] * (rows - 1)
    shape = (2 * tracers, cells)
    end = jnp.where(iota(shape, 0) < tracers, far, near)
    pick = iota(shape, 1) == (iota(shape, 0) % tracers) * rows + end
    pick = jnp.where(pick, 1.0, 0.0).astype(BF16)
    shape = (tile, 2 * LANES)
    far, near = (1 - odd[1]) * (tile - 1), odd[1] * (tile - 1)
    is_end = iota(shape, 0) == jnp.where(iota(shape, 1) < LANES, far, near)
    level = iota(shape, 1) % LANES - pl.program_id(0) * levels
    columns = jnp.zeros((cells, 2 * LANES), F32)
    for l in range(levels):
        x = state_ref[:, l].reshape(cells, tile)
        picked = dot(pick, x, ((1,), (0,)))
        row_a_ref[l] = picked[:tracers].astype(BF16)
        row_b_ref[l] = picked[tracers:].astype(BF16)
        mark = jnp.where(is_end & (level == l), 1.0, 0.0).astype(BF16)
        columns = columns + dot(x, mark, ((1,), (0,)))

    @pl.when(pl.program_id(0) == 0)
    def _():
        col_a_ref[...] = columns[:, :LANES].astype(BF16)
        col_b_ref[...] = columns[:, LANES:].astype(BF16)

    @pl.when(pl.program_id(0) > 0)
    def _():
        col_a_ref[...] = (col_a_ref[...].astype(F32) + columns[:, :LANES]).astype(BF16)
        col_b_ref[...] = (col_b_ref[...].astype(F32) + columns[:, LANES:]).astype(BF16)

def edges(state, react_base, react_temp, info):
    tracers, levels, rows, tile = state.shape
    block = 16
    cells = tracers * rows
    rowed = jax.ShapeDtypeStruct((levels, tracers, tile), BF16)
    columned = jax.ShapeDtypeStruct((cells, LANES), BF16)
    row_spec = pl.BlockSpec((block, tracers, tile), lambda i, info: (i, 0, 0))
    col_spec = pl.BlockSpec((cells, LANES), lambda i, info: (0, 0))
    wide = (2 * cells, 2 * cells)
    return pl.pallas_call(
        edge_kernel,
        grid_spec=pltpu.PrefetchScalarGridSpec(
            num_scalar_prefetch=1,
            grid=(levels // block,),
            in_specs=[
                pl.BlockSpec((tracers, block, rows, tile), lambda i, info: (0, i, 0, 0)),
                pl.BlockSpec(react_base.shape, lambda i, info: (0, 0)),
                pl.BlockSpec(react_temp.shape, lambda i, info: (0, 0)),
            ],
            out_specs=[
                row_spec, row_spec, col_spec, col_spec, pl.BlockSpec(wide, lambda i, info: (0, 0)),
            ],
        ),
        out_shape=[rowed, rowed, columned, columned, jax.ShapeDtypeStruct(wide, BF16)],
        compiler_params=pltpu.CompilerParams(vmem_limit_bytes=52 * MIB),
        cost_estimate=cost(4 * state.size * 32, 2 * state.size),
        name="edges",
    )(info, state, react_base, react_temp)

def shifted(value, outer, axis, step):
    size = value[0].shape[axis]
    turned = [pltpu.roll(v, -step % size, axis) for v in value]
    place = lax.broadcasted_iota(jnp.int32, value[0].shape, axis)
    at_end = place == (size - 1 if step == 1 else 0)
    following = turned[1:] + [outer] if step == 1 else [outer] + turned[:-1]
    return [jnp.where(at_end, f, t) for f, t in zip(following, turned)]

def chem_kernel(scale, k, info, *refs):
    state_ref, row_a_ref, row_b_ref, col_a_ref, col_b_ref, grid_ref, react_ref = refs[:7]
    new_ref, active_ref, south, north, advected, rounded = refs[-6:]
    tracers, levels, rows, tile = state_ref.shape
    cells = tracers * rows
    odd_band, odd_tile = info[BAND] % 2 == 1, info[ME] % 2 == 1
    first = ((info[ME] ^ k) * pl.num_programs(0) + pl.program_id(0)) * levels

    def column(value):
        return pltpu.roll(value, lax.rem(LANES - first, LANES), 1)

    a, b = col_a_ref[...].astype(F32), col_b_ref[...].astype(F32)
    west, east = column(jnp.where(odd_tile, a, b)), column(jnp.where(odd_tile, b, a))
    row = lax.broadcasted_iota(jnp.int32, (rows, tile), 0)
    lane = lax.broadcasted_iota(jnp.int32, (rows, tile), 1)
    ids, points = IDS, IDS + active_ref.shape[0]
    count = jnp.full((rows, tile), info[points], jnp.int32)
    for j in range(1, rows):
        count = jnp.where(row == j, info[points + j], count)
    mask = jnp.where(info[ME] * tile + lane < count, 1.0, 0.0)
    across = [slice(v * LANES, (v + 1) * LANES) for v in range(tile // LANES)]
    along = [slice(v * SUBLANES, (v + 1) * SUBLANES) for v in range(rows // SUBLANES)]

    for l in range(levels):
        wind_u = grid_ref[0, l].astype(F32) * (scale * 0.1)
        wind_v = grid_ref[1, l].astype(F32) * (scale * 0.1)
        from_east, from_west = 0.05 - wind_u, 0.05 + wind_u
        from_north, from_south = 0.05 - wind_v, 0.05 + wind_v
        a, b = row_a_ref[l].astype(F32), row_b_ref[l].astype(F32)
        south[l] = jnp.where(odd_band, a, b)
        north[l] = jnp.where(odd_band, b, a)
        for t in range(tracers):
            cell = slice(t * rows, (t + 1) * rows)
            x = state_ref[t, l].astype(F32)
            outer = [jnp.broadcast_to(col[cell, l : l + 1], (rows, LANES)) for col in (east, west)]
            parts = [x[:, v] for v in across]
            qe = jnp.concatenate(shifted(parts, outer[0], 1, 1), axis=1)
            qw = jnp.concatenate(shifted(parts, outer[1], 1, -1), axis=1)
            shape = (SUBLANES, tile)
            outer = [jnp.broadcast_to(ref[l, t : t + 1], shape) for ref in (north, south)]
            parts = [x[v] for v in along]
            qn = jnp.concatenate(shifted(parts, outer[0], 0, 1), axis=0)
            qs = jnp.concatenate(shifted(parts, outer[1], 0, -1), axis=0)
            moved = 0.8 * x + from_east * qe + from_west * qw + from_north * qn + from_south * qs
            advected[l, cell] = moved
            rounded[l, cell] = moved.astype(BF16)
    for l in range(levels):
        temper = grid_ref[2, l].astype(F32) * scale
        high = rounded[l]
        terms = dot(react_ref[...], jnp.concatenate([high, high], axis=0), ((1,), (0,)))
        for t in range(tracers):
            cell = slice(t * rows, (t + 1) * rows)
            warm = slice(cells + t * rows, cells + (t + 1) * rows)
            reacted = (advected[l, cell] + terms[cell] + temper * terms[warm]) * mask
            new_ref[t, l] = reacted.astype(BF16)
    for a in range(active_ref.shape[0]):
        active_ref[a] = new_ref[info[ids + a]]

def chemistry(state, halos, grid, react, info, k, actives, waves, before):
    tracers, levels, rows, tile = state.shape
    fields, own = grid.shape[:2]
    some = 4 if own % 4 == 0 else own
    steps = own // some
    cells = tracers * rows
    scale = 1.0 / float(np.sqrt(np.float32(waves)))

    def whole(shape):
        return pl.BlockSpec(shape, lambda i, info: (0,) * len(shape))

    row_spec = pl.BlockSpec((some, tracers, tile), lambda i, info: ((info[ME] ^ k) * steps + i, 0, 0))
    state_spec = pl.BlockSpec(
        (tracers, some, rows, tile), lambda i, info: (0, (info[ME] ^ k) * steps + i, 0, 0)
    )

    operands = [state, *halos, grid, react]
    in_specs = [
        state_spec,
        row_spec,
        row_spec,
        whole(halos[2].shape),
        whole(halos[3].shape),
        pl.BlockSpec((fields, some, rows, tile), lambda i, info: (0, i, 0, 0)),
        whole(react.shape),
    ]
    aliases = {}
    if before is not None:
        aliases = {1 + len(operands): 0}
        operands.append(before)
        in_specs.append(pl.BlockSpec(memory_space=pl.ANY))
    return pl.pallas_call(
        functools.partial(chem_kernel, scale, k),
        grid_spec=pltpu.PrefetchScalarGridSpec(
            num_scalar_prefetch=1,
            grid=(steps,),
            in_specs=in_specs,
            out_specs=[
                state_spec,
                pl.BlockSpec((actives, some, rows, tile), lambda i, info: (0, i, 0, 0)),
            ],
            scratch_shapes=[
                pltpu.VMEM((some, tracers, tile), F32),
                pltpu.VMEM((some, tracers, tile), F32),
                pltpu.VMEM((some, cells, tile), F32),
                pltpu.VMEM((some, cells, tile), BF16),
            ],
        ),
        out_shape=[
            jax.ShapeDtypeStruct(state.shape, BF16),
            jax.ShapeDtypeStruct((actives, own, rows, tile), BF16),
        ],
        input_output_aliases=aliases,
        compiler_params=pltpu.CompilerParams(vmem_limit_bytes=16 * MIB),
        cost_estimate=cost(own * cells * tile, own * tile),
        name="chemistry",
    )(info, *operands)

def spread(parts, order, info, tiles, before):
    actives, own, rows, tile = parts[0].shape
    count = len(order)
    operands, aliases = list(parts), {}
    in_specs = [pl.BlockSpec(parts[0].shape, lambda i, info: (0, 0, 0, 0))] * count
    if before is not None:
        operands.append(before)
        in_specs.append(pl.BlockSpec(memory_space=pl.ANY))
        aliases = {1 + count: 0}

    def partner(i):
        k = order[0]
        for at in range(1, count):
            k = jnp.where(i == at, order[at], k)
        return k

    def kernel(info, *refs):
        for at in range(count):

            @pl.when(pl.program_id(0) == at)
            def _():
                refs[-1][...] = refs[at][...].astype(F32)

    return pl.pallas_call(
        kernel,
        grid_spec=pltpu.PrefetchScalarGridSpec(
            num_scalar_prefetch=1,
            grid=(count,),
            in_specs=in_specs,
            out_specs=pl.BlockSpec(
                (actives, own, rows, tile), lambda i, info: (0, 0, 0, info[ME] ^ partner(i))
            ),
        ),
        out_shape=jax.ShapeDtypeStruct((actives, own, rows, tiles * tile), F32),
        input_output_aliases=aliases,
        compiler_params=pltpu.CompilerParams(vmem_limit_bytes=12 * MIB),
        cost_estimate=cost(actives, actives),
        name="spread",
    )(info, *operands)

def legendre_kernel(spectral_ref, legendre_ref, out_ref, rows_of, sums):
    parts, own, block, size = spectral_ref.shape
    bands, _, rows, pitch = out_ref.shape
    share = block * pl.num_programs(0)
    step = pl.program_id(0)
    lines = parts * own
    apart, stretch = block + 1, pitch + 1

    @pl.when(step == 0)
    def _():
        for h in range(sums.shape[0]):
            for l in range(own):
                tail = pl.ds(l * stretch + parts * share, pitch - parts * share)
                sums[h, tail, :] = jnp.zeros((pitch - parts * share, LANES), F32)

    for v in range(size // LANES):
        part = spectral_ref[:, :, :, v * LANES : (v + 1) * LANES].astype(F32)
        part = part.reshape(lines, block, LANES)
        for i in range(lines):
            rows_of[v, pl.ds(i * apart, block), :] = part[i]
    def line(m):
        x = [rows_of[v, pl.ds(m, lines, stride=apart), :] for v in range(size // LANES)]
        return jnp.concatenate(x, axis=1).astype(BF16)

    wide = legendre_ref.shape[2]
    group = max(1, 2 * LANES // wide)
    for m in range(0, block, group):
        both = range(m, m + group)
        x = jnp.concatenate([line(i) for i in both], axis=0)
        y = jnp.concatenate([legendre_ref[i] for i in both], axis=1)
        product = dot(x, y, ((1,), (0,)))
        for i in both:
            result = product[(i - m) * lines : (i - m + 1) * lines, (i - m) * wide : (i - m + 1) * wide]
            for r in range(parts):
                at = r * share + step * block + i
                for h in range(sums.shape[0]):
                    piece = result[r * own : (r + 1) * own, h * LANES : (h + 1) * LANES]
                    sums[h, pl.ds(at, own, stride=stretch), :] = piece

    @pl.when(step == pl.num_programs(0) - 1)
    def _():
        some = LANES // rows
        for l in range(own):
            for h in range(sums.shape[0]):
                turned = sums[h, pl.ds(l * stretch, pitch), :].T.astype(BF16)
                out_ref[h * some : (h + 1) * some, l] = turned.reshape(some, rows, pitch)

def legendre_sums(spectral, legendre, bands):
    parts, own, share, size = spectral.shape
    rows = legendre.shape[2] // bands
    pitch = -(-parts * share // LANES) * LANES
    block = 16 if share % 16 == 0 else 8
    shape = (bands, own, rows, pitch)
    return pl.pallas_call(
        legendre_kernel,
        grid=(share // block,),
        in_specs=[
            pl.BlockSpec((parts, own, block, size), lambda i: (0, 0, i, 0)),
            pl.BlockSpec((block,) + legendre.shape[1:], lambda i: (i, 0, 0)),
        ],
        out_specs=pl.BlockSpec(shape, lambda i: (0, 0, 0, 0)),
        out_shape=pltpu.VMEM(shape, BF16),
        scratch_shapes=[
            pltpu.VMEM((size // LANES, parts * own * (block + 1), LANES), F32),
            pltpu.VMEM((legendre.shape[2] // LANES, own * (pitch + 1), LANES), F32),
        ],
        compiler_params=pltpu.CompilerParams(vmem_limit_bytes=54 * MIB),
        cost_estimate=cost(2 * parts * own * legendre.size, 2 * (spectral.size + legendre.size)),
        name="legendre",
    )(spectral, legendre)

def exchange(value, axis, pairs):
    return lax.ppermute(value, axis, [p for a, b in pairs for p in ((a, b), (b, a))])

def neighbours(axis, first):
    size = lax.axis_size(axis)
    return [(i, i + 1) for i in range(first, size - 1, 2)]

def partners(axis, k):
    return [(i, i ^ k) for i in range(lax.axis_size(axis)) if i < i ^ k]

def body(spectral, legendre, wave_ids, points, tracers, react_base, react_temp, active_ids):
    bands, tiles = lax.axis_size("lat"), lax.axis_size("lon")
    tile = tracers.shape[3]
    waves = wave_ids.shape[0]
    band, me = lax.axis_index("lat"), lax.axis_index("lon")

    sent = legendre_sums(spectral, legendre, bands)

    rows = points.shape[0]
    info = jnp.concatenate([jnp.stack([band, me]), active_ids, points]).astype(jnp.int32)
    sent, info = lax.optimization_barrier((sent, info))
    recv = lax.all_to_all(sent, "lat", split_axis=0, concat_axis=0, tiled=True)
    *ends, react = edges(tracers, react_base, react_temp, info)
    halos = [
        exchange(ends[0], "lat", neighbours("lat", 0)),
        exchange(ends[1], "lat", neighbours("lat", 1)),
        exchange(ends[2], "lon", neighbours("lon", 0)),
        exchange(ends[3], "lon", neighbours("lon", 1)),
    ]
    react, wave_ids = lax.optimization_barrier((react, wave_ids))
    table, twiddle = tables(info, wave_ids, rows, tiles * tile // LANES)
    recv, table, twiddle, react, halos = lax.optimization_barrier(
        (recv, table, twiddle, react, halos)
    )
    grids = synthesis(recv, table, twiddle, info, tiles, tile)

    middle, inner = list(range(tiles // 2, tiles)), list(range(1, tiles // 2))
    soon, late = middle[: tiles // 4], middle[tiles // 4 :]

    def send(value, k):
        return exchange(value, "lon", partners("lon", k))

    moved = {0: grids[0]} | {k: send(grids[k], k) for k in soon}
    new, active = None, {}
    for k in [0] + soon + late + inner:
        new, active[k] = chemistry(
            tracers, halos, moved[k], react, info, k, active_ids.shape[0], waves, new
        )
        if k:
            active[k] = send(active[k], k)
        else:
            rest = late + inner
            held, active[0] = lax.optimization_barrier(([grids[i] for i in rest], active[0]))
            moved |= {i: send(value, i) for i, value in zip(rest, held)}
    early, last = [0] + soon, late + inner
    spreaded = spread([active[k] for k in early], early, info, tiles, None)
    through = lax.optimization_barrier([active[k] for k in late])
    parts = lax.optimization_barrier(through + [active[k] for k in inner])
    return new, spread(parts, last, info, tiles, spreaded)

def solution(mesh):
    return jax.shard_map(
        body,
        mesh=mesh,
        in_specs=(
            P(None, "lon", "lat", None),
            P("lat", None, None),
            P(),
            P("lat"),
            P(None, None, "lat", "lon"),
            P(),
            P(),
            P(),
        ),
        out_specs=(P(None, None, "lat", "lon"), P(None, "lon", "lat", None)),
        check_vma=False,
    )
```
